32 devices in a mesh: section: 2 (over y), tensor: 2 (over x), dp: 8 (over z, core).
Axes of the slice: x: 2, y: 2, z: 4, core: 2. Of those that a mesh axis runs over, the one named last changes fastest.
Arguments:
- inputs: bfloat16 [2, 8192, 512], P(None, ('dp', 'tensor')), may hold values from -6 to 6
- cotangent: bfloat16 [2, 8192, 512], P(None, ('dp', 'tensor')), may hold values from -6 to 6
- lengths: int32 [2, 8], P(None, 'dp'), may hold values from 512 to 1024, as said below
- blocks: int32 [2, 8, 16, 3], P('section', 'tensor'), may hold values from 1 to 15
- feature_map: float32 [2, 8, 64, 256], P('section', 'tensor'), may hold values from -6 to 6
- w_qkv: bfloat16 [2, 512, 3, 512], P('section', None, None, 'tensor'), may hold values from -0.25 to 0.25
- b_qkv: bfloat16 [2, 3, 512], P('section', None, 'tensor'), may hold values from -4 to 4
- w_out: bfloat16 [2, 512, 512], P('section', 'tensor'), may hold values from -1 to 1
- w_up: bfloat16 [2, 512, 2048], P('section', None, 'tensor'), may hold values from -0.25 to 0.25
- b_up: bfloat16 [2, 2048], P('section', 'tensor'), may hold values from -4 to 4
- w_down: bfloat16 [2, 2048, 512], P('section', 'tensor'), may hold values from -0.125 to 0.125
- vector_params: bfloat16 [2, 6, 512], P('section'), may hold values from -4 to 4
Outputs:
- section_outputs: bfloat16 [2, 2, 8192, 512], P('section', None, ('dp', 'tensor'))
- input_grads: float32 [2, 2, 8192, 512], P('section', None, ('dp', 'tensor'))
- grad_qkv: float32 [2, 512, 3, 512], P('section', 'dp', None, 'tensor')
- grad_bqkv: float32 [2, 3, 512], P('section', None, ('tensor', 'dp'))
- grad_out: float32 [2, 512, 512], P('section', 'tensor', 'dp')
- grad_up: float32 [2, 512, 2048], P('section', 'dp', 'tensor')
- grad_bup: float32 [2, 2048], P('section', ('tensor', 'dp'))
- grad_down: float32 [2, 2048, 512], P('section', 'tensor', 'dp')
- grad_vectors: float32 [2, 6, 512], P('section', None, ('tensor', 'dp'))
The draws below stay inside these ranges and needn't reach their ends.
Inputs may be any that keep to these rules, and one draw needn't show every extreme that they name: `lengths`: in each sequence group, one micro-batch's sequence has all 1024 tokens; the others may be shorter. Entries name key blocks other than block 0 and may repeat within a list.
All inputs are finite; a program needn't handle non-finite values.
Results may differ from the reference program's by a relative error of at most 0.04.
Values may be sent and summed in bfloat16 or wider, within the bound.
No kernel may reach another device: no remote copies, remote signals or barrier semaphores. Data moves between devices by JAX's collectives and lax.ppermute only.
A program may use at most 320 MiB of HBM per device.

```python
import jax
import jax.numpy as jnp
from jax import lax

D = 512
HEADS = 8
HEAD = 64
FF = 2048
FEAT = 256
BLOCK = 64
NSEL = 3
MICRO = 2
SEQ_LEN = 1024
SECTIONS = 2
GROUPS = 8
TOKENS = 8192
NBLK = 16


def draw_lengths(key, part):
    key = jax.random.fold_in(key, 7)
    key_base, key_full = jax.random.split(key)
    base_len = jax.random.randint(key_base, (MICRO, GROUPS), SEQ_LEN // 2, SEQ_LEN + 1)
    full_batch = jax.random.randint(key_full, (GROUPS,), 0, MICRO)
    return jnp.where(jnp.arange(MICRO)[:, None] == full_batch[None, :], SEQ_LEN, base_len).astype(jnp.int32)


def with_ends(array, key, smallest, top_value):
    index_at = [jax.random.randint(jax.random.fold_in(key, axis), (), 0, length) for axis, length in enumerate(array.shape)]
    main_axis = array.shape.index(max(array.shape))
    neighbour = index_at[:main_axis] + [(index_at[main_axis] + 1) % array.shape[main_axis]] + index_at[main_axis + 1:]
    return array.at[tuple(index_at)].set(smallest).at[tuple(neighbour)].set(top_value)


def level_of(key, shape, cuts, least, largest):
    level, own = 1.0, jax.random.fold_in(key, 6)
    for axis_at, parts in cuts:
        draws = jnp.exp(jax.random.uniform(jax.random.fold_in(own, axis_at), (parts,), jnp.float32, least / len(cuts), largest / len(cuts)))
        level = level * jnp.repeat(draws, shape[axis_at] // parts).reshape([-1 if axis == axis_at else 1 for axis in range(len(shape))])
    return level


def bell_draw(key, extent, deviation, bound, pieces=(), dtype=jnp.bfloat16):
    entries = deviation * jax.random.normal(key, extent, jnp.float32)
    if pieces:
        entries = entries * level_of(key, extent, pieces, -0.22, 0.18)
    return jnp.clip(entries, -bound, bound).astype(dtype)


def setup_inputs(seed: int = 0) -> dict:
    keys = jax.random.split(jax.random.key(seed), 13)
    return {
        "inputs": bell_draw(keys[0], (MICRO, TOKENS, D), 1.0, 6.0, ((1, 16),)),
        "cotangent": bell_draw(keys[1], (MICRO, TOKENS, D), 1.0, 6.0, ((1, 16),)),
        "lengths": draw_lengths(jax.random.fold_in(keys[12], 71), 0),
        "blocks": with_ends(jax.random.randint(keys[3], (SECTIONS, HEADS, NBLK, NSEL), 1, NBLK), jax.random.fold_in(keys[3], 1), 1, NBLK - 1).astype(jnp.int32),
        "feature_map": bell_draw(keys[4], (SECTIONS, HEADS, HEAD, FEAT), 1.0, 6.0, ((0, 2), (1, 2)), jnp.float32),
        "w_qkv": bell_draw(keys[5], (SECTIONS, D, 3, D), D ** -0.5, 0.25, ((0, 2), (3, 2))),
        "b_qkv": bell_draw(keys[6], (SECTIONS, 3, D), 0.3, 4.0, ((0, 2), (2, 2))),
        "w_out": bell_draw(keys[7], (SECTIONS, D, D), (D // 16) ** -0.5, 1.0, ((0, 2), (1, 2))),
        "w_up": bell_draw(keys[8], (SECTIONS, D, FF), D ** -0.5, 0.25, ((0, 2), (2, 2))),
        "b_up": bell_draw(keys[9], (SECTIONS, FF), 0.3, 4.0, ((0, 2), (1, 2))),
        "w_down": bell_draw(keys[10], (SECTIONS, FF, D), FF ** -0.5, 0.125, ((0, 2), (1, 2))),
        "vector_params": bell_draw(keys[11], (SECTIONS, 6, D), 0.3, 4.0, ((0, 2),)),
    }


@jax.custom_vjp
def low(v):
    return lax.optimization_barrier(v.astype(jnp.bfloat16)).astype(jnp.float32)

@jax.custom_vjp
def low_back(v):
    return v

def low_keep(v):
    return (low(v), None)

def low_pass(kept, grad):
    return (grad,)

def back_keep(v):
    return (v, None)

def back_low(kept, grad):
    return (low(grad),)
low.defvjp(low_keep, low_pass)
low_back.defvjp(back_keep, back_low)
norm_eps = 1e-05
highest = lax.Precision.HIGHEST

def norm_rows(residual, gain_vec, shift_vec):
    row_mean = lax.optimization_barrier(jnp.mean(residual, axis=-1, keepdims=True))
    centred = residual - row_mean
    variance = lax.optimization_barrier(jnp.mean(centred * centred, axis=-1, keepdims=True))
    return centred * lax.rsqrt(variance + norm_eps) * (1.0 + gain_vec) + shift_vec

def pick_blocks(table_in, chosen):
    head_count, block_count = (chosen.shape[0], chosen.shape[1])
    blocks_in = table_in.reshape(head_count, block_count, BLOCK, table_in.shape[-1])
    taken_rows = jax.vmap(lambda one_table, index_rows: one_table[index_rows])(blocks_in, chosen)
    return taken_rows.reshape(head_count, block_count, -1, table_in.shape[-1])

def feature_of(vectors, features):
    feature_scale = HEAD ** (-0.25)
    projected = jnp.einsum('hld,hdf->hlf', vectors, features, precision=highest) * feature_scale
    return jnp.exp(projected - lax.optimization_barrier(jnp.sum(vectors * vectors, axis=-1, keepdims=True)) * (0.5 * feature_scale * feature_scale))

def attend(queries, key_vecs, value_vecs, length, block_list, features):
    head_count = queries.shape[0]
    block_count = SEQ_LEN // BLOCK
    key_live = (jnp.arange(SEQ_LEN) < length).astype(jnp.float32)
    chosen = jnp.concatenate([jnp.zeros((head_count, block_count, 1), jnp.int32), block_list.astype(jnp.int32)], axis=2)
    query_blocks = queries.reshape(head_count, block_count, BLOCK, HEAD)
    picked_keys = pick_blocks(key_vecs, chosen)
    picked_values = pick_blocks(value_vecs, chosen)
    picked_live = key_live.reshape(block_count, BLOCK)[chosen].reshape(head_count, block_count, -1)
    scores = jnp.einsum('hnqd,hnkd->hnqk', query_blocks, picked_keys, precision=highest)
    scores = low_back(scores * HEAD ** (-0.5))
    usable = picked_live[:, :, None, :] > 0.5
    scores = jnp.where(usable, scores, -1e+30)
    row_max = lax.optimization_barrier(jnp.max(scores, axis=-1, keepdims=True))
    weights_raw = jnp.exp(scores - row_max) * picked_live[:, :, None, :]
    weights_f = weights_raw / lax.optimization_barrier(jnp.sum(weights_raw, axis=-1, keepdims=True))
    sparse_out = jnp.einsum('hnqk,hnkd->hnqd', low(weights_f), picked_values, precision=highest)
    sparse_out = sparse_out.reshape(head_count, SEQ_LEN, HEAD)
    query_feats = feature_of(queries, features)
    key_feats = feature_of(key_vecs, features) * key_live[None, :, None]
    moments = jnp.einsum('hlf,hld->hfd', key_feats, value_vecs, precision=highest)
    totals = lax.optimization_barrier(jnp.sum(key_feats, axis=1))
    numerator = jnp.einsum('hlf,hfd->hld', query_feats, moments, precision=highest)
    denominator = jnp.einsum('hlf,hf->hl', query_feats, totals, precision=highest)
    return sparse_out + numerator / denominator[:, :, None]

def layer(residual, layer_params, length, block_list, features):
    qkv_mat, qkv_bias, out_mat, up_mat, up_bias, down_mat, vectors = layer_params
    normed = low(norm_rows(residual, vectors[0], vectors[1]))
    projected = jnp.einsum('ld,dce->lce', normed, qkv_mat, precision=highest) + qkv_bias[None]
    projected = low(low_back(projected))
    head_parts = projected.reshape(SEQ_LEN, 3, HEADS, HEAD).transpose(1, 2, 0, 3)
    mixed_heads = attend(head_parts[0], head_parts[1], head_parts[2], length, block_list, features)
    mixed_low = low(low_back(mixed_heads.transpose(1, 0, 2).reshape(SEQ_LEN, D)))
    hidden_res = residual + low_back(jnp.dot(mixed_low, out_mat, precision=highest) + vectors[4])
    normed_two = low(norm_rows(hidden_res, vectors[2], vectors[3]))
    pre_active = low_back(jnp.dot(normed_two, up_mat, precision=highest) + up_bias)
    active = low(jax.nn.gelu(pre_active, approximate=False))
    return hidden_res + low_back(jnp.dot(active, down_mat, precision=highest) + vectors[5])

def reference(inputs, cotangent, lengths, blocks, feature_map, w_qkv, b_qkv, w_out, w_up, b_up, w_down, vector_params):
    single = jnp.float32
    params = tuple((weight_set.astype(single) for weight_set in (w_qkv, b_qkv, w_out, w_up, b_up, w_down, vector_params)))
    seq_count = MICRO * GROUPS
    seq_inputs = inputs.astype(single).reshape(seq_count, SEQ_LEN, D)
    seq_lengths = lengths.reshape(seq_count).astype(jnp.int32)
    offsets = jnp.zeros((seq_count, SEQ_LEN, D), single)
    block_tables = blocks.astype(jnp.int32)
    features_all = feature_map.astype(single)

    def forward(params, seq_inputs, offsets):

        def one_sequence(entry_set):
            residual, offset, length = entry_set
            first_params = tuple((weight_set[0] for weight_set in params))
            second_params = tuple((weight_set[1] for weight_set in params))
            first_out = low(layer(residual, first_params, length, block_tables[0], features_all[0]))
            second_in = low_back(first_out) + offset
            second_out = low(layer(second_in, second_params, length, block_tables[1], features_all[1]))
            return (first_out, second_out)
        return lax.map(jax.checkpoint(one_sequence), (seq_inputs, offsets, seq_lengths))
    (firsts, seconds), pullback = jax.vjp(forward, params, seq_inputs, offsets)
    grad_params, grad_inputs, grad_offsets = pullback((jnp.zeros_like(firsts), cotangent.astype(single).reshape(seq_count, SEQ_LEN, D)))
    section_outputs = jnp.stack([firsts, seconds]).reshape(SECTIONS, MICRO, TOKENS, D).astype(jnp.bfloat16)
    input_grads = jnp.stack([grad_inputs, grad_offsets]).reshape(SECTIONS, MICRO, TOKENS, D)
    grad_qkv, grad_bqkv, grad_out, grad_up, grad_bup, grad_down, grad_vectors = grad_params
    return (section_outputs, input_grads, grad_qkv, grad_bqkv, grad_out, grad_up, grad_bup, grad_down, grad_vectors)
```

```python
import functools

import jax
import jax.numpy as jnp
from jax import lax
from jax.experimental import pallas as pl
from jax.experimental.pallas import tpu as pltpu
from jax.sharding import PartitionSpec as P

HEAD = 64
BLOCK = 64
NORM_EPS = 1e-5
bf = jnp.bfloat16
f32 = jnp.float32
LOG2E = 1.4426950408889634
F_SCALE = HEAD ** -0.25
ROWS = 256
VMEM_BYTES = 60 * 1024 * 1024
ANY = pl.BlockSpec(memory_space=pl.ANY)
WHOLE = pl.BlockSpec(memory_space=pltpu.VMEM)
SCALARS = pl.BlockSpec(memory_space=pltpu.SMEM)


def contract(left, right, left_dim, right_dim):
    return lax.dot_general(
        left, right, (((left_dim,), (right_dim,)), ((), ())), preferred_element_type=f32
    )


def pick_source(layer_no):
    section_no = lax.axis_index("section")
    same = lax.rem(lax.axis_index("dp"), 2) == lax.axis_index("tensor")
    return jnp.where(
        section_no == layer_no, jnp.where(same, 0, 1), jnp.where(same, 1, 2)
    )


def start_pick(source, candidates, target, sem):
    for number, candidate in enumerate(candidates):

        @pl.when(source == number)
        def _():
            pltpu.make_async_copy(candidate, target, sem).start()


def wait_pick(candidates, target, sem):
    pltpu.make_async_copy(candidates[0], target, sem).wait()


def small_row(small, row, width):
    return small[row : row + 1, :width].astype(f32)


def norm_stats(value):
    mean = jnp.mean(value, axis=-1, keepdims=True)
    centred = value - mean
    variance = jnp.mean(centred * centred, axis=-1, keepdims=True)
    scale = lax.rsqrt(variance + NORM_EPS)
    return centred * scale, scale


def lane_masks():
    lane = lax.broadcasted_iota(jnp.int32, (1, 2 * HEAD), 1)
    return lane < HEAD, lane >= HEAD


def swap_halves(value):
    return pltpu.roll(value, HEAD, 1)


def attn_forward_kernel(layer_no, n_heads, length_ref, blocks_ref, *refs):
    if layer_no == 0:
        x_ref, refs = refs[0], refs[1:]
    else:
        hidden_ref, part_a, part_b, refs = refs[0], refs[1], refs[2], refs[3:]
        small_prev, refs = refs[:3], refs[3:]
    small_c, wqkv_c, wout_c, fm_c, refs = refs[:3], refs[3:6], refs[6:9], refs[9:12], refs[12:]
    if layer_no == 1:
        x_ref, refs = refs[0], refs[1:]
    (branch_ref, qkv_out, normed_out, probs_out, qf_out, kf_out, mt_out, mixed_out) = refs[:8]
    (small, wqkv, wout, fm, qkv, normed, probs, qfeat, kfeat, mt, mixed, fcat, perf, qmask,
     in_sem, out_sem) = refs[8:24]
    seq, width = normed.shape
    n_chunks = seq // ROWS
    pairs = n_heads // 2
    feat = fm.shape[2]
    source = pick_source(layer_no)
    if layer_no == 1:
        small_before = refs[24]
        before = pick_source(0)
        start_pick(before, small_prev, small_before, in_sem.at[4])
    start_pick(source, small_c, small, in_sem.at[0])
    start_pick(source, wqkv_c, wqkv, in_sem.at[1])
    start_pick(source, fm_c, fm, in_sem.at[2])
    start_pick(source, wout_c, wout, in_sem.at[3])
    wait_pick(small_c, small, in_sem.at[0])
    if layer_no == 1:
        wait_pick(small_prev, small_before, in_sem.at[4])
    wait_pick(wqkv_c, wqkv, in_sem.at[1])
    length = length_ref[0]
    gain = 1.0 + small_row(small, 4, width)
    shift = small_row(small, 5, width)

    @pl.loop(0, n_chunks)
    def _(chunk):
        rows = pl.ds(pl.multiple_of(chunk * ROWS, ROWS), ROWS)
        if layer_no == 0:
            x = x_ref[rows, :].astype(f32)
        else:
            total = part_a[rows, :].astype(f32) + part_b[rows, :].astype(f32)
            x_low = (hidden_ref[rows, :] + total + small_row(small_before, 9, width)).astype(bf)
            x_ref[rows, :] = x_low
            x = x_low.astype(f32)
        zhat, _ = norm_stats(x)
        low = (zhat * gain + shift).astype(bf)
        normed[rows, :] = low
        for part in range(3):
            cols = n_heads * HEAD
            out = jnp.dot(low, wqkv[part], preferred_element_type=f32)
            qkv[part, rows, :] = (out + small_row(small, part, cols)).astype(bf)

    copies = [
        pltpu.make_async_copy(qkv, qkv_out, out_sem.at[0]),
        pltpu.make_async_copy(normed, normed_out, out_sem.at[1]),
    ]
    for copy in copies:
        copy.start()
    wait_pick(fm_c, fm, in_sem.at[2])
    in_first, in_second = lane_masks()
    masks = (in_first, in_second)
    for pair in range(pairs):
        cols = slice(pair * 2 * HEAD, (pair + 1) * 2 * HEAD)
        zero = jnp.zeros((HEAD, feat), bf)
        for a in range(2):
            scaled = fm[2 * pair + a] * (F_SCALE * LOG2E)
            high = scaled.astype(bf)
            rest = (scaled - high.astype(f32)).astype(bf)
            for part, piece in enumerate((high, rest)):
                row = part * 2 * HEAD + a * HEAD
                fcat[row : row + HEAD, a * feat : (a + 1) * feat] = piece
                fcat[row : row + HEAD, (1 - a) * feat : (2 - a) * feat] = zero

        def features(vectors):
            proj = jnp.dot(
                jnp.concatenate([vectors, vectors], axis=1), fcat[...], preferred_element_type=f32
            )
            value = vectors.astype(f32)
            square = value * value * (0.5 * F_SCALE * F_SCALE * LOG2E)
            return [
                jnp.exp2(
                    proj[:, a * feat : (a + 1) * feat]
                    - jnp.sum(jnp.where(masks[a], square, 0.0), axis=-1, keepdims=True)
                )
                for a in range(2)
            ]

        @pl.loop(0, n_chunks)
        def _(chunk):
            base = pl.multiple_of(chunk * ROWS, ROWS)
            rows = pl.ds(base, ROWS)
            live = lax.broadcasted_iota(jnp.int32, (ROWS, 1), 0) + base < length
            found = features(qkv[1, rows, cols])
            for a in range(2):
                kfeat[pair, rows, a * feat : (a + 1) * feat] = jnp.where(live, found[a], 0.0).astype(bf)

        values = qkv[2, :, cols].astype(f32)
        for a in range(2):
            extended = jnp.where(masks[a], values, 1.0).astype(bf)
            moment = contract(extended, kfeat[pair, :, a * feat : (a + 1) * feat], 0, 0)
            mt[2 * pair + a] = moment.astype(bf)

        @pl.loop(0, n_chunks)
        def _(chunk):
            rows = pl.ds(pl.multiple_of(chunk * ROWS, ROWS), ROWS)
            query = qkv[0, rows, cols]
            found = features(query)
            out = None
            for a in range(2):
                low = found[a].astype(bf)
                qfeat[pair, rows, a * feat : (a + 1) * feat] = low
                numer = contract(low, mt[2 * pair + a], 1, 1)
                value = numer / swap_halves(numer)
                out = value if a == 0 else jnp.where(in_first, out, value)
                scaled = query.astype(f32) * (HEAD ** -0.5)
                qmask[a, rows, :] = jnp.where(masks[a], scaled, 0.0).astype(bf)
            perf[rows, :] = out

        lane = lax.broadcasted_iota(jnp.int32, (1, 4 * BLOCK), 1)
        within = lax.rem(lane, BLOCK)

        @pl.loop(0, seq // BLOCK, unroll=2)
        def _(block):
            rows = pl.ds(pl.multiple_of(block * BLOCK, BLOCK), BLOCK)
            out = None
            for a in range(2):
                head = 2 * pair + a
                at = (head * (seq // BLOCK) + block) * 3
                starts = [pl.multiple_of(blocks_ref[at + i] * BLOCK, BLOCK) for i in range(3)]
                keys = jnp.concatenate(
                    [qkv[1, 0:BLOCK, cols]] + [qkv[1, pl.ds(b, BLOCK), cols] for b in starts], axis=0
                )
                values = jnp.concatenate(
                    [qkv[2, 0:BLOCK, cols]] + [qkv[2, pl.ds(b, BLOCK), cols] for b in starts], axis=0
                )
                position = within + jnp.where(
                    lane < BLOCK,
                    0,
                    jnp.where(
                        lane < 2 * BLOCK,
                        starts[0],
                        jnp.where(lane < 3 * BLOCK, starts[1], starts[2]),
                    ),
                )
                scores = contract(qmask[a, rows, :], keys, 1, 1)
                scores = jnp.where(position < length, scores, -1e30)
                top = jnp.max(scores, axis=-1, keepdims=True)
                raw = jnp.exp(scores - top)
                low = (raw * (1.0 / jnp.sum(raw, axis=-1, keepdims=True))).astype(bf)
                probs[head, rows, :] = low
                value = jnp.dot(low, values, preferred_element_type=f32)
                out = value if a == 0 else jnp.where(in_first, out, value)
            mixed[rows, cols] = (out + perf[rows, :]).astype(bf)

        more = [
            pltpu.make_async_copy(probs.at[2 * pair : 2 * pair + 2], probs_out.at[2 * pair : 2 * pair + 2], out_sem.at[2 + 4 * pair]),
            pltpu.make_async_copy(qfeat.at[pair], qf_out.at[pair], out_sem.at[3 + 4 * pair]),
            pltpu.make_async_copy(kfeat.at[pair], kf_out.at[pair], out_sem.at[4 + 4 * pair]),
            pltpu.make_async_copy(mt.at[2 * pair : 2 * pair + 2], mt_out.at[2 * pair : 2 * pair + 2], out_sem.at[5 + 4 * pair]),
        ]
        for copy in more:
            copy.start()
        copies += more
    wait_pick(wout_c, wout, in_sem.at[3])

    @pl.loop(0, n_chunks)
    def _(chunk):
        rows = pl.ds(pl.multiple_of(chunk * ROWS, ROWS), ROWS)
        low = mixed[rows, :]
        mixed_out[rows, :] = low
        branch_ref[rows, :] = jnp.dot(low, wout[...], preferred_element_type=f32).astype(bf)

    for copy in copies:
        copy.wait()


def attn_forward(layer_no, length, blocks, x_parts, weights, small_before):
    small_c, wqkv_c, wout_c, fm_c = weights
    _, width, part_width = wqkv_c[0].shape
    n_heads, _, feat = fm_c[0].shape
    seq = x_parts[0].shape[0]
    pairs = n_heads // 2
    shape = jax.ShapeDtypeStruct
    outs = [
        shape((seq, width), bf),
        shape((3, seq, part_width), bf),
        shape((seq, width), bf),
        shape((n_heads, seq, 4 * BLOCK), bf),
        shape((pairs, seq, 2 * feat), bf),
        shape((pairs, seq, 2 * feat), bf),
        shape((n_heads, 2 * HEAD, feat), bf),
        shape((seq, part_width), bf),
    ]
    out_specs = [WHOLE, ANY, ANY, ANY, ANY, ANY, ANY, WHOLE]
    scratch = [
        pltpu.VMEM(small_c[0].shape, bf),
        pltpu.VMEM(wqkv_c[0].shape, bf),
        pltpu.VMEM(wout_c[0].shape, bf),
        pltpu.VMEM(fm_c[0].shape, f32),
        pltpu.VMEM((3, seq, part_width), bf),
        pltpu.VMEM((seq, width), bf),
        pltpu.VMEM((n_heads, seq, 4 * BLOCK), bf),
        pltpu.VMEM((pairs, seq, 2 * feat), bf),
        pltpu.VMEM((pairs, seq, 2 * feat), bf),
        pltpu.VMEM((n_heads, 2 * HEAD, feat), bf),
        pltpu.VMEM((seq, part_width), bf),
        pltpu.VMEM((4 * HEAD, 2 * feat), bf),
        pltpu.VMEM((seq, 2 * HEAD), f32),
        pltpu.VMEM((2, seq, 2 * HEAD), bf),
        pltpu.SemaphoreType.DMA((5,)),
        pltpu.SemaphoreType.DMA((2 + 4 * pairs,)),
    ]
    operands = list(x_parts)
    specs = [WHOLE] * len(x_parts)
    if layer_no == 1:
        operands += list(small_before)
        specs += [ANY] * 3
        outs = [shape((seq, width), bf)] + outs
        out_specs = [WHOLE] + out_specs
        scratch.append(pltpu.VMEM(small_c[0].shape, bf))
    for group in weights:
        operands += list(group)
        specs += [ANY] * 3
    return pl.pallas_call(
        functools.partial(attn_forward_kernel, layer_no, n_heads),
        out_shape=outs,
        in_specs=[SCALARS, SCALARS] + specs,
        out_specs=out_specs,
        scratch_shapes=scratch,
        compiler_params=pltpu.CompilerParams(vmem_limit_bytes=VMEM_BYTES),
        cost_estimate=pl.CostEstimate(
            flops=4 * 10**9, bytes_accessed=16 * 2**20, transcendentals=3 * 2**20
        ),
        name=f"attn_forward_{layer_no}",
    )(length, blocks, *operands)


def gelu_parts(value):
    size = jnp.abs(value) * (0.5 ** 0.5)
    inverse = 1.0 / (1.0 + 0.3275911 * size)
    poly = inverse * (
        0.254829592
        + inverse
        * (-0.284496736 + inverse * (1.421413741 + inverse * (-1.453152027 + inverse * 1.061405429)))
    )
    bell = jnp.exp(-0.5 * value * value)
    tail = 0.5 * poly * bell
    below = jnp.where(value >= 0.0, 1.0 - tail, tail)
    return value * below, below + value * bell * (0.5 / 3.141592653589793) ** 0.5


def ffn_forward_kernel(layer_no, n_in, *refs):
    x_ref, part_a, part_b = refs[:3]
    small_c, wup_c, wdown_c = refs[3:6], refs[6:9], refs[9:12]
    out_ref, hidden_ref, normed_ref, active_ref, slope_ref = refs[12:17]
    small, wup, wdown, sems = refs[17:]

    @pl.when(pl.program_id(0) == 0)
    def _():
        source = pick_source(layer_no)
        start_pick(source, small_c, small, sems.at[0])
        start_pick(source, wup_c, wup, sems.at[1])
        start_pick(source, wdown_c, wdown, sems.at[2])
        wait_pick(small_c, small, sems.at[0])
        wait_pick(wup_c, wup, sems.at[1])
        wait_pick(wdown_c, wdown, sems.at[2])

    width = x_ref.shape[1]
    units = wup.shape[1]
    branch = part_a[...].astype(f32) + part_b[...].astype(f32)
    hidden = x_ref[...].astype(f32) + branch + small_row(small, 8, width)
    hidden_ref[...] = hidden
    zhat, _ = norm_stats(hidden)
    low = (zhat * (1.0 + small_row(small, 6, width)) + small_row(small, 7, width)).astype(bf)
    normed_ref[...] = low
    total = None
    step = 256
    for at in range(0, units, step):
        upper = jnp.dot(low, wup[:, at : at + step], preferred_element_type=f32)
        active, slope = gelu_parts(upper + small[3:4, at : at + step].astype(f32))
        active = active.astype(bf)
        active_ref[:, at : at + step] = active
        slope_ref[:, at : at + step] = slope.astype(bf)
        term = jnp.dot(active, wdown[at : at + step, :], preferred_element_type=f32)
        total = term if total is None else total + term
    out_ref[...] = total.astype(bf)


def ffn_forward(layer_no, x, part_a, part_b, weights):
    small_c, wup_c, wdown_c = weights
    seq, width = x.shape
    units = wup_c[0].shape[1]
    shape = jax.ShapeDtypeStruct
    rows = lambda cols: pl.BlockSpec((ROWS, cols), lambda i: (i, 0))
    return pl.pallas_call(
        functools.partial(ffn_forward_kernel, layer_no, 3),
        grid=(seq // ROWS,),
        out_shape=[
            shape((seq, width), bf),
            shape((seq, width), f32),
            shape((seq, width), bf),
            shape((seq, units), bf),
            shape((seq, units), bf),
        ],
        in_specs=[rows(width)] * 3 + [ANY] * 9,
        out_specs=[rows(width), rows(width), rows(width), rows(units), rows(units)],
        scratch_shapes=[
            pltpu.VMEM(small_c[0].shape, bf),
            pltpu.VMEM(wup_c[0].shape, bf),
            pltpu.VMEM(wdown_c[0].shape, bf),
            pltpu.SemaphoreType.DMA((3,)),
        ],
        compiler_params=pltpu.CompilerParams(vmem_limit_bytes=VMEM_BYTES),
        cost_estimate=pl.CostEstimate(
            flops=4 * seq * width * units, bytes_accessed=14 * 2**20, transcendentals=seq * units
        ),
        name=f"ffn_forward_{layer_no}",
    )(x, part_a, part_b, *small_c, *wup_c, *wdown_c)


def ffn_backward_kernel(layer_no, grad_ref, slope_ref, *refs):
    wup_c, wdown_c = refs[:3], refs[3:6]
    out_ref, gupper_ref, bias_ref = refs[6:9]
    wup, wdown, sems = refs[9:]

    @pl.when(pl.program_id(0) == 0)
    def _():
        source = pick_source(layer_no)
        start_pick(source, wdown_c, wdown, sems.at[0])
        start_pick(source, wup_c, wup, sems.at[1])
        bias_ref[...] = jnp.zeros_like(bias_ref)
        wait_pick(wdown_c, wdown, sems.at[0])
        wait_pick(wup_c, wup, sems.at[1])

    units = wup.shape[1]
    grad = grad_ref[...]
    total = None
    step = 256
    for at in range(0, units, step):
        gactive = contract(grad, wdown[at : at + step, :], 1, 1)
        gupper = (gactive * slope_ref[:, at : at + step].astype(f32)).astype(bf)
        gupper_ref[:, at : at + step] = gupper
        bias_ref[:, at : at + step] += fold_rows(gupper.astype(f32))
        term = contract(gupper, wup[:, at : at + step], 1, 1)
        total = term if total is None else total + term
    out_ref[...] = total.astype(bf)


def fold_rows(value):
    rows, cols = value.shape
    return jnp.sum(value.reshape(rows // 8, 8, cols), axis=0)


def ffn_backward(layer_no, grad, slope, weights):
    wup_c, wdown_c = weights
    seq, width = grad.shape
    units = wup_c[0].shape[1]
    shape = jax.ShapeDtypeStruct
    rows = lambda cols: pl.BlockSpec((ROWS, cols), lambda i: (i, 0))
    return pl.pallas_call(
        functools.partial(ffn_backward_kernel, layer_no),
        grid=(seq // ROWS,),
        out_shape=[shape((seq, width), bf), shape((seq, units), bf), shape((8, units), f32)],
        in_specs=[rows(width), rows(units)] + [ANY] * 6,
        out_specs=[rows(width), rows(units), pl.BlockSpec((8, units), lambda i: (0, 0))],
        scratch_shapes=[
            pltpu.VMEM(wup_c[0].shape, bf),
            pltpu.VMEM(wdown_c[0].shape, bf),
            pltpu.SemaphoreType.DMA((2,)),
        ],
        compiler_params=pltpu.CompilerParams(vmem_limit_bytes=VMEM_BYTES),
        cost_estimate=pl.CostEstimate(
            flops=4 * seq * width * units, bytes_accessed=8 * 2**20, transcendentals=0
        ),
        name=f"ffn_backward_{layer_no}",
    )(grad, slope, *wup_c, *wdown_c)


def attn_backward_kernel(layer_no, n_heads, blocks_ref, *refs):
    gy_ref, part_a, part_b, hidden_ref = refs[:4]
    qkv_in, probs_in, qf_in, kf_in, mt_in = refs[4:9]
    small_c, wqkv_c, wout_c, fm_c, refs = refs[9:12], refs[12:15], refs[15:18], refs[18:21], refs[21:]
    out_ref, ghidden_ref, gbranch_ref, dqkv_ref, vec_ref, bias_ref, refs = *refs[:6], refs[6:]
    (small, wqkv, wout, fm, qkv, probs, qfeat, kfeat, mt, gmix, gmask, qmask, gext, gt, fback,
     dq, dk, dv, sem) = refs
    seq, width = gy_ref.shape
    n_chunks = seq // ROWS
    pairs = n_heads // 2
    feat = fm.shape[2]
    source = pick_source(layer_no)
    start_pick(source, small_c, small, sem.at[0])
    start_pick(source, wout_c, wout, sem.at[1])
    loads = [
        pltpu.make_async_copy(qkv_in, qkv, sem.at[2]),
        pltpu.make_async_copy(mt_in, mt, sem.at[3]),
        pltpu.make_async_copy(qf_in, qfeat, sem.at[4]),
        pltpu.make_async_copy(kf_in, kfeat, sem.at[5]),
        pltpu.make_async_copy(probs_in, probs, sem.at[6]),
    ]
    for load in loads:
        load.start()
    start_pick(source, fm_c, fm, sem.at[7])
    start_pick(source, wqkv_c, wqkv, sem.at[8])
    vec_ref[...] = jnp.zeros_like(vec_ref)
    bias_ref[...] = jnp.zeros_like(bias_ref)
    wait_pick(small_c, small, sem.at[0])
    wait_pick(wout_c, wout, sem.at[1])
    gain = 1.0 + small_row(small, 6, width)
    in_first, in_second = lane_masks()
    masks = (in_first, in_second)

    @pl.loop(0, n_chunks)
    def _(chunk):
        rows = pl.ds(pl.multiple_of(chunk * ROWS, ROWS), ROWS)
        gnormed = part_a[rows, :].astype(f32) + part_b[rows, :].astype(f32)
        zhat, scale = norm_stats(hidden_ref[rows, :])
        scaled = gnormed * gain
        gy = gy_ref[rows, :].astype(f32)
        mean_one = jnp.mean(scaled, axis=-1, keepdims=True)
        mean_two = jnp.mean(scaled * zhat, axis=-1, keepdims=True)
        ghidden = gy + (scaled - mean_one - zhat * mean_two) * scale
        ghidden_ref[rows, :] = ghidden
        low = ghidden.astype(bf)
        gbranch_ref[rows, :] = low
        vec_ref[0] += fold_rows(gnormed * zhat)
        vec_ref[1] += fold_rows(gnormed)
        vec_ref[2] += fold_rows(low.astype(f32))
        vec_ref[3] += fold_rows(gy)
        gmix_low = contract(low, wout[...], 1, 1).astype(bf)
        gmix[rows, :] = gmix_low

    for load in loads[:4]:
        load.wait()
    wait_pick(fm_c, fm, sem.at[7])
    for pair in range(pairs):
        cols = slice(pair * 2 * HEAD, (pair + 1) * 2 * HEAD)
        for a in range(2):
            plain = fm[2 * pair + a] * F_SCALE
            high = plain.astype(bf).astype(f32)
            ones = jnp.ones((HEAD, feat), f32)
            none = jnp.zeros((HEAD, feat), f32)
            stack = [high, ones] if a == 0 else [ones, high]
            stack += [plain - high, none] if a == 0 else [none, plain - high]
            fback[a] = jnp.concatenate(stack, axis=0).astype(bf)

        def feature_back(a, gfeat, feats, vectors):
            gexpo = (gfeat * feats.astype(f32)).astype(bf)
            both = contract(gexpo, fback[a], 1, 1)
            both = both[:, : 2 * HEAD] + both[:, 2 * HEAD :]
            return both - (F_SCALE * F_SCALE) * swap_halves(both) * vectors

        @pl.loop(0, n_chunks)
        def _(chunk):
            rows = pl.ds(pl.multiple_of(chunk * ROWS, ROWS), ROWS)
            grad = gmix[rows, cols].astype(f32)
            query = qkv[0, rows, cols].astype(f32)
            out = None
            for a in range(2):
                gmask[a, rows, :] = jnp.where(masks[a], grad, 0.0).astype(bf)
                qmask[a, rows, :] = jnp.where(masks[a], query * (HEAD ** -0.5), 0.0).astype(bf)
                feats = qfeat[pair, rows, a * feat : (a + 1) * feat]
                moment = mt[2 * pair + a]
                numer = contract(feats, moment, 1, 1)
                inverse = 1.0 / swap_halves(numer)
                gnumer = grad * inverse
                other = swap_halves(gnumer * numer * inverse)
                both = jnp.where(masks[a], gnumer, -other).astype(bf)
                gext[a, rows, :] = both
                gfeat = jnp.dot(both, moment, preferred_element_type=f32)
                value = feature_back(a, gfeat, feats, query)
                out = value if a == 0 else jnp.where(in_first, out, value)
            dq[rows, :] = out

        for a in range(2):
            gt[a] = contract(gext[a], qfeat[pair, :, a * feat : (a + 1) * feat], 0, 0).astype(bf)

        @pl.loop(0, n_chunks)
        def _(chunk):
            rows = pl.ds(pl.multiple_of(chunk * ROWS, ROWS), ROWS)
            key = qkv[1, rows, cols].astype(f32)
            value_f = qkv[2, rows, cols].astype(f32)
            dk_out, dv_out = None, None
            for a in range(2):
                extended = jnp.where(masks[a], value_f, 1.0).astype(bf)
                feats = kfeat[pair, rows, a * feat : (a + 1) * feat]
                gfeat = jnp.dot(extended, gt[a], preferred_element_type=f32)
                dk_one = feature_back(a, gfeat, feats, key)
                dv_one = contract(feats, gt[a], 1, 1)
                dk_out = dk_one if a == 0 else jnp.where(in_first, dk_out, dk_one)
                dv_out = dv_one if a == 0 else jnp.where(in_first, dv_out, dv_one)
            dk[rows, :] = dk_out
            dv[rows, :] = dv_out

        if pair == 0:
            loads[4].wait()

        @pl.loop(0, seq // BLOCK, unroll=2)
        def _(block):
            rows = pl.ds(pl.multiple_of(block * BLOCK, BLOCK), BLOCK)
            out = None
            for a in range(2):
                head = 2 * pair + a
                at = (head * (seq // BLOCK) + block) * 3
                starts = [pl.multiple_of(blocks_ref[at + i] * BLOCK, BLOCK) for i in range(3)]
                keys = jnp.concatenate(
                    [qkv[1, 0:BLOCK, cols]] + [qkv[1, pl.ds(b, BLOCK), cols] for b in starts], axis=0
                )
                values = jnp.concatenate(
                    [qkv[2, 0:BLOCK, cols]] + [qkv[2, pl.ds(b, BLOCK), cols] for b in starts], axis=0
                )
                grad = gmask[a, rows, :]
                weights = probs[head, rows, :]
                weights_f = weights.astype(f32)
                gweights = contract(grad, values, 1, 1)
                inner = jnp.sum(weights_f * gweights, axis=-1, keepdims=True)
                gscores = (weights_f * (gweights - inner)).astype(bf)
                value = jnp.dot(gscores, keys, preferred_element_type=f32) * (HEAD ** -0.5)
                out = value if a == 0 else jnp.where(in_first, out, value)
                dkeys = contract(gscores, qmask[a, rows, :], 0, 0)
                dvalues = contract(weights, grad, 0, 0)
                for slot, start in enumerate([0] + starts):
                    here = slice(slot * BLOCK, (slot + 1) * BLOCK)
                    dk[pl.ds(start, BLOCK), :] += dkeys[here, :]
                    dv[pl.ds(start, BLOCK), :] += dvalues[here, :]
            dq[rows, :] += out

        @pl.loop(0, n_chunks)
        def _(chunk):
            rows = pl.ds(pl.multiple_of(chunk * ROWS, ROWS), ROWS)
            for part, total in enumerate((dq, dk, dv)):
                low = total[rows, :].astype(bf)
                dqkv_ref[part, rows, cols] = low
                bias_ref[part, :, cols] += fold_rows(low.astype(f32))

    wait_pick(wqkv_c, wqkv, sem.at[8])

    @pl.loop(0, n_chunks)
    def _(chunk):
        rows = pl.ds(pl.multiple_of(chunk * ROWS, ROWS), ROWS)
        total = None
        for part in range(3):
            term = contract(dqkv_ref[part, rows, :], wqkv[part], 1, 1)
            total = term if total is None else total + term
        out_ref[rows, :] = total.astype(bf)


def attn_backward(layer_no, blocks, gy, part_a, part_b, hidden, kept, weights):
    small_c, wqkv_c, wout_c, fm_c = weights
    seq, width = gy.shape
    _, _, part_width = wqkv_c[0].shape
    n_heads, _, feat = fm_c[0].shape
    pairs = n_heads // 2
    shape = jax.ShapeDtypeStruct
    operands = [gy, part_a, part_b, hidden, *kept]
    for group in weights:
        operands += list(group)
    return pl.pallas_call(
        functools.partial(attn_backward_kernel, layer_no, n_heads),
        out_shape=[
            shape((seq, width), bf),
            shape((seq, width), f32),
            shape((seq, width), bf),
            shape((3, seq, part_width), bf),
            shape((4, 8, width), f32),
            shape((3, 8, part_width), f32),
        ],
        in_specs=[SCALARS] + [WHOLE] * 4 + [ANY] * 17,
        out_specs=[WHOLE] * 6,
        scratch_shapes=[
            pltpu.VMEM(small_c[0].shape, bf),
            pltpu.VMEM(wqkv_c[0].shape, bf),
            pltpu.VMEM(wout_c[0].shape, bf),
            pltpu.VMEM(fm_c[0].shape, f32),
            pltpu.VMEM((3, seq, part_width), bf),
            pltpu.VMEM((n_heads, seq, 4 * BLOCK), bf),
            pltpu.VMEM((pairs, seq, 2 * feat), bf),
            pltpu.VMEM((pairs, seq, 2 * feat), bf),
            pltpu.VMEM((n_heads, 2 * HEAD, feat), bf),
            pltpu.VMEM((seq, part_width), bf),
            pltpu.VMEM((2, seq, 2 * HEAD), bf),
            pltpu.VMEM((2, seq, 2 * HEAD), bf),
            pltpu.VMEM((2, seq, 2 * HEAD), bf),
            pltpu.VMEM((2, 2 * HEAD, feat), bf),
            pltpu.VMEM((2, 4 * HEAD, feat), bf),
            pltpu.VMEM((seq, 2 * HEAD), f32),
            pltpu.VMEM((seq, 2 * HEAD), f32),
            pltpu.VMEM((seq, 2 * HEAD), f32),
            pltpu.SemaphoreType.DMA((9,)),
        ],
        compiler_params=pltpu.CompilerParams(vmem_limit_bytes=VMEM_BYTES),
        cost_estimate=pl.CostEstimate(
            flops=8 * 10**9, bytes_accessed=20 * 2**20, transcendentals=2**20
        ),
        name=f"attn_backward_{layer_no}",
    )(blocks, *operands)


def norm_backward_kernel(layer_no, x_ref, part_a, part_b, ghidden_ref, *refs):
    small_c = refs[:3]
    out_ref, low_ref, vec_ref, small, sems = refs[3:]

    @pl.when(pl.program_id(0) == 0)
    def _():
        start_pick(pick_source(layer_no), small_c, small, sems.at[0])
        vec_ref[...] = jnp.zeros_like(vec_ref)
        wait_pick(small_c, small, sems.at[0])

    width = x_ref.shape[1]
    gnormed = part_a[...].astype(f32) + part_b[...].astype(f32)
    zhat, scale = norm_stats(x_ref[...].astype(f32))
    scaled = gnormed * (1.0 + small_row(small, 4, width))
    mean_one = jnp.mean(scaled, axis=-1, keepdims=True)
    mean_two = jnp.mean(scaled * zhat, axis=-1, keepdims=True)
    total = ghidden_ref[...] + (scaled - mean_one - zhat * mean_two) * scale
    out_ref[...] = total
    low_ref[...] = total.astype(bf)
    vec_ref[0] += fold_rows(gnormed * zhat)
    vec_ref[1] += fold_rows(gnormed)


def norm_backward(layer_no, x, part_a, part_b, ghidden, small_c):
    seq, width = x.shape
    shape = jax.ShapeDtypeStruct
    rows = pl.BlockSpec((ROWS, width), lambda i: (i, 0))
    return pl.pallas_call(
        functools.partial(norm_backward_kernel, layer_no),
        grid=(seq // ROWS,),
        out_shape=[shape((seq, width), f32), shape((seq, width), bf), shape((2, 8, width), f32)],
        in_specs=[rows] * 4 + [ANY] * 3,
        out_specs=[rows, rows, pl.BlockSpec((2, 8, width), lambda i: (0, 0, 0))],
        scratch_shapes=[pltpu.VMEM(small_c[0].shape, bf), pltpu.SemaphoreType.DMA((1,))],
        compiler_params=pltpu.CompilerParams(vmem_limit_bytes=VMEM_BYTES),
        cost_estimate=pl.CostEstimate(
            flops=20 * seq * width, bytes_accessed=8 * 2**20, transcendentals=0
        ),
        name=f"norm_backward_{layer_no}",
    )(x, part_a, part_b, ghidden, *small_c)


def weight_grad_kernel(split, n_first, left_a, left_b, right_a, right_b, out_ref, turned):
    step = pl.program_id(0)
    _, n_rows, shard, cols = out_ref.shape

    @pl.when(step == 0)
    def _():
        turned[...] = left_a[...].T

    @pl.when(step == n_first)
    def _():
        turned[...] = left_b[...].T

    def emit(right):
        result = jnp.dot(turned[...], right, preferred_element_type=f32).astype(bf)
        for number in range(split * n_rows):
            out_ref[number % split, number // split] = result[number * shard : (number + 1) * shard]

    @pl.when(step < n_first)
    def _():
        emit(right_a[...])

    @pl.when(step >= n_first)
    def _():
        emit(right_b[...])


def weight_grads(name, dp_count, left_a, right_a, left_b, right_b):
    seq, width = left_a.shape
    step = 256
    if right_a.ndim == 3:
        n_first = right_a.shape[0]
        step = right_a.shape[2]
        spec_a = pl.BlockSpec((None, seq, step), lambda i: (jnp.minimum(i, n_first - 1), 0, 0))
    else:
        n_first = right_a.shape[1] // step
        spec_a = pl.BlockSpec((seq, step), lambda i: (0, jnp.minimum(i, n_first - 1)))
    n_second = right_b.shape[1] // step
    spec_b = pl.BlockSpec((seq, step), lambda i: (0, jnp.maximum(i - n_first, 0)))
    whole = pl.BlockSpec((seq, width), lambda i: (0, 0))
    n_steps = n_first + n_second
    shape = (2, dp_count // 2, width // dp_count, step * n_steps)
    return pl.pallas_call(
        functools.partial(weight_grad_kernel, 2, n_first),
        grid=(n_steps,),
        out_shape=jax.ShapeDtypeStruct(shape, bf),
        in_specs=[whole, whole, spec_a, spec_b],
        out_specs=pl.BlockSpec(shape[:3] + (step,), lambda i: (0, 0, 0, i)),
        scratch_shapes=[pltpu.VMEM((width, seq), bf)],
        compiler_params=pltpu.CompilerParams(vmem_limit_bytes=VMEM_BYTES),
        cost_estimate=pl.CostEstimate(
            flops=2 * seq * width * step * n_steps, bytes_accessed=8 * 2**20, transcendentals=0
        ),
        name=name,
    )(left_a, left_b, right_a, right_b)


ALL_AXES = ("section", "tensor", "dp")


def send(value, sizes, target):
    n_section, n_tensor, n_dp = sizes
    pairs = []
    for s in range(n_section):
        for t in range(n_tensor):
            for d in range(n_dp):
                goal = target(s, t, d // 2, d % 2)
                if goal is not None:
                    gs, gt, gz, gc = goal
                    number = (s * n_tensor + t) * n_dp + d
                    pairs.append((number, (gs * n_tensor + gt) * n_dp + 2 * gz + gc))
    return lax.ppermute(value, ALL_AXES, pairs)


def other_core(value, sizes):
    return send(value, sizes, lambda s, t, z, c: (s, t, z, 1 - c))


def chip_shards(
    sizes,
    inputs,
    cotangent,
    lengths,
    blocks,
    feature_map,
    w_qkv,
    b_qkv,
    w_out,
    w_up,
    b_up,
    w_down,
    vector_params,
):
    n_dp = sizes[2]
    n_z = n_dp // 2
    section_no = lax.axis_index("section")
    tensor_no = lax.axis_index("tensor")
    dp_no = lax.axis_index("dp")
    z_no, core = dp_no // 2, dp_no % 2
    same = core == tensor_no
    is_first = section_no == 0
    width = inputs.shape[2]
    half = inputs.shape[1]
    n_heads, n_blocks, n_listed = blocks.shape[1:]
    units = w_up.shape[2]
    part_width = w_qkv.shape[3]

    def to_sequence(array):
        own = array[section_no]
        first = send(
            own,
            sizes,
            lambda s, t, z, c: (s, t, z, 1 - c) if c == t else (s, 1 - t, z, c),
        )
        second = send(first, sizes, lambda s, t, z, c: (s, t, z, 1 - c) if c == t else None)
        near = jnp.where(same, own, first)
        far = jnp.where(same, first, second)
        swap = tensor_no == 1
        return jnp.concatenate(
            [jnp.where(swap, far, near), jnp.where(swap, near, far)], axis=0
        )

    x_first = to_sequence(inputs)

    def lane_row(array, count):
        flat = array.reshape(count, -1)
        return jnp.pad(flat, ((0, 0), (0, units - flat.shape[1])))

    small = jnp.concatenate(
        [
            lane_row(b_qkv, 3),
            lane_row(b_up, 1),
            lane_row(vector_params, 6),
            lane_row(blocks.astype(bf), 1),
            jnp.zeros((5, units), bf),
        ],
        axis=0,
    )

    def spread(array, by_x):
        first = send(
            array,
            sizes,
            lambda s, t, z, c: (1 - s, t, z, c) if c == t else (s, 1 - t, z, 1 - c),
        )
        if by_x:
            second = send(first, sizes, lambda s, t, z, c: (s, 1 - t, z, c) if c == t else None)
        else:
            second = send(first, sizes, lambda s, t, z, c: None if c == t else (1 - s, t, z, c))
        return (array, first, second)

    small_c = spread(small, True)
    wqkv_c = spread(w_qkv[0].transpose(1, 0, 2), True)
    fm_c = spread(feature_map[0], False)
    wout_c = spread(w_out[0], False)
    wup_c = spread(w_up[0], True)
    wdown_c = spread(w_down[0], False)

    lengths_here = jnp.where(same, lengths, other_core(lengths, sizes))
    length = lax.dynamic_slice_in_dim(lengths_here[:, 0], section_no, 1)

    def of_layer(layer_no, candidates):
        mine = section_no == layer_no
        return jnp.where(
            mine,
            jnp.where(same, candidates[0], candidates[1]),
            jnp.where(same, candidates[1], candidates[2]),
        )

    def exchange(value):
        return value, other_core(value, sizes)

    kept = []
    x_parts = (x_first,)
    outputs = []
    for layer_no in range(2):
        smalls = of_layer(layer_no, small_c)
        listed = smalls[10, : n_heads * n_blocks * n_listed].astype(jnp.int32)
        made = attn_forward(
            layer_no, length, listed, x_parts, (small_c, wqkv_c, wout_c, fm_c), small_c
        )
        if layer_no == 0:
            x = x_first
        else:
            x, made = made[0], made[1:]
            outputs.append(x)
        branch, qkv, normed, probs, qfeat, kfeat, mt, mixed = made
        result, hidden, normed_two, active, slope = ffn_forward(
            layer_no, x, *exchange(branch), (small_c, wup_c, wdown_c)
        )
        x_parts = (hidden, *exchange(result))
        kept.append(
            (x, normed, mixed, hidden, normed_two, active, slope, listed,
             (qkv, probs, qfeat, kfeat, mt))
        )

    grad = to_sequence(cotangent)

    def my_half(array):
        return lax.dynamic_slice_in_dim(array, core * half, half)

    def deliver(layer_no, rows):
        own = send(rows, sizes, lambda s, t, z, c: (s, c, z, t) if s == layer_no else None)
        other = send(rows, sizes, lambda s, t, z, c: None if s == layer_no else (1 - s, c, z, t))
        return own, other

    hidden, part_a, part_b = x_parts
    last_bias = of_layer(1, small_c)[9:10, :width].astype(f32)
    last = my_half(hidden) + (my_half(part_a).astype(f32) + my_half(part_b).astype(f32)) + last_bias
    out_pairs = [deliver(0, my_half(outputs[0])), deliver(1, last.astype(bf))]

    def gather_sum(layer_no, array):
        other = send(array, sizes, lambda s, t, z, c: None if c == t else (s, 1 - t, z, c))
        total = (array.astype(f32) + other.astype(f32)).astype(array.dtype)
        other = send(
            total, sizes, lambda s, t, z, c: (1 - s, t, z, c) if c == t and s != layer_no else None
        )
        total = (total.astype(f32) + other.astype(f32)).astype(array.dtype)
        away = lax.dynamic_index_in_dim(total, 1 - core, keepdims=False)
        stay = lax.dynamic_index_in_dim(total, core, keepdims=False)
        other = send(
            away, sizes, lambda s, t, z, c: (s, t, z, 1 - c) if c == t and s == layer_no else None
        )
        piece = jnp.where(same, stay, other)
        total = lax.dynamic_index_in_dim(piece, z_no, keepdims=False).astype(f32)
        for step in range(1, n_z):
            shard = lax.dynamic_index_in_dim(piece, (z_no + step) % n_z, keepdims=False)
            total = total + send(
                shard,
                sizes,
                lambda s, t, z, c: (s, t, (z + step) % n_z, c) if s == layer_no else None,
            ).astype(f32)
        return total

    sums = [None, None]
    grad_pairs = [None, None]
    for layer_no in (1, 0):
        x, normed, mixed, hidden, normed_two, active, slope, listed, attn_kept = kept[layer_no]
        gnormed_two, gupper, bias_up = ffn_backward(layer_no, grad, slope, (wup_c, wdown_c))
        part_a, part_b = exchange(gnormed_two)
        wide = weight_grads(f"ffn_grads_{layer_no}", n_dp, normed_two, gupper, grad, active)
        gnormed, ghidden, gbranch, gproj, vec_two, bias_qkv = attn_backward(
            layer_no, listed, grad, part_a, part_b, hidden, attn_kept,
            (small_c, wqkv_c, wout_c, fm_c),
        )
        part_a, part_b = exchange(gnormed)
        narrow = weight_grads(f"attn_grads_{layer_no}", n_dp, normed, gproj, gbranch, mixed)
        gx, gx_low, vec_one = norm_backward(layer_no, x, part_a, part_b, ghidden, small_c)
        vectors = jnp.concatenate([jnp.sum(vec_one, axis=1), jnp.sum(vec_two, axis=1)], axis=0)
        vectors = lax.dynamic_slice_in_dim(vectors, core * (width // 2), width // 2, axis=1)

        def by_shard(array):
            rows = array.reshape(array.shape[0], n_z, 2, -1)
            return rows.transpose(2, 1, 0, 3).reshape(2, n_z, -1)

        tiny = jnp.concatenate(
            [
                by_shard(vectors),
                by_shard(jnp.sum(bias_qkv, axis=1)),
                by_shard(jnp.sum(bias_up, axis=0, keepdims=True)),
            ],
            axis=2,
        )
        sums[layer_no] = tuple(gather_sum(layer_no, item) for item in (wide, narrow, tiny))
        grad_pairs[layer_no] = deliver(layer_no, my_half(gx_low))
        grad = gx_low

    def placed(pairs, dtype):
        own = jnp.where(is_first, pairs[0][0], pairs[1][0])
        other = jnp.where(is_first, pairs[0][1], pairs[1][1])
        return jnp.stack(
            [jnp.where(is_first, own, other), jnp.where(is_first, other, own)]
        )[None].astype(dtype)

    section_outputs = placed(out_pairs, bf)
    input_grads = placed(grad_pairs, f32)
    wide, narrow, tiny = (jnp.where(is_first, a, b) for a, b in zip(*sums))
    shard = width // n_dp
    grad_up, grad_down = wide[:, :units], wide[:, units:].T
    grad_qkv = narrow[:, : 3 * part_width].reshape(shard, 3, part_width)
    grad_out = narrow[:, 3 * part_width :].T
    n_vec = 6 * (width // 2 // n_dp)
    n_bias = 3 * (part_width // n_dp)
    grad_vectors = tiny[:n_vec].reshape(6, -1)
    grad_bqkv = tiny[n_vec : n_vec + n_bias].reshape(3, -1)
    grad_bup = tiny[n_vec + n_bias :]
    return (
        section_outputs,
        input_grads,
        grad_qkv[None],
        grad_bqkv[None],
        grad_out[None],
        grad_up[None],
        grad_bup[None],
        grad_down[None],
        grad_vectors[None],
    )


HEAD = 64
BLOCK = 64
SEQ_LEN = 1024


norm_eps = 1e-05
bfloat = jnp.bfloat16
single = jnp.float32


def shifted(value, axis, steps):
    count = lax.axis_size(axis)
    first, last = (max(0, -steps), min(count, count - steps))
    return lax.ppermute(value, axis, [(source, source + steps) for source in range(first, last)])


def norm_rows(residual, gain_vec, shift_vec):
    row_mean = jnp.mean(residual, axis=-1, keepdims=True)
    centred = residual - row_mean
    variance = jnp.mean(centred * centred, axis=-1, keepdims=True)
    return centred * lax.rsqrt(variance + norm_eps) * (1.0 + gain_vec) + shift_vec


def gelu_exact(pre_active):
    return jax.nn.gelu(pre_active, approximate=False)


def select_tree(flag_value, when_true, when_false):
    return jax.tree.map(
        lambda left_arr, right_arr: jnp.where(flag_value, left_arr, right_arr),
        when_true,
        when_false,
    )


def split_pieces(operand):
    if operand.dtype == bfloat:
        return (operand,)
    upper_part = operand.astype(bfloat)
    lower_part = (operand - upper_part.astype(single)).astype(bfloat)
    return (upper_part, lower_part)


def split_dot(form, left, right):
    left_pieces = split_pieces(left)
    right_pieces = split_pieces(right)
    total = None
    for left_no, left_piece in enumerate(left_pieces):
        for right_no, right_piece in enumerate(right_pieces):
            if left_no + right_no > 1:
                continue
            term = jnp.einsum(form, left_piece, right_piece, preferred_element_type=single)
            total = term if total is None else total + term
    return total


def sparse_layout(block_list, length):
    head_count, block_count = (block_list.shape[0], block_list.shape[1])
    chosen = jnp.concatenate(
        [jnp.zeros((head_count, block_count, 1), jnp.int32), block_list], axis=2
    )
    key_live = (jnp.arange(SEQ_LEN) < length).astype(single)
    picked_live = key_live.reshape(block_count, BLOCK)[chosen].reshape(head_count, block_count, -1)
    return (chosen, key_live, picked_live)


def pick_blocks(table_in, chosen):
    head_count, block_count = (chosen.shape[0], chosen.shape[1])
    blocks_in = table_in.reshape(head_count, block_count, BLOCK, table_in.shape[-1])
    taken_rows = jax.vmap(lambda one_table, index_rows: one_table[index_rows])(blocks_in, chosen)
    return taken_rows.reshape(head_count, block_count, -1, table_in.shape[-1])


def place_blocks(values_in, chosen):
    head_count, block_count, slot_count = chosen.shape
    parts_in = values_in.reshape(head_count, block_count, slot_count, BLOCK, values_in.shape[-1])
    zero_blocks = jnp.zeros((head_count, block_count, BLOCK, values_in.shape[-1]), single)
    placed = jax.vmap(lambda base_arr, index_rows, one_part: base_arr.at[index_rows].add(one_part))(
        zero_blocks, chosen, parts_in
    )
    return placed.reshape(head_count, SEQ_LEN, values_in.shape[-1])


def feature_of(vectors_low, features):
    feature_scale = HEAD ** (-0.25)
    vectors = vectors_low.astype(single)
    projected = split_dot("hld,hdf->hlf", vectors_low, features) * feature_scale
    return jnp.exp(
        projected
        - jnp.sum(vectors * vectors, axis=-1, keepdims=True) * (0.5 * feature_scale * feature_scale)
    )


def block_scores(query_blocks, picked_keys, picked_live):
    scores = jnp.einsum(
        "hnqd,hnkd->hnqk", query_blocks, picked_keys, preferred_element_type=single
    ) * HEAD ** (-0.5)
    return jnp.where(picked_live[:, :, None, :] > 0.5, scores, -1e30)


def attend_forward(queries, key_vecs, value_vecs, chosen, key_live, picked_live, features):
    head_count, block_count = (chosen.shape[0], chosen.shape[1])
    query_blocks = queries.reshape(head_count, block_count, BLOCK, HEAD)
    picked_keys = pick_blocks(key_vecs, chosen)
    picked_values = pick_blocks(value_vecs, chosen)
    scores = block_scores(query_blocks, picked_keys, picked_live)
    row_max = jnp.max(scores, axis=-1, keepdims=True)
    weights_raw = jnp.exp(scores - row_max) * picked_live[:, :, None, :]
    row_total = jnp.sum(weights_raw, axis=-1, keepdims=True)
    log_total = row_max + jnp.log(row_total)
    weights_low = (weights_raw / row_total).astype(bfloat)
    sparse_out = jnp.einsum(
        "hnqk,hnkd->hnqd", weights_low, picked_values, preferred_element_type=single
    )
    sparse_out = sparse_out.reshape(head_count, SEQ_LEN, HEAD)
    query_feats = feature_of(queries, features)
    key_feats = feature_of(key_vecs, features) * key_live[None, :, None]
    moments = split_dot("hlf,hld->hfd", key_feats, value_vecs)
    totals = jnp.sum(key_feats, axis=1)
    numerator = split_dot("hlf,hfd->hld", query_feats, moments)
    denominator = split_dot("hlf,hf->hl", query_feats, totals)
    perf_out = numerator / denominator[:, :, None]
    return (
        sparse_out + perf_out,
        (log_total, query_feats, key_feats, moments, totals, denominator, perf_out),
    )


def attend_backward(
    grad_heads, queries, key_vecs, value_vecs, chosen, picked_live, features, attn_keep
):
    log_total, query_feats, key_feats, moments, totals, denominator, perf_out = attn_keep
    head_count, block_count = (chosen.shape[0], chosen.shape[1])
    score_scale = HEAD ** (-0.5)
    query_blocks = queries.reshape(head_count, block_count, BLOCK, HEAD)
    grad_blocks = grad_heads.reshape(head_count, block_count, BLOCK, HEAD)
    picked_keys = pick_blocks(key_vecs, chosen)
    picked_values = pick_blocks(value_vecs, chosen)
    scores = block_scores(query_blocks, picked_keys, picked_live)
    weights_f = jnp.exp(scores - log_total) * picked_live[:, :, None, :]
    grad_weights = jnp.einsum(
        "hnqd,hnkd->hnqk", grad_blocks, picked_values, preferred_element_type=single
    )
    row_inner = jnp.sum(weights_f * grad_weights, axis=-1, keepdims=True)
    grad_scores = (weights_f * (grad_weights - row_inner)).astype(bfloat)
    grad_query = jnp.einsum(
        "hnqk,hnkd->hnqd", grad_scores, picked_keys, preferred_element_type=single
    )
    grad_query = grad_query.reshape(head_count, SEQ_LEN, HEAD) * score_scale
    grad_keys = place_blocks(
        jnp.einsum("hnqk,hnqd->hnkd", grad_scores, query_blocks, preferred_element_type=single)
        * score_scale,
        chosen,
    )
    grad_values = place_blocks(
        jnp.einsum(
            "hnqk,hnqd->hnkd", weights_f.astype(bfloat), grad_blocks, preferred_element_type=single
        ),
        chosen,
    )
    grad_float = grad_heads.astype(single)
    grad_numer = grad_float / denominator[:, :, None]
    grad_denom = -jnp.sum(grad_float * perf_out, axis=-1) / denominator
    grad_qfeat = (
        split_dot("hld,hfd->hlf", grad_numer, moments) + grad_denom[:, :, None] * totals[:, None, :]
    )
    grad_moments = split_dot("hlf,hld->hfd", query_feats, grad_numer)
    grad_totals = split_dot("hlf,hl->hf", query_feats, grad_denom)
    grad_kfeat = split_dot("hld,hfd->hlf", value_vecs, grad_moments) + grad_totals[:, None, :]
    grad_values = grad_values + split_dot("hlf,hfd->hld", key_feats, grad_moments)
    feature_scale = HEAD ** (-0.25)

    def feature_back(grad_feat, feats, vectors_low):
        grad_expo = grad_feat * feats
        direct = split_dot("hlf,hdf->hld", grad_expo, features) * feature_scale
        return direct - feature_scale * feature_scale * jnp.sum(
            grad_expo, axis=-1, keepdims=True
        ) * vectors_low.astype(single)

    grad_query = grad_query + feature_back(grad_qfeat, query_feats, queries)
    grad_keys = grad_keys + feature_back(grad_kfeat, key_feats, key_vecs)
    return (grad_query, grad_keys, grad_values)


def layer_forward(section_entry, length, layer_params, block_list, features):
    qkv_mat, qkv_bias, out_mat, up_mat, up_bias, down_mat, vectors = layer_params
    residual = section_entry.astype(single)
    normed = norm_rows(residual, vectors[0], vectors[1]).astype(bfloat)
    normed_all = lax.all_gather(normed, "tensor", axis=0, tiled=True)
    projected = (
        jnp.einsum("ld,dce->lce", normed_all, qkv_mat, preferred_element_type=single)
        + qkv_bias[None]
    )
    projected = projected.astype(bfloat)
    seq_len, part_width = (projected.shape[0], projected.shape[2])
    head_count = part_width // HEAD
    head_parts = projected.reshape(seq_len, 3, head_count, HEAD).transpose(1, 2, 0, 3)
    chosen, key_live, picked_live = sparse_layout(block_list, length)
    mixed_heads, attn_keep = attend_forward(
        head_parts[0], head_parts[1], head_parts[2], chosen, key_live, picked_live, features
    )
    mixed_low = mixed_heads.transpose(1, 0, 2).reshape(seq_len, part_width).astype(bfloat)
    row_block = mixed_low
    branch = lax.psum_scatter(
        jnp.dot(row_block, out_mat, preferred_element_type=single).astype(jnp.bfloat16),
        "tensor",
        scatter_dimension=0,
        tiled=True,
    ).astype(jnp.float32)
    hidden_res = residual + branch + vectors[4]
    normed_two = norm_rows(hidden_res, vectors[2], vectors[3]).astype(bfloat)
    normed_two_all = lax.all_gather(normed_two, "tensor", axis=0, tiled=True)
    pre_active = jnp.dot(normed_two_all, up_mat, preferred_element_type=single) + up_bias
    active = gelu_exact(pre_active).astype(bfloat)
    row_block = active
    result = (
        hidden_res
        + lax.psum_scatter(
            jnp.dot(row_block, down_mat, preferred_element_type=single).astype(jnp.bfloat16),
            "tensor",
            scatter_dimension=0,
            tiled=True,
        ).astype(jnp.float32)
        + vectors[5]
    )
    record = (
        residual,
        hidden_res,
        normed_all,
        head_parts,
        mixed_low,
        normed_two_all,
        pre_active,
        active,
        attn_keep,
        length,
    )
    return (result.astype(bfloat), record)


def layer_backward(grad_low, record, layer_params, block_list, features):
    qkv_mat, qkv_bias, out_mat, up_mat, up_bias, down_mat, vectors = layer_params
    (
        residual,
        hidden_res,
        normed_all,
        head_parts,
        mixed_low,
        normed_two_all,
        pre_active,
        active,
        attn_keep,
        length,
    ) = record
    seq_len, part_width = mixed_low.shape
    head_count = part_width // HEAD
    grad_output = grad_low.astype(single)
    grad_all = lax.all_gather(grad_low, "tensor", axis=0, tiled=True)
    grad_wdown = jnp.einsum("lf,ld->fd", active, grad_all, preferred_element_type=single)
    grad_active = jnp.einsum("ld,fd->lf", grad_all, down_mat, preferred_element_type=single)
    _, gelu_pull = jax.vjp(gelu_exact, pre_active)
    grad_upper = gelu_pull(grad_active)[0].astype(bfloat)
    grad_wup = jnp.einsum("ld,lf->df", normed_two_all, grad_upper, preferred_element_type=single)
    grad_bup = jnp.sum(grad_upper.astype(single), axis=0)
    row_block = grad_upper
    grad_normed_two = lax.psum_scatter(
        jnp.einsum("lf,df->ld", row_block, up_mat, preferred_element_type=single).astype(
            jnp.bfloat16
        ),
        "tensor",
        scatter_dimension=0,
        tiled=True,
    ).astype(jnp.float32)
    _, pull_two = jax.vjp(norm_rows, hidden_res, vectors[2], vectors[3])
    grad_hidden, grad_gain_two, grad_shift_two = pull_two(grad_normed_two)
    grad_hidden = grad_hidden + grad_output
    grad_hidden_low = grad_hidden.astype(bfloat)
    hidden_all = lax.all_gather(grad_hidden_low, "tensor", axis=0, tiled=True)
    grad_wout = jnp.einsum("le,ld->ed", mixed_low, hidden_all, preferred_element_type=single)
    grad_mixed = jnp.einsum("ld,ed->le", hidden_all, out_mat, preferred_element_type=single).astype(
        bfloat
    )
    grad_heads = grad_mixed.reshape(seq_len, head_count, HEAD).transpose(1, 0, 2)
    chosen, key_live, picked_live = sparse_layout(block_list, length)
    grad_query, grad_keys, grad_values = attend_backward(
        grad_heads,
        head_parts[0],
        head_parts[1],
        head_parts[2],
        chosen,
        picked_live,
        features,
        attn_keep,
    )
    grad_proj = (
        jnp.stack([grad_query, grad_keys, grad_values])
        .transpose(2, 0, 1, 3)
        .reshape(seq_len, 3, part_width)
        .astype(bfloat)
    )
    grad_wqkv = jnp.einsum("ld,lce->dce", normed_all, grad_proj, preferred_element_type=single)
    grad_bqkv = jnp.sum(grad_proj.astype(single), axis=0)
    row_block = grad_proj
    grad_normed = lax.psum_scatter(
        jnp.einsum("lce,dce->ld", row_block, qkv_mat, preferred_element_type=single).astype(
            jnp.bfloat16
        ),
        "tensor",
        scatter_dimension=0,
        tiled=True,
    ).astype(jnp.float32)
    _, pull_one = jax.vjp(norm_rows, residual, vectors[0], vectors[1])
    grad_resid, grad_gain_one, grad_shift_one = pull_one(grad_normed)
    grad_resid = grad_resid + grad_hidden
    weight_grads = (grad_wqkv, grad_bqkv, grad_wout, grad_wup, grad_bup, grad_wdown)
    vector_grads = jnp.stack(
        [
            grad_gain_one,
            grad_shift_one,
            grad_gain_two,
            grad_shift_two,
            jnp.sum(grad_hidden_low.astype(single), axis=0),
            jnp.sum(grad_output, axis=0),
        ]
    )
    return (grad_resid, weight_grads, vector_grads)


def shards(
    inputs,
    cotangent,
    lengths,
    blocks,
    feature_map,
    w_qkv,
    b_qkv,
    w_out,
    w_up,
    b_up,
    w_down,
    vector_params,
):
    section_no = lax.axis_index("section")
    is_first = section_no == 0
    is_last = section_no == lax.axis_size("section") - 1
    layer_params = (
        w_qkv[0],
        b_qkv[0].astype(single),
        w_out[0],
        w_up[0],
        b_up[0].astype(single),
        w_down[0],
        vector_params[0].astype(single),
    )
    block_list = blocks[0]
    features = feature_map[0]
    batch_count = inputs.shape[0]
    carried = jnp.zeros_like(inputs[0])
    records = []
    results = []
    for tick_no in range(batch_count + 1):
        batch_no = jnp.clip(tick_no - section_no, 0, batch_count - 1)
        section_entry = jnp.where(is_first, inputs[min(tick_no, batch_count - 1)], carried)
        result, record = layer_forward(
            section_entry, lengths[batch_no, 0], layer_params, block_list, features
        )
        records.append(record)
        results.append(result)
        if tick_no < batch_count:
            carried = shifted(result, "section", 1)
    section_outputs = jnp.stack(
        [
            jnp.where(is_first, results[batch_idx], results[batch_idx + 1])
            for batch_idx in range(batch_count)
        ]
    )[None]
    received = jnp.zeros_like(cotangent[0])
    grad_list = []
    local_sum = None
    vector_total = jnp.zeros((6, inputs.shape[2]), single)
    for tick_no in range(batch_count + 1):
        record = select_tree(
            is_last, records[min(tick_no + 1, batch_count)], records[max(tick_no - 1, 0)]
        )
        valid_flag = jnp.where(is_last, float(tick_no < batch_count), float(tick_no >= 1)).astype(
            single
        )
        grad_entry = jnp.where(is_last, cotangent[min(tick_no, batch_count - 1)], received)
        grad_resid, weight_grads, vector_grads = layer_backward(
            grad_entry, record, layer_params, block_list, features
        )
        weight_grads = tuple((valid_flag * addend for addend in weight_grads))
        vector_total = vector_total + valid_flag * vector_grads
        local_sum = (
            weight_grads
            if local_sum is None
            else tuple((summed + addend for summed, addend in zip(local_sum, weight_grads)))
        )
        grad_list.append(grad_resid)
        if tick_no < batch_count:
            received = shifted(grad_resid.astype(bfloat), "section", -1)
    final_grads = (
        lax.psum_scatter(
            local_sum[0].astype(jnp.bfloat16), "dp", scatter_dimension=0, tiled=True
        ).astype(jnp.float32),
        lax.psum_scatter(
            local_sum[1].astype(jnp.bfloat16), "dp", scatter_dimension=1, tiled=True
        ).astype(jnp.float32),
        lax.psum_scatter(
            local_sum[2].astype(jnp.bfloat16), "dp", scatter_dimension=1, tiled=True
        ).astype(jnp.float32),
        lax.psum_scatter(
            local_sum[3].astype(jnp.bfloat16), "dp", scatter_dimension=0, tiled=True
        ).astype(jnp.float32),
        lax.psum_scatter(
            local_sum[4].astype(jnp.bfloat16), "dp", scatter_dimension=0, tiled=True
        ).astype(jnp.float32),
        lax.psum_scatter(
            local_sum[5].astype(jnp.bfloat16), "dp", scatter_dimension=1, tiled=True
        ).astype(jnp.float32),
    )
    input_grads = jnp.stack(
        [
            jnp.where(is_first, grad_list[batch_idx + 1], grad_list[batch_idx])
            for batch_idx in range(batch_count)
        ]
    )[None]
    grad_vectors = lax.psum_scatter(
        vector_total, ("tensor", "dp"), scatter_dimension=1, tiled=True
    )[None]
    grad_wqkv, grad_bqkv, grad_wout, grad_wup, grad_bup, grad_wdown = final_grads
    return (
        section_outputs,
        input_grads,
        grad_wqkv[None],
        grad_bqkv[None],
        grad_wout[None],
        grad_wup[None],
        grad_bup[None],
        grad_wdown[None],
        grad_vectors,
    )


def solution(mesh):
    placed = (
        P(None, ("dp", "tensor"), None),
        P(None, ("dp", "tensor"), None),
        P(None, "dp"),
        P("section", "tensor", None, None),
        P("section", "tensor", None, None),
        P("section", None, None, "tensor"),
        P("section", None, "tensor"),
        P("section", "tensor", None),
        P("section", None, "tensor"),
        P("section", "tensor"),
        P("section", "tensor", None),
        P("section", None, None),
    )
    sizes = tuple(mesh.shape[axis] for axis in ALL_AXES)
    if sizes[0] == 2 and sizes[1] == 2 and sizes[2] % 2 == 0:
        body = functools.partial(chip_shards, sizes)
    else:
        body = shards
    return jax.shard_map(
        body,
        mesh=mesh,
        in_specs=placed,
        out_specs=(
            P("section", None, ("dp", "tensor"), None),
            P("section", None, ("dp", "tensor"), None),
            P("section", "dp", None, "tensor"),
            P("section", None, ("tensor", "dp")),
            P("section", "tensor", "dp"),
            P("section", "dp", "tensor"),
            P("section", ("tensor", "dp")),
            P("section", "tensor", "dp"),
            P("section", None, ("tensor", "dp")),
        ),
        check_vma=False,
    )
```

```python
import functools

import jax
import jax.numpy as jnp
from jax import lax
from jax.experimental import pallas as pl
from jax.experimental.pallas import tpu as pltpu
from jax.sharding import PartitionSpec as P

HEAD = 64
BLOCK = 64
NORM_EPS = 1e-5
bf = jnp.bfloat16
f32 = jnp.float32
LOG2E = 1.4426950408889634
F_SCALE = HEAD ** -0.25
ROWS = 1024
FFN_ROWS = 256
SPARSE_UNROLL = 8
PACK_ROWS = 32
PACK_SMALL = 96
TINY_ROWS = 16
VMEM_BYTES = 60 * 1024 * 1024
SHORT = pl.CostEstimate(flops=10**6, bytes_accessed=2**16, transcendentals=0)
ANY = pl.BlockSpec(memory_space=pl.ANY)
WHOLE = pl.BlockSpec(memory_space=pltpu.VMEM)
SCALARS = pl.BlockSpec(memory_space=pltpu.SMEM)


def contract(left, right, left_dim, right_dim):
    return lax.dot_general(
        left, right, (((left_dim,), (right_dim,)), ((), ())), preferred_element_type=f32
    )


def pick_source(layer_no):
    section_no = lax.axis_index("section")
    same = lax.rem(lax.axis_index("dp"), 2) == lax.axis_index("tensor")
    return jnp.where(section_no == layer_no, 0, 1) + jnp.where(same, 0, 2)


def start_pick(source, candidates, target, sem):
    for number, candidate in enumerate(candidates):

        @pl.when(source == number)
        def _():
            pltpu.make_async_copy(candidate, target, sem).start()


def wait_pick(candidates, target, sem):
    pltpu.make_async_copy(candidates[0], target, sem).wait()


def small_row(small, row, width):
    count = width // small.shape[1]
    rows = [small[row + i : row + i + 1, :].astype(f32) for i in range(count)]
    return jnp.concatenate(rows, axis=1)


def vector_row(small, number, width):
    return small_row(small, 8 + 2 * number, width)


def small_part(candidates):
    return [candidate.at[0:PACK_ROWS] for candidate in candidates]


def norm_stats(value):
    mean = jnp.mean(value, axis=-1, keepdims=True)
    centred = value - mean
    variance = jnp.mean(centred * centred, axis=-1, keepdims=True)
    scale = lax.rsqrt(variance + NORM_EPS)
    return centred * scale, scale


def lane_masks():
    lane = lax.broadcasted_iota(jnp.int32, (1, 2 * HEAD), 1)
    return lane < HEAD, lane >= HEAD


def swap_halves(value):
    return pltpu.roll(value, HEAD, 1)


def listed_starts(blocks_ref, pair, block, n_blocks):
    found = []
    for slot in range(3):
        two = []
        for a in range(2):
            listed = blocks_ref[(2 * pair + a) * n_blocks + block, slot]
            two.append(pl.multiple_of(listed * BLOCK, BLOCK))
        found.append(tuple(two))
    return found


def pick_rows(table, part, cols, starts, in_first):
    pieces = [table[part, 0:BLOCK, cols]]
    for one, two in starts:
        pieces.append(
            jnp.where(
                in_first,
                table[part, pl.ds(one, BLOCK), cols],
                table[part, pl.ds(two, BLOCK), cols],
            )
        )
    return jnp.concatenate(pieces, axis=0)


def stack_heads(target, chunk, value, masks):
    for number in range(ROWS // BLOCK):
        block = value[number * BLOCK : (number + 1) * BLOCK]
        for a in range(2):
            target[chunk * (ROWS // BLOCK) + number, a * BLOCK : (a + 1) * BLOCK] = jnp.where(
                masks[a], block, 0.0
            ).astype(bf)


def feature_rows(pack, n_heads, head):
    at = PACK_SMALL + head * HEAD
    return pack[at : at + HEAD].astype(f32) + pack[at + n_heads * HEAD : at + (n_heads + 1) * HEAD].astype(f32)


def qkv_weight(pack, n_heads, width, part):
    at = PACK_SMALL + 4 * n_heads * HEAD + part * width
    return pack[at : at + width]


def out_weights(pack, n_heads, part_width):
    at = PACK_SMALL + 2 * n_heads * HEAD
    return [pack[at + part * part_width : at + (part + 1) * part_width] for part in range(2)]


def pack_kernel(wqkv_ref, wout_ref, features_ref, bqkv_ref, bup_ref, vector_ref, blocks_ref, pack_ref):
    n_features, feat = features_ref.shape
    n_parts, width, part_width = wqkv_ref.shape

    def lane_rows(value):
        value = value.astype(f32)
        return [
            value[row : row + 1, at : at + feat]
            for row in range(value.shape[0])
            for at in range(0, value.shape[1], feat)
        ]

    blank = jnp.zeros((1, feat), f32)
    rows = lane_rows(bqkv_ref[...]) + [blank] + lane_rows(bup_ref[...]) + lane_rows(vector_ref[...])
    rows += [blank] * (PACK_ROWS - len(rows))
    pack_ref[0:PACK_ROWS] = jnp.concatenate(rows, axis=0).astype(bf)
    n_listed, n_slots = blocks_ref.shape
    pack_ref[PACK_ROWS:PACK_SMALL] = jnp.zeros((PACK_SMALL - PACK_ROWS, feat), bf)
    pack_ref[PACK_ROWS : PACK_ROWS + n_listed, 0:n_slots] = blocks_ref[...].astype(f32).astype(bf)
    at = PACK_SMALL
    features = features_ref[...]
    high = features.astype(bf)
    pack_ref[at : at + n_features] = high
    pack_ref[at + n_features : at + 2 * n_features] = (features - high.astype(f32)).astype(bf)
    at += 2 * n_features
    for part in range(2):
        pack_ref[at : at + part_width] = wout_ref[:, part * feat : (part + 1) * feat]
        at += part_width
    for part in range(n_parts):
        pack_ref[at : at + width] = wqkv_ref[part]
        at += width


def pack_weights(wqkv, wout, features, bqkv, bup, vectors, blocks):
    n_parts, width, part_width = wqkv.shape
    n_features, feat = features.shape
    n_rows = PACK_SMALL + 2 * n_features + 2 * part_width + n_parts * width
    return pl.pallas_call(
        pack_kernel,
        out_shape=jax.ShapeDtypeStruct((n_rows, feat), bf),
        in_specs=[WHOLE] * 7,
        out_specs=WHOLE,
        compiler_params=pltpu.CompilerParams(vmem_limit_bytes=VMEM_BYTES),
        cost_estimate=SHORT,
        name="pack_weights",
    )(wqkv, wout, features, bqkv, bup, vectors, blocks)


def attn_forward_kernel(layer_no, n_heads, length_ref, blocks_ref, *refs):
    if layer_no == 0:
        x_ref, refs = refs[0], refs[1:]
    else:
        hidden_ref, part_a, part_b, refs = refs[0], refs[1], refs[2], refs[3:]
        small_prev, refs = refs[:4], refs[4:]
    pack_c, refs = refs[:4], refs[4:]
    if layer_no == 1:
        x_ref, refs = refs[0], refs[1:]
    (branch_ref, qkv_out, normed_out, probs_out, qf_out, kf_out, mt_out, mixed_out) = refs[:8]
    (pack, qkv, normed, probs, qfeat, kfeat, mt, mixed, fcat, perf, qstack,
     in_sem, out_sem) = refs[8:21]
    seq, width = normed.shape
    n_chunks = seq // ROWS
    pairs = n_heads // 2
    part_width = qkv.shape[2]
    feat = pack.shape[1]
    small = pack.at[0:PACK_ROWS]
    source = pick_source(layer_no)
    if layer_no == 1:
        small_before = refs[21]
        before = pick_source(0)
        start_pick(before, small_part(small_prev), small_before, in_sem.at[1])
    start_pick(source, pack_c, pack, in_sem.at[0])
    wait_pick(pack_c, pack, in_sem.at[0])
    if layer_no == 1:
        wait_pick(small_part(small_prev), small_before, in_sem.at[1])
    length = length_ref[0]
    gain = 1.0 + vector_row(small, 0, width)
    shift = vector_row(small, 1, width)

    @pl.loop(0, n_chunks)
    def _(chunk):
        rows = pl.ds(pl.multiple_of(chunk * ROWS, ROWS), ROWS)
        if layer_no == 0:
            x = x_ref[rows, :].astype(f32)
        else:
            total = part_a[rows, :].astype(f32) + part_b[rows, :].astype(f32)
            x_low = (hidden_ref[rows, :] + total + vector_row(small_before, 5, width)).astype(bf)
            x_ref[rows, :] = x_low
            x = x_low.astype(f32)
        zhat, _ = norm_stats(x)
        low = (zhat * gain + shift).astype(bf)
        normed[rows, :] = low
        for part in range(3):
            cols = n_heads * HEAD
            out = jnp.dot(low, qkv_weight(pack, n_heads, width, part), preferred_element_type=f32)
            qkv[part, rows, :] = (out + small_row(small, part, cols)).astype(bf)

    copies = [
        pltpu.make_async_copy(qkv, qkv_out, out_sem.at[0]),
        pltpu.make_async_copy(normed, normed_out, out_sem.at[1]),
    ]
    for copy in copies:
        copy.start()
    in_first, in_second = lane_masks()
    masks = (in_first, in_second)
    key_row = lax.broadcasted_iota(jnp.int32, (BLOCK, 2 * HEAD), 0)
    for pair in range(pairs):
        cols = slice(pair * 2 * HEAD, (pair + 1) * 2 * HEAD)
        zero = jnp.zeros((HEAD, feat), bf)
        for a in range(2):
            scaled = feature_rows(pack, n_heads, 2 * pair + a) * (F_SCALE * LOG2E)
            high = scaled.astype(bf)
            rest = (scaled - high.astype(f32)).astype(bf)
            for part, piece in enumerate((high, rest)):
                row = part * 2 * HEAD + a * HEAD
                fcat[row : row + HEAD, a * feat : (a + 1) * feat] = piece
                fcat[row : row + HEAD, (1 - a) * feat : (2 - a) * feat] = zero

        def features(vectors):
            proj = jnp.dot(
                jnp.concatenate([vectors, vectors], axis=1), fcat[...], preferred_element_type=f32
            )
            value = vectors.astype(f32)
            square = value * value * (0.5 * F_SCALE * F_SCALE * LOG2E)
            return [
                jnp.exp2(
                    proj[:, a * feat : (a + 1) * feat]
                    - jnp.sum(jnp.where(masks[a], square, 0.0), axis=-1, keepdims=True)
                )
                for a in range(2)
            ]

        @pl.loop(0, n_chunks)
        def _(chunk):
            base = pl.multiple_of(chunk * ROWS, ROWS)
            rows = pl.ds(base, ROWS)
            live = lax.broadcasted_iota(jnp.int32, (ROWS, 1), 0) + base < length
            found = features(qkv[1, rows, cols])
            for a in range(2):
                kfeat[pair, rows, a * feat : (a + 1) * feat] = jnp.where(live, found[a], 0.0).astype(bf)

        values = qkv[2, :, cols].astype(f32)
        for a in range(2):
            extended = jnp.where(masks[a], values, 1.0).astype(bf)
            moment = contract(extended, kfeat[pair, :, a * feat : (a + 1) * feat], 0, 0)
            mt[2 * pair + a] = moment.astype(bf)

        @pl.loop(0, n_chunks)
        def _(chunk):
            rows = pl.ds(pl.multiple_of(chunk * ROWS, ROWS), ROWS)
            query = qkv[0, rows, cols]
            found = features(query)
            out = None
            for a in range(2):
                low = found[a].astype(bf)
                qfeat[pair, rows, a * feat : (a + 1) * feat] = low
                numer = contract(low, mt[2 * pair + a], 1, 1)
                value = numer / swap_halves(numer)
                out = value if a == 0 else jnp.where(in_first, out, value)
            perf[rows, :] = out
            stack_heads(qstack, chunk, query.astype(f32) * (HEAD ** -0.5), masks)

        @pl.loop(0, seq // BLOCK, unroll=SPARSE_UNROLL)
        def _(block):
            rows = pl.ds(pl.multiple_of(block * BLOCK, BLOCK), BLOCK)
            starts = listed_starts(blocks_ref, pair, block, seq // BLOCK)
            keys = pick_rows(qkv, 1, cols, starts, in_first)
            values = pick_rows(qkv, 2, cols, starts, in_first)
            scores = contract(keys, qstack[block], 1, 1)
            pieces = [scores[:BLOCK]]
            for slot, (one, two) in enumerate(starts):
                room = length - jnp.where(in_first, one, two)
                piece = scores[(slot + 1) * BLOCK : (slot + 2) * BLOCK]
                pieces.append(jnp.where(key_row < room, piece, -1e30))
            scores = jnp.concatenate(pieces, axis=0)
            raw = jnp.exp(scores - jnp.max(scores, axis=0, keepdims=True))
            low = (raw * (1.0 / jnp.sum(raw, axis=0, keepdims=True))).astype(bf)
            probs[pair, block] = low
            both = contract(low, values, 0, 0)
            out = jnp.where(in_first, both[:BLOCK], both[BLOCK:])
            mixed[rows, cols] = (out + perf[rows, :]).astype(bf)

        more = [
            pltpu.make_async_copy(probs.at[pair], probs_out.at[pair], out_sem.at[2 + 4 * pair]),
            pltpu.make_async_copy(qfeat.at[pair], qf_out.at[pair], out_sem.at[3 + 4 * pair]),
            pltpu.make_async_copy(kfeat.at[pair], kf_out.at[pair], out_sem.at[4 + 4 * pair]),
            pltpu.make_async_copy(mt.at[2 * pair : 2 * pair + 2], mt_out.at[2 * pair : 2 * pair + 2], out_sem.at[5 + 4 * pair]),
        ]
        for copy in more:
            copy.start()
        copies += more

    @pl.loop(0, n_chunks)
    def _(chunk):
        rows = pl.ds(pl.multiple_of(chunk * ROWS, ROWS), ROWS)
        low = mixed[rows, :]
        mixed_out[rows, :] = low
        for part, weight in enumerate(out_weights(pack, n_heads, part_width)):
            here = slice(part * feat, (part + 1) * feat)
            branch_ref[rows, here] = jnp.dot(low, weight, preferred_element_type=f32).astype(bf)

    for copy in copies:
        copy.wait()


def attn_forward(layer_no, n_heads, length, blocks, x_parts, pack_c, small_before):
    part_width, feat = n_heads * HEAD, pack_c[0].shape[1]
    seq, width = x_parts[0].shape
    pairs = n_heads // 2
    shape = jax.ShapeDtypeStruct
    outs = [
        shape((seq, width), bf),
        shape((3, seq, part_width), bf),
        shape((seq, width), bf),
        shape((pairs, seq // BLOCK, 4 * BLOCK, 2 * HEAD), bf),
        shape((pairs, seq, 2 * feat), bf),
        shape((pairs, seq, 2 * feat), bf),
        shape((n_heads, 2 * HEAD, feat), bf),
        shape((seq, part_width), bf),
    ]
    out_specs = [WHOLE, ANY, ANY, ANY, ANY, ANY, ANY, WHOLE]
    scratch = [
        pltpu.VMEM(pack_c[0].shape, bf),
        pltpu.VMEM((3, seq, part_width), bf),
        pltpu.VMEM((seq, width), bf),
        pltpu.VMEM((pairs, seq // BLOCK, 4 * BLOCK, 2 * HEAD), bf),
        pltpu.VMEM((pairs, seq, 2 * feat), bf),
        pltpu.VMEM((pairs, seq, 2 * feat), bf),
        pltpu.VMEM((n_heads, 2 * HEAD, feat), bf),
        pltpu.VMEM((seq, part_width), bf),
        pltpu.VMEM((4 * HEAD, 2 * feat), bf),
        pltpu.VMEM((seq, 2 * HEAD), f32),
        pltpu.VMEM((seq // BLOCK, 2 * BLOCK, 2 * HEAD), bf),
        pltpu.SemaphoreType.DMA((2,)),
        pltpu.SemaphoreType.DMA((2 + 4 * pairs,)),
    ]
    operands = list(x_parts)
    specs = [WHOLE] * len(x_parts)
    if layer_no == 1:
        operands += list(small_before)
        specs += [ANY] * 4
        outs = [shape((seq, width), bf)] + outs
        out_specs = [WHOLE] + out_specs
        scratch.append(pltpu.VMEM((PACK_ROWS, feat), bf))
    operands += list(pack_c)
    specs += [ANY] * 4
    return pl.pallas_call(
        functools.partial(attn_forward_kernel, layer_no, n_heads),
        out_shape=outs,
        in_specs=[SCALARS, SCALARS] + specs,
        out_specs=out_specs,
        scratch_shapes=scratch,
        compiler_params=pltpu.CompilerParams(vmem_limit_bytes=VMEM_BYTES),
        cost_estimate=SHORT,
        name=f"attn_forward_{layer_no}",
    )(length, blocks, *operands)


def gelu_parts(value):
    size = jnp.abs(value) * (0.5 ** 0.5)
    inverse = 1.0 / (1.0 + 0.3275911 * size)
    poly = inverse * (
        0.254829592
        + inverse
        * (-0.284496736 + inverse * (1.421413741 + inverse * (-1.453152027 + inverse * 1.061405429)))
    )
    bell = jnp.exp(-0.5 * value * value)
    tail = 0.5 * poly * bell
    below = jnp.where(value >= 0.0, 1.0 - tail, tail)
    return value * below, below + value * bell * (0.5 / 3.141592653589793) ** 0.5


def down_rows(wide, width, at, step):
    part, row = at // width, at % width
    return wide[width + row : width + row + step, part * width : (part + 1) * width]


def ffn_forward_kernel(layer_no, *refs):
    x_ref, part_a, part_b = refs[:3]
    small_c, wide_c = refs[3:7], refs[7:11]
    out_ref, hidden_ref, normed_ref, active_ref, slope_ref = refs[11:16]
    small, wide, sems = refs[16:]

    @pl.when(pl.program_id(0) == 0)
    def _():
        source = pick_source(layer_no)
        start_pick(source, small_part(small_c), small, sems.at[0])
        start_pick(source, wide_c, wide, sems.at[1])
        wait_pick(small_part(small_c), small, sems.at[0])
        wait_pick(wide_c, wide, sems.at[1])

    width = x_ref.shape[1]
    units = wide.shape[1]
    branch = part_a[...].astype(f32) + part_b[...].astype(f32)
    hidden = x_ref[...].astype(f32) + branch + vector_row(small, 4, width)
    hidden_ref[...] = hidden
    zhat, _ = norm_stats(hidden)
    low = (zhat * (1.0 + vector_row(small, 2, width)) + vector_row(small, 3, width)).astype(bf)
    normed_ref[...] = low
    total = None
    step = 256
    for at in range(0, units, step):
        upper = jnp.dot(low, wide[:width, at : at + step], preferred_element_type=f32)
        active, slope = gelu_parts(upper + small_row(small, 4 + at // step, step))
        active = active.astype(bf)
        active_ref[:, at : at + step] = active
        slope_ref[:, at : at + step] = slope.astype(bf)
        term = jnp.dot(active, down_rows(wide, width, at, step), preferred_element_type=f32)
        total = term if total is None else total + term
    out_ref[...] = total.astype(bf)


def ffn_forward(layer_no, x, part_a, part_b, weights):
    small_c, wide_c = weights
    seq, width = x.shape
    units = wide_c[0].shape[1]
    shape = jax.ShapeDtypeStruct
    rows = lambda cols: pl.BlockSpec((FFN_ROWS, cols), lambda i: (i, 0))
    return pl.pallas_call(
        functools.partial(ffn_forward_kernel, layer_no),
        grid=(seq // FFN_ROWS,),
        out_shape=[
            shape((seq, width), bf),
            shape((seq, width), f32),
            shape((seq, width), bf),
            shape((seq, units), bf),
            shape((seq, units), bf),
        ],
        in_specs=[rows(width)] * 3 + [ANY] * 8,
        out_specs=[rows(width), rows(width), rows(width), rows(units), rows(units)],
        scratch_shapes=[
            pltpu.VMEM((PACK_ROWS, small_c[0].shape[1]), bf),
            pltpu.VMEM(wide_c[0].shape, bf),
            pltpu.SemaphoreType.DMA((2,)),
        ],
        compiler_params=pltpu.CompilerParams(vmem_limit_bytes=VMEM_BYTES),
        cost_estimate=SHORT,
        name=f"ffn_forward_{layer_no}",
    )(x, part_a, part_b, *small_c, *wide_c)


def ffn_backward_kernel(layer_no, grad_ref, slope_ref, *refs):
    wide_c = refs[:4]
    out_ref, gupper_ref, bias_ref = refs[4:7]
    wide, sems = refs[7:]

    @pl.when(pl.program_id(0) == 0)
    def _():
        source = pick_source(layer_no)
        start_pick(source, wide_c, wide, sems.at[0])
        bias_ref[...] = jnp.zeros_like(bias_ref)
        wait_pick(wide_c, wide, sems.at[0])

    width = grad_ref.shape[1]
    units = wide.shape[1]
    grad = grad_ref[...]
    total = None
    step = 256
    for at in range(0, units, step):
        gactive = contract(grad, down_rows(wide, width, at, step), 1, 1)
        gupper = (gactive * slope_ref[:, at : at + step].astype(f32)).astype(bf)
        gupper_ref[:, at : at + step] = gupper
        bias_ref[:, at : at + step] += fold_rows(gupper.astype(f32))
        term = contract(gupper, wide[:width, at : at + step], 1, 1)
        total = term if total is None else total + term
    out_ref[...] = total.astype(bf)


def fold_rows(value):
    rows, cols = value.shape
    return jnp.sum(value.reshape(rows // 8, 8, cols), axis=0)


def ffn_backward(layer_no, grad, slope, weights):
    (wide_c,) = weights
    seq, width = grad.shape
    units = wide_c[0].shape[1]
    shape = jax.ShapeDtypeStruct
    rows = lambda cols: pl.BlockSpec((FFN_ROWS, cols), lambda i: (i, 0))
    return pl.pallas_call(
        functools.partial(ffn_backward_kernel, layer_no),
        grid=(seq // FFN_ROWS,),
        out_shape=[shape((seq, width), bf), shape((seq, units), bf), shape((8, units), f32)],
        in_specs=[rows(width), rows(units)] + [ANY] * 4,
        out_specs=[rows(width), rows(units), pl.BlockSpec((8, units), lambda i: (0, 0))],
        scratch_shapes=[
            pltpu.VMEM(wide_c[0].shape, bf),
            pltpu.SemaphoreType.DMA((1,)),
        ],
        compiler_params=pltpu.CompilerParams(vmem_limit_bytes=VMEM_BYTES),
        cost_estimate=SHORT,
        name=f"ffn_backward_{layer_no}",
    )(grad, slope, *wide_c)


def attn_backward_kernel(layer_no, n_heads, blocks_ref, *refs):
    gy_ref, part_a, part_b, hidden_ref, x_ref = refs[:5]
    qkv_in, probs_in, qf_in, kf_in, mt_in = refs[5:10]
    pack_c, refs = refs[10:14], refs[14:]
    out_ref, gbranch_ref, dqkv_ref, first_ref, vec_ref, bias_ref, refs = *refs[:6], refs[6:]
    (pack, qkv, probs, qfeat, kfeat, mt, gmix, gstack, qstack, gext, gt, fback,
     dq, dk, dv, sem) = refs
    seq, width = gy_ref.shape
    n_chunks = seq // ROWS
    pairs = n_heads // 2
    part_width = qkv.shape[2]
    feat = pack.shape[1]
    small = pack.at[0:PACK_ROWS]
    source = pick_source(layer_no)
    start_pick(source, pack_c, pack, sem.at[0])
    loads = [
        pltpu.make_async_copy(qkv_in, qkv, sem.at[2]),
        pltpu.make_async_copy(mt_in, mt, sem.at[3]),
        pltpu.make_async_copy(qf_in, qfeat, sem.at[4]),
        pltpu.make_async_copy(kf_in, kfeat, sem.at[5]),
        pltpu.make_async_copy(probs_in, probs, sem.at[6]),
    ]
    for load in loads:
        load.start()
    first_ref[...] = jnp.zeros_like(first_ref)
    vec_ref[...] = jnp.zeros_like(vec_ref)
    bias_ref[...] = jnp.zeros_like(bias_ref)
    wait_pick(pack_c, pack, sem.at[0])
    gain = 1.0 + vector_row(small, 2, width)
    in_first, in_second = lane_masks()
    masks = (in_first, in_second)

    @pl.loop(0, n_chunks)
    def _(chunk):
        rows = pl.ds(pl.multiple_of(chunk * ROWS, ROWS), ROWS)
        gnormed = part_a[rows, :].astype(f32) + part_b[rows, :].astype(f32)
        zhat, scale = norm_stats(hidden_ref[rows, :])
        scaled = gnormed * gain
        gy = gy_ref[rows, :].astype(f32)
        mean_one = jnp.mean(scaled, axis=-1, keepdims=True)
        mean_two = jnp.mean(scaled * zhat, axis=-1, keepdims=True)
        ghidden = gy + (scaled - mean_one - zhat * mean_two) * scale
        low = ghidden.astype(bf)
        gbranch_ref[rows, :] = low
        vec_ref[0] += fold_rows(gnormed * zhat)
        vec_ref[1] += fold_rows(gnormed)
        vec_ref[2] += fold_rows(low.astype(f32))
        vec_ref[3] += fold_rows(gy)
        first, second = out_weights(pack, n_heads, part_width)
        gmix[rows, :] = (contract(low[:, :feat], first, 1, 1) + contract(low[:, feat:], second, 1, 1)).astype(bf)

    for load in loads[:4]:
        load.wait()
    for pair in range(pairs):
        cols = slice(pair * 2 * HEAD, (pair + 1) * 2 * HEAD)
        for a in range(2):
            plain = feature_rows(pack, n_heads, 2 * pair + a) * F_SCALE
            high = plain.astype(bf).astype(f32)
            ones = jnp.ones((HEAD, feat), f32)
            none = jnp.zeros((HEAD, feat), f32)
            stack = [high, ones] if a == 0 else [ones, high]
            stack += [plain - high, none] if a == 0 else [none, plain - high]
            fback[a] = jnp.concatenate(stack, axis=0).astype(bf)

        def feature_back(a, gfeat, feats, vectors):
            gexpo = (gfeat * feats.astype(f32)).astype(bf)
            both = contract(gexpo, fback[a], 1, 1)
            both = both[:, : 2 * HEAD] + both[:, 2 * HEAD :]
            return both - (F_SCALE * F_SCALE) * swap_halves(both) * vectors

        @pl.loop(0, n_chunks)
        def _(chunk):
            rows = pl.ds(pl.multiple_of(chunk * ROWS, ROWS), ROWS)
            grad = gmix[rows, cols].astype(f32)
            query = qkv[0, rows, cols].astype(f32)
            out = None
            for a in range(2):
                feats = qfeat[pair, rows, a * feat : (a + 1) * feat]
                moment = mt[2 * pair + a]
                numer = contract(feats, moment, 1, 1)
                inverse = 1.0 / swap_halves(numer)
                gnumer = grad * inverse
                other = swap_halves(gnumer * numer * inverse)
                both = jnp.where(masks[a], gnumer, -other).astype(bf)
                gext[a, rows, :] = both
                gfeat = jnp.dot(both, moment, preferred_element_type=f32)
                value = feature_back(a, gfeat, feats, query)
                out = value if a == 0 else jnp.where(in_first, out, value)
            dq[rows, :] = out
            stack_heads(gstack, chunk, grad, masks)
            stack_heads(qstack, chunk, query * (HEAD ** -0.5), masks)

        for a in range(2):
            gt[a] = contract(gext[a], qfeat[pair, :, a * feat : (a + 1) * feat], 0, 0).astype(bf)

        @pl.loop(0, n_chunks)
        def _(chunk):
            rows = pl.ds(pl.multiple_of(chunk * ROWS, ROWS), ROWS)
            key = qkv[1, rows, cols].astype(f32)
            value_f = qkv[2, rows, cols].astype(f32)
            dk_out, dv_out = None, None
            for a in range(2):
                extended = jnp.where(masks[a], value_f, 1.0).astype(bf)
                feats = kfeat[pair, rows, a * feat : (a + 1) * feat]
                gfeat = jnp.dot(extended, gt[a], preferred_element_type=f32)
                dk_one = feature_back(a, gfeat, feats, key)
                dv_one = contract(feats, gt[a], 1, 1)
                dk_out = dk_one if a == 0 else jnp.where(in_first, dk_out, dk_one)
                dv_out = dv_one if a == 0 else jnp.where(in_first, dv_out, dv_one)
            dk[rows, :] = dk_out
            dv[rows, :] = dv_out

        if pair == 0:
            loads[4].wait()

        @pl.loop(0, seq // BLOCK, unroll=SPARSE_UNROLL)
        def _(block):
            rows = pl.ds(pl.multiple_of(block * BLOCK, BLOCK), BLOCK)
            starts = listed_starts(blocks_ref, pair, block, seq // BLOCK)
            keys = pick_rows(qkv, 1, cols, starts, in_first)
            values = pick_rows(qkv, 2, cols, starts, in_first)
            weights = probs[pair, block]
            weights_f = weights.astype(f32)
            grad = gstack[block]
            gweights = contract(values, grad, 1, 1)
            inner = jnp.sum(weights_f * gweights, axis=0, keepdims=True)
            gscores = (weights_f * (gweights - inner)).astype(bf)
            both = contract(gscores, keys, 0, 0)
            out = jnp.where(in_first, both[:BLOCK], both[BLOCK:]) * (HEAD ** -0.5)
            dkeys = jnp.dot(gscores, qstack[block], preferred_element_type=f32)
            dvalues = jnp.dot(weights, grad, preferred_element_type=f32)
            for total, part in ((dk, dkeys), (dv, dvalues)):
                total[0:BLOCK, :] += part[:BLOCK]
                for slot, (one, two) in enumerate(starts):
                    piece = part[(slot + 1) * BLOCK : (slot + 2) * BLOCK]
                    total[pl.ds(one, BLOCK), :] += jnp.where(in_first, piece, 0.0)
                    total[pl.ds(two, BLOCK), :] += jnp.where(in_first, 0.0, piece)
            dq[rows, :] += out

        @pl.loop(0, n_chunks)
        def _(chunk):
            rows = pl.ds(pl.multiple_of(chunk * ROWS, ROWS), ROWS)
            for part, total in enumerate((dq, dk, dv)):
                low = total[rows, :].astype(bf)
                dqkv_ref[part, rows, cols] = low
                bias_ref[part, :, cols] += fold_rows(low.astype(f32))


    @pl.loop(0, n_chunks)
    def _(chunk):
        rows = pl.ds(pl.multiple_of(chunk * ROWS, ROWS), ROWS)
        total = None
        for part in range(3):
            term = contract(dqkv_ref[part, rows, :], qkv_weight(pack, n_heads, width, part), 1, 1)
            total = term if total is None else total + term
        low = total.astype(bf)
        out_ref[rows, :] = low
        zhat, _ = norm_stats(x_ref[rows, :].astype(f32))
        total = low.astype(f32)
        first_ref[0] += fold_rows(total * zhat)
        first_ref[1] += fold_rows(total)


def attn_backward(layer_no, n_heads, blocks, gy, part_a, part_b, hidden, x, kept, pack_c):
    seq, width = gy.shape
    part_width, feat = n_heads * HEAD, pack_c[0].shape[1]
    pairs = n_heads // 2
    shape = jax.ShapeDtypeStruct
    operands = [gy, part_a, part_b, hidden, x, *kept, *pack_c]
    return pl.pallas_call(
        functools.partial(attn_backward_kernel, layer_no, n_heads),
        out_shape=[
            shape((seq, width), bf),
            shape((seq, width), bf),
            shape((3, seq, part_width), bf),
            shape((2, 8, width), f32),
            shape((4, 8, width), f32),
            shape((3, 8, part_width), f32),
        ],
        in_specs=[SCALARS] + [WHOLE] * 5 + [ANY] * 9,
        out_specs=[WHOLE] * 6,
        scratch_shapes=[
            pltpu.VMEM(pack_c[0].shape, bf),
            pltpu.VMEM((3, seq, part_width), bf),
            pltpu.VMEM((pairs, seq // BLOCK, 4 * BLOCK, 2 * HEAD), bf),
            pltpu.VMEM((pairs, seq, 2 * feat), bf),
            pltpu.VMEM((pairs, seq, 2 * feat), bf),
            pltpu.VMEM((n_heads, 2 * HEAD, feat), bf),
            pltpu.VMEM((seq, part_width), bf),
            pltpu.VMEM((seq // BLOCK, 2 * BLOCK, 2 * HEAD), bf),
            pltpu.VMEM((seq // BLOCK, 2 * BLOCK, 2 * HEAD), bf),
            pltpu.VMEM((2, seq, 2 * HEAD), bf),
            pltpu.VMEM((2, 2 * HEAD, feat), bf),
            pltpu.VMEM((2, 4 * HEAD, feat), bf),
            pltpu.VMEM((seq, 2 * HEAD), f32),
            pltpu.VMEM((seq, 2 * HEAD), f32),
            pltpu.VMEM((seq, 2 * HEAD), f32),
            pltpu.SemaphoreType.DMA((7,)),
        ],
        compiler_params=pltpu.CompilerParams(vmem_limit_bytes=VMEM_BYTES),
        cost_estimate=SHORT,
        name=f"attn_backward_{layer_no}",
    )(blocks, *operands)


def norm_backward_kernel(layer_no, x_ref, part_a, part_b, ghidden_ref, *refs):
    small_c = refs[:4]
    low_ref, small, sems = refs[4:]

    @pl.when(pl.program_id(0) == 0)
    def _():
        start_pick(pick_source(layer_no), small_part(small_c), small, sems.at[0])
        wait_pick(small_part(small_c), small, sems.at[0])

    width = x_ref.shape[1]
    gnormed = part_a[...].astype(f32) + part_b[...].astype(f32)
    zhat, scale = norm_stats(x_ref[...].astype(f32))
    scaled = gnormed * (1.0 + vector_row(small, 0, width))
    mean_one = jnp.mean(scaled, axis=-1, keepdims=True)
    mean_two = jnp.mean(scaled * zhat, axis=-1, keepdims=True)
    total = ghidden_ref[...].astype(f32) + (scaled - mean_one - zhat * mean_two) * scale
    low_ref[...] = total.astype(bf)


def norm_backward(layer_no, x, part_a, part_b, ghidden, small_c):
    seq, width = x.shape
    shape = jax.ShapeDtypeStruct
    rows = pl.BlockSpec((FFN_ROWS, width), lambda i: (i, 0))
    return pl.pallas_call(
        functools.partial(norm_backward_kernel, layer_no),
        grid=(seq // FFN_ROWS,),
        out_shape=shape((seq, width), bf),
        in_specs=[rows] * 4 + [ANY] * 4,
        out_specs=rows,
        scratch_shapes=[pltpu.VMEM((PACK_ROWS, small_c[0].shape[1]), bf), pltpu.SemaphoreType.DMA((1,))],
        compiler_params=pltpu.CompilerParams(vmem_limit_bytes=VMEM_BYTES),
        cost_estimate=SHORT,
        name=f"norm_backward_{layer_no}",
    )(x, part_a, part_b, ghidden, *small_c)


def tiny_rows(first, moved, vec, bias_qkv, bias_up):
    width = vec.shape[2]
    half = width // 2
    here = pl.ds(pl.multiple_of(lax.rem(lax.axis_index("dp"), 2) * half, half), half)
    total = lambda value: jnp.sum(value, axis=0, keepdims=True)
    parts = [total(first[i, :, here] + moved[i, :, here]) for i in range(2)]
    parts += [total(vec[i, :, here]) for i in range(4)]
    parts += [total(bias_qkv[i]) for i in range(3)] + [jnp.zeros((1, half), f32)]
    up = total(bias_up[...])
    parts += [up[:, at : at + half] for at in range(0, up.shape[1], half)]
    return [jnp.concatenate(parts[i : i + 2], axis=1) for i in range(0, len(parts), 2)]


def weight_grad_kernel(n_first, n_extra, left_a, left_b, right_a, right_b, *refs):
    keep_ref, away_ref, turned = refs[-3:]
    extra, sums = refs[:n_extra], refs[n_extra:-3]
    step = pl.program_id(0)
    total_rows, cols = keep_ref.shape
    per_half = pl.num_programs(0) // 2
    width = right_a.shape[1]
    n_rows = left_a.shape[1]
    first = step < n_first

    @pl.when(step == 0)
    def _():
        turned[...] = left_a[...].T
        for source, target in zip(extra, (keep_ref, away_ref)):
            target[:, per_half * width :] = source[...]
        if sums:
            rows = tiny_rows(*sums[:5]) + tiny_rows(*sums[5:])
            rows += [jnp.zeros_like(rows[0])] * (total_rows - n_rows - len(rows))
            low = jnp.concatenate(rows, axis=0).astype(bf)
            for target in (keep_ref, away_ref):
                target[n_rows:, :] = low

    @pl.when(step == n_first)
    def _():
        turned[...] = left_b[...].T

    right = jnp.where(first, right_a[...], right_b[...])
    result = jnp.dot(turned[...], right, preferred_element_type=f32).astype(bf)
    here = pl.ds(pl.multiple_of(lax.rem(step, per_half) * width, width), width)
    keep = step // per_half == lax.axis_index("section")
    n_shards = lax.axis_size("dp")
    shard = n_rows // n_shards
    for wanted, target in ((keep, keep_ref), (jnp.logical_not(keep), away_ref)):

        @pl.when(wanted)
        def _():
            for number in range(n_shards):
                at = ((number % 2) * (n_shards // 2) + number // 2) * shard
                target[at : at + shard, here] = result[number * shard : (number + 1) * shard]


def weight_grads(name, step, left_a, right_a, left_b, right_b, extra=(), sums=()):
    seq, width = left_a.shape
    if right_a.ndim == 3:
        n_first = right_a.shape[0]
        spec_a = pl.BlockSpec((None, seq, step), lambda i: (jnp.minimum(i, n_first - 1), 0, 0))
    else:
        n_first = right_a.shape[1] // step
        spec_a = pl.BlockSpec((seq, step), lambda i: (0, jnp.minimum(i, n_first - 1)))
    n_second = right_b.shape[1] // step
    spec_b = pl.BlockSpec((seq, step), lambda i: (0, jnp.maximum(i - n_first, 0)))
    whole = pl.BlockSpec((seq, width), lambda i: (0, 0))
    n_steps = n_first + n_second
    cols = step * (n_steps // 2) + (extra[0].shape[1] if extra else 0)
    shape = (width + (TINY_ROWS if sums else 0), cols)
    fixed = lambda shape: pl.BlockSpec(shape, lambda i: (0,) * len(shape))
    return pl.pallas_call(
        functools.partial(weight_grad_kernel, n_first, len(extra)),
        grid=(n_steps,),
        out_shape=[jax.ShapeDtypeStruct(shape, bf)] * 2,
        in_specs=[whole, whole, spec_a, spec_b] + [fixed(item.shape) for item in (*extra, *sums)],
        out_specs=[fixed(shape)] * 2,
        scratch_shapes=[pltpu.VMEM((width, seq), bf)],
        compiler_params=pltpu.CompilerParams(vmem_limit_bytes=VMEM_BYTES),
        cost_estimate=SHORT,
        name=name,
    )(left_a, left_b, right_a, right_b, *extra, *sums)


ALL_AXES = ("section", "tensor", "dp")


def send(value, sizes, target):
    n_section, n_tensor, n_dp = sizes
    pairs = []
    for s in range(n_section):
        for t in range(n_tensor):
            for d in range(n_dp):
                goal = target(s, t, d // 2, d % 2)
                if goal is not None:
                    gs, gt, gz, gc = goal
                    number = (s * n_tensor + t) * n_dp + d
                    pairs.append((number, (gs * n_tensor + gt) * n_dp + 2 * gz + gc))
    return lax.ppermute(value, ALL_AXES, pairs)


def other_core(value, sizes):
    return send(value, sizes, lambda s, t, z, c: (s, t, z, 1 - c))


def chip_shards(
    sizes,
    inputs,
    cotangent,
    lengths,
    blocks,
    feature_map,
    w_qkv,
    b_qkv,
    w_out,
    w_up,
    b_up,
    w_down,
    vector_params,
):
    n_dp = sizes[2]
    n_z = n_dp // 2
    section_no = lax.axis_index("section")
    tensor_no = lax.axis_index("tensor")
    dp_no = lax.axis_index("dp")
    z_no, core = dp_no // 2, dp_no % 2
    same = core == tensor_no
    is_first = section_no == 0
    width = inputs.shape[2]
    half = inputs.shape[1]
    n_heads, n_blocks, n_listed = blocks.shape[1:]
    feat = feature_map.shape[3]
    part_width = w_qkv.shape[3]

    def after(value, earlier):
        return lax.optimization_barrier((value, earlier))[0]

    def share_y(array):
        return send(array, sizes, lambda s, t, z, c: (1 - s, t, z, c) if c == t else None)

    def share_x(array):
        return send(array, sizes, lambda s, t, z, c: (s, 1 - t, z, c) if c == t else None)

    wide = jnp.concatenate(
        [w_up[0], jnp.concatenate([w_down[0][:width], w_down[0][width:]], axis=1)], axis=0
    )
    def halves(own, first, second):
        near = jnp.where(same, own, first)
        far = jnp.where(same, first, second)
        swap = tensor_no == 1
        return jnp.concatenate(
            [jnp.where(swap, far, near), jnp.where(swap, near, far)], axis=0
        )

    def cross(own):
        return send(
            own,
            sizes,
            lambda s, t, z, c: (s, t, z, 1 - c) if c == t else (s, 1 - t, z, c),
        )

    def to_sequence(own, first):
        second = send(first, sizes, lambda s, t, z, c: (s, t, z, 1 - c) if c == t else None)
        return halves(own, first, second)

    x_own = inputs[section_no]
    x_arrived = cross(x_own)
    pack = pack_weights(
        after(w_qkv[0].transpose(1, 0, 2), x_own),
        w_out[0],
        feature_map[0].reshape(n_heads * HEAD, feat),
        b_qkv[0],
        b_up,
        vector_params[0],
        blocks[0].reshape(n_heads * n_blocks, n_listed),
    )
    x_first = to_sequence(x_own, x_arrived)
    pack_y = share_y(pack)
    pack_x = share_x(pack)
    pack_both = share_x(after(pack_y, pack_x))
    pack_c = (pack, pack_y, pack_x, pack_both)
    wide_y = share_y(after(wide, pack_y))

    def share_wide(layer_no, earlier):
        def share(array, section):
            return send(
                after(array, earlier),
                sizes,
                lambda s, t, z, c: (s, 1 - t, z, c) if c == t and s == section else None,
            )

        return (wide, wide_y, share(wide, layer_no), share(wide_y, 1 - layer_no))

    weights = [(pack_c, share_wide(0, pack_both))]

    lengths_here = jnp.where(same, lengths, other_core(lengths, sizes))
    length = lax.dynamic_slice_in_dim(lengths_here[:, 0], section_no, 1)

    def of_layer(layer_no, candidates):
        mine = section_no == layer_no
        return jnp.where(
            same,
            jnp.where(mine, candidates[0], candidates[1]),
            jnp.where(mine, candidates[2], candidates[3]),
        )

    def exchange(value):
        return value, other_core(value, sizes)

    kept = []
    x_parts = (x_first,)
    outputs = []
    for layer_no in range(2):
        listed = of_layer(
            layer_no,
            [item[PACK_ROWS : PACK_ROWS + n_heads * n_blocks, :n_listed] for item in pack_c],
        )
        listed = listed.astype(jnp.int32)
        made = attn_forward(layer_no, n_heads, length, listed, x_parts, pack_c, pack_c)
        if layer_no == 0:
            x = x_first
        else:
            x, made = made[0], made[1:]
            outputs.append(x)
        branch, qkv, normed, probs, qfeat, kfeat, mt, mixed = made
        if layer_no == 0:
            grad_own = after(cotangent[section_no], (weights[0][1][2:], branch))
            grad_arrived = cross(grad_own)
            weights.append((pack_c, share_wide(1, (weights[0][1][2:], branch))))
        result, hidden, normed_two, active, slope = ffn_forward(
            layer_no, x, *exchange(branch), weights[layer_no]
        )
        x_parts = (hidden, *exchange(result))
        kept.append(
            (x, normed, mixed, hidden, normed_two, active, slope, listed,
             (qkv, probs, qfeat, kfeat, mt))
        )

    grad = to_sequence(grad_own, grad_arrived)

    def my_half(array):
        return lax.dynamic_slice_in_dim(array, core * half, half)

    def deliver(first_rows, second_rows):
        mine = jnp.where(is_first, first_rows, second_rows)
        theirs = jnp.where(is_first, second_rows, first_rows)
        own = send(mine, sizes, lambda s, t, z, c: (s, c, z, t))
        other = send(theirs, sizes, lambda s, t, z, c: (1 - s, c, z, t))
        return own, other

    hidden, part_a, part_b = x_parts
    last_bias = of_layer(1, [lane[18:20].reshape(1, width) for lane in pack_c]).astype(f32)
    last = my_half(hidden) + (my_half(part_a).astype(f32) + my_half(part_b).astype(f32)) + last_bias

    def plane_send(keep, away):
        by_x = send(keep, sizes, lambda s, t, z, c: None if c == t else (s, 1 - t, z, c))
        by_y = share_y(away)
        by_both = send(away, sizes, lambda s, t, z, c: None if c == t else (1 - s, 1 - t, z, c))
        return keep, by_x, by_y, by_both

    def core_sum(terms):
        total = terms[0].astype(f32)
        for term in terms[1:]:
            total = total + term.astype(f32)
        total = total.astype(bf)
        tail = total[width:]
        by_core = total[:width].reshape(2, width // 2, -1)
        other = lax.dynamic_index_in_dim(by_core, 1 - core, keepdims=False)
        arrived = send(
            jnp.concatenate([other, tail], axis=0),
            sizes,
            lambda s, t, z, c: (s, t, z, 1 - c) if c == t else None,
        )
        own = lax.dynamic_index_in_dim(by_core, core, keepdims=False)
        return jnp.where(same, jnp.concatenate([own, tail], axis=0), arrived)

    def line_send(piece):
        def shard_for(step):
            at = ((z_no + step) % n_z) * shard
            rows = lax.dynamic_slice_in_dim(piece, at, shard)
            return jnp.concatenate([rows, piece[width // 2 :]], axis=0)

        return [shard_for(0)] + [
            send(shard_for(step), sizes, lambda s, t, z, c: (s, t, (z + step) % n_z, c))
            for step in range(1, n_z)
        ]

    def line_sum(found):
        total = found[0].astype(f32)
        for part in found[1:]:
            total = total + part.astype(f32)
        return total

    def ffn_part(layer_no, grad, hold):
        normed_two, active, slope = kept[layer_no][4:7]
        gnormed_two, gupper, bias_up = ffn_backward(
            layer_no, after(grad, hold), slope, (weights[layer_no][1],)
        )
        parts = exchange(gnormed_two)
        return parts, gupper, bias_up

    def ffn_grads(layer_no, grad, gupper, hold, extra=()):
        normed_two, active = kept[layer_no][4:6]
        return weight_grads(
            f"ffn_grads_{layer_no}", 512, after(normed_two, hold), gupper, grad, active, extra
        )

    def attn_part(layer_no, grad, parts, hold):
        hidden, listed, attn_kept = kept[layer_no][3], kept[layer_no][7], kept[layer_no][8]
        gnormed, *rest = attn_backward(
            layer_no, n_heads, listed, grad, after(parts[0], hold), parts[1], hidden,
            kept[layer_no][0], attn_kept, pack_c,
        )
        gbranch, gproj, vec_one, vec_two, bias_qkv = rest
        sums = (vec_one, other_core(vec_one, sizes), vec_two, bias_qkv)
        return exchange(gnormed), gbranch, gproj, sums

    def attn_grads(layer_no, gproj, gbranch, hold, sums=()):
        normed, mixed = kept[layer_no][1:3]
        return weight_grads(
            f"attn_grads_{layer_no}", part_width, after(normed, hold), gproj, gbranch, mixed, (), sums
        )

    def norm_part(layer_no, parts, gbranch, hold):
        return norm_backward(
            layer_no, kept[layer_no][0], after(parts[0], hold), parts[1], gbranch, pack_c
        )

    shard = width // n_dp
    units = wide.shape[1]
    parts, gupper, bias_up = ffn_part(1, grad, x_parts[0])
    keep, away = ffn_grads(1, grad, gupper, parts[0])
    wide_one = plane_send(keep, away)
    parts, gbranch, gproj, sums = attn_part(1, grad, parts, keep)
    sums_one = (*sums, bias_up)
    wide_one = core_sum(after(wide_one, gbranch))
    line_one = line_send(wide_one)
    extra = attn_grads(1, gproj, gbranch, wide_one)
    grad = norm_part(1, parts, gbranch, extra[0])
    upper_grad = grad
    line_one = after(line_one, grad)
    out_pair = deliver(my_half(after(outputs[0], line_one)), last.astype(bf))
    parts, gupper, bias_up = ffn_part(0, grad, line_one)
    keep, away = ffn_grads(0, grad, gupper, parts[0], extra)
    keep, away, out_pair = after((keep, away, out_pair), keep)
    wide_zero = plane_send(keep, away)
    parts, gbranch, gproj, sums = attn_part(0, grad, parts, (keep, out_pair))
    wide_zero = after(wide_zero, gbranch)
    keep, away = attn_grads(
        0, gproj, gbranch, (parts[0], wide_zero), (*sums_one, *sums, bias_up)
    )
    narrow_zero = plane_send(keep, away)
    grad = norm_part(0, parts, gbranch, keep)
    line_wide = line_send(core_sum(after(wide_zero, keep)))
    narrow_zero, line_wide = after((narrow_zero, line_wide), grad)
    grad_pair = deliver(my_half(grad), my_half(upper_grad))
    line_narrow = line_send(core_sum(narrow_zero))
    line_narrow, grad_pair = after((line_narrow, grad_pair), grad)
    line_narrow = line_sum(after(line_narrow, grad_pair))
    line_wide = line_sum(line_wide)
    first_sum = jnp.concatenate([line_wide[:, :units], line_narrow[:shard]], axis=1)
    second_sum = jnp.concatenate([line_sum(line_one), line_wide[:, units:]], axis=1)
    gone = jnp.where(is_first, second_sum, first_sum).astype(bf)
    arrived = send(gone, sizes, lambda s, t, z, c: (1 - s, t, z, c)).astype(f32)
    stay = jnp.where(is_first, first_sum, second_sum)
    low_half = jnp.where(is_first, stay, arrived)
    high_half = jnp.where(is_first, arrived, stay)
    grad_up, grad_down = low_half[:, :units], high_half[:, :units]
    narrow = jnp.concatenate([low_half[:, units:], high_half[:, units:]], axis=1)
    rows = line_narrow[shard:]
    rows = jnp.where(is_first, rows[7:14], rows[:7]).reshape(14, width // 2)

    def own_columns(array):
        cols = array.reshape(-1, n_dp, array.shape[1] // n_dp)
        return lax.dynamic_index_in_dim(cols, dp_no, axis=1, keepdims=False)

    grad_vectors = own_columns(rows[:6])
    grad_bqkv = own_columns(rows[6:9])
    grad_bup = own_columns(rows[10:].reshape(1, -1))[0]

    def placed(pair, dtype):
        own, other = pair
        return jnp.stack(
            [jnp.where(is_first, own, other), jnp.where(is_first, other, own)]
        )[None].astype(dtype)

    section_outputs = placed(out_pair, bf)
    input_grads = placed(grad_pair, f32)
    grad_qkv = narrow[:, : 3 * part_width].reshape(shard, 3, part_width)
    grad_out = narrow[:, 3 * part_width :].T
    return (
        section_outputs,
        input_grads,
        grad_qkv[None],
        grad_bqkv[None],
        grad_out[None],
        grad_up[None],
        grad_bup[None],
        grad_down.T[None],
        grad_vectors[None],
    )


HEAD = 64
BLOCK = 64
SEQ_LEN = 1024


norm_eps = 1e-05
bfloat = jnp.bfloat16
single = jnp.float32


def shifted(value, axis, steps):
    count = lax.axis_size(axis)
    first, last = (max(0, -steps), min(count, count - steps))
    return lax.ppermute(value, axis, [(source, source + steps) for source in range(first, last)])


def norm_rows(residual, gain_vec, shift_vec):
    row_mean = jnp.mean(residual, axis=-1, keepdims=True)
    centred = residual - row_mean
    variance = jnp.mean(centred * centred, axis=-1, keepdims=True)
    return centred * lax.rsqrt(variance + norm_eps) * (1.0 + gain_vec) + shift_vec


def gelu_exact(pre_active):
    return jax.nn.gelu(pre_active, approximate=False)


def select_tree(flag_value, when_true, when_false):
    return jax.tree.map(
        lambda left_arr, right_arr: jnp.where(flag_value, left_arr, right_arr),
        when_true,
        when_false,
    )


def split_pieces(operand):
    if operand.dtype == bfloat:
        return (operand,)
    upper_part = operand.astype(bfloat)
    lower_part = (operand - upper_part.astype(single)).astype(bfloat)
    return (upper_part, lower_part)


def split_dot(form, left, right):
    left_pieces = split_pieces(left)
    right_pieces = split_pieces(right)
    total = None
    for left_no, left_piece in enumerate(left_pieces):
        for right_no, right_piece in enumerate(right_pieces):
            if left_no + right_no > 1:
                continue
            term = jnp.einsum(form, left_piece, right_piece, preferred_element_type=single)
            total = term if total is None else total + term
    return total


def sparse_layout(block_list, length):
    head_count, block_count = (block_list.shape[0], block_list.shape[1])
    chosen = jnp.concatenate(
        [jnp.zeros((head_count, block_count, 1), jnp.int32), block_list], axis=2
    )
    key_live = (jnp.arange(SEQ_LEN) < length).astype(single)
    picked_live = key_live.reshape(block_count, BLOCK)[chosen].reshape(head_count, block_count, -1)
    return (chosen, key_live, picked_live)


def pick_blocks(table_in, chosen):
    head_count, block_count = (chosen.shape[0], chosen.shape[1])
    blocks_in = table_in.reshape(head_count, block_count, BLOCK, table_in.shape[-1])
    taken_rows = jax.vmap(lambda one_table, index_rows: one_table[index_rows])(blocks_in, chosen)
    return taken_rows.reshape(head_count, block_count, -1, table_in.shape[-1])


def place_blocks(values_in, chosen):
    head_count, block_count, slot_count = chosen.shape
    parts_in = values_in.reshape(head_count, block_count, slot_count, BLOCK, values_in.shape[-1])
    zero_blocks = jnp.zeros((head_count, block_count, BLOCK, values_in.shape[-1]), single)
    placed = jax.vmap(lambda base_arr, index_rows, one_part: base_arr.at[index_rows].add(one_part))(
        zero_blocks, chosen, parts_in
    )
    return placed.reshape(head_count, SEQ_LEN, values_in.shape[-1])


def feature_of(vectors_low, features):
    feature_scale = HEAD ** (-0.25)
    vectors = vectors_low.astype(single)
    projected = split_dot("hld,hdf->hlf", vectors_low, features) * feature_scale
    return jnp.exp(
        projected
        - jnp.sum(vectors * vectors, axis=-1, keepdims=True) * (0.5 * feature_scale * feature_scale)
    )


def block_scores(query_blocks, picked_keys, picked_live):
    scores = jnp.einsum(
        "hnqd,hnkd->hnqk", query_blocks, picked_keys, preferred_element_type=single
    ) * HEAD ** (-0.5)
    return jnp.where(picked_live[:, :, None, :] > 0.5, scores, -1e30)


def attend_forward(queries, key_vecs, value_vecs, chosen, key_live, picked_live, features):
    head_count, block_count = (chosen.shape[0], chosen.shape[1])
    query_blocks = queries.reshape(head_count, block_count, BLOCK, HEAD)
    picked_keys = pick_blocks(key_vecs, chosen)
    picked_values = pick_blocks(value_vecs, chosen)
    scores = block_scores(query_blocks, picked_keys, picked_live)
    row_max = jnp.max(scores, axis=-1, keepdims=True)
    weights_raw = jnp.exp(scores - row_max) * picked_live[:, :, None, :]
    row_total = jnp.sum(weights_raw, axis=-1, keepdims=True)
    log_total = row_max + jnp.log(row_total)
    weights_low = (weights_raw / row_total).astype(bfloat)
    sparse_out = jnp.einsum(
        "hnqk,hnkd->hnqd", weights_low, picked_values, preferred_element_type=single
    )
    sparse_out = sparse_out.reshape(head_count, SEQ_LEN, HEAD)
    query_feats = feature_of(queries, features)
    key_feats = feature_of(key_vecs, features) * key_live[None, :, None]
    moments = split_dot("hlf,hld->hfd", key_feats, value_vecs)
    totals = jnp.sum(key_feats, axis=1)
    numerator = split_dot("hlf,hfd->hld", query_feats, moments)
    denominator = split_dot("hlf,hf->hl", query_feats, totals)
    perf_out = numerator / denominator[:, :, None]
    return (
        sparse_out + perf_out,
        (log_total, query_feats, key_feats, moments, totals, denominator, perf_out),
    )


def attend_backward(
    grad_heads, queries, key_vecs, value_vecs, chosen, picked_live, features, attn_keep
):
    log_total, query_feats, key_feats, moments, totals, denominator, perf_out = attn_keep
    head_count, block_count = (chosen.shape[0], chosen.shape[1])
    score_scale = HEAD ** (-0.5)
    query_blocks = queries.reshape(head_count, block_count, BLOCK, HEAD)
    grad_blocks = grad_heads.reshape(head_count, block_count, BLOCK, HEAD)
    picked_keys = pick_blocks(key_vecs, chosen)
    picked_values = pick_blocks(value_vecs, chosen)
    scores = block_scores(query_blocks, picked_keys, picked_live)
    weights_f = jnp.exp(scores - log_total) * picked_live[:, :, None, :]
    grad_weights = jnp.einsum(
        "hnqd,hnkd->hnqk", grad_blocks, picked_values, preferred_element_type=single
    )
    row_inner = jnp.sum(weights_f * grad_weights, axis=-1, keepdims=True)
    grad_scores = (weights_f * (grad_weights - row_inner)).astype(bfloat)
    grad_query = jnp.einsum(
        "hnqk,hnkd->hnqd", grad_scores, picked_keys, preferred_element_type=single
    )
    grad_query = grad_query.reshape(head_count, SEQ_LEN, HEAD) * score_scale
    grad_keys = place_blocks(
        jnp.einsum("hnqk,hnqd->hnkd", grad_scores, query_blocks, preferred_element_type=single)
        * score_scale,
        chosen,
    )
    grad_values = place_blocks(
        jnp.einsum(
            "hnqk,hnqd->hnkd", weights_f.astype(bfloat), grad_blocks, preferred_element_type=single
        ),
        chosen,
    )
    grad_float = grad_heads.astype(single)
    grad_numer = grad_float / denominator[:, :, None]
    grad_denom = -jnp.sum(grad_float * perf_out, axis=-1) / denominator
    grad_qfeat = (
        split_dot("hld,hfd->hlf", grad_numer, moments) + grad_denom[:, :, None] * totals[:, None, :]
    )
    grad_moments = split_dot("hlf,hld->hfd", query_feats, grad_numer)
    grad_totals = split_dot("hlf,hl->hf", query_feats, grad_denom)
    grad_kfeat = split_dot("hld,hfd->hlf", value_vecs, grad_moments) + grad_totals[:, None, :]
    grad_values = grad_values + split_dot("hlf,hfd->hld", key_feats, grad_moments)
    feature_scale = HEAD ** (-0.25)

    def feature_back(grad_feat, feats, vectors_low):
        grad_expo = grad_feat * feats
        direct = split_dot("hlf,hdf->hld", grad_expo, features) * feature_scale
        return direct - feature_scale * feature_scale * jnp.sum(
            grad_expo, axis=-1, keepdims=True
        ) * vectors_low.astype(single)

    grad_query = grad_query + feature_back(grad_qfeat, query_feats, queries)
    grad_keys = grad_keys + feature_back(grad_kfeat, key_feats, key_vecs)
    return (grad_query, grad_keys, grad_values)


def layer_forward(section_entry, length, layer_params, block_list, features):
    qkv_mat, qkv_bias, out_mat, up_mat, up_bias, down_mat, vectors = layer_params
    residual = section_entry.astype(single)
    normed = norm_rows(residual, vectors[0], vectors[1]).astype(bfloat)
    normed_all = lax.all_gather(normed, "tensor", axis=0, tiled=True)
    projected = (
        jnp.einsum("ld,dce->lce", normed_all, qkv_mat, preferred_element_type=single)
        + qkv_bias[None]
    )
    projected = projected.astype(bfloat)
    seq_len, part_width = (projected.shape[0], projected.shape[2])
    head_count = part_width // HEAD
    head_parts = projected.reshape(seq_len, 3, head_count, HEAD).transpose(1, 2, 0, 3)
    chosen, key_live, picked_live = sparse_layout(block_list, length)
    mixed_heads, attn_keep = attend_forward(
        head_parts[0], head_parts[1], head_parts[2], chosen, key_live, picked_live, features
    )
    mixed_low = mixed_heads.transpose(1, 0, 2).reshape(seq_len, part_width).astype(bfloat)
    row_block = mixed_low
    branch = lax.psum_scatter(
        jnp.dot(row_block, out_mat, preferred_element_type=single).astype(jnp.bfloat16),
        "tensor",
        scatter_dimension=0,
        tiled=True,
    ).astype(jnp.float32)
    hidden_res = residual + branch + vectors[4]
    normed_two = norm_rows(hidden_res, vectors[2], vectors[3]).astype(bfloat)
    normed_two_all = lax.all_gather(normed_two, "tensor", axis=0, tiled=True)
    pre_active = jnp.dot(normed_two_all, up_mat, preferred_element_type=single) + up_bias
    active = gelu_exact(pre_active).astype(bfloat)
    row_block = active
    result = (
        hidden_res
        + lax.psum_scatter(
            jnp.dot(row_block, down_mat, preferred_element_type=single).astype(jnp.bfloat16),
            "tensor",
            scatter_dimension=0,
            tiled=True,
        ).astype(jnp.float32)
        + vectors[5]
    )
    record = (
        residual,
        hidden_res,
        normed_all,
        head_parts,
        mixed_low,
        normed_two_all,
        pre_active,
        active,
        attn_keep,
        length,
    )
    return (result.astype(bfloat), record)


def layer_backward(grad_low, record, layer_params, block_list, features):
    qkv_mat, qkv_bias, out_mat, up_mat, up_bias, down_mat, vectors = layer_params
    (
        residual,
        hidden_res,
        normed_all,
        head_parts,
        mixed_low,
        normed_two_all,
        pre_active,
        active,
        attn_keep,
        length,
    ) = record
    seq_len, part_width = mixed_low.shape
    head_count = part_width // HEAD
    grad_output = grad_low.astype(single)
    grad_all = lax.all_gather(grad_low, "tensor", axis=0, tiled=True)
    grad_wdown = jnp.einsum("lf,ld->fd", active, grad_all, preferred_element_type=single)
    grad_active = jnp.einsum("ld,fd->lf", grad_all, down_mat, preferred_element_type=single)
    _, gelu_pull = jax.vjp(gelu_exact, pre_active)
    grad_upper = gelu_pull(grad_active)[0].astype(bfloat)
    grad_wup = jnp.einsum("ld,lf->df", normed_two_all, grad_upper, preferred_element_type=single)
    grad_bup = jnp.sum(grad_upper.astype(single), axis=0)
    row_block = grad_upper
    grad_normed_two = lax.psum_scatter(
        jnp.einsum("lf,df->ld", row_block, up_mat, preferred_element_type=single).astype(
            jnp.bfloat16
        ),
        "tensor",
        scatter_dimension=0,
        tiled=True,
    ).astype(jnp.float32)
    _, pull_two = jax.vjp(norm_rows, hidden_res, vectors[2], vectors[3])
    grad_hidden, grad_gain_two, grad_shift_two = pull_two(grad_normed_two)
    grad_hidden = grad_hidden + grad_output
    grad_hidden_low = grad_hidden.astype(bfloat)
    hidden_all = lax.all_gather(grad_hidden_low, "tensor", axis=0, tiled=True)
    grad_wout = jnp.einsum("le,ld->ed", mixed_low, hidden_all, preferred_element_type=single)
    grad_mixed = jnp.einsum("ld,ed->le", hidden_all, out_mat, preferred_element_type=single).astype(
        bfloat
    )
    grad_heads = grad_mixed.reshape(seq_len, head_count, HEAD).transpose(1, 0, 2)
    chosen, key_live, picked_live = sparse_layout(block_list, length)
    grad_query, grad_keys, grad_values = attend_backward(
        grad_heads,
        head_parts[0],
        head_parts[1],
        head_parts[2],
        chosen,
        picked_live,
        features,
        attn_keep,
    )
    grad_proj = (
        jnp.stack([grad_query, grad_keys, grad_values])
        .transpose(2, 0, 1, 3)
        .reshape(seq_len, 3, part_width)
        .astype(bfloat)
    )
    grad_wqkv = jnp.einsum("ld,lce->dce", normed_all, grad_proj, preferred_element_type=single)
    grad_bqkv = jnp.sum(grad_proj.astype(single), axis=0)
    row_block = grad_proj
    grad_normed = lax.psum_scatter(
        jnp.einsum("lce,dce->ld", row_block, qkv_mat, preferred_element_type=single).astype(
            jnp.bfloat16
        ),
        "tensor",
        scatter_dimension=0,
        tiled=True,
    ).astype(jnp.float32)
    _, pull_one = jax.vjp(norm_rows, residual, vectors[0], vectors[1])
    grad_resid, grad_gain_one, grad_shift_one = pull_one(grad_normed)
    grad_resid = grad_resid + grad_hidden
    weight_grads = (grad_wqkv, grad_bqkv, grad_wout, grad_wup, grad_bup, grad_wdown)
    vector_grads = jnp.stack(
        [
            grad_gain_one,
            grad_shift_one,
            grad_gain_two,
            grad_shift_two,
            jnp.sum(grad_hidden_low.astype(single), axis=0),
            jnp.sum(grad_output, axis=0),
        ]
    )
    return (grad_resid, weight_grads, vector_grads)


def shards(
    inputs,
    cotangent,
    lengths,
    blocks,
    feature_map,
    w_qkv,
    b_qkv,
    w_out,
    w_up,
    b_up,
    w_down,
    vector_params,
):
    section_no = lax.axis_index("section")
    is_first = section_no == 0
    is_last = section_no == lax.axis_size("section") - 1
    layer_params = (
        w_qkv[0],
        b_qkv[0].astype(single),
        w_out[0],
        w_up[0],
        b_up[0].astype(single),
        w_down[0],
        vector_params[0].astype(single),
    )
    block_list = blocks[0]
    features = feature_map[0]
    batch_count = inputs.shape[0]
    carried = jnp.zeros_like(inputs[0])
    records = []
    results = []
    for tick_no in range(batch_count + 1):
        batch_no = jnp.clip(tick_no - section_no, 0, batch_count - 1)
        section_entry = jnp.where(is_first, inputs[min(tick_no, batch_count - 1)], carried)
        result, record = layer_forward(
            section_entry, lengths[batch_no, 0], layer_params, block_list, features
        )
        records.append(record)
        results.append(result)
        if tick_no < batch_count:
            carried = shifted(result, "section", 1)
    section_outputs = jnp.stack(
        [
            jnp.where(is_first, results[batch_idx], results[batch_idx + 1])
            for batch_idx in range(batch_count)
        ]
    )[None]
    received = jnp.zeros_like(cotangent[0])
    grad_list = []
    local_sum = None
    vector_total = jnp.zeros((6, inputs.shape[2]), single)
    for tick_no in range(batch_count + 1):
        record = select_tree(
            is_last, records[min(tick_no + 1, batch_count)], records[max(tick_no - 1, 0)]
        )
        valid_flag = jnp.where(is_last, float(tick_no < batch_count), float(tick_no >= 1)).astype(
            single
        )
        grad_entry = jnp.where(is_last, cotangent[min(tick_no, batch_count - 1)], received)
        grad_resid, weight_grads, vector_grads = layer_backward(
            grad_entry, record, layer_params, block_list, features
        )
        weight_grads = tuple((valid_flag * addend for addend in weight_grads))
        vector_total = vector_total + valid_flag * vector_grads
        local_sum = (
            weight_grads
            if local_sum is None
            else tuple((summed + addend for summed, addend in zip(local_sum, weight_grads)))
        )
        grad_list.append(grad_resid)
        if tick_no < batch_count:
            received = shifted(grad_resid.astype(bfloat), "section", -1)
    final_grads = (
        lax.psum_scatter(
            local_sum[0].astype(jnp.bfloat16), "dp", scatter_dimension=0, tiled=True
        ).astype(jnp.float32),
        lax.psum_scatter(
            local_sum[1].astype(jnp.bfloat16), "dp", scatter_dimension=1, tiled=True
        ).astype(jnp.float32),
        lax.psum_scatter(
            local_sum[2].astype(jnp.bfloat16), "dp", scatter_dimension=1, tiled=True
        ).astype(jnp.float32),
        lax.psum_scatter(
            local_sum[3].astype(jnp.bfloat16), "dp", scatter_dimension=0, tiled=True
        ).astype(jnp.float32),
        lax.psum_scatter(
            local_sum[4].astype(jnp.bfloat16), "dp", scatter_dimension=0, tiled=True
        ).astype(jnp.float32),
        lax.psum_scatter(
            local_sum[5].astype(jnp.bfloat16), "dp", scatter_dimension=1, tiled=True
        ).astype(jnp.float32),
    )
    input_grads = jnp.stack(
        [
            jnp.where(is_first, grad_list[batch_idx + 1], grad_list[batch_idx])
            for batch_idx in range(batch_count)
        ]
    )[None]
    grad_vectors = lax.psum_scatter(
        vector_total, ("tensor", "dp"), scatter_dimension=1, tiled=True
    )[None]
    grad_wqkv, grad_bqkv, grad_wout, grad_wup, grad_bup, grad_wdown = final_grads
    return (
        section_outputs,
        input_grads,
        grad_wqkv[None],
        grad_bqkv[None],
        grad_wout[None],
        grad_wup[None],
        grad_bup[None],
        grad_wdown[None],
        grad_vectors,
    )


def solution(mesh):
    placed = (
        P(None, ("dp", "tensor"), None),
        P(None, ("dp", "tensor"), None),
        P(None, "dp"),
        P("section", "tensor", None, None),
        P("section", "tensor", None, None),
        P("section", None, None, "tensor"),
        P("section", None, "tensor"),
        P("section", "tensor", None),
        P("section", None, "tensor"),
        P("section", "tensor"),
        P("section", "tensor", None),
        P("section", None, None),
    )
    sizes = tuple(mesh.shape[axis] for axis in ALL_AXES)
    if sizes[0] == 2 and sizes[1] == 2 and sizes[2] % 2 == 0:
        body = functools.partial(chip_shards, sizes)
    else:
        body = shards
    return jax.shard_map(
        body,
        mesh=mesh,
        in_specs=placed,
        out_specs=(
            P("section", None, ("dp", "tensor"), None),
            P("section", None, ("dp", "tensor"), None),
            P("section", "dp", None, "tensor"),
            P("section", None, ("tensor", "dp")),
            P("section", "tensor", "dp"),
            P("section", "dp", "tensor"),
            P("section", ("tensor", "dp")),
            P("section", "tensor", "dp"),
            P("section", None, ("tensor", "dp")),
        ),
        check_vma=False,
    )
```

```python
import functools

import jax
import jax.numpy as jnp
from jax import lax
from jax.experimental import pallas as pl
from jax.experimental.pallas import tpu as pltpu
from jax.sharding import PartitionSpec as P

HEAD = 64
BLOCK = 64
NORM_EPS = 1e-5
bf = jnp.bfloat16
f32 = jnp.float32
LOG2E = 1.4426950408889634
F_SCALE = HEAD ** -0.25
ROWS = 1024
FFN_ROWS = 256
SPARSE_UNROLL = 8
PACK_ROWS = 32
PACK_SMALL = 96
TINY_ROWS = 16
N_QUARTERS = 4
MIB = 1024 * 1024
SHORT = pl.CostEstimate(flops=10**6, bytes_accessed=2**16, transcendentals=0)
ANY = pl.BlockSpec(memory_space=pl.ANY)
WHOLE = pl.BlockSpec(memory_space=pltpu.VMEM)
SCALARS = pl.BlockSpec(memory_space=pltpu.SMEM)


def contract(left, right, left_dim, right_dim):
    return lax.dot_general(
        left, right, (((left_dim,), (right_dim,)), ((), ())), preferred_element_type=f32
    )


def pick_source(layer_no):
    section_no = lax.axis_index("section")
    same = lax.rem(lax.axis_index("dp"), 2) == lax.axis_index("tensor")
    return jnp.where(section_no == layer_no, 0, 1) + jnp.where(same, 0, 2)


def start_pick(source, candidates, target, sem):
    for number, candidate in enumerate(candidates):

        @pl.when(source == number)
        def _():
            pltpu.make_async_copy(candidate, target, sem).start()


def wait_pick(candidates, target, sem):
    pltpu.make_async_copy(candidates[0], target, sem).wait()


def small_row(small, row, width):
    count = width // small.shape[1]
    rows = [small[row + i : row + i + 1, :].astype(f32) for i in range(count)]
    return jnp.concatenate(rows, axis=1)


def vector_row(small, number, width):
    return small_row(small, 8 + 2 * number, width)


def small_part(candidates):
    return [candidate.at[0:PACK_ROWS] for candidate in candidates]


def norm_stats(value):
    mean = jnp.mean(value, axis=-1, keepdims=True)
    centred = value - mean
    variance = jnp.mean(centred * centred, axis=-1, keepdims=True)
    scale = lax.rsqrt(variance + NORM_EPS)
    return centred * scale, scale


def lane_masks():
    lane = lax.broadcasted_iota(jnp.int32, (1, 2 * HEAD), 1)
    return lane < HEAD, lane >= HEAD


def swap_halves(value):
    return pltpu.roll(value, HEAD, 1)


def listed_starts(blocks_ref, pair, block, n_blocks):
    found = []
    for slot in range(3):
        two = []
        for a in range(2):
            listed = blocks_ref[(2 * pair + a) * n_blocks + block, slot]
            two.append(pl.multiple_of(listed * BLOCK, BLOCK))
        found.append(tuple(two))
    return found


def pick_rows(table, part, cols, starts, in_first):
    pieces = [table[part, 0:BLOCK, cols]]
    for one, two in starts:
        pieces.append(
            jnp.where(
                in_first,
                table[part, pl.ds(one, BLOCK), cols],
                table[part, pl.ds(two, BLOCK), cols],
            )
        )
    return jnp.concatenate(pieces, axis=0)


def stack_heads(target, chunk, value, masks):
    for number in range(ROWS // BLOCK):
        block = value[number * BLOCK : (number + 1) * BLOCK]
        for a in range(2):
            target[chunk * (ROWS // BLOCK) + number, a * BLOCK : (a + 1) * BLOCK] = jnp.where(
                masks[a], block, 0.0
            ).astype(bf)


def feature_rows(pack, n_heads, head):
    at = PACK_SMALL + head * HEAD
    return pack[at : at + HEAD].astype(f32) + pack[at + n_heads * HEAD : at + (n_heads + 1) * HEAD].astype(f32)


def qkv_weight(pack, n_heads, width, part):
    at = PACK_SMALL + 4 * n_heads * HEAD + part * width
    return pack[at : at + width]


def out_weights(pack, n_heads, part_width):
    at = PACK_SMALL + 2 * n_heads * HEAD
    return [pack[at + part * part_width : at + (part + 1) * part_width] for part in range(2)]


def pack_kernel(wqkv_ref, wout_ref, features_ref, bqkv_ref, bup_ref, vector_ref, blocks_ref, pack_ref):
    n_features, feat = features_ref.shape
    n_parts, width, part_width = wqkv_ref.shape

    def lane_rows(value):
        value = value.astype(f32)
        return [
            value[row : row + 1, at : at + feat]
            for row in range(value.shape[0])
            for at in range(0, value.shape[1], feat)
        ]

    blank = jnp.zeros((1, feat), f32)
    rows = lane_rows(bqkv_ref[...]) + [blank] + lane_rows(bup_ref[...]) + lane_rows(vector_ref[...])
    rows += [blank] * (PACK_ROWS - len(rows))
    pack_ref[0:PACK_ROWS] = jnp.concatenate(rows, axis=0).astype(bf)
    n_listed, n_slots = blocks_ref.shape
    pack_ref[PACK_ROWS:PACK_SMALL] = jnp.zeros((PACK_SMALL - PACK_ROWS, feat), bf)
    pack_ref[PACK_ROWS : PACK_ROWS + n_listed, 0:n_slots] = blocks_ref[...].astype(f32).astype(bf)
    at = PACK_SMALL
    features = features_ref[...]
    high = features.astype(bf)
    pack_ref[at : at + n_features] = high
    pack_ref[at + n_features : at + 2 * n_features] = (features - high.astype(f32)).astype(bf)
    at += 2 * n_features
    for part in range(2):
        pack_ref[at : at + part_width] = wout_ref[:, part * feat : (part + 1) * feat]
        at += part_width
    for part in range(n_parts):
        pack_ref[at : at + width] = wqkv_ref[part]
        at += width


def pack_weights(wqkv, wout, features, bqkv, bup, vectors, blocks):
    n_parts, width, part_width = wqkv.shape
    n_features, feat = features.shape
    n_rows = PACK_SMALL + 2 * n_features + 2 * part_width + n_parts * width
    return pl.pallas_call(
        pack_kernel,
        out_shape=jax.ShapeDtypeStruct((n_rows, feat), bf),
        in_specs=[WHOLE] * 7,
        out_specs=WHOLE,
        compiler_params=pltpu.CompilerParams(vmem_limit_bytes=16 * MIB),
        cost_estimate=SHORT,
        name="pack_weights",
    )(wqkv, wout, features, bqkv, bup, vectors, blocks)


def attn_forward_kernel(layer_no, n_heads, length_ref, blocks_ref, *refs):
    if layer_no == 0:
        x_ref, refs = refs[0], refs[1:]
    else:
        hidden_ref, part_a, part_b, refs = refs[0], refs[1], refs[2], refs[3:]
        small_prev, refs = refs[:4], refs[4:]
    pack_c, refs = refs[:4], refs[4:]
    if layer_no == 1:
        x_ref, refs = refs[0], refs[1:]
    (branch_ref, qkv_out, normed_out, probs_out, qf_out, kf_out, mt_out, mixed_out) = refs[:8]
    (pack, qkv, normed, probs, qfeat, kfeat, mt, mixed, fcat, perf, qstack,
     in_sem, out_sem) = refs[8:21]
    seq, width = normed.shape
    n_chunks = seq // ROWS
    pairs = n_heads // 2
    part_width = qkv.shape[2]
    feat = pack.shape[1]
    small = pack.at[0:PACK_ROWS]
    source = pick_source(layer_no)
    if layer_no == 1:
        small_before = refs[21]
        before = pick_source(0)
        start_pick(before, small_part(small_prev), small_before, in_sem.at[1])
    start_pick(source, pack_c, pack, in_sem.at[0])
    wait_pick(pack_c, pack, in_sem.at[0])
    if layer_no == 1:
        wait_pick(small_part(small_prev), small_before, in_sem.at[1])
    length = length_ref[0]
    gain = 1.0 + vector_row(small, 0, width)
    shift = vector_row(small, 1, width)

    @pl.loop(0, n_chunks)
    def _(chunk):
        rows = pl.ds(pl.multiple_of(chunk * ROWS, ROWS), ROWS)
        if layer_no == 0:
            x = x_ref[rows, :].astype(f32)
        else:
            total = part_a[rows, :].astype(f32) + part_b[rows, :].astype(f32)
            x_low = (hidden_ref[rows, :] + total + vector_row(small_before, 5, width)).astype(bf)
            x_ref[rows, :] = x_low
            x = x_low.astype(f32)
        zhat, _ = norm_stats(x)
        low = (zhat * gain + shift).astype(bf)
        normed[rows, :] = low
        for part in range(3):
            cols = n_heads * HEAD
            out = jnp.dot(low, qkv_weight(pack, n_heads, width, part), preferred_element_type=f32)
            qkv[part, rows, :] = (out + small_row(small, part, cols)).astype(bf)

    copies = [
        pltpu.make_async_copy(qkv, qkv_out, out_sem.at[0]),
        pltpu.make_async_copy(normed, normed_out, out_sem.at[1]),
    ]
    for copy in copies:
        copy.start()
    in_first, in_second = lane_masks()
    masks = (in_first, in_second)
    key_row = lax.broadcasted_iota(jnp.int32, (BLOCK, 2 * HEAD), 0)
    for pair in range(pairs):
        cols = slice(pair * 2 * HEAD, (pair + 1) * 2 * HEAD)
        zero = jnp.zeros((HEAD, feat), bf)
        for a in range(2):
            scaled = feature_rows(pack, n_heads, 2 * pair + a) * (F_SCALE * LOG2E)
            high = scaled.astype(bf)
            rest = (scaled - high.astype(f32)).astype(bf)
            for part, piece in enumerate((high, rest)):
                row = part * 2 * HEAD + a * HEAD
                fcat[row : row + HEAD, a * feat : (a + 1) * feat] = piece
                fcat[row : row + HEAD, (1 - a) * feat : (2 - a) * feat] = zero

        def features(vectors):
            proj = jnp.dot(
                jnp.concatenate([vectors, vectors], axis=1), fcat[...], preferred_element_type=f32
            )
            value = vectors.astype(f32)
            square = value * value * (0.5 * F_SCALE * F_SCALE * LOG2E)
            return [
                jnp.exp2(
                    proj[:, a * feat : (a + 1) * feat]
                    - jnp.sum(jnp.where(masks[a], square, 0.0), axis=-1, keepdims=True)
                )
                for a in range(2)
            ]

        @pl.loop(0, n_chunks)
        def _(chunk):
            base = pl.multiple_of(chunk * ROWS, ROWS)
            rows = pl.ds(base, ROWS)
            live = lax.broadcasted_iota(jnp.int32, (ROWS, 1), 0) + base < length
            found = features(qkv[1, rows, cols])
            for a in range(2):
                kfeat[pair, rows, a * feat : (a + 1) * feat] = jnp.where(live, found[a], 0.0).astype(bf)

        values = qkv[2, :, cols].astype(f32)
        for a in range(2):
            extended = jnp.where(masks[a], values, 1.0).astype(bf)
            moment = contract(extended, kfeat[pair, :, a * feat : (a + 1) * feat], 0, 0)
            mt[2 * pair + a] = moment.astype(bf)

        @pl.loop(0, n_chunks)
        def _(chunk):
            rows = pl.ds(pl.multiple_of(chunk * ROWS, ROWS), ROWS)
            query = qkv[0, rows, cols]
            found = features(query)
            out = None
            for a in range(2):
                low = found[a].astype(bf)
                qfeat[pair, rows, a * feat : (a + 1) * feat] = low
                numer = contract(low, mt[2 * pair + a], 1, 1)
                value = numer / swap_halves(numer)
                out = value if a == 0 else jnp.where(in_first, out, value)
            perf[rows, :] = out
            stack_heads(qstack, chunk, query.astype(f32) * (HEAD ** -0.5), masks)

        @pl.loop(0, seq // BLOCK, unroll=SPARSE_UNROLL)
        def _(block):
            rows = pl.ds(pl.multiple_of(block * BLOCK, BLOCK), BLOCK)
            starts = listed_starts(blocks_ref, pair, block, seq // BLOCK)
            keys = pick_rows(qkv, 1, cols, starts, in_first)
            values = pick_rows(qkv, 2, cols, starts, in_first)
            scores = contract(keys, qstack[block], 1, 1)
            pieces = [scores[:BLOCK]]
            for slot, (one, two) in enumerate(starts):
                room = length - jnp.where(in_first, one, two)
                piece = scores[(slot + 1) * BLOCK : (slot + 2) * BLOCK]
                pieces.append(jnp.where(key_row < room, piece, -1e30))
            scores = jnp.concatenate(pieces, axis=0)
            raw = jnp.exp(scores - jnp.max(scores, axis=0, keepdims=True))
            low = (raw * (1.0 / jnp.sum(raw, axis=0, keepdims=True))).astype(bf)
            probs[pair, block] = low
            both = contract(low, values, 0, 0)
            out = jnp.where(in_first, both[:BLOCK], both[BLOCK:])
            mixed[rows, cols] = (out + perf[rows, :]).astype(bf)

        more = [
            pltpu.make_async_copy(probs.at[pair], probs_out.at[pair], out_sem.at[2 + 4 * pair]),
            pltpu.make_async_copy(qfeat.at[pair], qf_out.at[pair], out_sem.at[3 + 4 * pair]),
            pltpu.make_async_copy(kfeat.at[pair], kf_out.at[pair], out_sem.at[4 + 4 * pair]),
            pltpu.make_async_copy(mt.at[2 * pair : 2 * pair + 2], mt_out.at[2 * pair : 2 * pair + 2], out_sem.at[5 + 4 * pair]),
        ]
        for copy in more:
            copy.start()
        copies += more

    @pl.loop(0, n_chunks)
    def _(chunk):
        rows = pl.ds(pl.multiple_of(chunk * ROWS, ROWS), ROWS)
        low = mixed[rows, :]
        mixed_out[rows, :] = low
        for part, weight in enumerate(out_weights(pack, n_heads, part_width)):
            here = slice(part * feat, (part + 1) * feat)
            branch_ref[rows, here] = jnp.dot(low, weight, preferred_element_type=f32).astype(bf)

    for copy in copies:
        copy.wait()


def attn_forward(layer_no, n_heads, length, blocks, x_parts, pack_c, small_before):
    part_width, feat = n_heads * HEAD, pack_c[0].shape[1]
    seq, width = x_parts[0].shape
    pairs = n_heads // 2
    shape = jax.ShapeDtypeStruct
    outs = [
        shape((seq, width), bf),
        shape((3, seq, part_width), bf),
        shape((seq, width), bf),
        shape((pairs, seq // BLOCK, 4 * BLOCK, 2 * HEAD), bf),
        shape((pairs, seq, 2 * feat), bf),
        shape((pairs, seq, 2 * feat), bf),
        shape((n_heads, 2 * HEAD, feat), bf),
        shape((seq, part_width), bf),
    ]
    out_specs = [WHOLE, ANY, ANY, ANY, ANY, ANY, ANY, WHOLE]
    scratch = [
        pltpu.VMEM(pack_c[0].shape, bf),
        pltpu.VMEM((3, seq, part_width), bf),
        pltpu.VMEM((seq, width), bf),
        pltpu.VMEM((pairs, seq // BLOCK, 4 * BLOCK, 2 * HEAD), bf),
        pltpu.VMEM((pairs, seq, 2 * feat), bf),
        pltpu.VMEM((pairs, seq, 2 * feat), bf),
        pltpu.VMEM((n_heads, 2 * HEAD, feat), bf),
        pltpu.VMEM((seq, part_width), bf),
        pltpu.VMEM((4 * HEAD, 2 * feat), bf),
        pltpu.VMEM((seq, 2 * HEAD), f32),
        pltpu.VMEM((seq // BLOCK, 2 * BLOCK, 2 * HEAD), bf),
        pltpu.SemaphoreType.DMA((2,)),
        pltpu.SemaphoreType.DMA((2 + 4 * pairs,)),
    ]
    operands = list(x_parts)
    specs = [WHOLE] * len(x_parts)
    if layer_no == 1:
        operands += list(small_before)
        specs += [ANY] * 4
        outs = [shape((seq, width), bf)] + outs
        out_specs = [WHOLE] + out_specs
        scratch.append(pltpu.VMEM((PACK_ROWS, feat), bf))
    operands += list(pack_c)
    specs += [ANY] * 4
    return pl.pallas_call(
        functools.partial(attn_forward_kernel, layer_no, n_heads),
        out_shape=outs,
        in_specs=[SCALARS, SCALARS] + specs,
        out_specs=out_specs,
        scratch_shapes=scratch,
        compiler_params=pltpu.CompilerParams(vmem_limit_bytes=60 * MIB),
        cost_estimate=SHORT,
        name=f"attn_forward_{layer_no}",
    )(length, blocks, *operands)


def gelu_parts(value):
    inverse = 1.0 / (1.0 + (0.3275911 * 0.5 ** 0.5) * jnp.abs(value))
    bell = jnp.exp2(value * value * (-0.5 * LOG2E))
    poly = inverse * (
        0.127414796
        + inverse
        * (-0.142248368 + inverse * (0.7107068705 + inverse * (-0.7265760135 + inverse * 0.5307027145)))
    )
    tail = poly * bell
    below = jnp.where(value >= 0.0, 1.0 - tail, tail)
    return value * below, below + value * bell * (0.5 / 3.141592653589793) ** 0.5


def down_rows(wide, width, at, step):
    part, row = at // width, at % width
    return wide[width + row : width + row + step, part * width : (part + 1) * width]


def ffn_forward_kernel(layer_no, *refs):
    x_ref, part_a, part_b = refs[:3]
    small_c, wide_c = refs[3:7], refs[7:11]
    out_ref, hidden_ref, normed_ref, active_ref, slope_ref = refs[11:16]
    small, wide, sems = refs[16:]

    @pl.when(pl.program_id(0) == 0)
    def _():
        source = pick_source(layer_no)
        start_pick(source, small_part(small_c), small, sems.at[0])
        start_pick(source, wide_c, wide, sems.at[1])
        wait_pick(small_part(small_c), small, sems.at[0])
        wait_pick(wide_c, wide, sems.at[1])

    width = x_ref.shape[1]
    units = wide.shape[1]
    branch = part_a[...].astype(f32) + part_b[...].astype(f32)
    hidden = x_ref[...].astype(f32) + branch + vector_row(small, 4, width)
    hidden_ref[...] = hidden
    zhat, _ = norm_stats(hidden)
    low = (zhat * (1.0 + vector_row(small, 2, width)) + vector_row(small, 3, width)).astype(bf)
    normed_ref[...] = low
    total = None
    step = 256
    for at in range(0, units, step):
        upper = jnp.dot(low, wide[:width, at : at + step], preferred_element_type=f32)
        active, slope = gelu_parts(upper + small_row(small, 4 + at // step, step))
        active = active.astype(bf)
        active_ref[:, at : at + step] = active
        slope_ref[:, at : at + step] = slope.astype(bf)
        term = jnp.dot(active, down_rows(wide, width, at, step), preferred_element_type=f32)
        total = term if total is None else total + term
    out_ref[...] = total.astype(bf)


def ffn_forward(layer_no, x, part_a, part_b, weights):
    small_c, wide_c = weights
    seq, width = x.shape
    units = wide_c[0].shape[1]
    shape = jax.ShapeDtypeStruct
    rows = lambda cols: pl.BlockSpec((FFN_ROWS, cols), lambda i: (i, 0))
    return pl.pallas_call(
        functools.partial(ffn_forward_kernel, layer_no),
        grid=(seq // FFN_ROWS,),
        out_shape=[
            shape((seq, width), bf),
            shape((seq, width), f32),
            shape((seq, width), bf),
            shape((seq, units), bf),
            shape((seq, units), bf),
        ],
        in_specs=[rows(width)] * 3 + [ANY] * 8,
        out_specs=[rows(width), rows(width), rows(width), rows(units), rows(units)],
        scratch_shapes=[
            pltpu.VMEM((PACK_ROWS, small_c[0].shape[1]), bf),
            pltpu.VMEM(wide_c[0].shape, bf),
            pltpu.SemaphoreType.DMA((2,)),
        ],
        compiler_params=pltpu.CompilerParams(vmem_limit_bytes=(60, 22)[layer_no] * MIB),
        cost_estimate=SHORT,
        name=f"ffn_forward_{layer_no}",
    )(x, part_a, part_b, *small_c, *wide_c)


def ffn_backward_kernel(layer_no, grad_ref, slope_ref, *refs):
    wide_c = refs[:4]
    out_ref, gupper_ref, bias_ref = refs[4:7]
    wide, sems = refs[7:]

    @pl.when(pl.program_id(0) == 0)
    def _():
        source = pick_source(layer_no)
        start_pick(source, wide_c, wide, sems.at[0])
        bias_ref[...] = jnp.zeros_like(bias_ref)
        wait_pick(wide_c, wide, sems.at[0])

    width = grad_ref.shape[1]
    units = wide.shape[1]
    grad = grad_ref[...]
    total = None
    step = 256
    for at in range(0, units, step):
        gactive = contract(grad, down_rows(wide, width, at, step), 1, 1)
        gupper = (gactive * slope_ref[:, at : at + step].astype(f32)).astype(bf)
        gupper_ref[:, at : at + step] = gupper
        bias_ref[:, at : at + step] += fold_rows(gupper.astype(f32))
        term = contract(gupper, wide[:width, at : at + step], 1, 1)
        total = term if total is None else total + term
    out_ref[...] = total.astype(bf)


def fold_rows(value):
    rows, cols = value.shape
    return jnp.sum(value.reshape(rows // 8, 8, cols), axis=0)


def ffn_backward(layer_no, grad, slope, weights):
    (wide_c,) = weights
    seq, width = grad.shape
    units = wide_c[0].shape[1]
    shape = jax.ShapeDtypeStruct
    rows = lambda cols: pl.BlockSpec((FFN_ROWS, cols), lambda i: (i, 0))
    return pl.pallas_call(
        functools.partial(ffn_backward_kernel, layer_no),
        grid=(seq // FFN_ROWS,),
        out_shape=[shape((seq, width), bf), shape((seq, units), bf), shape((8, units), f32)],
        in_specs=[rows(width), rows(units)] + [ANY] * 4,
        out_specs=[rows(width), rows(units), pl.BlockSpec((8, units), lambda i: (0, 0))],
        scratch_shapes=[
            pltpu.VMEM(wide_c[0].shape, bf),
            pltpu.SemaphoreType.DMA((1,)),
        ],
        compiler_params=pltpu.CompilerParams(vmem_limit_bytes=18 * MIB),
        cost_estimate=SHORT,
        name=f"ffn_backward_{layer_no}",
    )(grad, slope, *wide_c)


def attn_backward_kernel(layer_no, n_heads, blocks_ref, *refs):
    gy_ref, part_a, part_b, hidden_ref, x_ref = refs[:5]
    qkv_in, probs_in, qf_in, kf_in, mt_in = refs[5:10]
    pack_c, refs = refs[10:14], refs[14:]
    out_ref, gbranch_ref, dqkv_ref, first_ref, vec_ref, bias_ref, refs = *refs[:6], refs[6:]
    (pack, qkv, probs, qfeat, kfeat, mt, gmix, gstack, qstack, gext, gt, fback,
     dq, dk, dv, sem) = refs
    seq, width = gy_ref.shape
    n_chunks = seq // ROWS
    pairs = n_heads // 2
    part_width = qkv.shape[2]
    feat = pack.shape[1]
    small = pack.at[0:PACK_ROWS]
    source = pick_source(layer_no)
    start_pick(source, pack_c, pack, sem.at[0])
    loads = [
        pltpu.make_async_copy(qkv_in, qkv, sem.at[2]),
        pltpu.make_async_copy(mt_in, mt, sem.at[3]),
        pltpu.make_async_copy(qf_in, qfeat, sem.at[4]),
        pltpu.make_async_copy(kf_in, kfeat, sem.at[5]),
        pltpu.make_async_copy(probs_in, probs, sem.at[6]),
    ]
    for load in loads:
        load.start()
    first_ref[...] = jnp.zeros_like(first_ref)
    vec_ref[...] = jnp.zeros_like(vec_ref)
    bias_ref[...] = jnp.zeros_like(bias_ref)
    wait_pick(pack_c, pack, sem.at[0])
    gain = 1.0 + vector_row(small, 2, width)
    in_first, in_second = lane_masks()
    masks = (in_first, in_second)

    @pl.loop(0, n_chunks)
    def _(chunk):
        rows = pl.ds(pl.multiple_of(chunk * ROWS, ROWS), ROWS)
        gnormed = part_a[rows, :].astype(f32) + part_b[rows, :].astype(f32)
        zhat, scale = norm_stats(hidden_ref[rows, :])
        scaled = gnormed * gain
        gy = gy_ref[rows, :].astype(f32)
        mean_one = jnp.mean(scaled, axis=-1, keepdims=True)
        mean_two = jnp.mean(scaled * zhat, axis=-1, keepdims=True)
        ghidden = gy + (scaled - mean_one - zhat * mean_two) * scale
        low = ghidden.astype(bf)
        gbranch_ref[rows, :] = low
        vec_ref[0] += fold_rows(gnormed * zhat)
        vec_ref[1] += fold_rows(gnormed)
        vec_ref[2] += fold_rows(low.astype(f32))
        vec_ref[3] += fold_rows(gy)
        first, second = out_weights(pack, n_heads, part_width)
        gmix[rows, :] = (contract(low[:, :feat], first, 1, 1) + contract(low[:, feat:], second, 1, 1)).astype(bf)

    for load in loads[:4]:
        load.wait()
    for pair in range(pairs):
        cols = slice(pair * 2 * HEAD, (pair + 1) * 2 * HEAD)
        for a in range(2):
            plain = feature_rows(pack, n_heads, 2 * pair + a) * F_SCALE
            high = plain.astype(bf).astype(f32)
            ones = jnp.ones((HEAD, feat), f32)
            none = jnp.zeros((HEAD, feat), f32)
            stack = [high, ones] if a == 0 else [ones, high]
            stack += [plain - high, none] if a == 0 else [none, plain - high]
            fback[a] = jnp.concatenate(stack, axis=0).astype(bf)

        def feature_back(a, gfeat, feats, vectors):
            gexpo = (gfeat * feats.astype(f32)).astype(bf)
            both = contract(gexpo, fback[a], 1, 1)
            both = both[:, : 2 * HEAD] + both[:, 2 * HEAD :]
            return both - (F_SCALE * F_SCALE) * swap_halves(both) * vectors

        @pl.loop(0, n_chunks)
        def _(chunk):
            rows = pl.ds(pl.multiple_of(chunk * ROWS, ROWS), ROWS)
            grad = gmix[rows, cols].astype(f32)
            query = qkv[0, rows, cols].astype(f32)
            out = None
            for a in range(2):
                feats = qfeat[pair, rows, a * feat : (a + 1) * feat]
                moment = mt[2 * pair + a]
                numer = contract(feats, moment, 1, 1)
                inverse = 1.0 / swap_halves(numer)
                gnumer = grad * inverse
                other = swap_halves(gnumer * numer * inverse)
                both = jnp.where(masks[a], gnumer, -other).astype(bf)
                gext[a, rows, :] = both
                gfeat = jnp.dot(both, moment, preferred_element_type=f32)
                value = feature_back(a, gfeat, feats, query)
                out = value if a == 0 else jnp.where(in_first, out, value)
            dq[rows, :] = out
            stack_heads(gstack, chunk, grad, masks)
            stack_heads(qstack, chunk, query * (HEAD ** -0.5), masks)

        for a in range(2):
            gt[a] = contract(gext[a], qfeat[pair, :, a * feat : (a + 1) * feat], 0, 0).astype(bf)

        @pl.loop(0, n_chunks)
        def _(chunk):
            rows = pl.ds(pl.multiple_of(chunk * ROWS, ROWS), ROWS)
            key = qkv[1, rows, cols].astype(f32)
            value_f = qkv[2, rows, cols].astype(f32)
            dk_out, dv_out = None, None
            for a in range(2):
                extended = jnp.where(masks[a], value_f, 1.0).astype(bf)
                feats = kfeat[pair, rows, a * feat : (a + 1) * feat]
                gfeat = jnp.dot(extended, gt[a], preferred_element_type=f32)
                dk_one = feature_back(a, gfeat, feats, key)
                dv_one = contract(feats, gt[a], 1, 1)
                dk_out = dk_one if a == 0 else jnp.where(in_first, dk_out, dk_one)
                dv_out = dv_one if a == 0 else jnp.where(in_first, dv_out, dv_one)
            dk[rows, :] = dk_out
            dv[rows, :] = dv_out

        if pair == 0:
            loads[4].wait()

        @pl.loop(0, seq // BLOCK, unroll=SPARSE_UNROLL)
        def _(block):
            rows = pl.ds(pl.multiple_of(block * BLOCK, BLOCK), BLOCK)
            starts = listed_starts(blocks_ref, pair, block, seq // BLOCK)
            keys = pick_rows(qkv, 1, cols, starts, in_first)
            values = pick_rows(qkv, 2, cols, starts, in_first)
            weights = probs[pair, block]
            weights_f = weights.astype(f32)
            grad = gstack[block]
            gweights = contract(values, grad, 1, 1)
            inner = jnp.sum(weights_f * gweights, axis=0, keepdims=True)
            gscores = (weights_f * (gweights - inner)).astype(bf)
            both = contract(gscores, keys, 0, 0)
            out = jnp.where(in_first, both[:BLOCK], both[BLOCK:]) * (HEAD ** -0.5)
            dkeys = jnp.dot(gscores, qstack[block], preferred_element_type=f32)
            dvalues = jnp.dot(weights, grad, preferred_element_type=f32)
            for total, part in ((dk, dkeys), (dv, dvalues)):
                total[0:BLOCK, :] += part[:BLOCK]
                for slot, (one, two) in enumerate(starts):
                    piece = part[(slot + 1) * BLOCK : (slot + 2) * BLOCK]
                    total[pl.ds(one, BLOCK), :] += jnp.where(in_first, piece, 0.0)
                    total[pl.ds(two, BLOCK), :] += jnp.where(in_first, 0.0, piece)
            dq[rows, :] += out

        @pl.loop(0, n_chunks)
        def _(chunk):
            rows = pl.ds(pl.multiple_of(chunk * ROWS, ROWS), ROWS)
            for part, total in enumerate((dq, dk, dv)):
                low = total[rows, :].astype(bf)
                dqkv_ref[part, rows, cols] = low
                bias_ref[part, :, cols] += fold_rows(low.astype(f32))


    @pl.loop(0, n_chunks)
    def _(chunk):
        rows = pl.ds(pl.multiple_of(chunk * ROWS, ROWS), ROWS)
        total = None
        for part in range(3):
            term = contract(dqkv_ref[part, rows, :], qkv_weight(pack, n_heads, width, part), 1, 1)
            total = term if total is None else total + term
        low = total.astype(bf)
        out_ref[rows, :] = low
        zhat, _ = norm_stats(x_ref[rows, :].astype(f32))
        total = low.astype(f32)
        first_ref[0] += fold_rows(total * zhat)
        first_ref[1] += fold_rows(total)


def attn_backward(layer_no, n_heads, blocks, gy, part_a, part_b, hidden, x, kept, pack_c):
    seq, width = gy.shape
    part_width, feat = n_heads * HEAD, pack_c[0].shape[1]
    pairs = n_heads // 2
    shape = jax.ShapeDtypeStruct
    operands = [gy, part_a, part_b, hidden, x, *kept, *pack_c]
    return pl.pallas_call(
        functools.partial(attn_backward_kernel, layer_no, n_heads),
        out_shape=[
            shape((seq, width), bf),
            shape((seq, width), bf),
            shape((3, seq, part_width), bf),
            shape((2, 8, width), f32),
            shape((4, 8, width), f32),
            shape((3, 8, part_width), f32),
        ],
        in_specs=[SCALARS] + [WHOLE] * 5 + [ANY] * 9,
        out_specs=[WHOLE] * 6,
        scratch_shapes=[
            pltpu.VMEM(pack_c[0].shape, bf),
            pltpu.VMEM((3, seq, part_width), bf),
            pltpu.VMEM((pairs, seq // BLOCK, 4 * BLOCK, 2 * HEAD), bf),
            pltpu.VMEM((pairs, seq, 2 * feat), bf),
            pltpu.VMEM((pairs, seq, 2 * feat), bf),
            pltpu.VMEM((n_heads, 2 * HEAD, feat), bf),
            pltpu.VMEM((seq, part_width), bf),
            pltpu.VMEM((seq // BLOCK, 2 * BLOCK, 2 * HEAD), bf),
            pltpu.VMEM((seq // BLOCK, 2 * BLOCK, 2 * HEAD), bf),
            pltpu.VMEM((2, seq, 2 * HEAD), bf),
            pltpu.VMEM((2, 2 * HEAD, feat), bf),
            pltpu.VMEM((2, 4 * HEAD, feat), bf),
            pltpu.VMEM((seq, 2 * HEAD), f32),
            pltpu.VMEM((seq, 2 * HEAD), f32),
            pltpu.VMEM((seq, 2 * HEAD), f32),
            pltpu.SemaphoreType.DMA((7,)),
        ],
        compiler_params=pltpu.CompilerParams(vmem_limit_bytes=46 * MIB),
        cost_estimate=SHORT,
        name=f"attn_backward_{layer_no}",
    )(blocks, *operands)


def norm_backward_kernel(layer_no, x_ref, part_a, part_b, ghidden_ref, *refs):
    small_c = refs[:4]
    low_ref, small, sems = refs[4:]

    @pl.when(pl.program_id(0) == 0)
    def _():
        start_pick(pick_source(layer_no), small_part(small_c), small, sems.at[0])
        wait_pick(small_part(small_c), small, sems.at[0])

    width = x_ref.shape[1]
    gnormed = part_a[...].astype(f32) + part_b[...].astype(f32)
    zhat, scale = norm_stats(x_ref[...].astype(f32))
    scaled = gnormed * (1.0 + vector_row(small, 0, width))
    mean_one = jnp.mean(scaled, axis=-1, keepdims=True)
    mean_two = jnp.mean(scaled * zhat, axis=-1, keepdims=True)
    total = ghidden_ref[...].astype(f32) + (scaled - mean_one - zhat * mean_two) * scale
    low_ref[...] = total.astype(bf)


def norm_backward(layer_no, x, part_a, part_b, ghidden, small_c):
    seq, width = x.shape
    shape = jax.ShapeDtypeStruct
    rows = pl.BlockSpec((FFN_ROWS, width), lambda i: (i, 0))
    return pl.pallas_call(
        functools.partial(norm_backward_kernel, layer_no),
        grid=(seq // FFN_ROWS,),
        out_shape=shape((seq, width), bf),
        in_specs=[rows] * 4 + [ANY] * 4,
        out_specs=rows,
        scratch_shapes=[pltpu.VMEM((PACK_ROWS, small_c[0].shape[1]), bf), pltpu.SemaphoreType.DMA((1,))],
        compiler_params=pltpu.CompilerParams(vmem_limit_bytes=12 * MIB),
        cost_estimate=SHORT,
        name=f"norm_backward_{layer_no}",
    )(x, part_a, part_b, ghidden, *small_c)


def tiny_rows(first, moved, vec, bias_qkv, bias_up):
    width = vec.shape[2]
    half = width // 2
    here = pl.ds(pl.multiple_of(lax.rem(lax.axis_index("dp"), 2) * half, half), half)
    total = lambda value: jnp.sum(value, axis=0, keepdims=True)
    parts = [total(first[i, :, here] + moved[i, :, here]) for i in range(2)]
    parts += [total(vec[i, :, here]) for i in range(4)]
    parts += [total(bias_qkv[i]) for i in range(3)] + [jnp.zeros((1, half), f32)]
    up = total(bias_up[...])
    parts += [up[:, at : at + half] for at in range(0, up.shape[1], half)]
    return [jnp.concatenate(parts[i : i + 2], axis=1) for i in range(0, len(parts), 2)]


def weight_grad_kernel(n_first, n_extra, left_a, left_b, right_a, right_b, *refs):
    keep_ref, away_ref, turned = refs[-3:]
    extra, sums = refs[:n_extra], refs[n_extra:-3]
    step = pl.program_id(0)
    total_rows, cols = keep_ref.shape
    per_half = pl.num_programs(0) // 2
    width = right_a.shape[1]
    n_rows = left_a.shape[1]
    first = step < n_first

    @pl.when(step == 0)
    def _():
        turned[...] = left_a[...].T
        for source, target in zip(extra, (keep_ref, away_ref)):
            target[:, per_half * width :] = source[...]
        if sums:
            rows = tiny_rows(*sums[:5]) + tiny_rows(*sums[5:])
            rows += [jnp.zeros_like(rows[0])] * (total_rows - n_rows - len(rows))
            low = jnp.concatenate(rows, axis=0).astype(bf)
            for target in (keep_ref, away_ref):
                target[n_rows:, :] = low

    @pl.when(step == n_first)
    def _():
        turned[...] = left_b[...].T

    right = jnp.where(first, right_a[...], right_b[...])
    result = jnp.dot(turned[...], right, preferred_element_type=f32).astype(bf)
    here = pl.ds(pl.multiple_of(lax.rem(step, per_half) * width, width), width)
    keep = step // per_half == lax.axis_index("section")
    n_shards = lax.axis_size("dp")
    shard = n_rows // n_shards
    for wanted, target in ((keep, keep_ref), (jnp.logical_not(keep), away_ref)):

        @pl.when(wanted)
        def _():
            for number in range(n_shards):
                at = ((number % 2) * (n_shards // 2) + number // 2) * shard
                target[at : at + shard, here] = result[number * shard : (number + 1) * shard]


def weight_grads(name, step, left_a, right_a, left_b, right_b, extra=(), sums=()):
    seq, width = left_a.shape
    if right_a.ndim == 3:
        n_first = right_a.shape[0]
        spec_a = pl.BlockSpec((None, seq, step), lambda i: (jnp.minimum(i, n_first - 1), 0, 0))
    else:
        n_first = right_a.shape[1] // step
        spec_a = pl.BlockSpec((seq, step), lambda i: (0, jnp.minimum(i, n_first - 1)))
    n_second = right_b.shape[1] // step
    spec_b = pl.BlockSpec((seq, step), lambda i: (0, jnp.maximum(i - n_first, 0)))
    whole = pl.BlockSpec((seq, width), lambda i: (0, 0))
    n_steps = n_first + n_second
    cols = step * (n_steps // 2) + (extra[0].shape[1] if extra else 0)
    shape = (width + (TINY_ROWS if sums else 0), cols)
    fixed = lambda shape: pl.BlockSpec(shape, lambda i: (0,) * len(shape))
    return pl.pallas_call(
        functools.partial(weight_grad_kernel, n_first, len(extra)),
        grid=(n_steps,),
        out_shape=[jax.ShapeDtypeStruct(shape, bf)] * 2,
        in_specs=[whole, whole, spec_a, spec_b] + [fixed(item.shape) for item in (*extra, *sums)],
        out_specs=[fixed(shape)] * 2,
        scratch_shapes=[pltpu.VMEM((width, seq), bf)],
        compiler_params=pltpu.CompilerParams(vmem_limit_bytes=20 * MIB),
        cost_estimate=SHORT,
        name=name,
    )(left_a, left_b, right_a, right_b, *extra, *sums)


ALL_AXES = ("section", "tensor", "dp")


def send(value, sizes, target):
    n_section, n_tensor, n_dp = sizes
    pairs = []
    for s in range(n_section):
        for t in range(n_tensor):
            for d in range(n_dp):
                goal = target(s, t, d // 2, d % 2)
                if goal is not None:
                    gs, gt, gz, gc = goal
                    number = (s * n_tensor + t) * n_dp + d
                    pairs.append((number, (gs * n_tensor + gt) * n_dp + 2 * gz + gc))
    return lax.ppermute(value, ALL_AXES, pairs)


def other_core(value, sizes):
    return send(value, sizes, lambda s, t, z, c: (s, t, z, 1 - c))


def chip_shards(
    sizes,
    inputs,
    cotangent,
    lengths,
    blocks,
    feature_map,
    w_qkv,
    b_qkv,
    w_out,
    w_up,
    b_up,
    w_down,
    vector_params,
):
    n_dp = sizes[2]
    n_z = n_dp // 2
    section_no = lax.axis_index("section")
    tensor_no = lax.axis_index("tensor")
    dp_no = lax.axis_index("dp")
    z_no, core = dp_no // 2, dp_no % 2
    same = core == tensor_no
    is_first = section_no == 0
    width = inputs.shape[2]
    half = inputs.shape[1]
    n_heads, n_blocks, n_listed = blocks.shape[1:]
    feat = feature_map.shape[3]
    part_width = w_qkv.shape[3]

    def after(value, earlier):
        return lax.optimization_barrier((value, earlier))[0]

    def share_y(array):
        return send(array, sizes, lambda s, t, z, c: (1 - s, t, z, c) if c == t else None)

    def share_x(array):
        return send(array, sizes, lambda s, t, z, c: (s, 1 - t, z, c) if c == t else None)

    wide = jnp.concatenate(
        [w_up[0], jnp.concatenate([w_down[0][:width], w_down[0][width:]], axis=1)], axis=0
    )
    def halves(own, first, second):
        near = jnp.where(same, own, first)
        far = jnp.where(same, first, second)
        swap = tensor_no == 1
        return jnp.concatenate(
            [jnp.where(swap, far, near), jnp.where(swap, near, far)], axis=0
        )

    def cross(own):
        return send(
            own,
            sizes,
            lambda s, t, z, c: (s, t, z, 1 - c) if c == t else (s, 1 - t, z, c),
        )

    def to_sequence(own, first):
        second = send(first, sizes, lambda s, t, z, c: (s, t, z, 1 - c) if c == t else None)
        return halves(own, first, second)

    x_own = inputs[section_no]
    x_arrived = cross(x_own)
    pack = pack_weights(
        after(w_qkv[0].transpose(1, 0, 2), x_own),
        w_out[0],
        feature_map[0].reshape(n_heads * HEAD, feat),
        b_qkv[0],
        b_up,
        vector_params[0],
        blocks[0].reshape(n_heads * n_blocks, n_listed),
    )
    x_first = to_sequence(x_own, x_arrived)
    pack_y = share_y(pack)
    pack_x = share_x(pack)
    pack_both = share_x(after(pack_y, pack_x))
    pack_c = (pack, pack_y, pack_x, pack_both)
    wide_y = share_y(after(wide, pack_y))

    def share_wide(layer_no, earlier):
        def share(array, section):
            return send(
                after(array, earlier),
                sizes,
                lambda s, t, z, c: (s, 1 - t, z, c) if c == t and s == section else None,
            )

        return (wide, wide_y, share(wide, layer_no), share(wide_y, 1 - layer_no))

    lengths_here = jnp.where(same, lengths, other_core(lengths, sizes))
    length = lax.dynamic_slice_in_dim(lengths_here[:, 0], section_no, 1)

    weights = [(pack_c, share_wide(0, pack_both))]

    def of_layer(layer_no, candidates):
        mine = section_no == layer_no
        return jnp.where(
            same,
            jnp.where(mine, candidates[0], candidates[1]),
            jnp.where(mine, candidates[2], candidates[3]),
        )

    def exchange(value):
        return value, other_core(value, sizes)

    kept = []
    x_parts = (x_first,)
    outputs = []
    for layer_no in range(2):
        listed = of_layer(
            layer_no,
            [item[PACK_ROWS : PACK_ROWS + n_heads * n_blocks, :n_listed] for item in pack_c],
        )
        listed = listed.astype(jnp.int32)
        made = attn_forward(layer_no, n_heads, length, listed, x_parts, pack_c, pack_c)
        if layer_no == 0:
            x = x_first
        else:
            x, made = made[0], made[1:]
            outputs.append(x)
        branch, qkv, normed, probs, qfeat, kfeat, mt, mixed = made
        if layer_no == 0:
            grad_own = after(cotangent[section_no], (weights[0][1][2:], branch))
            grad_arrived = cross(grad_own)
            weights.append((pack_c, share_wide(1, (weights[0][1][2:], branch))))
        result, hidden, normed_two, active, slope = ffn_forward(
            layer_no, x, *exchange(branch), weights[layer_no]
        )
        x_parts = (hidden, *exchange(result))
        kept.append(
            (x, normed, mixed, hidden, normed_two, active, slope, listed,
             (qkv, probs, qfeat, kfeat, mt))
        )

    grad = to_sequence(grad_own, grad_arrived)

    def my_half(array):
        return lax.dynamic_slice_in_dim(array, core * half, half)

    def deliver(first_rows, second_rows):
        mine = jnp.where(is_first, first_rows, second_rows)
        theirs = jnp.where(is_first, second_rows, first_rows)
        own = send(mine, sizes, lambda s, t, z, c: (s, c, z, t))
        other = send(theirs, sizes, lambda s, t, z, c: (1 - s, c, z, t))
        return own, other

    hidden, part_a, part_b = x_parts
    last_bias = of_layer(1, [lane[18:20].reshape(1, width) for lane in pack_c]).astype(f32)
    last = my_half(hidden) + (my_half(part_a).astype(f32) + my_half(part_b).astype(f32)) + last_bias

    def plane_send(keep, away, hold=None):
        by_x = send(keep, sizes, lambda s, t, z, c: None if c == t else (s, 1 - t, z, c))
        by_y = share_y(away)
        late = away if hold is None else after(away, hold)
        by_both = send(late, sizes, lambda s, t, z, c: None if c == t else (1 - s, 1 - t, z, c))
        return keep, by_x, by_y, by_both

    def plane_sum(terms):
        total = terms[0].astype(f32)
        for term in terms[1:]:
            total = total + term.astype(f32)
        return total.astype(bf)

    def core_share(total):
        tail = total[width:]
        by_core = total[:width].reshape(2, width // 2, -1)
        other = lax.dynamic_index_in_dim(by_core, 1 - core, keepdims=False)
        arrived = send(
            jnp.concatenate([other, tail], axis=0),
            sizes,
            lambda s, t, z, c: (s, t, z, 1 - c) if c == t else None,
        )
        own = lax.dynamic_index_in_dim(by_core, core, keepdims=False)
        return jnp.where(same, jnp.concatenate([own, tail], axis=0), arrived)

    def line_send(piece):
        def shard_for(step):
            at = ((z_no + step) % n_z) * shard
            rows = lax.dynamic_slice_in_dim(piece, at, shard)
            return jnp.concatenate([rows, piece[width // 2 :]], axis=0)

        return [shard_for(0)] + [
            send(shard_for(step), sizes, lambda s, t, z, c: (s, t, (z + step) % n_z, c))
            for step in range(1, n_z)
        ]

    def line_sum(found):
        total = found[0].astype(f32)
        for part in found[1:]:
            total = total + part.astype(f32)
        return total

    def ffn_part(layer_no, grad, hold):
        normed_two, active, slope = kept[layer_no][4:7]
        gnormed_two, gupper, bias_up = ffn_backward(
            layer_no, after(grad, hold), slope, (weights[layer_no][1],)
        )
        parts = exchange(gnormed_two)
        return parts, gupper, bias_up

    def ffn_grads(layer_no, grad, gupper, hold, extra=()):
        normed_two, active = kept[layer_no][4:6]
        return weight_grads(
            f"ffn_grads_{layer_no}", 512, after(normed_two, hold), gupper, grad, active, extra
        )

    def attn_part(layer_no, grad, parts, hold):
        hidden, listed, attn_kept = kept[layer_no][3], kept[layer_no][7], kept[layer_no][8]
        gnormed, *rest = attn_backward(
            layer_no, n_heads, listed, grad, after(parts[0], hold), parts[1], hidden,
            kept[layer_no][0], attn_kept, pack_c,
        )
        gbranch, gproj, vec_one, vec_two, bias_qkv = rest
        sums = (vec_one, other_core(vec_one, sizes), vec_two, bias_qkv)
        return exchange(gnormed), gbranch, gproj, sums

    def attn_grads(layer_no, gproj, gbranch, hold, sums=()):
        normed, mixed = kept[layer_no][1:3]
        return weight_grads(
            f"attn_grads_{layer_no}", part_width, after(normed, hold), gproj, gbranch, mixed, (), sums
        )

    def norm_part(layer_no, parts, gbranch, hold):
        return norm_backward(
            layer_no, kept[layer_no][0], after(parts[0], hold), parts[1], gbranch, pack_c
        )

    shard = width // n_dp
    units = wide.shape[1]
    parts, gupper, bias_up = ffn_part(1, grad, x_parts[0])
    keep, away = ffn_grads(1, grad, gupper, parts[0])
    parts, gbranch, gproj, sums = attn_part(1, grad, parts, keep)
    wide_one = plane_send(keep, away, gbranch)
    sums_one = (*sums, bias_up)
    extra = attn_grads(1, gproj, gbranch, parts[0])
    grad = norm_part(1, parts, gbranch, extra[0])
    upper_grad = grad
    parts, gupper, bias_up = ffn_part(0, grad, grad)
    keep, away = ffn_grads(0, grad, gupper, parts[0], extra)
    keep, away, wide_one = after((keep, away, wide_one), keep)
    wide_zero = plane_send(keep, away)
    parts, gbranch, gproj, sums = attn_part(0, grad, parts, (keep, wide_one))
    wide_zero, wide_one = after((wide_zero, wide_one), gbranch)
    keep, away = attn_grads(
        0, gproj, gbranch, parts[0], (*sums_one, *sums, bias_up)
    )
    keep, away, wide_zero, wide_one = after((keep, away, wide_zero, wide_one), keep)
    keep, away = after((keep, away), wide_zero)
    narrow_zero = plane_send(keep, away)
    piece = core_share(jnp.concatenate([plane_sum(wide_one), plane_sum(wide_zero)], axis=1))
    line_wide = line_send(piece)
    grad = norm_part(0, parts, gbranch, (keep, line_wide))
    out_pair = deliver(my_half(after(outputs[0], narrow_zero)), last.astype(bf))
    grad_pair = deliver(my_half(after(grad, narrow_zero)), my_half(upper_grad))
    piece = core_share(plane_sum(narrow_zero))
    line_narrow = line_send(after(piece, line_wide))
    line_narrow = line_sum(after(line_narrow, (out_pair, grad_pair)))
    line_wide = line_sum(line_wide)
    first_sum = jnp.concatenate([line_wide[:, units : 2 * units], line_narrow[:shard]], axis=1)
    second_sum = jnp.concatenate([line_wide[:, :units], line_wide[:, 2 * units :]], axis=1)
    gone = jnp.where(is_first, second_sum, first_sum).astype(bf)
    arrived = send(gone, sizes, lambda s, t, z, c: (1 - s, t, z, c)).astype(f32)
    stay = jnp.where(is_first, first_sum, second_sum)
    low_half = jnp.where(is_first, stay, arrived)
    high_half = jnp.where(is_first, arrived, stay)
    grad_up, grad_down = low_half[:, :units], high_half[:, :units]
    narrow = jnp.concatenate([low_half[:, units:], high_half[:, units:]], axis=1)
    rows = line_narrow[shard:]
    rows = jnp.where(is_first, rows[7:14], rows[:7]).reshape(14, width // 2)

    def own_columns(array):
        cols = array.reshape(-1, n_dp, array.shape[1] // n_dp)
        return lax.dynamic_index_in_dim(cols, dp_no, axis=1, keepdims=False)

    grad_vectors = own_columns(rows[:6])
    grad_bqkv = own_columns(rows[6:9])
    grad_bup = own_columns(rows[10:].reshape(1, -1))[0]

    def placed(pair, dtype):
        own, other = pair
        return jnp.stack(
            [jnp.where(is_first, own, other), jnp.where(is_first, other, own)]
        )[None].astype(dtype)

    section_outputs = placed(out_pair, bf)
    input_grads = placed(grad_pair, f32)
    grad_qkv = narrow[:, : 3 * part_width].reshape(shard, 3, part_width)
    grad_out = narrow[:, 3 * part_width :].T
    return (
        section_outputs,
        input_grads,
        grad_qkv[None],
        grad_bqkv[None],
        grad_out[None],
        grad_up[None],
        grad_bup[None],
        grad_down.T[None],
        grad_vectors[None],
    )


HEAD = 64
BLOCK = 64
SEQ_LEN = 1024


norm_eps = 1e-05
bfloat = jnp.bfloat16
single = jnp.float32


def shifted(value, axis, steps):
    count = lax.axis_size(axis)
    first, last = (max(0, -steps), min(count, count - steps))
    return lax.ppermute(value, axis, [(source, source + steps) for source in range(first, last)])


def norm_rows(residual, gain_vec, shift_vec):
    row_mean = jnp.mean(residual, axis=-1, keepdims=True)
    centred = residual - row_mean
    variance = jnp.mean(centred * centred, axis=-1, keepdims=True)
    return centred * lax.rsqrt(variance + norm_eps) * (1.0 + gain_vec) + shift_vec


def gelu_exact(pre_active):
    return jax.nn.gelu(pre_active, approximate=False)


def select_tree(flag_value, when_true, when_false):
    return jax.tree.map(
        lambda left_arr, right_arr: jnp.where(flag_value, left_arr, right_arr),
        when_true,
        when_false,
    )


def split_pieces(operand):
    if operand.dtype == bfloat:
        return (operand,)
    upper_part = operand.astype(bfloat)
    lower_part = (operand - upper_part.astype(single)).astype(bfloat)
    return (upper_part, lower_part)


def split_dot(form, left, right):
    left_pieces = split_pieces(left)
    right_pieces = split_pieces(right)
    total = None
    for left_no, left_piece in enumerate(left_pieces):
        for right_no, right_piece in enumerate(right_pieces):
            if left_no + right_no > 1:
                continue
            term = jnp.einsum(form, left_piece, right_piece, preferred_element_type=single)
            total = term if total is None else total + term
    return total


def sparse_layout(block_list, length):
    head_count, block_count = (block_list.shape[0], block_list.shape[1])
    chosen = jnp.concatenate(
        [jnp.zeros((head_count, block_count, 1), jnp.int32), block_list], axis=2
    )
    key_live = (jnp.arange(SEQ_LEN) < length).astype(single)
    picked_live = key_live.reshape(block_count, BLOCK)[chosen].reshape(head_count, block_count, -1)
    return (chosen, key_live, picked_live)


def pick_blocks(table_in, chosen):
    head_count, block_count = (chosen.shape[0], chosen.shape[1])
    blocks_in = table_in.reshape(head_count, block_count, BLOCK, table_in.shape[-1])
    taken_rows = jax.vmap(lambda one_table, index_rows: one_table[index_rows])(blocks_in, chosen)
    return taken_rows.reshape(head_count, block_count, -1, table_in.shape[-1])


def place_blocks(values_in, chosen):
    head_count, block_count, slot_count = chosen.shape
    parts_in = values_in.reshape(head_count, block_count, slot_count, BLOCK, values_in.shape[-1])
    zero_blocks = jnp.zeros((head_count, block_count, BLOCK, values_in.shape[-1]), single)
    placed = jax.vmap(lambda base_arr, index_rows, one_part: base_arr.at[index_rows].add(one_part))(
        zero_blocks, chosen, parts_in
    )
    return placed.reshape(head_count, SEQ_LEN, values_in.shape[-1])


def feature_of(vectors_low, features):
    feature_scale = HEAD ** (-0.25)
    vectors = vectors_low.astype(single)
    projected = split_dot("hld,hdf->hlf", vectors_low, features) * feature_scale
    return jnp.exp(
        projected
        - jnp.sum(vectors * vectors, axis=-1, keepdims=True) * (0.5 * feature_scale * feature_scale)
    )


def block_scores(query_blocks, picked_keys, picked_live):
    scores = jnp.einsum(
        "hnqd,hnkd->hnqk", query_blocks, picked_keys, preferred_element_type=single
    ) * HEAD ** (-0.5)
    return jnp.where(picked_live[:, :, None, :] > 0.5, scores, -1e30)


def attend_forward(queries, key_vecs, value_vecs, chosen, key_live, picked_live, features):
    head_count, block_count = (chosen.shape[0], chosen.shape[1])
    query_blocks = queries.reshape(head_count, block_count, BLOCK, HEAD)
    picked_keys = pick_blocks(key_vecs, chosen)
    picked_values = pick_blocks(value_vecs, chosen)
    scores = block_scores(query_blocks, picked_keys, picked_live)
    row_max = jnp.max(scores, axis=-1, keepdims=True)
    weights_raw = jnp.exp(scores - row_max) * picked_live[:, :, None, :]
    row_total = jnp.sum(weights_raw, axis=-1, keepdims=True)
    log_total = row_max + jnp.log(row_total)
    weights_low = (weights_raw / row_total).astype(bfloat)
    sparse_out = jnp.einsum(
        "hnqk,hnkd->hnqd", weights_low, picked_values, preferred_element_type=single
    )
    sparse_out = sparse_out.reshape(head_count, SEQ_LEN, HEAD)
    query_feats = feature_of(queries, features)
    key_feats = feature_of(key_vecs, features) * key_live[None, :, None]
    moments = split_dot("hlf,hld->hfd", key_feats, value_vecs)
    totals = jnp.sum(key_feats, axis=1)
    numerator = split_dot("hlf,hfd->hld", query_feats, moments)
    denominator = split_dot("hlf,hf->hl", query_feats, totals)
    perf_out = numerator / denominator[:, :, None]
    return (
        sparse_out + perf_out,
        (log_total, query_feats, key_feats, moments, totals, denominator, perf_out),
    )


def attend_backward(
    grad_heads, queries, key_vecs, value_vecs, chosen, picked_live, features, attn_keep
):
    log_total, query_feats, key_feats, moments, totals, denominator, perf_out = attn_keep
    head_count, block_count = (chosen.shape[0], chosen.shape[1])
    score_scale = HEAD ** (-0.5)
    query_blocks = queries.reshape(head_count, block_count, BLOCK, HEAD)
    grad_blocks = grad_heads.reshape(head_count, block_count, BLOCK, HEAD)
    picked_keys = pick_blocks(key_vecs, chosen)
    picked_values = pick_blocks(value_vecs, chosen)
    scores = block_scores(query_blocks, picked_keys, picked_live)
    weights_f = jnp.exp(scores - log_total) * picked_live[:, :, None, :]
    grad_weights = jnp.einsum(
        "hnqd,hnkd->hnqk", grad_blocks, picked_values, preferred_element_type=single
    )
    row_inner = jnp.sum(weights_f * grad_weights, axis=-1, keepdims=True)
    grad_scores = (weights_f * (grad_weights - row_inner)).astype(bfloat)
    grad_query = jnp.einsum(
        "hnqk,hnkd->hnqd", grad_scores, picked_keys, preferred_element_type=single
    )
    grad_query = grad_query.reshape(head_count, SEQ_LEN, HEAD) * score_scale
    grad_keys = place_blocks(
        jnp.einsum("hnqk,hnqd->hnkd", grad_scores, query_blocks, preferred_element_type=single)
        * score_scale,
        chosen,
    )
    grad_values = place_blocks(
        jnp.einsum(
            "hnqk,hnqd->hnkd", weights_f.astype(bfloat), grad_blocks, preferred_element_type=single
        ),
        chosen,
    )
    grad_float = grad_heads.astype(single)
    grad_numer = grad_float / denominator[:, :, None]
    grad_denom = -jnp.sum(grad_float * perf_out, axis=-1) / denominator
    grad_qfeat = (
        split_dot("hld,hfd->hlf", grad_numer, moments) + grad_denom[:, :, None] * totals[:, None, :]
    )
    grad_moments = split_dot("hlf,hld->hfd", query_feats, grad_numer)
    grad_totals = split_dot("hlf,hl->hf", query_feats, grad_denom)
    grad_kfeat = split_dot("hld,hfd->hlf", value_vecs, grad_moments) + grad_totals[:, None, :]
    grad_values = grad_values + split_dot("hlf,hfd->hld", key_feats, grad_moments)
    feature_scale = HEAD ** (-0.25)

    def feature_back(grad_feat, feats, vectors_low):
        grad_expo = grad_feat * feats
        direct = split_dot("hlf,hdf->hld", grad_expo, features) * feature_scale
        return direct - feature_scale * feature_scale * jnp.sum(
            grad_expo, axis=-1, keepdims=True
        ) * vectors_low.astype(single)

    grad_query = grad_query + feature_back(grad_qfeat, query_feats, queries)
    grad_keys = grad_keys + feature_back(grad_kfeat, key_feats, key_vecs)
    return (grad_query, grad_keys, grad_values)


def layer_forward(section_entry, length, layer_params, block_list, features):
    qkv_mat, qkv_bias, out_mat, up_mat, up_bias, down_mat, vectors = layer_params
    residual = section_entry.astype(single)
    normed = norm_rows(residual, vectors[0], vectors[1]).astype(bfloat)
    normed_all = lax.all_gather(normed, "tensor", axis=0, tiled=True)
    projected = (
        jnp.einsum("ld,dce->lce", normed_all, qkv_mat, preferred_element_type=single)
        + qkv_bias[None]
    )
    projected = projected.astype(bfloat)
    seq_len, part_width = (projected.shape[0], projected.shape[2])
    head_count = part_width // HEAD
    head_parts = projected.reshape(seq_len, 3, head_count, HEAD).transpose(1, 2, 0, 3)
    chosen, key_live, picked_live = sparse_layout(block_list, length)
    mixed_heads, attn_keep = attend_forward(
        head_parts[0], head_parts[1], head_parts[2], chosen, key_live, picked_live, features
    )
    mixed_low = mixed_heads.transpose(1, 0, 2).reshape(seq_len, part_width).astype(bfloat)
    row_block = mixed_low
    branch = lax.psum_scatter(
        jnp.dot(row_block, out_mat, preferred_element_type=single).astype(jnp.bfloat16),
        "tensor",
        scatter_dimension=0,
        tiled=True,
    ).astype(jnp.float32)
    hidden_res = residual + branch + vectors[4]
    normed_two = norm_rows(hidden_res, vectors[2], vectors[3]).astype(bfloat)
    normed_two_all = lax.all_gather(normed_two, "tensor", axis=0, tiled=True)
    pre_active = jnp.dot(normed_two_all, up_mat, preferred_element_type=single) + up_bias
    active = gelu_exact(pre_active).astype(bfloat)
    row_block = active
    result = (
        hidden_res
        + lax.psum_scatter(
            jnp.dot(row_block, down_mat, preferred_element_type=single).astype(jnp.bfloat16),
            "tensor",
            scatter_dimension=0,
            tiled=True,
        ).astype(jnp.float32)
        + vectors[5]
    )
    record = (
        residual,
        hidden_res,
        normed_all,
        head_parts,
        mixed_low,
        normed_two_all,
        pre_active,
        active,
        attn_keep,
        length,
    )
    return (result.astype(bfloat), record)


def layer_backward(grad_low, record, layer_params, block_list, features):
    qkv_mat, qkv_bias, out_mat, up_mat, up_bias, down_mat, vectors = layer_params
    (
        residual,
        hidden_res,
        normed_all,
        head_parts,
        mixed_low,
        normed_two_all,
        pre_active,
        active,
        attn_keep,
        length,
    ) = record
    seq_len, part_width = mixed_low.shape
    head_count = part_width // HEAD
    grad_output = grad_low.astype(single)
    grad_all = lax.all_gather(grad_low, "tensor", axis=0, tiled=True)
    grad_wdown = jnp.einsum("lf,ld->fd", active, grad_all, preferred_element_type=single)
    grad_active = jnp.einsum("ld,fd->lf", grad_all, down_mat, preferred_element_type=single)
    _, gelu_pull = jax.vjp(gelu_exact, pre_active)
    grad_upper = gelu_pull(grad_active)[0].astype(bfloat)
    grad_wup = jnp.einsum("ld,lf->df", normed_two_all, grad_upper, preferred_element_type=single)
    grad_bup = jnp.sum(grad_upper.astype(single), axis=0)
    row_block = grad_upper
    grad_normed_two = lax.psum_scatter(
        jnp.einsum("lf,df->ld", row_block, up_mat, preferred_element_type=single).astype(
            jnp.bfloat16
        ),
        "tensor",
        scatter_dimension=0,
        tiled=True,
    ).astype(jnp.float32)
    _, pull_two = jax.vjp(norm_rows, hidden_res, vectors[2], vectors[3])
    grad_hidden, grad_gain_two, grad_shift_two = pull_two(grad_normed_two)
    grad_hidden = grad_hidden + grad_output
    grad_hidden_low = grad_hidden.astype(bfloat)
    hidden_all = lax.all_gather(grad_hidden_low, "tensor", axis=0, tiled=True)
    grad_wout = jnp.einsum("le,ld->ed", mixed_low, hidden_all, preferred_element_type=single)
    grad_mixed = jnp.einsum("ld,ed->le", hidden_all, out_mat, preferred_element_type=single).astype(
        bfloat
    )
    grad_heads = grad_mixed.reshape(seq_len, head_count, HEAD).transpose(1, 0, 2)
    chosen, key_live, picked_live = sparse_layout(block_list, length)
    grad_query, grad_keys, grad_values = attend_backward(
        grad_heads,
        head_parts[0],
        head_parts[1],
        head_parts[2],
        chosen,
        picked_live,
        features,
        attn_keep,
    )
    grad_proj = (
        jnp.stack([grad_query, grad_keys, grad_values])
        .transpose(2, 0, 1, 3)
        .reshape(seq_len, 3, part_width)
        .astype(bfloat)
    )
    grad_wqkv = jnp.einsum("ld,lce->dce", normed_all, grad_proj, preferred_element_type=single)
    grad_bqkv = jnp.sum(grad_proj.astype(single), axis=0)
    row_block = grad_proj
    grad_normed = lax.psum_scatter(
        jnp.einsum("lce,dce->ld", row_block, qkv_mat, preferred_element_type=single).astype(
            jnp.bfloat16
        ),
        "tensor",
        scatter_dimension=0,
        tiled=True,
    ).astype(jnp.float32)
    _, pull_one = jax.vjp(norm_rows, residual, vectors[0], vectors[1])
    grad_resid, grad_gain_one, grad_shift_one = pull_one(grad_normed)
    grad_resid = grad_resid + grad_hidden
    weight_grads = (grad_wqkv, grad_bqkv, grad_wout, grad_wup, grad_bup, grad_wdown)
    vector_grads = jnp.stack(
        [
            grad_gain_one,
            grad_shift_one,
            grad_gain_two,
            grad_shift_two,
            jnp.sum(grad_hidden_low.astype(single), axis=0),
            jnp.sum(grad_output, axis=0),
        ]
    )
    return (grad_resid, weight_grads, vector_grads)


def shards(
    inputs,
    cotangent,
    lengths,
    blocks,
    feature_map,
    w_qkv,
    b_qkv,
    w_out,
    w_up,
    b_up,
    w_down,
    vector_params,
):
    section_no = lax.axis_index("section")
    is_first = section_no == 0
    is_last = section_no == lax.axis_size("section") - 1
    layer_params = (
        w_qkv[0],
        b_qkv[0].astype(single),
        w_out[0],
        w_up[0],
        b_up[0].astype(single),
        w_down[0],
        vector_params[0].astype(single),
    )
    block_list = blocks[0]
    features = feature_map[0]
    batch_count = inputs.shape[0]
    carried = jnp.zeros_like(inputs[0])
    records = []
    results = []
    for tick_no in range(batch_count + 1):
        batch_no = jnp.clip(tick_no - section_no, 0, batch_count - 1)
        section_entry = jnp.where(is_first, inputs[min(tick_no, batch_count - 1)], carried)
        result, record = layer_forward(
            section_entry, lengths[batch_no, 0], layer_params, block_list, features
        )
        records.append(record)
        results.append(result)
        if tick_no < batch_count:
            carried = shifted(result, "section", 1)
    section_outputs = jnp.stack(
        [
            jnp.where(is_first, results[batch_idx], results[batch_idx + 1])
            for batch_idx in range(batch_count)
        ]
    )[None]
    received = jnp.zeros_like(cotangent[0])
    grad_list = []
    local_sum = None
    vector_total = jnp.zeros((6, inputs.shape[2]), single)
    for tick_no in range(batch_count + 1):
        record = select_tree(
            is_last, records[min(tick_no + 1, batch_count)], records[max(tick_no - 1, 0)]
        )
        valid_flag = jnp.where(is_last, float(tick_no < batch_count), float(tick_no >= 1)).astype(
            single
        )
        grad_entry = jnp.where(is_last, cotangent[min(tick_no, batch_count - 1)], received)
        grad_resid, weight_grads, vector_grads = layer_backward(
            grad_entry, record, layer_params, block_list, features
        )
        weight_grads = tuple((valid_flag * addend for addend in weight_grads))
        vector_total = vector_total + valid_flag * vector_grads
        local_sum = (
            weight_grads
            if local_sum is None
            else tuple((summed + addend for summed, addend in zip(local_sum, weight_grads)))
        )
        grad_list.append(grad_resid)
        if tick_no < batch_count:
            received = shifted(grad_resid.astype(bfloat), "section", -1)
    final_grads = (
        lax.psum_scatter(
            local_sum[0].astype(jnp.bfloat16), "dp", scatter_dimension=0, tiled=True
        ).astype(jnp.float32),
        lax.psum_scatter(
            local_sum[1].astype(jnp.bfloat16), "dp", scatter_dimension=1, tiled=True
        ).astype(jnp.float32),
        lax.psum_scatter(
            local_sum[2].astype(jnp.bfloat16), "dp", scatter_dimension=1, tiled=True
        ).astype(jnp.float32),
        lax.psum_scatter(
            local_sum[3].astype(jnp.bfloat16), "dp", scatter_dimension=0, tiled=True
        ).astype(jnp.float32),
        lax.psum_scatter(
            local_sum[4].astype(jnp.bfloat16), "dp", scatter_dimension=0, tiled=True
        ).astype(jnp.float32),
        lax.psum_scatter(
            local_sum[5].astype(jnp.bfloat16), "dp", scatter_dimension=1, tiled=True
        ).astype(jnp.float32),
    )
    input_grads = jnp.stack(
        [
            jnp.where(is_first, grad_list[batch_idx + 1], grad_list[batch_idx])
            for batch_idx in range(batch_count)
        ]
    )[None]
    grad_vectors = lax.psum_scatter(
        vector_total, ("tensor", "dp"), scatter_dimension=1, tiled=True
    )[None]
    grad_wqkv, grad_bqkv, grad_wout, grad_wup, grad_bup, grad_wdown = final_grads
    return (
        section_outputs,
        input_grads,
        grad_wqkv[None],
        grad_bqkv[None],
        grad_wout[None],
        grad_wup[None],
        grad_bup[None],
        grad_wdown[None],
        grad_vectors,
    )


def solution(mesh):
    placed = (
        P(None, ("dp", "tensor"), None),
        P(None, ("dp", "tensor"), None),
        P(None, "dp"),
        P("section", "tensor", None, None),
        P("section", "tensor", None, None),
        P("section", None, None, "tensor"),
        P("section", None, "tensor"),
        P("section", "tensor", None),
        P("section", None, "tensor"),
        P("section", "tensor"),
        P("section", "tensor", None),
        P("section", None, None),
    )
    sizes = tuple(mesh.shape[axis] for axis in ALL_AXES)
    if sizes[0] == 2 and sizes[1] == 2 and sizes[2] % 2 == 0:
        body = functools.partial(chip_shards, sizes)
    else:
        body = shards
    return jax.shard_map(
        body,
        mesh=mesh,
        in_specs=placed,
        out_specs=(
            P("section", None, ("dp", "tensor"), None),
            P("section", None, ("dp", "tensor"), None),
            P("section", "dp", None, "tensor"),
            P("section", None, ("tensor", "dp")),
            P("section", "tensor", "dp"),
            P("section", "dp", "tensor"),
            P("section", ("tensor", "dp")),
            P("section", "tensor", "dp"),
            P("section", None, ("tensor", "dp")),
        ),
        check_vma=False,
    )
```

```python
import functools

import jax
import jax.numpy as jnp
from jax import lax
from jax.experimental import pallas as pl
from jax.experimental.pallas import tpu as pltpu
from jax.sharding import PartitionSpec as P

HEAD = 64
BLOCK = 64
NORM_EPS = 1e-5
bf = jnp.bfloat16
f32 = jnp.float32
LOG2E = 1.4426950408889634
F_SCALE = HEAD ** -0.25
ROWS = 1024
FFN_ROWS = 256
SPARSE_UNROLL = 8
PACK_ROWS = 32
PACK_SMALL = 96
LANES = 128
N_QUARTERS = 4
MIB = 1024 * 1024
SHORT = pl.CostEstimate(flops=10**6, bytes_accessed=2**16, transcendentals=0)
ANY = pl.BlockSpec(memory_space=pl.ANY)
WHOLE = pl.BlockSpec(memory_space=pltpu.VMEM)
SCALARS = pl.BlockSpec(memory_space=pltpu.SMEM)


def contract(left, right, left_dim, right_dim):
    return lax.dot_general(
        left, right, (((left_dim,), (right_dim,)), ((), ())), preferred_element_type=f32
    )


def pick_source(layer_no):
    section_no = lax.axis_index("section")
    same = lax.rem(lax.axis_index("dp"), 2) == lax.axis_index("tensor")
    return jnp.where(section_no == layer_no, 0, 1) + jnp.where(same, 0, 2)


def start_pick(source, candidates, target, sem):
    for number, candidate in enumerate(candidates):

        @pl.when(source == number)
        def _():
            pltpu.make_async_copy(candidate, target, sem).start()


def wait_pick(candidates, target, sem):
    pltpu.make_async_copy(candidates[0], target, sem).wait()


def small_row(small, row, width):
    count = width // small.shape[1]
    rows = [small[row + i : row + i + 1, :].astype(f32) for i in range(count)]
    return jnp.concatenate(rows, axis=1)


def vector_row(small, number, width):
    return small_row(small, 8 + 2 * number, width)


def small_part(candidates):
    return [candidate.at[0:PACK_ROWS] for candidate in candidates]


def norm_stats(value):
    mean = jnp.mean(value, axis=-1, keepdims=True)
    centred = value - mean
    variance = jnp.mean(centred * centred, axis=-1, keepdims=True)
    scale = lax.rsqrt(variance + NORM_EPS)
    return centred * scale, scale


def lane_masks():
    lane = lax.broadcasted_iota(jnp.int32, (1, 2 * HEAD), 1)
    return lane < HEAD, lane >= HEAD


def swap_halves(value):
    return pltpu.roll(value, HEAD, 1)


def listed_starts(blocks_ref, pair, block, n_blocks):
    found = []
    for slot in range(3):
        two = []
        for a in range(2):
            listed = blocks_ref[(2 * pair + a) * n_blocks + block, slot]
            two.append(pl.multiple_of(listed * BLOCK, BLOCK))
        found.append(tuple(two))
    return found


def pick_rows(table, part, cols, starts, in_first):
    pieces = [table[part, 0:BLOCK, cols]]
    for one, two in starts:
        pieces.append(
            jnp.where(
                in_first,
                table[part, pl.ds(one, BLOCK), cols],
                table[part, pl.ds(two, BLOCK), cols],
            )
        )
    return jnp.concatenate(pieces, axis=0)


def stack_heads(target, chunk, value, masks):
    for number in range(ROWS // BLOCK):
        block = value[number * BLOCK : (number + 1) * BLOCK]
        for a in range(2):
            target[chunk * (ROWS // BLOCK) + number, a * BLOCK : (a + 1) * BLOCK] = jnp.where(
                masks[a], block, 0.0
            ).astype(bf)


def feature_rows(pack, n_heads, head):
    at = PACK_SMALL + head * HEAD
    return pack[at : at + HEAD].astype(f32) + pack[at + n_heads * HEAD : at + (n_heads + 1) * HEAD].astype(f32)


def qkv_weight(pack, n_heads, width, part):
    at = PACK_SMALL + 4 * n_heads * HEAD + part * width
    return pack[at : at + width]


def out_weights(pack, n_heads, part_width):
    at = PACK_SMALL + 2 * n_heads * HEAD
    return [pack[at + part * part_width : at + (part + 1) * part_width] for part in range(2)]


def pack_kernel(wqkv_ref, wout_ref, features_ref, bqkv_ref, bup_ref, vector_ref, blocks_ref, pack_ref):
    n_features, feat = features_ref.shape
    n_parts, width, part_width = wqkv_ref.shape

    def lane_rows(value):
        value = value.astype(f32)
        return [
            value[row : row + 1, at : at + feat]
            for row in range(value.shape[0])
            for at in range(0, value.shape[1], feat)
        ]

    blank = jnp.zeros((1, feat), f32)
    rows = lane_rows(bqkv_ref[...]) + [blank] + lane_rows(bup_ref[...]) + lane_rows(vector_ref[...])
    rows += [blank] * (PACK_ROWS - len(rows))
    pack_ref[0:PACK_ROWS] = jnp.concatenate(rows, axis=0).astype(bf)
    n_listed, n_slots = blocks_ref.shape
    pack_ref[PACK_ROWS:PACK_SMALL] = jnp.zeros((PACK_SMALL - PACK_ROWS, feat), bf)
    pack_ref[PACK_ROWS : PACK_ROWS + n_listed, 0:n_slots] = blocks_ref[...].astype(f32).astype(bf)
    at = PACK_SMALL
    features = features_ref[...]
    high = features.astype(bf)
    pack_ref[at : at + n_features] = high
    pack_ref[at + n_features : at + 2 * n_features] = (features - high.astype(f32)).astype(bf)
    at += 2 * n_features
    for part in range(2):
        pack_ref[at : at + part_width] = wout_ref[:, part * feat : (part + 1) * feat]
        at += part_width
    for part in range(n_parts):
        pack_ref[at : at + width] = wqkv_ref[part]
        at += width


def pack_weights(wqkv, wout, features, bqkv, bup, vectors, blocks):
    n_parts, width, part_width = wqkv.shape
    n_features, feat = features.shape
    n_rows = PACK_SMALL + 2 * n_features + 2 * part_width + n_parts * width
    return pl.pallas_call(
        pack_kernel,
        out_shape=jax.ShapeDtypeStruct((n_rows, feat), bf),
        in_specs=[WHOLE] * 7,
        out_specs=WHOLE,
        compiler_params=pltpu.CompilerParams(vmem_limit_bytes=16 * MIB),
        cost_estimate=SHORT,
        name="pack_weights",
    )(wqkv, wout, features, bqkv, bup, vectors, blocks)


def attn_forward_kernel(layer_no, n_heads, length_ref, blocks_ref, *refs):
    if layer_no == 0:
        x_ref, refs = refs[0], refs[1:]
    else:
        hidden_ref, part_a, part_b, refs = refs[0], refs[1], refs[2], refs[3:]
        small_prev, refs = refs[:4], refs[4:]
    pack_c, refs = refs[:4], refs[4:]
    if layer_no == 1:
        x_ref, refs = refs[0], refs[1:]
    (branch_ref, qkv_out, normed_out, probs_out, qf_out, kf_out, mt_out, mixed_out) = refs[:8]
    (pack, qkv, normed, probs, qfeat, kfeat, mt, mixed, fcat, perf, qstack,
     in_sem, out_sem) = refs[8:21]
    seq, width = normed.shape
    n_chunks = seq // ROWS
    pairs = n_heads // 2
    part_width = qkv.shape[2]
    feat = pack.shape[1]
    small = pack.at[0:PACK_ROWS]
    source = pick_source(layer_no)
    if layer_no == 1:
        small_before = refs[21]
        before = pick_source(0)
        start_pick(before, small_part(small_prev), small_before, in_sem.at[1])
    start_pick(source, pack_c, pack, in_sem.at[0])
    wait_pick(pack_c, pack, in_sem.at[0])
    if layer_no == 1:
        wait_pick(small_part(small_prev), small_before, in_sem.at[1])
    length = length_ref[0]
    gain = 1.0 + vector_row(small, 0, width)
    shift = vector_row(small, 1, width)

    @pl.loop(0, n_chunks)
    def _(chunk):
        rows = pl.ds(pl.multiple_of(chunk * ROWS, ROWS), ROWS)
        if layer_no == 0:
            x = x_ref[rows, :].astype(f32)
        else:
            total = part_a[rows, :].astype(f32) + part_b[rows, :].astype(f32)
            x_low = (hidden_ref[rows, :] + total + vector_row(small_before, 5, width)).astype(bf)
            x_ref[rows, :] = x_low
            x = x_low.astype(f32)
        zhat, _ = norm_stats(x)
        low = (zhat * gain + shift).astype(bf)
        normed[rows, :] = low
        for part in range(3):
            cols = n_heads * HEAD
            out = jnp.dot(low, qkv_weight(pack, n_heads, width, part), preferred_element_type=f32)
            qkv[part, rows, :] = (out + small_row(small, part, cols)).astype(bf)

    copies = [
        pltpu.make_async_copy(qkv, qkv_out, out_sem.at[0]),
        pltpu.make_async_copy(normed, normed_out, out_sem.at[1]),
    ]
    for copy in copies:
        copy.start()
    in_first, in_second = lane_masks()
    masks = (in_first, in_second)
    key_row = lax.broadcasted_iota(jnp.int32, (BLOCK, 2 * HEAD), 0)
    for pair in range(pairs):
        cols = slice(pair * 2 * HEAD, (pair + 1) * 2 * HEAD)
        zero = jnp.zeros((HEAD, feat), bf)
        for a in range(2):
            scaled = feature_rows(pack, n_heads, 2 * pair + a) * (F_SCALE * LOG2E)
            high = scaled.astype(bf)
            rest = (scaled - high.astype(f32)).astype(bf)
            for part, piece in enumerate((high, rest)):
                row = part * 2 * HEAD + a * HEAD
                fcat[row : row + HEAD, a * feat : (a + 1) * feat] = piece
                fcat[row : row + HEAD, (1 - a) * feat : (2 - a) * feat] = zero

        def features(vectors):
            proj = jnp.dot(
                jnp.concatenate([vectors, vectors], axis=1), fcat[...], preferred_element_type=f32
            )
            value = vectors.astype(f32)
            square = value * value * (0.5 * F_SCALE * F_SCALE * LOG2E)
            return [
                jnp.exp2(
                    proj[:, a * feat : (a + 1) * feat]
                    - jnp.sum(jnp.where(masks[a], square, 0.0), axis=-1, keepdims=True)
                )
                for a in range(2)
            ]

        @pl.loop(0, n_chunks)
        def _(chunk):
            base = pl.multiple_of(chunk * ROWS, ROWS)
            rows = pl.ds(base, ROWS)
            live = lax.broadcasted_iota(jnp.int32, (ROWS, 1), 0) + base < length
            found = features(qkv[1, rows, cols])
            for a in range(2):
                kfeat[pair, rows, a * feat : (a + 1) * feat] = jnp.where(live, found[a], 0.0).astype(bf)

        values = qkv[2, :, cols].astype(f32)
        for a in range(2):
            extended = jnp.where(masks[a], values, 1.0).astype(bf)
            moment = contract(extended, kfeat[pair, :, a * feat : (a + 1) * feat], 0, 0)
            mt[2 * pair + a] = moment.astype(bf)

        @pl.loop(0, n_chunks)
        def _(chunk):
            rows = pl.ds(pl.multiple_of(chunk * ROWS, ROWS), ROWS)
            query = qkv[0, rows, cols]
            found = features(query)
            out = None
            for a in range(2):
                low = found[a].astype(bf)
                qfeat[pair, rows, a * feat : (a + 1) * feat] = low
                numer = contract(low, mt[2 * pair + a], 1, 1)
                value = numer / swap_halves(numer)
                out = value if a == 0 else jnp.where(in_first, out, value)
            perf[rows, :] = out
            stack_heads(qstack, chunk, query.astype(f32) * (HEAD ** -0.5), masks)

        @pl.loop(0, seq // BLOCK, unroll=SPARSE_UNROLL)
        def _(block):
            rows = pl.ds(pl.multiple_of(block * BLOCK, BLOCK), BLOCK)
            starts = listed_starts(blocks_ref, pair, block, seq // BLOCK)
            keys = pick_rows(qkv, 1, cols, starts, in_first)
            values = pick_rows(qkv, 2, cols, starts, in_first)
            scores = contract(keys, qstack[block], 1, 1)
            pieces = [scores[:BLOCK]]
            for slot, (one, two) in enumerate(starts):
                room = length - jnp.where(in_first, one, two)
                piece = scores[(slot + 1) * BLOCK : (slot + 2) * BLOCK]
                pieces.append(jnp.where(key_row < room, piece, -1e30))
            scores = jnp.concatenate(pieces, axis=0)
            raw = jnp.exp(scores - jnp.max(scores, axis=0, keepdims=True))
            low = (raw * (1.0 / jnp.sum(raw, axis=0, keepdims=True))).astype(bf)
            probs[pair, block] = low
            both = contract(low, values, 0, 0)
            out = jnp.where(in_first, both[:BLOCK], both[BLOCK:])
            mixed[rows, cols] = (out + perf[rows, :]).astype(bf)

        more = [
            pltpu.make_async_copy(probs.at[pair], probs_out.at[pair], out_sem.at[2 + 4 * pair]),
            pltpu.make_async_copy(qfeat.at[pair], qf_out.at[pair], out_sem.at[3 + 4 * pair]),
            pltpu.make_async_copy(kfeat.at[pair], kf_out.at[pair], out_sem.at[4 + 4 * pair]),
            pltpu.make_async_copy(mt.at[2 * pair : 2 * pair + 2], mt_out.at[2 * pair : 2 * pair + 2], out_sem.at[5 + 4 * pair]),
        ]
        for copy in more:
            copy.start()
        copies += more

    @pl.loop(0, n_chunks)
    def _(chunk):
        rows = pl.ds(pl.multiple_of(chunk * ROWS, ROWS), ROWS)
        low = mixed[rows, :]
        mixed_out[rows, :] = low
        for part, weight in enumerate(out_weights(pack, n_heads, part_width)):
            here = slice(part * feat, (part + 1) * feat)
            branch_ref[rows, here] = jnp.dot(low, weight, preferred_element_type=f32).astype(bf)

    for copy in copies:
        copy.wait()


def attn_forward(layer_no, n_heads, length, blocks, x_parts, pack_c, small_before):
    part_width, feat = n_heads * HEAD, pack_c[0].shape[1]
    seq, width = x_parts[0].shape
    pairs = n_heads // 2
    shape = jax.ShapeDtypeStruct
    outs = [
        shape((seq, width), bf),
        shape((3, seq, part_width), bf),
        shape((seq, width), bf),
        shape((pairs, seq // BLOCK, 4 * BLOCK, 2 * HEAD), bf),
        shape((pairs, seq, 2 * feat), bf),
        shape((pairs, seq, 2 * feat), bf),
        shape((n_heads, 2 * HEAD, feat), bf),
        shape((seq, part_width), bf),
    ]
    out_specs = [WHOLE, ANY, ANY, ANY, ANY, ANY, ANY, WHOLE]
    scratch = [
        pltpu.VMEM(pack_c[0].shape, bf),
        pltpu.VMEM((3, seq, part_width), bf),
        pltpu.VMEM((seq, width), bf),
        pltpu.VMEM((pairs, seq // BLOCK, 4 * BLOCK, 2 * HEAD), bf),
        pltpu.VMEM((pairs, seq, 2 * feat), bf),
        pltpu.VMEM((pairs, seq, 2 * feat), bf),
        pltpu.VMEM((n_heads, 2 * HEAD, feat), bf),
        pltpu.VMEM((seq, part_width), bf),
        pltpu.VMEM((4 * HEAD, 2 * feat), bf),
        pltpu.VMEM((seq, 2 * HEAD), f32),
        pltpu.VMEM((seq // BLOCK, 2 * BLOCK, 2 * HEAD), bf),
        pltpu.SemaphoreType.DMA((2,)),
        pltpu.SemaphoreType.DMA((2 + 4 * pairs,)),
    ]
    operands = list(x_parts)
    specs = [WHOLE] * len(x_parts)
    if layer_no == 1:
        operands += list(small_before)
        specs += [ANY] * 4
        outs = [shape((seq, width), bf)] + outs
        out_specs = [WHOLE] + out_specs
        scratch.append(pltpu.VMEM((PACK_ROWS, feat), bf))
    operands += list(pack_c)
    specs += [ANY] * 4
    return pl.pallas_call(
        functools.partial(attn_forward_kernel, layer_no, n_heads),
        out_shape=outs,
        in_specs=[SCALARS, SCALARS] + specs,
        out_specs=out_specs,
        scratch_shapes=scratch,
        compiler_params=pltpu.CompilerParams(vmem_limit_bytes=60 * MIB),
        cost_estimate=SHORT,
        name=f"attn_forward_{layer_no}",
    )(length, blocks, *operands)


def gelu_parts(value):
    inverse = 1.0 / (1.0 + (0.3275911 * 0.5 ** 0.5) * jnp.abs(value))
    bell = jnp.exp2(value * value * (-0.5 * LOG2E))
    poly = inverse * (
        0.127414796
        + inverse
        * (-0.142248368 + inverse * (0.7107068705 + inverse * (-0.7265760135 + inverse * 0.5307027145)))
    )
    tail = poly * bell
    below = jnp.where(value >= 0.0, 1.0 - tail, tail)
    return value * below, below + value * bell * (0.5 / 3.141592653589793) ** 0.5


def down_rows(wide, width, at, step):
    part, row = at // width, at % width
    return wide[width + row : width + row + step, part * width : (part + 1) * width]


def ffn_forward_kernel(layer_no, *refs):
    x_ref, part_a, part_b = refs[:3]
    small_c, wide_c = refs[3:7], refs[7:11]
    out_ref, hidden_ref, normed_ref, active_ref, slope_ref = refs[11:16]
    small, wide, sems = refs[16:]

    @pl.when(pl.program_id(0) == 0)
    def _():
        source = pick_source(layer_no)
        start_pick(source, small_part(small_c), small, sems.at[0])
        start_pick(source, wide_c, wide, sems.at[1])
        wait_pick(small_part(small_c), small, sems.at[0])
        wait_pick(wide_c, wide, sems.at[1])

    width = x_ref.shape[1]
    units = wide.shape[1]
    branch = part_a[...].astype(f32) + part_b[...].astype(f32)
    hidden = x_ref[...].astype(f32) + branch + vector_row(small, 4, width)
    hidden_ref[...] = hidden
    zhat, _ = norm_stats(hidden)
    low = (zhat * (1.0 + vector_row(small, 2, width)) + vector_row(small, 3, width)).astype(bf)
    normed_ref[...] = low
    total = None
    step = 256
    for at in range(0, units, step):
        upper = jnp.dot(low, wide[:width, at : at + step], preferred_element_type=f32)
        active, slope = gelu_parts(upper + small_row(small, 4 + at // step, step))
        active = active.astype(bf)
        active_ref[:, at : at + step] = active
        slope_ref[:, at : at + step] = slope.astype(bf)
        term = jnp.dot(active, down_rows(wide, width, at, step), preferred_element_type=f32)
        total = term if total is None else total + term
    out_ref[...] = total.astype(bf)


def ffn_forward(layer_no, x, part_a, part_b, weights):
    small_c, wide_c = weights
    seq, width = x.shape
    units = wide_c[0].shape[1]
    shape = jax.ShapeDtypeStruct
    rows = lambda cols: pl.BlockSpec((FFN_ROWS, cols), lambda i: (i, 0))
    return pl.pallas_call(
        functools.partial(ffn_forward_kernel, layer_no),
        grid=(seq // FFN_ROWS,),
        out_shape=[
            shape((seq, width), bf),
            shape((seq, width), f32),
            shape((seq, width), bf),
            shape((seq, units), bf),
            shape((seq, units), bf),
        ],
        in_specs=[rows(width)] * 3 + [ANY] * 8,
        out_specs=[rows(width), rows(width), rows(width), rows(units), rows(units)],
        scratch_shapes=[
            pltpu.VMEM((PACK_ROWS, small_c[0].shape[1]), bf),
            pltpu.VMEM(wide_c[0].shape, bf),
            pltpu.SemaphoreType.DMA((2,)),
        ],
        compiler_params=pltpu.CompilerParams(vmem_limit_bytes=(60, 22)[layer_no] * MIB),
        cost_estimate=SHORT,
        name=f"ffn_forward_{layer_no}",
    )(x, part_a, part_b, *small_c, *wide_c)


def ffn_backward_kernel(layer_no, grad_ref, slope_ref, *refs):
    wide_c = refs[:4]
    out_ref, gupper_ref, bias_ref = refs[4:7]
    wide, sems = refs[7:]

    @pl.when(pl.program_id(0) == 0)
    def _():
        source = pick_source(layer_no)
        start_pick(source, wide_c, wide, sems.at[0])
        bias_ref[...] = jnp.zeros_like(bias_ref)
        wait_pick(wide_c, wide, sems.at[0])

    width = grad_ref.shape[1]
    units = wide.shape[1]
    grad = grad_ref[...]
    total = None
    step = 256
    for at in range(0, units, step):
        gactive = contract(grad, down_rows(wide, width, at, step), 1, 1)
        gupper = (gactive * slope_ref[:, at : at + step].astype(f32)).astype(bf)
        gupper_ref[:, at : at + step] = gupper
        bias_ref[:, at : at + step] += fold_rows(gupper.astype(f32))
        term = contract(gupper, wide[:width, at : at + step], 1, 1)
        total = term if total is None else total + term
    out_ref[...] = total.astype(bf)


def fold_rows(value):
    rows, cols = value.shape
    return jnp.sum(value.reshape(rows // 8, 8, cols), axis=0)


def ffn_backward(layer_no, grad, slope, weights):
    (wide_c,) = weights
    seq, width = grad.shape
    units = wide_c[0].shape[1]
    shape = jax.ShapeDtypeStruct
    rows = lambda cols: pl.BlockSpec((FFN_ROWS, cols), lambda i: (i, 0))
    return pl.pallas_call(
        functools.partial(ffn_backward_kernel, layer_no),
        grid=(seq // FFN_ROWS,),
        out_shape=[shape((seq, width), bf), shape((seq, units), bf), shape((8, units), f32)],
        in_specs=[rows(width), rows(units)] + [ANY] * 4,
        out_specs=[rows(width), rows(units), pl.BlockSpec((8, units), lambda i: (0, 0))],
        scratch_shapes=[
            pltpu.VMEM(wide_c[0].shape, bf),
            pltpu.SemaphoreType.DMA((1,)),
        ],
        compiler_params=pltpu.CompilerParams(vmem_limit_bytes=18 * MIB),
        cost_estimate=SHORT,
        name=f"ffn_backward_{layer_no}",
    )(grad, slope, *wide_c)


def attn_backward_kernel(layer_no, n_heads, blocks_ref, *refs):
    gy_ref, part_a, part_b, hidden_ref, x_ref = refs[:5]
    qkv_in, probs_in, qf_in, kf_in, mt_in = refs[5:10]
    pack_c, refs = refs[10:14], refs[14:]
    out_ref, gbranch_ref, dqkv_ref, first_ref, vec_ref, bias_ref, refs = *refs[:6], refs[6:]
    (pack, qkv, probs, qfeat, kfeat, mt, gmix, gstack, qstack, gext, gt, fback,
     dq, dk, dv, sem) = refs
    seq, width = gy_ref.shape
    n_chunks = seq // ROWS
    pairs = n_heads // 2
    part_width = qkv.shape[2]
    feat = pack.shape[1]
    small = pack.at[0:PACK_ROWS]
    source = pick_source(layer_no)
    start_pick(source, pack_c, pack, sem.at[0])
    loads = [
        pltpu.make_async_copy(qkv_in, qkv, sem.at[2]),
        pltpu.make_async_copy(mt_in, mt, sem.at[3]),
        pltpu.make_async_copy(qf_in, qfeat, sem.at[4]),
        pltpu.make_async_copy(kf_in, kfeat, sem.at[5]),
        pltpu.make_async_copy(probs_in, probs, sem.at[6]),
    ]
    for load in loads:
        load.start()
    first_ref[...] = jnp.zeros_like(first_ref)
    vec_ref[...] = jnp.zeros_like(vec_ref)
    bias_ref[...] = jnp.zeros_like(bias_ref)
    wait_pick(pack_c, pack, sem.at[0])
    gain = 1.0 + vector_row(small, 2, width)
    in_first, in_second = lane_masks()
    masks = (in_first, in_second)

    @pl.loop(0, n_chunks)
    def _(chunk):
        rows = pl.ds(pl.multiple_of(chunk * ROWS, ROWS), ROWS)
        gnormed = part_a[rows, :].astype(f32) + part_b[rows, :].astype(f32)
        zhat, scale = norm_stats(hidden_ref[rows, :])
        scaled = gnormed * gain
        gy = gy_ref[rows, :].astype(f32)
        mean_one = jnp.mean(scaled, axis=-1, keepdims=True)
        mean_two = jnp.mean(scaled * zhat, axis=-1, keepdims=True)
        ghidden = gy + (scaled - mean_one - zhat * mean_two) * scale
        low = ghidden.astype(bf)
        gbranch_ref[rows, :] = low
        vec_ref[0] += fold_rows(gnormed * zhat)
        vec_ref[1] += fold_rows(gnormed)
        vec_ref[2] += fold_rows(low.astype(f32))
        vec_ref[3] += fold_rows(gy)
        first, second = out_weights(pack, n_heads, part_width)
        gmix[rows, :] = (contract(low[:, :feat], first, 1, 1) + contract(low[:, feat:], second, 1, 1)).astype(bf)

    for load in loads[:4]:
        load.wait()
    for pair in range(pairs):
        cols = slice(pair * 2 * HEAD, (pair + 1) * 2 * HEAD)
        for a in range(2):
            plain = feature_rows(pack, n_heads, 2 * pair + a) * F_SCALE
            high = plain.astype(bf).astype(f32)
            ones = jnp.ones((HEAD, feat), f32)
            none = jnp.zeros((HEAD, feat), f32)
            stack = [high, ones] if a == 0 else [ones, high]
            stack += [plain - high, none] if a == 0 else [none, plain - high]
            fback[a] = jnp.concatenate(stack, axis=0).astype(bf)

        def feature_back(a, gfeat, feats, vectors):
            gexpo = (gfeat * feats.astype(f32)).astype(bf)
            both = contract(gexpo, fback[a], 1, 1)
            both = both[:, : 2 * HEAD] + both[:, 2 * HEAD :]
            return both - (F_SCALE * F_SCALE) * swap_halves(both) * vectors

        @pl.loop(0, n_chunks)
        def _(chunk):
            rows = pl.ds(pl.multiple_of(chunk * ROWS, ROWS), ROWS)
            grad = gmix[rows, cols].astype(f32)
            query = qkv[0, rows, cols].astype(f32)
            out = None
            for a in range(2):
                feats = qfeat[pair, rows, a * feat : (a + 1) * feat]
                moment = mt[2 * pair + a]
                numer = contract(feats, moment, 1, 1)
                inverse = 1.0 / swap_halves(numer)
                gnumer = grad * inverse
                other = swap_halves(gnumer * numer * inverse)
                both = jnp.where(masks[a], gnumer, -other).astype(bf)
                gext[a, rows, :] = both
                gfeat = jnp.dot(both, moment, preferred_element_type=f32)
                value = feature_back(a, gfeat, feats, query)
                out = value if a == 0 else jnp.where(in_first, out, value)
            dq[rows, :] = out
            stack_heads(gstack, chunk, grad, masks)
            stack_heads(qstack, chunk, query * (HEAD ** -0.5), masks)

        for a in range(2):
            gt[a] = contract(gext[a], qfeat[pair, :, a * feat : (a + 1) * feat], 0, 0).astype(bf)

        @pl.loop(0, n_chunks)
        def _(chunk):
            rows = pl.ds(pl.multiple_of(chunk * ROWS, ROWS), ROWS)
            key = qkv[1, rows, cols].astype(f32)
            value_f = qkv[2, rows, cols].astype(f32)
            dk_out, dv_out = None, None
            for a in range(2):
                extended = jnp.where(masks[a], value_f, 1.0).astype(bf)
                feats = kfeat[pair, rows, a * feat : (a + 1) * feat]
                gfeat = jnp.dot(extended, gt[a], preferred_element_type=f32)
                dk_one = feature_back(a, gfeat, feats, key)
                dv_one = contract(feats, gt[a], 1, 1)
                dk_out = dk_one if a == 0 else jnp.where(in_first, dk_out, dk_one)
                dv_out = dv_one if a == 0 else jnp.where(in_first, dv_out, dv_one)
            dk[rows, :] = dk_out
            dv[rows, :] = dv_out

        if pair == 0:
            loads[4].wait()

        @pl.loop(0, seq // BLOCK, unroll=SPARSE_UNROLL)
        def _(block):
            rows = pl.ds(pl.multiple_of(block * BLOCK, BLOCK), BLOCK)
            starts = listed_starts(blocks_ref, pair, block, seq // BLOCK)
            keys = pick_rows(qkv, 1, cols, starts, in_first)
            values = pick_rows(qkv, 2, cols, starts, in_first)
            weights = probs[pair, block]
            weights_f = weights.astype(f32)
            grad = gstack[block]
            gweights = contract(values, grad, 1, 1)
            inner = jnp.sum(weights_f * gweights, axis=0, keepdims=True)
            gscores = (weights_f * (gweights - inner)).astype(bf)
            both = contract(gscores, keys, 0, 0)
            out = jnp.where(in_first, both[:BLOCK], both[BLOCK:]) * (HEAD ** -0.5)
            dkeys = jnp.dot(gscores, qstack[block], preferred_element_type=f32)
            dvalues = jnp.dot(weights, grad, preferred_element_type=f32)
            for total, part in ((dk, dkeys), (dv, dvalues)):
                total[0:BLOCK, :] += part[:BLOCK]
                for slot, (one, two) in enumerate(starts):
                    piece = part[(slot + 1) * BLOCK : (slot + 2) * BLOCK]
                    total[pl.ds(one, BLOCK), :] += jnp.where(in_first, piece, 0.0)
                    total[pl.ds(two, BLOCK), :] += jnp.where(in_first, 0.0, piece)
            dq[rows, :] += out

        @pl.loop(0, n_chunks)
        def _(chunk):
            rows = pl.ds(pl.multiple_of(chunk * ROWS, ROWS), ROWS)
            for part, total in enumerate((dq, dk, dv)):
                low = total[rows, :].astype(bf)
                dqkv_ref[part, rows, cols] = low
                bias_ref[part, :, cols] += fold_rows(low.astype(f32))


    @pl.loop(0, n_chunks)
    def _(chunk):
        rows = pl.ds(pl.multiple_of(chunk * ROWS, ROWS), ROWS)
        total = None
        for part in range(3):
            term = contract(dqkv_ref[part, rows, :], qkv_weight(pack, n_heads, width, part), 1, 1)
            total = term if total is None else total + term
        low = total.astype(bf)
        out_ref[rows, :] = low
        zhat, _ = norm_stats(x_ref[rows, :].astype(f32))
        total = low.astype(f32)
        first_ref[0] += fold_rows(total * zhat)
        first_ref[1] += fold_rows(total)


def attn_backward(layer_no, n_heads, blocks, gy, part_a, part_b, hidden, x, kept, pack_c):
    seq, width = gy.shape
    part_width, feat = n_heads * HEAD, pack_c[0].shape[1]
    pairs = n_heads // 2
    shape = jax.ShapeDtypeStruct
    operands = [gy, part_a, part_b, hidden, x, *kept, *pack_c]
    return pl.pallas_call(
        functools.partial(attn_backward_kernel, layer_no, n_heads),
        out_shape=[
            shape((seq, width), bf),
            shape((seq, width), bf),
            shape((3, seq, part_width), bf),
            shape((2, 8, width), f32),
            shape((4, 8, width), f32),
            shape((3, 8, part_width), f32),
        ],
        in_specs=[SCALARS] + [WHOLE] * 5 + [ANY] * 9,
        out_specs=[WHOLE] * 6,
        scratch_shapes=[
            pltpu.VMEM(pack_c[0].shape, bf),
            pltpu.VMEM((3, seq, part_width), bf),
            pltpu.VMEM((pairs, seq // BLOCK, 4 * BLOCK, 2 * HEAD), bf),
            pltpu.VMEM((pairs, seq, 2 * feat), bf),
            pltpu.VMEM((pairs, seq, 2 * feat), bf),
            pltpu.VMEM((n_heads, 2 * HEAD, feat), bf),
            pltpu.VMEM((seq, part_width), bf),
            pltpu.VMEM((seq // BLOCK, 2 * BLOCK, 2 * HEAD), bf),
            pltpu.VMEM((seq // BLOCK, 2 * BLOCK, 2 * HEAD), bf),
            pltpu.VMEM((2, seq, 2 * HEAD), bf),
            pltpu.VMEM((2, 2 * HEAD, feat), bf),
            pltpu.VMEM((2, 4 * HEAD, feat), bf),
            pltpu.VMEM((seq, 2 * HEAD), f32),
            pltpu.VMEM((seq, 2 * HEAD), f32),
            pltpu.VMEM((seq, 2 * HEAD), f32),
            pltpu.SemaphoreType.DMA((7,)),
        ],
        compiler_params=pltpu.CompilerParams(vmem_limit_bytes=46 * MIB),
        cost_estimate=SHORT,
        name=f"attn_backward_{layer_no}",
    )(blocks, *operands)


def norm_backward_kernel(layer_no, x_ref, part_a, part_b, ghidden_ref, *refs):
    small_c = refs[:4]
    low_ref, small, sems = refs[4:]

    @pl.when(pl.program_id(0) == 0)
    def _():
        start_pick(pick_source(layer_no), small_part(small_c), small, sems.at[0])
        wait_pick(small_part(small_c), small, sems.at[0])

    width = x_ref.shape[1]
    gnormed = part_a[...].astype(f32) + part_b[...].astype(f32)
    zhat, scale = norm_stats(x_ref[...].astype(f32))
    scaled = gnormed * (1.0 + vector_row(small, 0, width))
    mean_one = jnp.mean(scaled, axis=-1, keepdims=True)
    mean_two = jnp.mean(scaled * zhat, axis=-1, keepdims=True)
    total = ghidden_ref[...].astype(f32) + (scaled - mean_one - zhat * mean_two) * scale
    low_ref[...] = total.astype(bf)


def norm_backward(layer_no, x, part_a, part_b, ghidden, small_c):
    seq, width = x.shape
    shape = jax.ShapeDtypeStruct
    rows = pl.BlockSpec((FFN_ROWS, width), lambda i: (i, 0))
    return pl.pallas_call(
        functools.partial(norm_backward_kernel, layer_no),
        grid=(seq // FFN_ROWS,),
        out_shape=shape((seq, width), bf),
        in_specs=[rows] * 4 + [ANY] * 4,
        out_specs=rows,
        scratch_shapes=[pltpu.VMEM((PACK_ROWS, small_c[0].shape[1]), bf), pltpu.SemaphoreType.DMA((1,))],
        compiler_params=pltpu.CompilerParams(vmem_limit_bytes=(60, 12)[layer_no] * MIB),
        cost_estimate=SHORT,
        name=f"norm_backward_{layer_no}",
    )(x, part_a, part_b, ghidden, *small_c)


def tiny_rows(first, moved, vec, bias_qkv, bias_up):
    half = vec.shape[2] // 2
    here = pl.ds(pl.multiple_of(lax.rem(lax.axis_index("dp"), 2) * half, half), half)
    total = lambda value: jnp.sum(value, axis=0, keepdims=True)
    rows = [total(first[i, :, here] + moved[i, :, here]) for i in range(2)]
    rows += [total(vec[i, :, here]) for i in range(4)]
    rows += [total(bias_qkv[i]) for i in range(3)] + [total(bias_up[...])]
    return [row[:, at : at + LANES] for row in rows for at in range(0, row.shape[1], LANES)]


def weight_grad_kernel(n_first, n_extra, left_a, left_b, right_a, right_b, *refs):
    keep_ref, away_ref, turned = refs[-3:]
    extra, sums = refs[:n_extra], refs[n_extra:-3]
    step = pl.program_id(0)
    shard = left_a.shape[1] // lax.axis_size("dp")
    per_half = pl.num_programs(0) // 2
    width = right_a.shape[1]
    n_rows = left_a.shape[1]
    first = step < n_first

    @pl.when(step == 0)
    def _():
        turned[...] = left_a[...].T
        for source, target in zip(extra, (keep_ref, away_ref)):
            target[:, per_half * width :] = source[...]
        if sums:
            rows = tiny_rows(*sums[:5]) + tiny_rows(*sums[5:])
            low = jnp.concatenate(rows, axis=0).astype(bf)
            low = jnp.concatenate([low, jnp.zeros((shard - low.shape[0], LANES), bf)], axis=0)
            for target in (keep_ref, away_ref):
                for at in range(0, n_rows, shard):
                    target[at : at + shard, per_half * width :] = low

    @pl.when(step == n_first)
    def _():
        turned[...] = left_b[...].T

    right = jnp.where(first, right_a[...], right_b[...])
    result = jnp.dot(turned[...], right, preferred_element_type=f32).astype(bf)
    here = pl.ds(pl.multiple_of(lax.rem(step, per_half) * width, width), width)
    keep = step // per_half == lax.axis_index("section")
    for wanted, target in ((keep, keep_ref), (jnp.logical_not(keep), away_ref)):

        @pl.when(wanted)
        def _():
            target[:n_rows, here] = result


def weight_grads(name, step, left_a, right_a, left_b, right_b, extra=(), sums=()):
    seq, width = left_a.shape
    if right_a.ndim == 3:
        n_first = right_a.shape[0]
        spec_a = pl.BlockSpec((None, seq, step), lambda i: (jnp.minimum(i, n_first - 1), 0, 0))
    else:
        n_first = right_a.shape[1] // step
        spec_a = pl.BlockSpec((seq, step), lambda i: (0, jnp.minimum(i, n_first - 1)))
    n_second = right_b.shape[1] // step
    spec_b = pl.BlockSpec((seq, step), lambda i: (0, jnp.maximum(i - n_first, 0)))
    whole = pl.BlockSpec((seq, width), lambda i: (0, 0))
    n_steps = n_first + n_second
    cols = step * (n_steps // 2) + (extra[0].shape[1] if extra else 0)
    shape = (width, cols + (LANES if sums else 0))
    fixed = lambda shape: pl.BlockSpec(shape, lambda i: (0,) * len(shape))
    return pl.pallas_call(
        functools.partial(weight_grad_kernel, n_first, len(extra)),
        grid=(n_steps,),
        out_shape=[jax.ShapeDtypeStruct(shape, bf)] * 2,
        in_specs=[whole, whole, spec_a, spec_b] + [fixed(item.shape) for item in (*extra, *sums)],
        out_specs=[fixed(shape)] * 2,
        scratch_shapes=[pltpu.VMEM((width, seq), bf)],
        compiler_params=pltpu.CompilerParams(vmem_limit_bytes=20 * MIB),
        cost_estimate=SHORT,
        name=name,
    )(left_a, left_b, right_a, right_b, *extra, *sums)


ALL_AXES = ("section", "tensor", "dp")


def send(value, sizes, target):
    n_section, n_tensor, n_dp = sizes
    pairs = []
    for s in range(n_section):
        for t in range(n_tensor):
            for d in range(n_dp):
                goal = target(s, t, d // 2, d % 2)
                if goal is not None:
                    gs, gt, gz, gc = goal
                    number = (s * n_tensor + t) * n_dp + d
                    pairs.append((number, (gs * n_tensor + gt) * n_dp + 2 * gz + gc))
    return lax.ppermute(value, ALL_AXES, pairs)


def other_core(value, sizes):
    return send(value, sizes, lambda s, t, z, c: (s, t, z, 1 - c))


def chip_shards(
    sizes,
    inputs,
    cotangent,
    lengths,
    blocks,
    feature_map,
    w_qkv,
    b_qkv,
    w_out,
    w_up,
    b_up,
    w_down,
    vector_params,
):
    n_dp = sizes[2]
    n_z = n_dp // 2
    section_no = lax.axis_index("section")
    tensor_no = lax.axis_index("tensor")
    dp_no = lax.axis_index("dp")
    z_no, core = dp_no // 2, dp_no % 2
    same = core == tensor_no
    is_first = section_no == 0
    width = inputs.shape[2]
    half = inputs.shape[1]
    n_heads, n_blocks, n_listed = blocks.shape[1:]
    feat = feature_map.shape[3]
    part_width = w_qkv.shape[3]

    def after(value, earlier):
        return lax.optimization_barrier((value, earlier))[0]

    def share_y(array):
        return send(array, sizes, lambda s, t, z, c: (1 - s, t, z, c) if c == t else None)

    def share_x(array):
        return send(array, sizes, lambda s, t, z, c: (s, 1 - t, z, c) if c == t else None)

    wide = jnp.concatenate(
        [w_up[0], jnp.concatenate([w_down[0][:width], w_down[0][width:]], axis=1)], axis=0
    )
    def halves(own, first, second):
        near = jnp.where(same, own, first)
        far = jnp.where(same, first, second)
        swap = tensor_no == 1
        return jnp.concatenate(
            [jnp.where(swap, far, near), jnp.where(swap, near, far)], axis=0
        )

    def cross(own):
        return send(
            own,
            sizes,
            lambda s, t, z, c: (s, t, z, 1 - c) if c == t else (s, 1 - t, z, c),
        )

    def to_sequence(own, first):
        second = send(first, sizes, lambda s, t, z, c: (s, t, z, 1 - c) if c == t else None)
        return halves(own, first, second)

    x_own = inputs[section_no]
    x_arrived = cross(x_own)
    pack = pack_weights(
        after(w_qkv[0].transpose(1, 0, 2), x_own),
        w_out[0],
        feature_map[0].reshape(n_heads * HEAD, feat),
        b_qkv[0],
        b_up,
        vector_params[0],
        blocks[0].reshape(n_heads * n_blocks, n_listed),
    )
    x_first = to_sequence(x_own, x_arrived)
    pack_y = share_y(pack)
    pack_x = share_x(pack)
    pack_both = share_x(after(pack_y, pack_x))
    pack_c = (pack, pack_y, pack_x, pack_both)
    wide_y = share_y(after(wide, pack_y))

    def share_wide(layer_no, earlier):
        def share(array, section):
            return send(
                after(array, earlier),
                sizes,
                lambda s, t, z, c: (s, 1 - t, z, c) if c == t and s == section else None,
            )

        return (wide, wide_y, share(wide, layer_no), share(wide_y, 1 - layer_no))

    lengths_here = jnp.where(same, lengths, other_core(lengths, sizes))
    length = lax.dynamic_slice_in_dim(lengths_here[:, 0], section_no, 1)

    weights = [(pack_c, share_wide(0, pack_both))]

    def of_layer(layer_no, candidates):
        mine = section_no == layer_no
        return jnp.where(
            same,
            jnp.where(mine, candidates[0], candidates[1]),
            jnp.where(mine, candidates[2], candidates[3]),
        )

    def exchange(value):
        return value, other_core(value, sizes)

    kept = []
    x_parts = (x_first,)
    outputs = []
    for layer_no in range(2):
        listed = of_layer(
            layer_no,
            [item[PACK_ROWS : PACK_ROWS + n_heads * n_blocks, :n_listed] for item in pack_c],
        )
        listed = listed.astype(jnp.int32)
        made = attn_forward(layer_no, n_heads, length, listed, x_parts, pack_c, pack_c)
        if layer_no == 0:
            x = x_first
        else:
            x, made = made[0], made[1:]
            outputs.append(x)
        branch, qkv, normed, probs, qfeat, kfeat, mt, mixed = made
        if layer_no == 0:
            grad_own = after(cotangent[section_no], (weights[0][1][2:], branch))
            grad_arrived = cross(grad_own)
            weights.append((pack_c, share_wide(1, (weights[0][1][2:], branch))))
        result, hidden, normed_two, active, slope = ffn_forward(
            layer_no, x, *exchange(branch), weights[layer_no]
        )
        x_parts = (hidden, *exchange(result))
        kept.append(
            (x, normed, mixed, hidden, normed_two, active, slope, listed,
             (qkv, probs, qfeat, kfeat, mt))
        )

    grad = to_sequence(grad_own, grad_arrived)

    def my_half(array):
        return lax.dynamic_slice_in_dim(array, core * half, half)

    def deliver(first_rows, second_rows):
        mine = jnp.where(is_first, first_rows, second_rows)
        theirs = jnp.where(is_first, second_rows, first_rows)
        own = send(mine, sizes, lambda s, t, z, c: (s, c, z, t))
        other = send(theirs, sizes, lambda s, t, z, c: (1 - s, c, z, t))
        return own, other

    hidden, part_a, part_b = x_parts
    last_bias = of_layer(1, [lane[18:20].reshape(1, width) for lane in pack_c]).astype(f32)
    last = my_half(hidden) + (my_half(part_a).astype(f32) + my_half(part_b).astype(f32)) + last_bias

    def plane_send(keep, away, hold=None):
        by_x = send(keep, sizes, lambda s, t, z, c: None if c == t else (s, 1 - t, z, c))
        by_y = share_y(away)
        late = away if hold is None else after(away, hold)
        by_both = send(late, sizes, lambda s, t, z, c: None if c == t else (1 - s, 1 - t, z, c))
        return keep, by_x, by_y, by_both

    def plane_sum(terms):
        total = terms[0].astype(f32)
        for term in terms[1:]:
            total = total + term.astype(f32)
        return total.astype(bf)

    def line_send(arrays):
        def shard_for(step):
            at = ((z_no + step) % n_z) * pair
            rows = [lax.dynamic_slice_in_dim(array, at, pair) for array in arrays]
            return jnp.concatenate(rows, axis=1)

        def turn(step):
            return lambda s, t, z, c: (s, t, (z + step) % n_z, c) if c == t else None

        return [shard_for(0)] + [
            send(shard_for(step), sizes, turn(step)) for step in range(1, n_z)
        ]

    def line_sum(found):
        total = found[0].astype(f32)
        for part in found[1:]:
            total = total + part.astype(f32)
        return total

    def ffn_part(layer_no, grad, hold):
        normed_two, active, slope = kept[layer_no][4:7]
        gnormed_two, gupper, bias_up = ffn_backward(
            layer_no, after(grad, hold), slope, (weights[layer_no][1],)
        )
        parts = exchange(gnormed_two)
        return parts, gupper, bias_up

    def ffn_grads(layer_no, grad, gupper, hold, extra=()):
        normed_two, active = kept[layer_no][4:6]
        return weight_grads(
            f"ffn_grads_{layer_no}", 512, after(normed_two, hold), gupper, grad, active, extra
        )

    def attn_part(layer_no, grad, parts, hold):
        hidden, listed, attn_kept = kept[layer_no][3], kept[layer_no][7], kept[layer_no][8]
        gnormed, *rest = attn_backward(
            layer_no, n_heads, listed, grad, after(parts[0], hold), parts[1], hidden,
            kept[layer_no][0], attn_kept, pack_c,
        )
        gbranch, gproj, vec_one, vec_two, bias_qkv = rest
        sums = (vec_one, other_core(vec_one, sizes), vec_two, bias_qkv)
        return exchange(gnormed), gbranch, gproj, sums

    def attn_grads(layer_no, gproj, gbranch, hold, sums=()):
        normed, mixed = kept[layer_no][1:3]
        return weight_grads(
            f"attn_grads_{layer_no}", part_width, after(normed, hold), gproj, gbranch, mixed, (), sums
        )

    def norm_part(layer_no, parts, gbranch, hold):
        return norm_backward(
            layer_no, kept[layer_no][0], after(parts[0], hold), parts[1], gbranch, pack_c
        )

    shard, pair = width // n_dp, width // n_z
    units = wide.shape[1]
    parts, gupper, bias_up = ffn_part(1, grad, x_parts[0])
    keep, away = ffn_grads(1, grad, gupper, parts[0])
    parts, gbranch, gproj, sums = attn_part(1, grad, parts, (keep, x_parts))
    wide_one = plane_send(keep, away, gbranch)
    sums_one = (*sums, bias_up)
    extra = attn_grads(1, gproj, gbranch, parts[0])
    grad = norm_part(1, parts, gbranch, extra[0])
    upper_grad = grad
    parts, gupper, bias_up = ffn_part(0, grad, grad)
    keep, away = ffn_grads(0, grad, gupper, parts[0], extra)
    keep, away, wide_one = after((keep, away, wide_one), keep)
    wide_zero = plane_send(keep, away)
    parts, gbranch, gproj, sums = attn_part(0, grad, parts, (keep, wide_one))
    wide_zero, wide_one = after((wide_zero, wide_one), gbranch)
    keep, away = attn_grads(
        0, gproj, gbranch, parts[0], (*sums_one, *sums, bias_up)
    )
    keep, away, wide_zero, wide_one = after((keep, away, wide_zero, wide_one), keep)
    keep, away, parts = after((keep, away, parts), (wide_zero, parts))
    out_pair = deliver(*after((my_half(outputs[0]), last.astype(bf)), wide_zero))
    keep, away = after((keep, away), out_pair)
    narrow_zero = plane_send(keep, away)
    line_wide = line_send([plane_sum(wide_one), plane_sum(wide_zero)])
    grad = norm_part(0, parts, gbranch, keep)
    line_narrow = line_send([after(plane_sum(narrow_zero), line_wide)])
    grad_pair = deliver(*after((my_half(grad), my_half(upper_grad)), line_narrow[0]))
    line_narrow = line_sum(after(line_narrow, grad_pair))
    line_wide = line_sum(line_wide)
    n_narrow = line_narrow.shape[1] - LANES
    rest = line_narrow[:, n_narrow:]
    first_sum = jnp.concatenate([line_wide[:, units : 2 * units], line_narrow], axis=1)
    second_sum = jnp.concatenate([line_wide[:, :units], line_wide[:, 2 * units :], rest], axis=1)

    def for_core(layer, number):
        return lax.dynamic_slice_in_dim(layer, number * shard, shard)

    mine = jnp.where(is_first, first_sum, second_sum)
    theirs = jnp.where(is_first, second_sum, first_sum)

    def cast(value, target):
        return send(
            value.astype(bf), sizes, lambda s, t, z, c: target(s, t, z) if c == t else None
        ).astype(f32)

    near = cast(for_core(mine, 1 - core), lambda s, t, z: (s, t, z, 1 - t))
    far = cast(for_core(theirs, core), lambda s, t, z: (1 - s, t, z, t))
    cross_far = cast(for_core(theirs, 1 - core), lambda s, t, z: (1 - s, t, z, 1 - t))
    stay = jnp.where(same, for_core(mine, core), near)
    arrived = jnp.where(same, far, cross_far)
    low_half = jnp.where(is_first, stay, arrived)
    high_half = jnp.where(is_first, arrived, stay)
    grad_up, grad_down = low_half[:, :units], high_half[:, :units]
    narrow = jnp.concatenate(
        [low_half[:, units : units + n_narrow], high_half[:, units : units + n_narrow]], axis=1
    )
    rows = stay[:, units + n_narrow :]
    n_rows = 9 * (width // 2 // LANES) + units // LANES
    rows = jnp.where(is_first, rows[n_rows : 2 * n_rows], rows[:n_rows])
    halves_found = rows[: n_rows - units // LANES].reshape(9, width // 2)

    def own_columns(array):
        cols = array.reshape(-1, n_dp, array.shape[1] // n_dp)
        return lax.dynamic_index_in_dim(cols, dp_no, axis=1, keepdims=False)

    grad_vectors = own_columns(halves_found[:6])
    grad_bqkv = own_columns(halves_found[6:])
    grad_bup = own_columns(rows[n_rows - units // LANES :].reshape(1, -1))[0]

    def placed(pair, dtype):
        own, other = pair
        return jnp.stack(
            [jnp.where(is_first, own, other), jnp.where(is_first, other, own)]
        )[None].astype(dtype)

    section_outputs = placed(out_pair, bf)
    input_grads = placed(grad_pair, f32)
    grad_qkv = narrow[:, : 3 * part_width].reshape(shard, 3, part_width)
    grad_out = narrow[:, 3 * part_width :].T
    return (
        section_outputs,
        input_grads,
        grad_qkv[None],
        grad_bqkv[None],
        grad_out[None],
        grad_up[None],
        grad_bup[None],
        grad_down.T[None],
        grad_vectors[None],
    )


HEAD = 64
BLOCK = 64
SEQ_LEN = 1024


norm_eps = 1e-05
bfloat = jnp.bfloat16
single = jnp.float32


def shifted(value, axis, steps):
    count = lax.axis_size(axis)
    first, last = (max(0, -steps), min(count, count - steps))
    return lax.ppermute(value, axis, [(source, source + steps) for source in range(first, last)])


def norm_rows(residual, gain_vec, shift_vec):
    row_mean = jnp.mean(residual, axis=-1, keepdims=True)
    centred = residual - row_mean
    variance = jnp.mean(centred * centred, axis=-1, keepdims=True)
    return centred * lax.rsqrt(variance + norm_eps) * (1.0 + gain_vec) + shift_vec


def gelu_exact(pre_active):
    return jax.nn.gelu(pre_active, approximate=False)


def select_tree(flag_value, when_true, when_false):
    return jax.tree.map(
        lambda left_arr, right_arr: jnp.where(flag_value, left_arr, right_arr),
        when_true,
        when_false,
    )


def split_pieces(operand):
    if operand.dtype == bfloat:
        return (operand,)
    upper_part = operand.astype(bfloat)
    lower_part = (operand - upper_part.astype(single)).astype(bfloat)
    return (upper_part, lower_part)


def split_dot(form, left, right):
    left_pieces = split_pieces(left)
    right_pieces = split_pieces(right)
    total = None
    for left_no, left_piece in enumerate(left_pieces):
        for right_no, right_piece in enumerate(right_pieces):
            if left_no + right_no > 1:
                continue
            term = jnp.einsum(form, left_piece, right_piece, preferred_element_type=single)
            total = term if total is None else total + term
    return total


def sparse_layout(block_list, length):
    head_count, block_count = (block_list.shape[0], block_list.shape[1])
    chosen = jnp.concatenate(
        [jnp.zeros((head_count, block_count, 1), jnp.int32), block_list], axis=2
    )
    key_live = (jnp.arange(SEQ_LEN) < length).astype(single)
    picked_live = key_live.reshape(block_count, BLOCK)[chosen].reshape(head_count, block_count, -1)
    return (chosen, key_live, picked_live)


def pick_blocks(table_in, chosen):
    head_count, block_count = (chosen.shape[0], chosen.shape[1])
    blocks_in = table_in.reshape(head_count, block_count, BLOCK, table_in.shape[-1])
    taken_rows = jax.vmap(lambda one_table, index_rows: one_table[index_rows])(blocks_in, chosen)
    return taken_rows.reshape(head_count, block_count, -1, table_in.shape[-1])


def place_blocks(values_in, chosen):
    head_count, block_count, slot_count = chosen.shape
    parts_in = values_in.reshape(head_count, block_count, slot_count, BLOCK, values_in.shape[-1])
    zero_blocks = jnp.zeros((head_count, block_count, BLOCK, values_in.shape[-1]), single)
    placed = jax.vmap(lambda base_arr, index_rows, one_part: base_arr.at[index_rows].add(one_part))(
        zero_blocks, chosen, parts_in
    )
    return placed.reshape(head_count, SEQ_LEN, values_in.shape[-1])


def feature_of(vectors_low, features):
    feature_scale = HEAD ** (-0.25)
    vectors = vectors_low.astype(single)
    projected = split_dot("hld,hdf->hlf", vectors_low, features) * feature_scale
    return jnp.exp(
        projected
        - jnp.sum(vectors * vectors, axis=-1, keepdims=True) * (0.5 * feature_scale * feature_scale)
    )


def block_scores(query_blocks, picked_keys, picked_live):
    scores = jnp.einsum(
        "hnqd,hnkd->hnqk", query_blocks, picked_keys, preferred_element_type=single
    ) * HEAD ** (-0.5)
    return jnp.where(picked_live[:, :, None, :] > 0.5, scores, -1e30)


def attend_forward(queries, key_vecs, value_vecs, chosen, key_live, picked_live, features):
    head_count, block_count = (chosen.shape[0], chosen.shape[1])
    query_blocks = queries.reshape(head_count, block_count, BLOCK, HEAD)
    picked_keys = pick_blocks(key_vecs, chosen)
    picked_values = pick_blocks(value_vecs, chosen)
    scores = block_scores(query_blocks, picked_keys, picked_live)
    row_max = jnp.max(scores, axis=-1, keepdims=True)
    weights_raw = jnp.exp(scores - row_max) * picked_live[:, :, None, :]
    row_total = jnp.sum(weights_raw, axis=-1, keepdims=True)
    log_total = row_max + jnp.log(row_total)
    weights_low = (weights_raw / row_total).astype(bfloat)
    sparse_out = jnp.einsum(
        "hnqk,hnkd->hnqd", weights_low, picked_values, preferred_element_type=single
    )
    sparse_out = sparse_out.reshape(head_count, SEQ_LEN, HEAD)
    query_feats = feature_of(queries, features)
    key_feats = feature_of(key_vecs, features) * key_live[None, :, None]
    moments = split_dot("hlf,hld->hfd", key_feats, value_vecs)
    totals = jnp.sum(key_feats, axis=1)
    numerator = split_dot("hlf,hfd->hld", query_feats, moments)
    denominator = split_dot("hlf,hf->hl", query_feats, totals)
    perf_out = numerator / denominator[:, :, None]
    return (
        sparse_out + perf_out,
        (log_total, query_feats, key_feats, moments, totals, denominator, perf_out),
    )


def attend_backward(
    grad_heads, queries, key_vecs, value_vecs, chosen, picked_live, features, attn_keep
):
    log_total, query_feats, key_feats, moments, totals, denominator, perf_out = attn_keep
    head_count, block_count = (chosen.shape[0], chosen.shape[1])
    score_scale = HEAD ** (-0.5)
    query_blocks = queries.reshape(head_count, block_count, BLOCK, HEAD)
    grad_blocks = grad_heads.reshape(head_count, block_count, BLOCK, HEAD)
    picked_keys = pick_blocks(key_vecs, chosen)
    picked_values = pick_blocks(value_vecs, chosen)
    scores = block_scores(query_blocks, picked_keys, picked_live)
    weights_f = jnp.exp(scores - log_total) * picked_live[:, :, None, :]
    grad_weights = jnp.einsum(
        "hnqd,hnkd->hnqk", grad_blocks, picked_values, preferred_element_type=single
    )
    row_inner = jnp.sum(weights_f * grad_weights, axis=-1, keepdims=True)
    grad_scores = (weights_f * (grad_weights - row_inner)).astype(bfloat)
    grad_query = jnp.einsum(
        "hnqk,hnkd->hnqd", grad_scores, picked_keys, preferred_element_type=single
    )
    grad_query = grad_query.reshape(head_count, SEQ_LEN, HEAD) * score_scale
    grad_keys = place_blocks(
        jnp.einsum("hnqk,hnqd->hnkd", grad_scores, query_blocks, preferred_element_type=single)
        * score_scale,
        chosen,
    )
    grad_values = place_blocks(
        jnp.einsum(
            "hnqk,hnqd->hnkd", weights_f.astype(bfloat), grad_blocks, preferred_element_type=single
        ),
        chosen,
    )
    grad_float = grad_heads.astype(single)
    grad_numer = grad_float / denominator[:, :, None]
    grad_denom = -jnp.sum(grad_float * perf_out, axis=-1) / denominator
    grad_qfeat = (
        split_dot("hld,hfd->hlf", grad_numer, moments) + grad_denom[:, :, None] * totals[:, None, :]
    )
    grad_moments = split_dot("hlf,hld->hfd", query_feats, grad_numer)
    grad_totals = split_dot("hlf,hl->hf", query_feats, grad_denom)
    grad_kfeat = split_dot("hld,hfd->hlf", value_vecs, grad_moments) + grad_totals[:, None, :]
    grad_values = grad_values + split_dot("hlf,hfd->hld", key_feats, grad_moments)
    feature_scale = HEAD ** (-0.25)

    def feature_back(grad_feat, feats, vectors_low):
        grad_expo = grad_feat * feats
        direct = split_dot("hlf,hdf->hld", grad_expo, features) * feature_scale
        return direct - feature_scale * feature_scale * jnp.sum(
            grad_expo, axis=-1, keepdims=True
        ) * vectors_low.astype(single)

    grad_query = grad_query + feature_back(grad_qfeat, query_feats, queries)
    grad_keys = grad_keys + feature_back(grad_kfeat, key_feats, key_vecs)
    return (grad_query, grad_keys, grad_values)


def layer_forward(section_entry, length, layer_params, block_list, features):
    qkv_mat, qkv_bias, out_mat, up_mat, up_bias, down_mat, vectors = layer_params
    residual = section_entry.astype(single)
    normed = norm_rows(residual, vectors[0], vectors[1]).astype(bfloat)
    normed_all = lax.all_gather(normed, "tensor", axis=0, tiled=True)
    projected = (
        jnp.einsum("ld,dce->lce", normed_all, qkv_mat, preferred_element_type=single)
        + qkv_bias[None]
    )
    projected = projected.astype(bfloat)
    seq_len, part_width = (projected.shape[0], projected.shape[2])
    head_count = part_width // HEAD
    head_parts = projected.reshape(seq_len, 3, head_count, HEAD).transpose(1, 2, 0, 3)
    chosen, key_live, picked_live = sparse_layout(block_list, length)
    mixed_heads, attn_keep = attend_forward(
        head_parts[0], head_parts[1], head_parts[2], chosen, key_live, picked_live, features
    )
    mixed_low = mixed_heads.transpose(1, 0, 2).reshape(seq_len, part_width).astype(bfloat)
    row_block = mixed_low
    branch = lax.psum_scatter(
        jnp.dot(row_block, out_mat, preferred_element_type=single).astype(jnp.bfloat16),
        "tensor",
        scatter_dimension=0,
        tiled=True,
    ).astype(jnp.float32)
    hidden_res = residual + branch + vectors[4]
    normed_two = norm_rows(hidden_res, vectors[2], vectors[3]).astype(bfloat)
    normed_two_all = lax.all_gather(normed_two, "tensor", axis=0, tiled=True)
    pre_active = jnp.dot(normed_two_all, up_mat, preferred_element_type=single) + up_bias
    active = gelu_exact(pre_active).astype(bfloat)
    row_block = active
    result = (
        hidden_res
        + lax.psum_scatter(
            jnp.dot(row_block, down_mat, preferred_element_type=single).astype(jnp.bfloat16),
            "tensor",
            scatter_dimension=0,
            tiled=True,
        ).astype(jnp.float32)
        + vectors[5]
    )
    record = (
        residual,
        hidden_res,
        normed_all,
        head_parts,
        mixed_low,
        normed_two_all,
        pre_active,
        active,
        attn_keep,
        length,
    )
    return (result.astype(bfloat), record)


def layer_backward(grad_low, record, layer_params, block_list, features):
    qkv_mat, qkv_bias, out_mat, up_mat, up_bias, down_mat, vectors = layer_params
    (
        residual,
        hidden_res,
        normed_all,
        head_parts,
        mixed_low,
        normed_two_all,
        pre_active,
        active,
        attn_keep,
        length,
    ) = record
    seq_len, part_width = mixed_low.shape
    head_count = part_width // HEAD
    grad_output = grad_low.astype(single)
    grad_all = lax.all_gather(grad_low, "tensor", axis=0, tiled=True)
    grad_wdown = jnp.einsum("lf,ld->fd", active, grad_all, preferred_element_type=single)
    grad_active = jnp.einsum("ld,fd->lf", grad_all, down_mat, preferred_element_type=single)
    _, gelu_pull = jax.vjp(gelu_exact, pre_active)
    grad_upper = gelu_pull(grad_active)[0].astype(bfloat)
    grad_wup = jnp.einsum("ld,lf->df", normed_two_all, grad_upper, preferred_element_type=single)
    grad_bup = jnp.sum(grad_upper.astype(single), axis=0)
    row_block = grad_upper
    grad_normed_two = lax.psum_scatter(
        jnp.einsum("lf,df->ld", row_block, up_mat, preferred_element_type=single).astype(
            jnp.bfloat16
        ),
        "tensor",
        scatter_dimension=0,
        tiled=True,
    ).astype(jnp.float32)
    _, pull_two = jax.vjp(norm_rows, hidden_res, vectors[2], vectors[3])
    grad_hidden, grad_gain_two, grad_shift_two = pull_two(grad_normed_two)
    grad_hidden = grad_hidden + grad_output
    grad_hidden_low = grad_hidden.astype(bfloat)
    hidden_all = lax.all_gather(grad_hidden_low, "tensor", axis=0, tiled=True)
    grad_wout = jnp.einsum("le,ld->ed", mixed_low, hidden_all, preferred_element_type=single)
    grad_mixed = jnp.einsum("ld,ed->le", hidden_all, out_mat, preferred_element_type=single).astype(
        bfloat
    )
    grad_heads = grad_mixed.reshape(seq_len, head_count, HEAD).transpose(1, 0, 2)
    chosen, key_live, picked_live = sparse_layout(block_list, length)
    grad_query, grad_keys, grad_values = attend_backward(
        grad_heads,
        head_parts[0],
        head_parts[1],
        head_parts[2],
        chosen,
        picked_live,
        features,
        attn_keep,
    )
    grad_proj = (
        jnp.stack([grad_query, grad_keys, grad_values])
        .transpose(2, 0, 1, 3)
        .reshape(seq_len, 3, part_width)
        .astype(bfloat)
    )
    grad_wqkv = jnp.einsum("ld,lce->dce", normed_all, grad_proj, preferred_element_type=single)
    grad_bqkv = jnp.sum(grad_proj.astype(single), axis=0)
    row_block = grad_proj
    grad_normed = lax.psum_scatter(
        jnp.einsum("lce,dce->ld", row_block, qkv_mat, preferred_element_type=single).astype(
            jnp.bfloat16
        ),
        "tensor",
        scatter_dimension=0,
        tiled=True,
    ).astype(jnp.float32)
    _, pull_one = jax.vjp(norm_rows, residual, vectors[0], vectors[1])
    grad_resid, grad_gain_one, grad_shift_one = pull_one(grad_normed)
    grad_resid = grad_resid + grad_hidden
    weight_grads = (grad_wqkv, grad_bqkv, grad_wout, grad_wup, grad_bup, grad_wdown)
    vector_grads = jnp.stack(
        [
            grad_gain_one,
            grad_shift_one,
            grad_gain_two,
            grad_shift_two,
            jnp.sum(grad_hidden_low.astype(single), axis=0),
            jnp.sum(grad_output, axis=0),
        ]
    )
    return (grad_resid, weight_grads, vector_grads)


def shards(
    inputs,
    cotangent,
    lengths,
    blocks,
    feature_map,
    w_qkv,
    b_qkv,
    w_out,
    w_up,
    b_up,
    w_down,
    vector_params,
):
    section_no = lax.axis_index("section")
    is_first = section_no == 0
    is_last = section_no == lax.axis_size("section") - 1
    layer_params = (
        w_qkv[0],
        b_qkv[0].astype(single),
        w_out[0],
        w_up[0],
        b_up[0].astype(single),
        w_down[0],
        vector_params[0].astype(single),
    )
    block_list = blocks[0]
    features = feature_map[0]
    batch_count = inputs.shape[0]
    carried = jnp.zeros_like(inputs[0])
    records = []
    results = []
    for tick_no in range(batch_count + 1):
        batch_no = jnp.clip(tick_no - section_no, 0, batch_count - 1)
        section_entry = jnp.where(is_first, inputs[min(tick_no, batch_count - 1)], carried)
        result, record = layer_forward(
            section_entry, lengths[batch_no, 0], layer_params, block_list, features
        )
        records.append(record)
        results.append(result)
        if tick_no < batch_count:
            carried = shifted(result, "section", 1)
    section_outputs = jnp.stack(
        [
            jnp.where(is_first, results[batch_idx], results[batch_idx + 1])
            for batch_idx in range(batch_count)
        ]
    )[None]
    received = jnp.zeros_like(cotangent[0])
    grad_list = []
    local_sum = None
    vector_total = jnp.zeros((6, inputs.shape[2]), single)
    for tick_no in range(batch_count + 1):
        record = select_tree(
            is_last, records[min(tick_no + 1, batch_count)], records[max(tick_no - 1, 0)]
        )
        valid_flag = jnp.where(is_last, float(tick_no < batch_count), float(tick_no >= 1)).astype(
            single
        )
        grad_entry = jnp.where(is_last, cotangent[min(tick_no, batch_count - 1)], received)
        grad_resid, weight_grads, vector_grads = layer_backward(
            grad_entry, record, layer_params, block_list, features
        )
        weight_grads = tuple((valid_flag * addend for addend in weight_grads))
        vector_total = vector_total + valid_flag * vector_grads
        local_sum = (
            weight_grads
            if local_sum is None
            else tuple((summed + addend for summed, addend in zip(local_sum, weight_grads)))
        )
        grad_list.append(grad_resid)
        if tick_no < batch_count:
            received = shifted(grad_resid.astype(bfloat), "section", -1)
    final_grads = (
        lax.psum_scatter(
            local_sum[0].astype(jnp.bfloat16), "dp", scatter_dimension=0, tiled=True
        ).astype(jnp.float32),
        lax.psum_scatter(
            local_sum[1].astype(jnp.bfloat16), "dp", scatter_dimension=1, tiled=True
        ).astype(jnp.float32),
        lax.psum_scatter(
            local_sum[2].astype(jnp.bfloat16), "dp", scatter_dimension=1, tiled=True
        ).astype(jnp.float32),
        lax.psum_scatter(
            local_sum[3].astype(jnp.bfloat16), "dp", scatter_dimension=0, tiled=True
        ).astype(jnp.float32),
        lax.psum_scatter(
            local_sum[4].astype(jnp.bfloat16), "dp", scatter_dimension=0, tiled=True
        ).astype(jnp.float32),
        lax.psum_scatter(
            local_sum[5].astype(jnp.bfloat16), "dp", scatter_dimension=1, tiled=True
        ).astype(jnp.float32),
    )
    input_grads = jnp.stack(
        [
            jnp.where(is_first, grad_list[batch_idx + 1], grad_list[batch_idx])
            for batch_idx in range(batch_count)
        ]
    )[None]
    grad_vectors = lax.psum_scatter(
        vector_total, ("tensor", "dp"), scatter_dimension=1, tiled=True
    )[None]
    grad_wqkv, grad_bqkv, grad_wout, grad_wup, grad_bup, grad_wdown = final_grads
    return (
        section_outputs,
        input_grads,
        grad_wqkv[None],
        grad_bqkv[None],
        grad_wout[None],
        grad_wup[None],
        grad_bup[None],
        grad_wdown[None],
        grad_vectors,
    )


def solution(mesh):
    placed = (
        P(None, ("dp", "tensor"), None),
        P(None, ("dp", "tensor"), None),
        P(None, "dp"),
        P("section", "tensor", None, None),
        P("section", "tensor", None, None),
        P("section", None, None, "tensor"),
        P("section", None, "tensor"),
        P("section", "tensor", None),
        P("section", None, "tensor"),
        P("section", "tensor"),
        P("section", "tensor", None),
        P("section", None, None),
    )
    sizes = tuple(mesh.shape[axis] for axis in ALL_AXES)
    if sizes[0] == 2 and sizes[1] == 2 and sizes[2] % 2 == 0:
        body = functools.partial(chip_shards, sizes)
    else:
        body = shards
    return jax.shard_map(
        body,
        mesh=mesh,
        in_specs=placed,
        out_specs=(
            P("section", None, ("dp", "tensor"), None),
            P("section", None, ("dp", "tensor"), None),
            P("section", "dp", None, "tensor"),
            P("section", None, ("tensor", "dp")),
            P("section", "tensor", "dp"),
            P("section", "dp", "tensor"),
            P("section", ("tensor", "dp")),
            P("section", "tensor", "dp"),
            P("section", None, ("tensor", "dp")),
        ),
        check_vma=False,
    )
```

```python
import functools

import jax
import jax.numpy as jnp
from jax import lax
from jax.experimental import pallas as pl
from jax.experimental.pallas import tpu as pltpu
from jax.sharding import PartitionSpec as P

HEAD = 64
BLOCK = 64
NORM_EPS = 1e-5
bf = jnp.bfloat16
f32 = jnp.float32
LOG2E = 1.4426950408889634
F_SCALE = HEAD ** -0.25
ROWS = 1024
FFN_ROWS = 256
SPARSE_UNROLL = 8
PACK_ROWS = 32
PACK_SMALL = 96
LANES = 128
N_QUARTERS = 4
MIB = 1024 * 1024
SHORT = pl.CostEstimate(flops=10**6, bytes_accessed=2**16, transcendentals=0)
ANY = pl.BlockSpec(memory_space=pl.ANY)
WHOLE = pl.BlockSpec(memory_space=pltpu.VMEM)
SCALARS = pl.BlockSpec(memory_space=pltpu.SMEM)


def contract(left, right, left_dim, right_dim):
    return lax.dot_general(
        left, right, (((left_dim,), (right_dim,)), ((), ())), preferred_element_type=f32
    )


def pick_source(layer_no):
    section_no = lax.axis_index("section")
    same = lax.rem(lax.axis_index("dp"), 2) == lax.axis_index("tensor")
    return jnp.where(section_no == layer_no, 0, 1) + jnp.where(same, 0, 2)


def start_pick(source, candidates, target, sem):
    for number, candidate in enumerate(candidates):

        @pl.when(source == number)
        def _():
            pltpu.make_async_copy(candidate, target, sem).start()


def wait_pick(candidates, target, sem):
    pltpu.make_async_copy(candidates[0], target, sem).wait()


def small_row(small, row, width):
    count = width // small.shape[1]
    rows = [small[row + i : row + i + 1, :].astype(f32) for i in range(count)]
    return jnp.concatenate(rows, axis=1)


def vector_row(small, number, width):
    return small_row(small, 8 + 2 * number, width)


def small_part(candidates):
    return [candidate.at[0:PACK_ROWS] for candidate in candidates]


def norm_stats(value):
    mean = jnp.mean(value, axis=-1, keepdims=True)
    centred = value - mean
    variance = jnp.mean(centred * centred, axis=-1, keepdims=True)
    scale = lax.rsqrt(variance + NORM_EPS)
    return centred * scale, scale


def lane_masks():
    lane = lax.broadcasted_iota(jnp.int32, (1, 2 * HEAD), 1)
    return lane < HEAD, lane >= HEAD


def swap_halves(value):
    return pltpu.roll(value, HEAD, 1)


def listed_starts(blocks_ref, pair, block, n_blocks):
    found = []
    for slot in range(3):
        two = []
        for a in range(2):
            listed = blocks_ref[(2 * pair + a) * n_blocks + block, slot]
            two.append(pl.multiple_of(listed * BLOCK, BLOCK))
        found.append(tuple(two))
    return found


def pick_rows(table, part, cols, starts, in_first):
    pieces = [table[part, 0:BLOCK, cols]]
    for one, two in starts:
        pieces.append(
            jnp.where(
                in_first,
                table[part, pl.ds(one, BLOCK), cols],
                table[part, pl.ds(two, BLOCK), cols],
            )
        )
    return jnp.concatenate(pieces, axis=0)


def stack_heads(target, chunk, value, masks):
    for number in range(ROWS // BLOCK):
        block = value[number * BLOCK : (number + 1) * BLOCK]
        for a in range(2):
            target[chunk * (ROWS // BLOCK) + number, a * BLOCK : (a + 1) * BLOCK] = jnp.where(
                masks[a], block, 0.0
            ).astype(bf)


def feature_rows(pack, n_heads, head):
    at = PACK_SMALL + head * HEAD
    return pack[at : at + HEAD].astype(f32) + pack[at + n_heads * HEAD : at + (n_heads + 1) * HEAD].astype(f32)


def qkv_weight(pack, n_heads, width, part):
    at = PACK_SMALL + 4 * n_heads * HEAD + part * width
    return pack[at : at + width]


def out_weights(pack, n_heads, part_width):
    at = PACK_SMALL + 2 * n_heads * HEAD
    return [pack[at + part * part_width : at + (part + 1) * part_width] for part in range(2)]


def pack_kernel(wqkv_ref, wout_ref, features_ref, bqkv_ref, bup_ref, vector_ref, blocks_ref, pack_ref):
    n_features, feat = features_ref.shape
    n_parts, width, part_width = wqkv_ref.shape

    def lane_rows(value):
        value = value.astype(f32)
        return [
            value[row : row + 1, at : at + feat]
            for row in range(value.shape[0])
            for at in range(0, value.shape[1], feat)
        ]

    blank = jnp.zeros((1, feat), f32)
    rows = lane_rows(bqkv_ref[...]) + [blank] + lane_rows(bup_ref[...]) + lane_rows(vector_ref[...])
    rows += [blank] * (PACK_ROWS - len(rows))
    pack_ref[0:PACK_ROWS] = jnp.concatenate(rows, axis=0).astype(bf)
    n_listed, n_slots = blocks_ref.shape
    pack_ref[PACK_ROWS:PACK_SMALL] = jnp.zeros((PACK_SMALL - PACK_ROWS, feat), bf)
    pack_ref[PACK_ROWS : PACK_ROWS + n_listed, 0:n_slots] = blocks_ref[...].astype(f32).astype(bf)
    at = PACK_SMALL
    features = features_ref[...]
    high = features.astype(bf)
    pack_ref[at : at + n_features] = high
    pack_ref[at + n_features : at + 2 * n_features] = (features - high.astype(f32)).astype(bf)
    at += 2 * n_features
    for part in range(2):
        pack_ref[at : at + part_width] = wout_ref[:, part * feat : (part + 1) * feat]
        at += part_width
    for part in range(n_parts):
        pack_ref[at : at + width] = wqkv_ref[part]
        at += width


def pack_weights(wqkv, wout, features, bqkv, bup, vectors, blocks):
    n_parts, width, part_width = wqkv.shape
    n_features, feat = features.shape
    n_rows = PACK_SMALL + 2 * n_features + 2 * part_width + n_parts * width
    return pl.pallas_call(
        pack_kernel,
        out_shape=jax.ShapeDtypeStruct((n_rows, feat), bf),
        in_specs=[WHOLE] * 7,
        out_specs=WHOLE,
        compiler_params=pltpu.CompilerParams(vmem_limit_bytes=16 * MIB),
        cost_estimate=SHORT,
        name="pack_weights",
    )(wqkv, wout, features, bqkv, bup, vectors, blocks)


def attn_forward_kernel(layer_no, n_heads, length_ref, blocks_ref, *refs):
    if layer_no == 0:
        x_ref, refs = refs[0], refs[1:]
    else:
        rows_in, refs = refs[:3], refs[3:]
        small_prev, refs = refs[:4], refs[4:]
    pack_c, refs = refs[:4], refs[4:]
    if layer_no == 1:
        x_ref, refs = refs[0], refs[1:]
    (branch_ref, qkv_out, normed_out, probs_out, qf_out, kf_out, mt_out, mixed_out) = refs[:8]
    (pack, qkv, normed, probs, qfeat, kfeat, mt, mixed, fcat, perf, qstack,
     in_sem, out_sem) = refs[8:21]
    seq, width = normed.shape
    n_chunks = seq // ROWS
    pairs = n_heads // 2
    part_width = qkv.shape[2]
    feat = pack.shape[1]
    small = pack.at[0:PACK_ROWS]
    source = pick_source(layer_no)
    if layer_no == 1:
        small_before, hidden_ref, part_a, part_b, row_sem = refs[21:]
        row_loads = [
            pltpu.make_async_copy(item, target, row_sem.at[number])
            for number, (item, target) in enumerate(zip(rows_in, (hidden_ref, part_a, part_b)))
        ]
        for load in row_loads:
            load.start()
        before = pick_source(0)
        start_pick(before, small_part(small_prev), small_before, in_sem.at[1])
    start_pick(source, pack_c, pack, in_sem.at[0])
    wait_pick(pack_c, pack, in_sem.at[0])
    if layer_no == 1:
        wait_pick(small_part(small_prev), small_before, in_sem.at[1])
        for load in row_loads:
            load.wait()
    length = length_ref[0]
    gain = 1.0 + vector_row(small, 0, width)
    shift = vector_row(small, 1, width)

    @pl.loop(0, n_chunks)
    def _(chunk):
        rows = pl.ds(pl.multiple_of(chunk * ROWS, ROWS), ROWS)
        if layer_no == 0:
            x = x_ref[rows, :].astype(f32)
        else:
            total = part_a[rows, :].astype(f32) + part_b[rows, :].astype(f32)
            x_low = (hidden_ref[rows, :].astype(f32) + total + vector_row(small_before, 5, width)).astype(bf)
            x_ref[rows, :] = x_low
            x = x_low.astype(f32)
        zhat, _ = norm_stats(x)
        low = (zhat * gain + shift).astype(bf)
        normed[rows, :] = low
        for part in range(3):
            cols = n_heads * HEAD
            out = jnp.dot(low, qkv_weight(pack, n_heads, width, part), preferred_element_type=f32)
            qkv[part, rows, :] = (out + small_row(small, part, cols)).astype(bf)

    copies = [
        pltpu.make_async_copy(qkv, qkv_out, out_sem.at[0]),
        pltpu.make_async_copy(normed, normed_out, out_sem.at[1]),
    ]
    for copy in copies:
        copy.start()
    in_first, in_second = lane_masks()
    masks = (in_first, in_second)
    key_row = lax.broadcasted_iota(jnp.int32, (BLOCK, 2 * HEAD), 0)
    for pair in range(pairs):
        cols = slice(pair * 2 * HEAD, (pair + 1) * 2 * HEAD)
        zero = jnp.zeros((HEAD, feat), bf)
        for a in range(2):
            scaled = feature_rows(pack, n_heads, 2 * pair + a) * (F_SCALE * LOG2E)
            high = scaled.astype(bf)
            rest = (scaled - high.astype(f32)).astype(bf)
            for part, piece in enumerate((high, rest)):
                row = part * 2 * HEAD + a * HEAD
                fcat[row : row + HEAD, a * feat : (a + 1) * feat] = piece
                fcat[row : row + HEAD, (1 - a) * feat : (2 - a) * feat] = zero

        def features(vectors):
            proj = jnp.dot(
                jnp.concatenate([vectors, vectors], axis=1), fcat[...], preferred_element_type=f32
            )
            value = vectors.astype(f32)
            square = value * value * (0.5 * F_SCALE * F_SCALE * LOG2E)
            return [
                jnp.exp2(
                    proj[:, a * feat : (a + 1) * feat]
                    - jnp.sum(jnp.where(masks[a], square, 0.0), axis=-1, keepdims=True)
                )
                for a in range(2)
            ]

        @pl.loop(0, n_chunks)
        def _(chunk):
            base = pl.multiple_of(chunk * ROWS, ROWS)
            rows = pl.ds(base, ROWS)
            live = lax.broadcasted_iota(jnp.int32, (ROWS, 1), 0) + base < length
            found = features(qkv[1, rows, cols])
            for a in range(2):
                kfeat[pair, rows, a * feat : (a + 1) * feat] = jnp.where(live, found[a], 0.0).astype(bf)

        values = qkv[2, :, cols].astype(f32)
        for a in range(2):
            extended = jnp.where(masks[a], values, 1.0).astype(bf)
            moment = contract(extended, kfeat[pair, :, a * feat : (a + 1) * feat], 0, 0)
            mt[2 * pair + a] = moment.astype(bf)

        @pl.loop(0, n_chunks)
        def _(chunk):
            rows = pl.ds(pl.multiple_of(chunk * ROWS, ROWS), ROWS)
            query = qkv[0, rows, cols]
            found = features(query)
            out = None
            for a in range(2):
                low = found[a].astype(bf)
                qfeat[pair, rows, a * feat : (a + 1) * feat] = low
                numer = contract(low, mt[2 * pair + a], 1, 1)
                value = numer / swap_halves(numer)
                out = value if a == 0 else jnp.where(in_first, out, value)
            perf[rows, :] = out
            stack_heads(qstack, chunk, query.astype(f32) * (HEAD ** -0.5), masks)

        @pl.loop(0, seq // BLOCK, unroll=SPARSE_UNROLL)
        def _(block):
            rows = pl.ds(pl.multiple_of(block * BLOCK, BLOCK), BLOCK)
            starts = listed_starts(blocks_ref, pair, block, seq // BLOCK)
            keys = pick_rows(qkv, 1, cols, starts, in_first)
            values = pick_rows(qkv, 2, cols, starts, in_first)
            scores = contract(keys, qstack[block], 1, 1)
            pieces = [scores[:BLOCK]]
            for slot, (one, two) in enumerate(starts):
                room = length - jnp.where(in_first, one, two)
                piece = scores[(slot + 1) * BLOCK : (slot + 2) * BLOCK]
                pieces.append(jnp.where(key_row < room, piece, -1e30))
            scores = jnp.concatenate(pieces, axis=0)
            raw = jnp.exp(scores - jnp.max(scores, axis=0, keepdims=True))
            low = (raw * (1.0 / jnp.sum(raw, axis=0, keepdims=True))).astype(bf)
            probs[pair, block] = low
            both = contract(low, values, 0, 0)
            out = jnp.where(in_first, both[:BLOCK], both[BLOCK:])
            mixed[rows, cols] = (out + perf[rows, :]).astype(bf)

        more = [
            pltpu.make_async_copy(probs.at[pair], probs_out.at[pair], out_sem.at[2 + 4 * pair]),
            pltpu.make_async_copy(qfeat.at[pair], qf_out.at[pair], out_sem.at[3 + 4 * pair]),
            pltpu.make_async_copy(kfeat.at[pair], kf_out.at[pair], out_sem.at[4 + 4 * pair]),
            pltpu.make_async_copy(mt.at[2 * pair : 2 * pair + 2], mt_out.at[2 * pair : 2 * pair + 2], out_sem.at[5 + 4 * pair]),
        ]
        for copy in more:
            copy.start()
        copies += more

    @pl.loop(0, n_chunks)
    def _(chunk):
        rows = pl.ds(pl.multiple_of(chunk * ROWS, ROWS), ROWS)
        low = mixed[rows, :]
        mixed_out[rows, :] = low
        for part, weight in enumerate(out_weights(pack, n_heads, part_width)):
            here = slice(part * feat, (part + 1) * feat)
            branch_ref[rows, here] = jnp.dot(low, weight, preferred_element_type=f32).astype(bf)

    for copy in copies:
        copy.wait()


def attn_forward(layer_no, n_heads, length, blocks, x_parts, pack_c, small_before):
    part_width, feat = n_heads * HEAD, pack_c[0].shape[1]
    seq, width = x_parts[0].shape
    pairs = n_heads // 2
    shape = jax.ShapeDtypeStruct
    outs = [
        shape((seq, width), bf),
        shape((3, seq, part_width), bf),
        shape((seq, width), bf),
        shape((pairs, seq // BLOCK, 4 * BLOCK, 2 * HEAD), bf),
        shape((pairs, seq, 2 * feat), bf),
        shape((pairs, seq, 2 * feat), bf),
        shape((n_heads, 2 * HEAD, feat), bf),
        shape((seq, part_width), bf),
    ]
    out_specs = [WHOLE, ANY, ANY, ANY, ANY, ANY, ANY, WHOLE]
    scratch = [
        pltpu.VMEM(pack_c[0].shape, bf),
        pltpu.VMEM((3, seq, part_width), bf),
        pltpu.VMEM((seq, width), bf),
        pltpu.VMEM((pairs, seq // BLOCK, 4 * BLOCK, 2 * HEAD), bf),
        pltpu.VMEM((pairs, seq, 2 * feat), bf),
        pltpu.VMEM((pairs, seq, 2 * feat), bf),
        pltpu.VMEM((n_heads, 2 * HEAD, feat), bf),
        pltpu.VMEM((seq, part_width), bf),
        pltpu.VMEM((4 * HEAD, 2 * feat), bf),
        pltpu.VMEM((seq, 2 * HEAD), f32),
        pltpu.VMEM((seq // BLOCK, 2 * BLOCK, 2 * HEAD), bf),
        pltpu.SemaphoreType.DMA((2,)),
        pltpu.SemaphoreType.DMA((2 + 4 * pairs,)),
    ]
    operands = list(x_parts)
    specs = [WHOLE if layer_no == 0 else ANY] * len(x_parts)
    if layer_no == 1:
        operands += list(small_before)
        specs += [ANY] * 4
        outs = [shape((seq, width), bf)] + outs
        out_specs = [WHOLE] + out_specs
        scratch.append(pltpu.VMEM((PACK_ROWS, feat), bf))
        scratch += [pltpu.VMEM((seq, width), bf)] * 3 + [pltpu.SemaphoreType.DMA((3,))]
    operands += list(pack_c)
    specs += [ANY] * 4
    return pl.pallas_call(
        functools.partial(attn_forward_kernel, layer_no, n_heads),
        out_shape=outs,
        in_specs=[SCALARS, SCALARS] + specs,
        out_specs=out_specs,
        scratch_shapes=scratch,
        compiler_params=pltpu.CompilerParams(vmem_limit_bytes=60 * MIB),
        cost_estimate=SHORT,
        name=f"attn_forward_{layer_no}",
    )(length, blocks, *operands)


def gelu_parts(value):
    inverse = 1.0 / (1.0 + (0.3275911 * 0.5 ** 0.5) * jnp.abs(value))
    bell = jnp.exp2(value * value * (-0.5 * LOG2E))
    poly = inverse * (
        0.127414796
        + inverse
        * (-0.142248368 + inverse * (0.7107068705 + inverse * (-0.7265760135 + inverse * 0.5307027145)))
    )
    tail = poly * bell
    below = jnp.where(value >= 0.0, 1.0 - tail, tail)
    return value * below, below + value * bell * (0.5 / 3.141592653589793) ** 0.5


def down_rows(wide, width, at, step):
    part, row = at // width, at % width
    return wide[width + row : width + row + step, part * width : (part + 1) * width]


def ffn_forward_kernel(layer_no, *refs):
    x_ref, part_a, part_b = refs[:3]
    small_c, wide_c = refs[3:7], refs[7:11]
    out_ref, hidden_ref, normed_ref, active_ref, slope_ref = refs[11:16]
    small, wide, sems = refs[16:]

    @pl.when(pl.program_id(0) == 0)
    def _():
        source = pick_source(layer_no)
        start_pick(source, small_part(small_c), small, sems.at[0])
        start_pick(source, wide_c, wide, sems.at[1])
        wait_pick(small_part(small_c), small, sems.at[0])
        wait_pick(wide_c, wide, sems.at[1])

    width = x_ref.shape[1]
    units = wide.shape[1]
    branch = part_a[...].astype(f32) + part_b[...].astype(f32)
    hidden = x_ref[...].astype(f32) + branch + vector_row(small, 4, width)
    hidden_ref[...] = hidden.astype(bf)
    zhat, _ = norm_stats(hidden)
    low = (zhat * (1.0 + vector_row(small, 2, width)) + vector_row(small, 3, width)).astype(bf)
    normed_ref[...] = low
    total = None
    step = 256
    for at in range(0, units, step):
        upper = jnp.dot(low, wide[:width, at : at + step], preferred_element_type=f32)
        active, slope = gelu_parts(upper + small_row(small, 4 + at // step, step))
        active = active.astype(bf)
        active_ref[:, at : at + step] = active
        slope_ref[:, at : at + step] = slope.astype(bf)
        term = jnp.dot(active, down_rows(wide, width, at, step), preferred_element_type=f32)
        total = term if total is None else total + term
    out_ref[...] = total.astype(bf)


def ffn_forward(layer_no, x, part_a, part_b, weights):
    small_c, wide_c = weights
    seq, width = x.shape
    units = wide_c[0].shape[1]
    shape = jax.ShapeDtypeStruct
    rows = lambda cols: pl.BlockSpec((FFN_ROWS, cols), lambda i: (i, 0))
    return pl.pallas_call(
        functools.partial(ffn_forward_kernel, layer_no),
        grid=(seq // FFN_ROWS,),
        out_shape=[
            shape((seq, width), bf),
            shape((seq, width), bf),
            shape((seq, width), bf),
            shape((seq, units), bf),
            shape((seq, units), bf),
        ],
        in_specs=[rows(width)] * 3 + [ANY] * 8,
        out_specs=[rows(width), rows(width), rows(width), rows(units), rows(units)],
        scratch_shapes=[
            pltpu.VMEM((PACK_ROWS, small_c[0].shape[1]), bf),
            pltpu.VMEM(wide_c[0].shape, bf),
            pltpu.SemaphoreType.DMA((2,)),
        ],
        compiler_params=pltpu.CompilerParams(vmem_limit_bytes=(60, 22)[layer_no] * MIB),
        cost_estimate=SHORT,
        name=f"ffn_forward_{layer_no}",
    )(x, part_a, part_b, *small_c, *wide_c)


def ffn_backward_kernel(layer_no, grad_ref, slope_ref, *refs):
    wide_c = refs[:4]
    out_ref, gupper_ref, bias_ref = refs[4:7]
    wide, sems = refs[7:]

    @pl.when(pl.program_id(0) == 0)
    def _():
        source = pick_source(layer_no)
        start_pick(source, wide_c, wide, sems.at[0])
        bias_ref[...] = jnp.zeros_like(bias_ref)
        wait_pick(wide_c, wide, sems.at[0])

    width = grad_ref.shape[1]
    units = wide.shape[1]
    grad = grad_ref[...]
    total = None
    step = 256
    for at in range(0, units, step):
        gactive = contract(grad, down_rows(wide, width, at, step), 1, 1)
        gupper = (gactive * slope_ref[:, at : at + step].astype(f32)).astype(bf)
        gupper_ref[:, at : at + step] = gupper
        bias_ref[:, at : at + step] += fold_rows(gupper.astype(f32))
        term = contract(gupper, wide[:width, at : at + step], 1, 1)
        total = term if total is None else total + term
    out_ref[...] = total.astype(bf)


def fold_rows(value):
    rows, cols = value.shape
    return jnp.sum(value.reshape(rows // 8, 8, cols), axis=0)


def ffn_backward(layer_no, grad, slope, weights):
    (wide_c,) = weights
    seq, width = grad.shape
    units = wide_c[0].shape[1]
    shape = jax.ShapeDtypeStruct
    rows = lambda cols: pl.BlockSpec((FFN_ROWS, cols), lambda i: (i, 0))
    return pl.pallas_call(
        functools.partial(ffn_backward_kernel, layer_no),
        grid=(seq // FFN_ROWS,),
        out_shape=[shape((seq, width), bf), shape((seq, units), bf), shape((8, units), f32)],
        in_specs=[rows(width), rows(units)] + [ANY] * 4,
        out_specs=[rows(width), rows(units), pl.BlockSpec((8, units), lambda i: (0, 0))],
        scratch_shapes=[
            pltpu.VMEM(wide_c[0].shape, bf),
            pltpu.SemaphoreType.DMA((1,)),
        ],
        compiler_params=pltpu.CompilerParams(vmem_limit_bytes=18 * MIB),
        cost_estimate=SHORT,
        name=f"ffn_backward_{layer_no}",
    )(grad, slope, *wide_c)


def attn_backward_kernel(layer_no, n_heads, blocks_ref, *refs):
    rows_in = refs[:5]
    qkv_in, probs_in, qf_in, kf_in, mt_in = refs[5:10]
    pack_c, refs = refs[10:14], refs[14:]
    out_ref, gbranch_ref, dqkv_ref, first_ref, vec_ref, bias_ref, refs = *refs[:6], refs[6:]
    (pack, qkv, probs, qfeat, kfeat, mt, gmix, gstack, qstack, gext, gt, fback,
     dq, dk, dv, gy_ref, part_a, part_b, hidden_ref, x_ref, sem, row_sem) = refs
    seq, width = gy_ref.shape
    n_chunks = seq // ROWS
    pairs = n_heads // 2
    part_width = qkv.shape[2]
    feat = pack.shape[1]
    small = pack.at[0:PACK_ROWS]
    source = pick_source(layer_no)
    start_pick(source, pack_c, pack, sem.at[0])
    row_loads = [
        pltpu.make_async_copy(item, target, row_sem.at[number])
        for number, (item, target) in enumerate(
            zip(rows_in, (gy_ref, part_a, part_b, hidden_ref, x_ref))
        )
    ]
    for load in row_loads:
        load.start()
    loads = [
        pltpu.make_async_copy(qkv_in, qkv, sem.at[2]),
        pltpu.make_async_copy(mt_in, mt, sem.at[3]),
        pltpu.make_async_copy(qf_in, qfeat, sem.at[4]),
        pltpu.make_async_copy(kf_in, kfeat, sem.at[5]),
        pltpu.make_async_copy(probs_in, probs, sem.at[6]),
    ]
    for load in loads:
        load.start()
    first_ref[...] = jnp.zeros_like(first_ref)
    vec_ref[...] = jnp.zeros_like(vec_ref)
    bias_ref[...] = jnp.zeros_like(bias_ref)
    wait_pick(pack_c, pack, sem.at[0])
    for load in row_loads[:4]:
        load.wait()
    gain = 1.0 + vector_row(small, 2, width)
    in_first, in_second = lane_masks()
    masks = (in_first, in_second)

    @pl.loop(0, n_chunks)
    def _(chunk):
        rows = pl.ds(pl.multiple_of(chunk * ROWS, ROWS), ROWS)
        gnormed = part_a[rows, :].astype(f32) + part_b[rows, :].astype(f32)
        zhat, scale = norm_stats(hidden_ref[rows, :].astype(f32))
        scaled = gnormed * gain
        gy = gy_ref[rows, :].astype(f32)
        mean_one = jnp.mean(scaled, axis=-1, keepdims=True)
        mean_two = jnp.mean(scaled * zhat, axis=-1, keepdims=True)
        ghidden = gy + (scaled - mean_one - zhat * mean_two) * scale
        low = ghidden.astype(bf)
        gbranch_ref[rows, :] = low
        vec_ref[0] += fold_rows(gnormed * zhat)
        vec_ref[1] += fold_rows(gnormed)
        vec_ref[2] += fold_rows(low.astype(f32))
        vec_ref[3] += fold_rows(gy)
        first, second = out_weights(pack, n_heads, part_width)
        gmix[rows, :] = (contract(low[:, :feat], first, 1, 1) + contract(low[:, feat:], second, 1, 1)).astype(bf)

    for load in loads[:4]:
        load.wait()
    for pair in range(pairs):
        cols = slice(pair * 2 * HEAD, (pair + 1) * 2 * HEAD)
        for a in range(2):
            plain = feature_rows(pack, n_heads, 2 * pair + a) * F_SCALE
            high = plain.astype(bf).astype(f32)
            ones = jnp.ones((HEAD, feat), f32)
            none = jnp.zeros((HEAD, feat), f32)
            stack = [high, ones] if a == 0 else [ones, high]
            stack += [plain - high, none] if a == 0 else [none, plain - high]
            fback[a] = jnp.concatenate(stack, axis=0).astype(bf)

        def feature_back(a, gfeat, feats, vectors):
            gexpo = (gfeat * feats.astype(f32)).astype(bf)
            both = contract(gexpo, fback[a], 1, 1)
            both = both[:, : 2 * HEAD] + both[:, 2 * HEAD :]
            return both - (F_SCALE * F_SCALE) * swap_halves(both) * vectors

        @pl.loop(0, n_chunks)
        def _(chunk):
            rows = pl.ds(pl.multiple_of(chunk * ROWS, ROWS), ROWS)
            grad = gmix[rows, cols].astype(f32)
            query = qkv[0, rows, cols].astype(f32)
            out = None
            for a in range(2):
                feats = qfeat[pair, rows, a * feat : (a + 1) * feat]
                moment = mt[2 * pair + a]
                numer = contract(feats, moment, 1, 1)
                inverse = 1.0 / swap_halves(numer)
                gnumer = grad * inverse
                other = swap_halves(gnumer * numer * inverse)
                both = jnp.where(masks[a], gnumer, -other).astype(bf)
                gext[a, rows, :] = both
                gfeat = jnp.dot(both, moment, preferred_element_type=f32)
                value = feature_back(a, gfeat, feats, query)
                out = value if a == 0 else jnp.where(in_first, out, value)
            dq[rows, :] = out
            stack_heads(gstack, chunk, grad, masks)
            stack_heads(qstack, chunk, query * (HEAD ** -0.5), masks)

        for a in range(2):
            gt[a] = contract(gext[a], qfeat[pair, :, a * feat : (a + 1) * feat], 0, 0).astype(bf)

        @pl.loop(0, n_chunks)
        def _(chunk):
            rows = pl.ds(pl.multiple_of(chunk * ROWS, ROWS), ROWS)
            key = qkv[1, rows, cols].astype(f32)
            value_f = qkv[2, rows, cols].astype(f32)
            dk_out, dv_out = None, None
            for a in range(2):
                extended = jnp.where(masks[a], value_f, 1.0).astype(bf)
                feats = kfeat[pair, rows, a * feat : (a + 1) * feat]
                gfeat = jnp.dot(extended, gt[a], preferred_element_type=f32)
                dk_one = feature_back(a, gfeat, feats, key)
                dv_one = contract(feats, gt[a], 1, 1)
                dk_out = dk_one if a == 0 else jnp.where(in_first, dk_out, dk_one)
                dv_out = dv_one if a == 0 else jnp.where(in_first, dv_out, dv_one)
            dk[rows, :] = dk_out
            dv[rows, :] = dv_out

        if pair == 0:
            loads[4].wait()

        @pl.loop(0, seq // BLOCK, unroll=SPARSE_UNROLL)
        def _(block):
            rows = pl.ds(pl.multiple_of(block * BLOCK, BLOCK), BLOCK)
            starts = listed_starts(blocks_ref, pair, block, seq // BLOCK)
            keys = pick_rows(qkv, 1, cols, starts, in_first)
            values = pick_rows(qkv, 2, cols, starts, in_first)
            weights = probs[pair, block]
            weights_f = weights.astype(f32)
            grad = gstack[block]
            gweights = contract(values, grad, 1, 1)
            inner = jnp.sum(weights_f * gweights, axis=0, keepdims=True)
            gscores = (weights_f * (gweights - inner)).astype(bf)
            both = contract(gscores, keys, 0, 0)
            out = jnp.where(in_first, both[:BLOCK], both[BLOCK:]) * (HEAD ** -0.5)
            dkeys = jnp.dot(gscores, qstack[block], preferred_element_type=f32)
            dvalues = jnp.dot(weights, grad, preferred_element_type=f32)
            for total, part in ((dk, dkeys), (dv, dvalues)):
                total[0:BLOCK, :] += part[:BLOCK]
                for slot, (one, two) in enumerate(starts):
                    piece = part[(slot + 1) * BLOCK : (slot + 2) * BLOCK]
                    total[pl.ds(one, BLOCK), :] += jnp.where(in_first, piece, 0.0)
                    total[pl.ds(two, BLOCK), :] += jnp.where(in_first, 0.0, piece)
            dq[rows, :] += out

        @pl.loop(0, n_chunks)
        def _(chunk):
            rows = pl.ds(pl.multiple_of(chunk * ROWS, ROWS), ROWS)
            for part, total in enumerate((dq, dk, dv)):
                low = total[rows, :].astype(bf)
                dqkv_ref[part, rows, cols] = low
                bias_ref[part, :, cols] += fold_rows(low.astype(f32))


    row_loads[4].wait()

    @pl.loop(0, n_chunks)
    def _(chunk):
        rows = pl.ds(pl.multiple_of(chunk * ROWS, ROWS), ROWS)
        total = None
        for part in range(3):
            term = contract(dqkv_ref[part, rows, :], qkv_weight(pack, n_heads, width, part), 1, 1)
            total = term if total is None else total + term
        low = total.astype(bf)
        out_ref[rows, :] = low
        zhat, _ = norm_stats(x_ref[rows, :].astype(f32))
        total = low.astype(f32)
        first_ref[0] += fold_rows(total * zhat)
        first_ref[1] += fold_rows(total)


def attn_backward(layer_no, n_heads, blocks, gy, part_a, part_b, hidden, x, kept, pack_c):
    seq, width = gy.shape
    part_width, feat = n_heads * HEAD, pack_c[0].shape[1]
    pairs = n_heads // 2
    shape = jax.ShapeDtypeStruct
    operands = [gy, part_a, part_b, hidden, x, *kept, *pack_c]
    return pl.pallas_call(
        functools.partial(attn_backward_kernel, layer_no, n_heads),
        out_shape=[
            shape((seq, width), bf),
            shape((seq, width), bf),
            shape((3, seq, part_width), bf),
            shape((2, 8, width), f32),
            shape((4, 8, width), f32),
            shape((3, 8, part_width), f32),
        ],
        in_specs=[SCALARS] + [ANY] * 14,
        out_specs=[WHOLE] * 6,
        scratch_shapes=[
            pltpu.VMEM(pack_c[0].shape, bf),
            pltpu.VMEM((3, seq, part_width), bf),
            pltpu.VMEM((pairs, seq // BLOCK, 4 * BLOCK, 2 * HEAD), bf),
            pltpu.VMEM((pairs, seq, 2 * feat), bf),
            pltpu.VMEM((pairs, seq, 2 * feat), bf),
            pltpu.VMEM((n_heads, 2 * HEAD, feat), bf),
            pltpu.VMEM((seq, part_width), bf),
            pltpu.VMEM((seq // BLOCK, 2 * BLOCK, 2 * HEAD), bf),
            pltpu.VMEM((seq // BLOCK, 2 * BLOCK, 2 * HEAD), bf),
            pltpu.VMEM((2, seq, 2 * HEAD), bf),
            pltpu.VMEM((2, 2 * HEAD, feat), bf),
            pltpu.VMEM((2, 4 * HEAD, feat), bf),
            pltpu.VMEM((seq, 2 * HEAD), f32),
            pltpu.VMEM((seq, 2 * HEAD), f32),
            pltpu.VMEM((seq, 2 * HEAD), f32),
            *[pltpu.VMEM((seq, width), bf)] * 5,
            pltpu.SemaphoreType.DMA((7,)),
            pltpu.SemaphoreType.DMA((5,)),
        ],
        compiler_params=pltpu.CompilerParams(vmem_limit_bytes=(53, 46)[layer_no] * MIB),
        cost_estimate=SHORT,
        name=f"attn_backward_{layer_no}",
    )(blocks, *operands)


def norm_backward_kernel(layer_no, x_ref, part_a, part_b, ghidden_ref, *refs):
    small_c = refs[:4]
    low_ref, small, sems = refs[4:]

    @pl.when(pl.program_id(0) == 0)
    def _():
        start_pick(pick_source(layer_no), small_part(small_c), small, sems.at[0])
        wait_pick(small_part(small_c), small, sems.at[0])

    width = x_ref.shape[1]
    gnormed = part_a[...].astype(f32) + part_b[...].astype(f32)
    zhat, scale = norm_stats(x_ref[...].astype(f32))
    scaled = gnormed * (1.0 + vector_row(small, 0, width))
    mean_one = jnp.mean(scaled, axis=-1, keepdims=True)
    mean_two = jnp.mean(scaled * zhat, axis=-1, keepdims=True)
    total = ghidden_ref[...].astype(f32) + (scaled - mean_one - zhat * mean_two) * scale
    low_ref[...] = total.astype(bf)


def norm_backward(layer_no, x, part_a, part_b, ghidden, small_c):
    seq, width = x.shape
    shape = jax.ShapeDtypeStruct
    rows = pl.BlockSpec((FFN_ROWS, width), lambda i: (i, 0))
    return pl.pallas_call(
        functools.partial(norm_backward_kernel, layer_no),
        grid=(seq // FFN_ROWS,),
        out_shape=shape((seq, width), bf),
        in_specs=[rows] * 4 + [ANY] * 4,
        out_specs=rows,
        scratch_shapes=[pltpu.VMEM((PACK_ROWS, small_c[0].shape[1]), bf), pltpu.SemaphoreType.DMA((1,))],
        compiler_params=pltpu.CompilerParams(vmem_limit_bytes=(60, 12)[layer_no] * MIB),
        cost_estimate=SHORT,
        name=f"norm_backward_{layer_no}",
    )(x, part_a, part_b, ghidden, *small_c)


def tiny_rows(first, moved, vec, bias_qkv, bias_up):
    half = vec.shape[2] // 2
    here = pl.ds(pl.multiple_of(lax.rem(lax.axis_index("dp"), 2) * half, half), half)
    total = lambda value: jnp.sum(value, axis=0, keepdims=True)
    rows = [total(first[i, :, here] + moved[i, :, here]) for i in range(2)]
    rows += [total(vec[i, :, here]) for i in range(4)]
    rows += [total(bias_qkv[i]) for i in range(3)] + [total(bias_up[...])]
    return [row[:, at : at + LANES] for row in rows for at in range(0, row.shape[1], LANES)]


def weight_grad_kernel(n_first, n_extra, left_a, left_b, right_a, right_b, *refs):
    keep_ref, away_ref, turned = refs[-3:]
    extra, sums = refs[:n_extra], refs[n_extra:-3]
    step = pl.program_id(0)
    shard = left_a.shape[1] // lax.axis_size("dp")
    per_half = pl.num_programs(0) // 2
    width = right_a.shape[1]
    n_rows = left_a.shape[1]
    first = step < n_first

    @pl.when(step == 0)
    def _():
        turned[...] = left_a[...].T
        for source, target in zip(extra, (keep_ref, away_ref)):
            target[:, per_half * width :] = source[...]
        if sums:
            rows = tiny_rows(*sums[:5]) + tiny_rows(*sums[5:])
            low = jnp.concatenate(rows, axis=0).astype(bf)
            low = jnp.concatenate([low, jnp.zeros((shard - low.shape[0], LANES), bf)], axis=0)
            for target in (keep_ref, away_ref):
                for at in range(0, n_rows, shard):
                    target[at : at + shard, per_half * width :] = low

    @pl.when(step == n_first)
    def _():
        turned[...] = left_b[...].T

    right = jnp.where(first, right_a[...], right_b[...])
    result = jnp.dot(turned[...], right, preferred_element_type=f32).astype(bf)
    here = pl.ds(pl.multiple_of(lax.rem(step, per_half) * width, width), width)
    keep = step // per_half == lax.axis_index("section")
    for wanted, target in ((keep, keep_ref), (jnp.logical_not(keep), away_ref)):

        @pl.when(wanted)
        def _():
            target[:n_rows, here] = result


def weight_grads(name, step, left_a, right_a, left_b, right_b, extra=(), sums=()):
    seq, width = left_a.shape
    if right_a.ndim == 3:
        n_first = right_a.shape[0]
        spec_a = pl.BlockSpec((None, seq, step), lambda i: (jnp.minimum(i, n_first - 1), 0, 0))
    else:
        n_first = right_a.shape[1] // step
        spec_a = pl.BlockSpec((seq, step), lambda i: (0, jnp.minimum(i, n_first - 1)))
    n_second = right_b.shape[1] // step
    spec_b = pl.BlockSpec((seq, step), lambda i: (0, jnp.maximum(i - n_first, 0)))
    whole = pl.BlockSpec((seq, width), lambda i: (0, 0))
    n_steps = n_first + n_second
    cols = step * (n_steps // 2) + (extra[0].shape[1] if extra else 0)
    shape = (width, cols + (LANES if sums else 0))
    fixed = lambda shape: pl.BlockSpec(shape, lambda i: (0,) * len(shape))
    return pl.pallas_call(
        functools.partial(weight_grad_kernel, n_first, len(extra)),
        grid=(n_steps,),
        out_shape=[jax.ShapeDtypeStruct(shape, bf)] * 2,
        in_specs=[whole, whole, spec_a, spec_b] + [fixed(item.shape) for item in (*extra, *sums)],
        out_specs=[fixed(shape)] * 2,
        scratch_shapes=[pltpu.VMEM((width, seq), bf)],
        compiler_params=pltpu.CompilerParams(vmem_limit_bytes=20 * MIB),
        cost_estimate=SHORT,
        name=name,
    )(left_a, left_b, right_a, right_b, *extra, *sums)


ALL_AXES = ("section", "tensor", "dp")


def send(value, sizes, target):
    n_section, n_tensor, n_dp = sizes
    pairs = []
    for s in range(n_section):
        for t in range(n_tensor):
            for d in range(n_dp):
                goal = target(s, t, d // 2, d % 2)
                if goal is not None:
                    gs, gt, gz, gc = goal
                    number = (s * n_tensor + t) * n_dp + d
                    pairs.append((number, (gs * n_tensor + gt) * n_dp + 2 * gz + gc))
    return lax.ppermute(value, ALL_AXES, pairs)


def other_core(value, sizes):
    return send(value, sizes, lambda s, t, z, c: (s, t, z, 1 - c))


def chip_shards(
    sizes,
    inputs,
    cotangent,
    lengths,
    blocks,
    feature_map,
    w_qkv,
    b_qkv,
    w_out,
    w_up,
    b_up,
    w_down,
    vector_params,
):
    n_dp = sizes[2]
    n_z = n_dp // 2
    section_no = lax.axis_index("section")
    tensor_no = lax.axis_index("tensor")
    dp_no = lax.axis_index("dp")
    z_no, core = dp_no // 2, dp_no % 2
    same = core == tensor_no
    is_first = section_no == 0
    width = inputs.shape[2]
    half = inputs.shape[1]
    n_heads, n_blocks, n_listed = blocks.shape[1:]
    feat = feature_map.shape[3]
    part_width = w_qkv.shape[3]

    def after(value, earlier):
        return lax.optimization_barrier((value, earlier))[0]

    def share_y(array):
        return send(array, sizes, lambda s, t, z, c: (1 - s, t, z, c) if c == t else None)

    def share_x(array):
        return send(array, sizes, lambda s, t, z, c: (s, 1 - t, z, c) if c == t else None)

    wide = jnp.concatenate(
        [w_up[0], jnp.concatenate([w_down[0][:width], w_down[0][width:]], axis=1)], axis=0
    )
    def halves(own, first, second):
        near = jnp.where(same, own, first)
        far = jnp.where(same, first, second)
        swap = tensor_no == 1
        return jnp.concatenate(
            [jnp.where(swap, far, near), jnp.where(swap, near, far)], axis=0
        )

    def cross(own):
        return send(
            own,
            sizes,
            lambda s, t, z, c: (s, t, z, 1 - c) if c == t else (s, 1 - t, z, c),
        )

    def to_sequence(own, first):
        second = send(first, sizes, lambda s, t, z, c: (s, t, z, 1 - c) if c == t else None)
        return halves(own, first, second)

    x_own = inputs[section_no]
    x_arrived = cross(x_own)
    pack = pack_weights(
        w_qkv[0].transpose(1, 0, 2),
        w_out[0],
        feature_map[0].reshape(n_heads * HEAD, feat),
        b_qkv[0],
        b_up,
        vector_params[0],
        blocks[0].reshape(n_heads * n_blocks, n_listed),
    )
    x_first = to_sequence(x_own, x_arrived)
    pack_y = share_y(pack)
    pack_x = share_x(pack)
    pack_both = share_x(after(pack_y, pack_x))
    pack_c = (pack, pack_y, pack_x, pack_both)
    wide_y = share_y(after(wide, pack_y))

    def share_wide(layer_no, earlier):
        def share(array, section):
            return send(
                after(array, earlier),
                sizes,
                lambda s, t, z, c: (s, 1 - t, z, c) if c == t and s == section else None,
            )

        return (wide, wide_y, share(wide, layer_no), share(wide_y, 1 - layer_no))

    lengths_here = jnp.where(same, lengths, other_core(lengths, sizes))
    length = lax.dynamic_slice_in_dim(lengths_here[:, 0], section_no, 1)

    weights = [(pack_c, share_wide(0, (pack_both, x_first, length)))]

    def of_layer(layer_no, candidates):
        mine = section_no == layer_no
        return jnp.where(
            same,
            jnp.where(mine, candidates[0], candidates[1]),
            jnp.where(mine, candidates[2], candidates[3]),
        )

    def exchange(value):
        return value, other_core(value, sizes)

    kept = []
    x_parts = (x_first,)
    outputs = []
    for layer_no in range(2):
        listed = of_layer(
            layer_no,
            [item[PACK_ROWS : PACK_ROWS + n_heads * n_blocks, :n_listed] for item in pack_c],
        )
        listed = listed.astype(jnp.int32)
        made = attn_forward(layer_no, n_heads, length, listed, x_parts, pack_c, pack_c)
        if layer_no == 0:
            x = x_first
        else:
            x, made = made[0], made[1:]
            outputs.append(x)
        branch, qkv, normed, probs, qfeat, kfeat, mt, mixed = made
        if layer_no == 0:
            grad_own = after(cotangent[section_no], (weights[0][1][2:], branch))
            grad_arrived = cross(grad_own)
            weights.append((pack_c, share_wide(1, (weights[0][1][2:], branch))))
        result, hidden, normed_two, active, slope = ffn_forward(
            layer_no, x, *exchange(branch), weights[layer_no]
        )
        x_parts = (hidden, *exchange(result))
        kept.append(
            (x, normed, mixed, hidden, normed_two, active, slope, listed,
             (qkv, probs, qfeat, kfeat, mt))
        )

    grad = to_sequence(grad_own, grad_arrived)

    def my_half(array):
        return lax.dynamic_slice_in_dim(array, core * half, half)

    def deliver(first_rows, second_rows):
        mine = jnp.where(is_first, first_rows, second_rows)
        theirs = jnp.where(is_first, second_rows, first_rows)
        own = send(mine, sizes, lambda s, t, z, c: (s, c, z, t))
        other = send(theirs, sizes, lambda s, t, z, c: (1 - s, c, z, t))
        return own, other

    hidden, part_a, part_b = x_parts
    last_bias = of_layer(1, [lane[18:20].reshape(1, width) for lane in pack_c]).astype(f32)
    last = my_half(hidden).astype(f32) + (my_half(part_a).astype(f32) + my_half(part_b).astype(f32)) + last_bias

    def plane_send(keep, away, hold=None):
        by_x = send(keep, sizes, lambda s, t, z, c: None if c == t else (s, 1 - t, z, c))
        by_y = share_y(away)
        late = away if hold is None else after(away, hold)
        by_both = send(late, sizes, lambda s, t, z, c: None if c == t else (1 - s, 1 - t, z, c))
        return keep, by_x, by_y, by_both

    def plane_sum(terms):
        total = terms[0].astype(f32)
        for term in terms[1:]:
            total = total + term.astype(f32)
        return total.astype(bf)

    def line_send(arrays):
        def shard_for(step):
            at = ((z_no + step) % n_z) * pair
            rows = [lax.dynamic_slice_in_dim(array, at, pair) for array in arrays]
            return jnp.concatenate(rows, axis=1)

        def turn(step):
            return lambda s, t, z, c: (s, t, (z + step) % n_z, c) if c == t else None

        return [shard_for(0)] + [
            send(shard_for(step), sizes, turn(step)) for step in range(1, n_z)
        ]

    def line_sum(found):
        total = found[0].astype(f32)
        for part in found[1:]:
            total = total + part.astype(f32)
        return total

    def ffn_part(layer_no, grad, hold):
        normed_two, active, slope = kept[layer_no][4:7]
        gnormed_two, gupper, bias_up = ffn_backward(
            layer_no, after(grad, hold), slope, (weights[layer_no][1],)
        )
        parts = exchange(gnormed_two)
        return parts, gupper, bias_up

    def ffn_grads(layer_no, grad, gupper, hold, extra=()):
        normed_two, active = kept[layer_no][4:6]
        return weight_grads(
            f"ffn_grads_{layer_no}", 512, after(normed_two, hold), gupper, grad, active, extra
        )

    def attn_part(layer_no, grad, parts, hold):
        hidden, listed, attn_kept = kept[layer_no][3], kept[layer_no][7], kept[layer_no][8]
        gnormed, *rest = attn_backward(
            layer_no, n_heads, listed, grad, after(parts[0], hold), parts[1], hidden,
            kept[layer_no][0], attn_kept, pack_c,
        )
        gbranch, gproj, vec_one, vec_two, bias_qkv = rest
        sums = (vec_one, other_core(vec_one, sizes), vec_two, bias_qkv)
        return exchange(gnormed), gbranch, gproj, sums

    def attn_grads(layer_no, gproj, gbranch, hold, sums=()):
        normed, mixed = kept[layer_no][1:3]
        return weight_grads(
            f"attn_grads_{layer_no}", part_width, after(normed, hold), gproj, gbranch, mixed, (), sums
        )

    def norm_part(layer_no, parts, gbranch, hold):
        return norm_backward(
            layer_no, kept[layer_no][0], after(parts[0], hold), parts[1], gbranch, pack_c
        )

    shard, pair = width // n_dp, width // n_z
    units = wide.shape[1]
    parts, gupper, bias_up = ffn_part(1, grad, x_parts[0])
    keep, away = ffn_grads(1, grad, gupper, parts[0])
    parts, gbranch, gproj, sums = attn_part(1, grad, parts, (keep, x_parts))
    wide_one = plane_send(keep, away, gbranch)
    sums_one = (*sums, bias_up)
    extra = attn_grads(1, gproj, gbranch, parts[0])
    grad = norm_part(1, parts, gbranch, extra[0])
    upper_grad = grad
    parts, gupper, bias_up = ffn_part(0, grad, grad)
    keep, away = ffn_grads(0, grad, gupper, parts[0], extra)
    keep, away, wide_one = after((keep, away, wide_one), keep)
    wide_zero = plane_send(keep, away)
    parts, gbranch, gproj, sums = attn_part(0, grad, parts, (keep, wide_one))
    wide_zero, wide_one = after((wide_zero, wide_one), gbranch)
    keep, away = attn_grads(
        0, gproj, gbranch, parts[0], (*sums_one, *sums, bias_up)
    )
    keep, away, wide_zero, wide_one = after((keep, away, wide_zero, wide_one), keep)
    keep, away, parts = after((keep, away, parts), (wide_zero, parts))
    narrow_zero = plane_send(keep, away)
    out_pair = deliver(*after((my_half(outputs[0]), last.astype(bf)), narrow_zero))
    line_wide = line_send([plane_sum(wide_one), plane_sum(wide_zero)])
    grad = norm_part(0, parts, gbranch, keep)
    line_narrow = line_send([after(plane_sum(narrow_zero), (line_wide, out_pair))])
    grad_pair = deliver(*after((my_half(grad), my_half(upper_grad)), line_narrow[0]))
    line_narrow = line_sum(after(line_narrow, grad_pair))
    line_wide = line_sum(line_wide)
    n_narrow = line_narrow.shape[1] - LANES
    rest = line_narrow[:, n_narrow:]
    first_sum = jnp.concatenate([line_wide[:, units : 2 * units], line_narrow], axis=1)
    second_sum = jnp.concatenate([line_wide[:, :units], line_wide[:, 2 * units :], rest], axis=1)

    def for_core(layer, number):
        return lax.dynamic_slice_in_dim(layer, number * shard, shard)

    mine = jnp.where(is_first, first_sum, second_sum)
    theirs = jnp.where(is_first, second_sum, first_sum)

    def cast(value, target):
        return send(
            value.astype(bf), sizes, lambda s, t, z, c: target(s, t, z) if c == t else None
        ).astype(f32)

    near = cast(for_core(mine, 1 - core), lambda s, t, z: (s, t, z, 1 - t))
    far = cast(for_core(theirs, core), lambda s, t, z: (1 - s, t, z, t))
    cross_far = cast(for_core(theirs, 1 - core), lambda s, t, z: (1 - s, t, z, 1 - t))
    stay = jnp.where(same, for_core(mine, core), near)
    arrived = jnp.where(same, far, cross_far)
    low_half = jnp.where(is_first, stay, arrived)
    high_half = jnp.where(is_first, arrived, stay)
    grad_up, grad_down = low_half[:, :units], high_half[:, :units]
    narrow = jnp.concatenate(
        [low_half[:, units : units + n_narrow], high_half[:, units : units + n_narrow]], axis=1
    )
    rows = stay[:, units + n_narrow :]
    n_rows = 9 * (width // 2 // LANES) + units // LANES
    rows = jnp.where(is_first, rows[n_rows : 2 * n_rows], rows[:n_rows])
    halves_found = rows[: n_rows - units // LANES].reshape(9, width // 2)

    def own_columns(array):
        cols = array.reshape(-1, n_dp, array.shape[1] // n_dp)
        return lax.dynamic_index_in_dim(cols, dp_no, axis=1, keepdims=False)

    grad_vectors = own_columns(halves_found[:6])
    grad_bqkv = own_columns(halves_found[6:])
    grad_bup = own_columns(rows[n_rows - units // LANES :].reshape(1, -1))[0]

    def placed(pair, dtype):
        own, other = pair
        return jnp.stack(
            [jnp.where(is_first, own, other), jnp.where(is_first, other, own)]
        )[None].astype(dtype)

    section_outputs = placed(out_pair, bf)
    input_grads = placed(grad_pair, f32)
    grad_qkv = narrow[:, : 3 * part_width].reshape(shard, 3, part_width)
    grad_out = narrow[:, 3 * part_width :].T
    return (
        section_outputs,
        input_grads,
        grad_qkv[None],
        grad_bqkv[None],
        grad_out[None],
        grad_up[None],
        grad_bup[None],
        grad_down.T[None],
        grad_vectors[None],
    )


HEAD = 64
BLOCK = 64
SEQ_LEN = 1024


norm_eps = 1e-05
bfloat = jnp.bfloat16
single = jnp.float32


def shifted(value, axis, steps):
    count = lax.axis_size(axis)
    first, last = (max(0, -steps), min(count, count - steps))
    return lax.ppermute(value, axis, [(source, source + steps) for source in range(first, last)])


def norm_rows(residual, gain_vec, shift_vec):
    row_mean = jnp.mean(residual, axis=-1, keepdims=True)
    centred = residual - row_mean
    variance = jnp.mean(centred * centred, axis=-1, keepdims=True)
    return centred * lax.rsqrt(variance + norm_eps) * (1.0 + gain_vec) + shift_vec


def gelu_exact(pre_active):
    return jax.nn.gelu(pre_active, approximate=False)


def select_tree(flag_value, when_true, when_false):
    return jax.tree.map(
        lambda left_arr, right_arr: jnp.where(flag_value, left_arr, right_arr),
        when_true,
        when_false,
    )


def split_pieces(operand):
    if operand.dtype == bfloat:
        return (operand,)
    upper_part = operand.astype(bfloat)
    lower_part = (operand - upper_part.astype(single)).astype(bfloat)
    return (upper_part, lower_part)


def split_dot(form, left, right):
    left_pieces = split_pieces(left)
    right_pieces = split_pieces(right)
    total = None
    for left_no, left_piece in enumerate(left_pieces):
        for right_no, right_piece in enumerate(right_pieces):
            if left_no + right_no > 1:
                continue
            term = jnp.einsum(form, left_piece, right_piece, preferred_element_type=single)
            total = term if total is None else total + term
    return total


def sparse_layout(block_list, length):
    head_count, block_count = (block_list.shape[0], block_list.shape[1])
    chosen = jnp.concatenate(
        [jnp.zeros((head_count, block_count, 1), jnp.int32), block_list], axis=2
    )
    key_live = (jnp.arange(SEQ_LEN) < length).astype(single)
    picked_live = key_live.reshape(block_count, BLOCK)[chosen].reshape(head_count, block_count, -1)
    return (chosen, key_live, picked_live)


def pick_blocks(table_in, chosen):
    head_count, block_count = (chosen.shape[0], chosen.shape[1])
    blocks_in = table_in.reshape(head_count, block_count, BLOCK, table_in.shape[-1])
    taken_rows = jax.vmap(lambda one_table, index_rows: one_table[index_rows])(blocks_in, chosen)
    return taken_rows.reshape(head_count, block_count, -1, table_in.shape[-1])


def place_blocks(values_in, chosen):
    head_count, block_count, slot_count = chosen.shape
    parts_in = values_in.reshape(head_count, block_count, slot_count, BLOCK, values_in.shape[-1])
    zero_blocks = jnp.zeros((head_count, block_count, BLOCK, values_in.shape[-1]), single)
    placed = jax.vmap(lambda base_arr, index_rows, one_part: base_arr.at[index_rows].add(one_part))(
        zero_blocks, chosen, parts_in
    )
    return placed.reshape(head_count, SEQ_LEN, values_in.shape[-1])


def feature_of(vectors_low, features):
    feature_scale = HEAD ** (-0.25)
    vectors = vectors_low.astype(single)
    projected = split_dot("hld,hdf->hlf", vectors_low, features) * feature_scale
    return jnp.exp(
        projected
        - jnp.sum(vectors * vectors, axis=-1, keepdims=True) * (0.5 * feature_scale * feature_scale)
    )


def block_scores(query_blocks, picked_keys, picked_live):
    scores = jnp.einsum(
        "hnqd,hnkd->hnqk", query_blocks, picked_keys, preferred_element_type=single
    ) * HEAD ** (-0.5)
    return jnp.where(picked_live[:, :, None, :] > 0.5, scores, -1e30)


def attend_forward(queries, key_vecs, value_vecs, chosen, key_live, picked_live, features):
    head_count, block_count = (chosen.shape[0], chosen.shape[1])
    query_blocks = queries.reshape(head_count, block_count, BLOCK, HEAD)
    picked_keys = pick_blocks(key_vecs, chosen)
    picked_values = pick_blocks(value_vecs, chosen)
    scores = block_scores(query_blocks, picked_keys, picked_live)
    row_max = jnp.max(scores, axis=-1, keepdims=True)
    weights_raw = jnp.exp(scores - row_max) * picked_live[:, :, None, :]
    row_total = jnp.sum(weights_raw, axis=-1, keepdims=True)
    log_total = row_max + jnp.log(row_total)
    weights_low = (weights_raw / row_total).astype(bfloat)
    sparse_out = jnp.einsum(
        "hnqk,hnkd->hnqd", weights_low, picked_values, preferred_element_type=single
    )
    sparse_out = sparse_out.reshape(head_count, SEQ_LEN, HEAD)
    query_feats = feature_of(queries, features)
    key_feats = feature_of(key_vecs, features) * key_live[None, :, None]
    moments = split_dot("hlf,hld->hfd", key_feats, value_vecs)
    totals = jnp.sum(key_feats, axis=1)
    numerator = split_dot("hlf,hfd->hld", query_feats, moments)
    denominator = split_dot("hlf,hf->hl", query_feats, totals)
    perf_out = numerator / denominator[:, :, None]
    return (
        sparse_out + perf_out,
        (log_total, query_feats, key_feats, moments, totals, denominator, perf_out),
    )


def attend_backward(
    grad_heads, queries, key_vecs, value_vecs, chosen, picked_live, features, attn_keep
):
    log_total, query_feats, key_feats, moments, totals, denominator, perf_out = attn_keep
    head_count, block_count = (chosen.shape[0], chosen.shape[1])
    score_scale = HEAD ** (-0.5)
    query_blocks = queries.reshape(head_count, block_count, BLOCK, HEAD)
    grad_blocks = grad_heads.reshape(head_count, block_count, BLOCK, HEAD)
    picked_keys = pick_blocks(key_vecs, chosen)
    picked_values = pick_blocks(value_vecs, chosen)
    scores = block_scores(query_blocks, picked_keys, picked_live)
    weights_f = jnp.exp(scores - log_total) * picked_live[:, :, None, :]
    grad_weights = jnp.einsum(
        "hnqd,hnkd->hnqk", grad_blocks, picked_values, preferred_element_type=single
    )
    row_inner = jnp.sum(weights_f * grad_weights, axis=-1, keepdims=True)
    grad_scores = (weights_f * (grad_weights - row_inner)).astype(bfloat)
    grad_query = jnp.einsum(
        "hnqk,hnkd->hnqd", grad_scores, picked_keys, preferred_element_type=single
    )
    grad_query = grad_query.reshape(head_count, SEQ_LEN, HEAD) * score_scale
    grad_keys = place_blocks(
        jnp.einsum("hnqk,hnqd->hnkd", grad_scores, query_blocks, preferred_element_type=single)
        * score_scale,
        chosen,
    )
    grad_values = place_blocks(
        jnp.einsum(
            "hnqk,hnqd->hnkd", weights_f.astype(bfloat), grad_blocks, preferred_element_type=single
        ),
        chosen,
    )
    grad_float = grad_heads.astype(single)
    grad_numer = grad_float / denominator[:, :, None]
    grad_denom = -jnp.sum(grad_float * perf_out, axis=-1) / denominator
    grad_qfeat = (
        split_dot("hld,hfd->hlf", grad_numer, moments) + grad_denom[:, :, None] * totals[:, None, :]
    )
    grad_moments = split_dot("hlf,hld->hfd", query_feats, grad_numer)
    grad_totals = split_dot("hlf,hl->hf", query_feats, grad_denom)
    grad_kfeat = split_dot("hld,hfd->hlf", value_vecs, grad_moments) + grad_totals[:, None, :]
    grad_values = grad_values + split_dot("hlf,hfd->hld", key_feats, grad_moments)
    feature_scale = HEAD ** (-0.25)

    def feature_back(grad_feat, feats, vectors_low):
        grad_expo = grad_feat * feats
        direct = split_dot("hlf,hdf->hld", grad_expo, features) * feature_scale
        return direct - feature_scale * feature_scale * jnp.sum(
            grad_expo, axis=-1, keepdims=True
        ) * vectors_low.astype(single)

    grad_query = grad_query + feature_back(grad_qfeat, query_feats, queries)
    grad_keys = grad_keys + feature_back(grad_kfeat, key_feats, key_vecs)
    return (grad_query, grad_keys, grad_values)


def layer_forward(section_entry, length, layer_params, block_list, features):
    qkv_mat, qkv_bias, out_mat, up_mat, up_bias, down_mat, vectors = layer_params
    residual = section_entry.astype(single)
    normed = norm_rows(residual, vectors[0], vectors[1]).astype(bfloat)
    normed_all = lax.all_gather(normed, "tensor", axis=0, tiled=True)
    projected = (
        jnp.einsum("ld,dce->lce", normed_all, qkv_mat, preferred_element_type=single)
        + qkv_bias[None]
    )
    projected = projected.astype(bfloat)
    seq_len, part_width = (projected.shape[0], projected.shape[2])
    head_count = part_width // HEAD
    head_parts = projected.reshape(seq_len, 3, head_count, HEAD).transpose(1, 2, 0, 3)
    chosen, key_live, picked_live = sparse_layout(block_list, length)
    mixed_heads, attn_keep = attend_forward(
        head_parts[0], head_parts[1], head_parts[2], chosen, key_live, picked_live, features
    )
    mixed_low = mixed_heads.transpose(1, 0, 2).reshape(seq_len, part_width).astype(bfloat)
    row_block = mixed_low
    branch = lax.psum_scatter(
        jnp.dot(row_block, out_mat, preferred_element_type=single).astype(jnp.bfloat16),
        "tensor",
        scatter_dimension=0,
        tiled=True,
    ).astype(jnp.float32)
    hidden_res = residual + branch + vectors[4]
    normed_two = norm_rows(hidden_res, vectors[2], vectors[3]).astype(bfloat)
    normed_two_all = lax.all_gather(normed_two, "tensor", axis=0, tiled=True)
    pre_active = jnp.dot(normed_two_all, up_mat, preferred_element_type=single) + up_bias
    active = gelu_exact(pre_active).astype(bfloat)
    row_block = active
    result = (
        hidden_res
        + lax.psum_scatter(
            jnp.dot(row_block, down_mat, preferred_element_type=single).astype(jnp.bfloat16),
            "tensor",
            scatter_dimension=0,
            tiled=True,
        ).astype(jnp.float32)
        + vectors[5]
    )
    record = (
        residual,
        hidden_res,
        normed_all,
        head_parts,
        mixed_low,
        normed_two_all,
        pre_active,
        active,
        attn_keep,
        length,
    )
    return (result.astype(bfloat), record)


def layer_backward(grad_low, record, layer_params, block_list, features):
    qkv_mat, qkv_bias, out_mat, up_mat, up_bias, down_mat, vectors = layer_params
    (
        residual,
        hidden_res,
        normed_all,
        head_parts,
        mixed_low,
        normed_two_all,
        pre_active,
        active,
        attn_keep,
        length,
    ) = record
    seq_len, part_width = mixed_low.shape
    head_count = part_width // HEAD
    grad_output = grad_low.astype(single)
    grad_all = lax.all_gather(grad_low, "tensor", axis=0, tiled=True)
    grad_wdown = jnp.einsum("lf,ld->fd", active, grad_all, preferred_element_type=single)
    grad_active = jnp.einsum("ld,fd->lf", grad_all, down_mat, preferred_element_type=single)
    _, gelu_pull = jax.vjp(gelu_exact, pre_active)
    grad_upper = gelu_pull(grad_active)[0].astype(bfloat)
    grad_wup = jnp.einsum("ld,lf->df", normed_two_all, grad_upper, preferred_element_type=single)
    grad_bup = jnp.sum(grad_upper.astype(single), axis=0)
    row_block = grad_upper
    grad_normed_two = lax.psum_scatter(
        jnp.einsum("lf,df->ld", row_block, up_mat, preferred_element_type=single).astype(
            jnp.bfloat16
        ),
        "tensor",
        scatter_dimension=0,
        tiled=True,
    ).astype(jnp.float32)
    _, pull_two = jax.vjp(norm_rows, hidden_res, vectors[2], vectors[3])
    grad_hidden, grad_gain_two, grad_shift_two = pull_two(grad_normed_two)
    grad_hidden = grad_hidden + grad_output
    grad_hidden_low = grad_hidden.astype(bfloat)
    hidden_all = lax.all_gather(grad_hidden_low, "tensor", axis=0, tiled=True)
    grad_wout = jnp.einsum("le,ld->ed", mixed_low, hidden_all, preferred_element_type=single)
    grad_mixed = jnp.einsum("ld,ed->le", hidden_all, out_mat, preferred_element_type=single).astype(
        bfloat
    )
    grad_heads = grad_mixed.reshape(seq_len, head_count, HEAD).transpose(1, 0, 2)
    chosen, key_live, picked_live = sparse_layout(block_list, length)
    grad_query, grad_keys, grad_values = attend_backward(
        grad_heads,
        head_parts[0],
        head_parts[1],
        head_parts[2],
        chosen,
        picked_live,
        features,
        attn_keep,
    )
    grad_proj = (
        jnp.stack([grad_query, grad_keys, grad_values])
        .transpose(2, 0, 1, 3)
        .reshape(seq_len, 3, part_width)
        .astype(bfloat)
    )
    grad_wqkv = jnp.einsum("ld,lce->dce", normed_all, grad_proj, preferred_element_type=single)
    grad_bqkv = jnp.sum(grad_proj.astype(single), axis=0)
    row_block = grad_proj
    grad_normed = lax.psum_scatter(
        jnp.einsum("lce,dce->ld", row_block, qkv_mat, preferred_element_type=single).astype(
            jnp.bfloat16
        ),
        "tensor",
        scatter_dimension=0,
        tiled=True,
    ).astype(jnp.float32)
    _, pull_one = jax.vjp(norm_rows, residual, vectors[0], vectors[1])
    grad_resid, grad_gain_one, grad_shift_one = pull_one(grad_normed)
    grad_resid = grad_resid + grad_hidden
    weight_grads = (grad_wqkv, grad_bqkv, grad_wout, grad_wup, grad_bup, grad_wdown)
    vector_grads = jnp.stack(
        [
            grad_gain_one,
            grad_shift_one,
            grad_gain_two,
            grad_shift_two,
            jnp.sum(grad_hidden_low.astype(single), axis=0),
            jnp.sum(grad_output, axis=0),
        ]
    )
    return (grad_resid, weight_grads, vector_grads)


def shards(
    inputs,
    cotangent,
    lengths,
    blocks,
    feature_map,
    w_qkv,
    b_qkv,
    w_out,
    w_up,
    b_up,
    w_down,
    vector_params,
):
    section_no = lax.axis_index("section")
    is_first = section_no == 0
    is_last = section_no == lax.axis_size("section") - 1
    layer_params = (
        w_qkv[0],
        b_qkv[0].astype(single),
        w_out[0],
        w_up[0],
        b_up[0].astype(single),
        w_down[0],
        vector_params[0].astype(single),
    )
    block_list = blocks[0]
    features = feature_map[0]
    batch_count = inputs.shape[0]
    carried = jnp.zeros_like(inputs[0])
    records = []
    results = []
    for tick_no in range(batch_count + 1):
        batch_no = jnp.clip(tick_no - section_no, 0, batch_count - 1)
        section_entry = jnp.where(is_first, inputs[min(tick_no, batch_count - 1)], carried)
        result, record = layer_forward(
            section_entry, lengths[batch_no, 0], layer_params, block_list, features
        )
        records.append(record)
        results.append(result)
        if tick_no < batch_count:
            carried = shifted(result, "section", 1)
    section_outputs = jnp.stack(
        [
            jnp.where(is_first, results[batch_idx], results[batch_idx + 1])
            for batch_idx in range(batch_count)
        ]
    )[None]
    received = jnp.zeros_like(cotangent[0])
    grad_list = []
    local_sum = None
    vector_total = jnp.zeros((6, inputs.shape[2]), single)
    for tick_no in range(batch_count + 1):
        record = select_tree(
            is_last, records[min(tick_no + 1, batch_count)], records[max(tick_no - 1, 0)]
        )
        valid_flag = jnp.where(is_last, float(tick_no < batch_count), float(tick_no >= 1)).astype(
            single
        )
        grad_entry = jnp.where(is_last, cotangent[min(tick_no, batch_count - 1)], received)
        grad_resid, weight_grads, vector_grads = layer_backward(
            grad_entry, record, layer_params, block_list, features
        )
        weight_grads = tuple((valid_flag * addend for addend in weight_grads))
        vector_total = vector_total + valid_flag * vector_grads
        local_sum = (
            weight_grads
            if local_sum is None
            else tuple((summed + addend for summed, addend in zip(local_sum, weight_grads)))
        )
        grad_list.append(grad_resid)
        if tick_no < batch_count:
            received = shifted(grad_resid.astype(bfloat), "section", -1)
    final_grads = (
        lax.psum_scatter(
            local_sum[0].astype(jnp.bfloat16), "dp", scatter_dimension=0, tiled=True
        ).astype(jnp.float32),
        lax.psum_scatter(
            local_sum[1].astype(jnp.bfloat16), "dp", scatter_dimension=1, tiled=True
        ).astype(jnp.float32),
        lax.psum_scatter(
            local_sum[2].astype(jnp.bfloat16), "dp", scatter_dimension=1, tiled=True
        ).astype(jnp.float32),
        lax.psum_scatter(
            local_sum[3].astype(jnp.bfloat16), "dp", scatter_dimension=0, tiled=True
        ).astype(jnp.float32),
        lax.psum_scatter(
            local_sum[4].astype(jnp.bfloat16), "dp", scatter_dimension=0, tiled=True
        ).astype(jnp.float32),
        lax.psum_scatter(
            local_sum[5].astype(jnp.bfloat16), "dp", scatter_dimension=1, tiled=True
        ).astype(jnp.float32),
    )
    input_grads = jnp.stack(
        [
            jnp.where(is_first, grad_list[batch_idx + 1], grad_list[batch_idx])
            for batch_idx in range(batch_count)
        ]
    )[None]
    grad_vectors = lax.psum_scatter(
        vector_total, ("tensor", "dp"), scatter_dimension=1, tiled=True
    )[None]
    grad_wqkv, grad_bqkv, grad_wout, grad_wup, grad_bup, grad_wdown = final_grads
    return (
        section_outputs,
        input_grads,
        grad_wqkv[None],
        grad_bqkv[None],
        grad_wout[None],
        grad_wup[None],
        grad_bup[None],
        grad_wdown[None],
        grad_vectors,
    )


def solution(mesh):
    placed = (
        P(None, ("dp", "tensor"), None),
        P(None, ("dp", "tensor"), None),
        P(None, "dp"),
        P("section", "tensor", None, None),
        P("section", "tensor", None, None),
        P("section", None, None, "tensor"),
        P("section", None, "tensor"),
        P("section", "tensor", None),
        P("section", None, "tensor"),
        P("section", "tensor"),
        P("section", "tensor", None),
        P("section", None, None),
    )
    sizes = tuple(mesh.shape[axis] for axis in ALL_AXES)
    if sizes[0] == 2 and sizes[1] == 2 and sizes[2] % 2 == 0:
        body = functools.partial(chip_shards, sizes)
    else:
        body = shards
    return jax.shard_map(
        body,
        mesh=mesh,
        in_specs=placed,
        out_specs=(
            P("section", None, ("dp", "tensor"), None),
            P("section", None, ("dp", "tensor"), None),
            P("section", "dp", None, "tensor"),
            P("section", None, ("tensor", "dp")),
            P("section", "tensor", "dp"),
            P("section", "dp", "tensor"),
            P("section", ("tensor", "dp")),
            P("section", "tensor", "dp"),
            P("section", None, ("tensor", "dp")),
        ),
        check_vma=False,
    )
```

```python
import functools

import jax
import jax.numpy as jnp
from jax import lax
from jax.experimental import pallas as pl
from jax.experimental.pallas import tpu as pltpu
from jax.sharding import PartitionSpec as P

HEAD = 64
BLOCK = 64
NORM_EPS = 1e-5
bf = jnp.bfloat16
f32 = jnp.float32
LOG2E = 1.4426950408889634
F_SCALE = HEAD ** -0.25
ROWS = 1024
FFN_ROWS = 512
SPARSE_UNROLL = 8
PACK_ROWS = 32
PACK_SMALL = 96
LANES = 128
N_QUARTERS = 4
MIB = 1024 * 1024
SHORT = pl.CostEstimate(flops=10**6, bytes_accessed=2**16, transcendentals=0)
ANY = pl.BlockSpec(memory_space=pl.ANY)
WHOLE = pl.BlockSpec(memory_space=pltpu.VMEM)
SCALARS = pl.BlockSpec(memory_space=pltpu.SMEM)


def contract(left, right, left_dim, right_dim):
    return lax.dot_general(
        left, right, (((left_dim,), (right_dim,)), ((), ())), preferred_element_type=f32
    )


def pick_source(layer_no):
    section_no = lax.axis_index("section")
    same = lax.rem(lax.axis_index("dp"), 2) == lax.axis_index("tensor")
    return jnp.where(section_no == layer_no, 0, 1) + jnp.where(same, 0, 2)


def start_pick(source, candidates, target, sem):
    for number, candidate in enumerate(candidates):

        @pl.when(source == number)
        def _():
            pltpu.make_async_copy(candidate, target, sem).start()


def wait_pick(candidates, target, sem):
    pltpu.make_async_copy(candidates[0], target, sem).wait()


def small_row(small, row, width):
    count = width // small.shape[1]
    rows = [small[row + i : row + i + 1, :].astype(f32) for i in range(count)]
    return jnp.concatenate(rows, axis=1)


def vector_row(small, number, width):
    return small_row(small, 8 + 2 * number, width)


def small_part(candidates):
    return [candidate.at[0:PACK_ROWS] for candidate in candidates]


def norm_stats(value):
    mean = jnp.mean(value, axis=-1, keepdims=True)
    centred = value - mean
    variance = jnp.mean(centred * centred, axis=-1, keepdims=True)
    scale = lax.rsqrt(variance + NORM_EPS)
    return centred * scale, scale


def lane_masks():
    lane = lax.broadcasted_iota(jnp.int32, (1, 2 * HEAD), 1)
    return lane < HEAD, lane >= HEAD


def swap_halves(value):
    return pltpu.roll(value, HEAD, 1)


def listed_starts(blocks_ref, pair, block, n_blocks):
    found = []
    for slot in range(3):
        two = []
        for a in range(2):
            listed = blocks_ref[(2 * pair + a) * n_blocks + block, slot]
            two.append(pl.multiple_of(listed * BLOCK, BLOCK))
        found.append(tuple(two))
    return found


def pick_rows(table, part, cols, starts, in_first):
    pieces = [table[part, 0:BLOCK, cols]]
    for one, two in starts:
        pieces.append(
            jnp.where(
                in_first,
                table[part, pl.ds(one, BLOCK), cols],
                table[part, pl.ds(two, BLOCK), cols],
            )
        )
    return jnp.concatenate(pieces, axis=0)


def stack_heads(target, chunk, value, masks):
    for number in range(ROWS // BLOCK):
        block = value[number * BLOCK : (number + 1) * BLOCK]
        for a in range(2):
            target[chunk * (ROWS // BLOCK) + number, a * BLOCK : (a + 1) * BLOCK] = jnp.where(
                masks[a], block, 0.0
            ).astype(bf)


def feature_rows(pack, n_heads, head):
    at = PACK_SMALL + head * HEAD
    return pack[at : at + HEAD].astype(f32) + pack[at + n_heads * HEAD : at + (n_heads + 1) * HEAD].astype(f32)


def qkv_weight(pack, n_heads, width, part):
    at = PACK_SMALL + 4 * n_heads * HEAD + part * width
    return pack[at : at + width]


def out_weights(pack, n_heads, part_width):
    at = PACK_SMALL + 2 * n_heads * HEAD
    return [pack[at + part * part_width : at + (part + 1) * part_width] for part in range(2)]


def pack_kernel(wqkv_ref, wout_ref, features_ref, bqkv_ref, bup_ref, vector_ref, blocks_ref, pack_ref):
    n_features, feat = features_ref.shape
    n_parts, width, part_width = wqkv_ref.shape

    def lane_rows(value):
        value = value.astype(f32)
        return [
            value[row : row + 1, at : at + feat]
            for row in range(value.shape[0])
            for at in range(0, value.shape[1], feat)
        ]

    blank = jnp.zeros((1, feat), f32)
    rows = lane_rows(bqkv_ref[...]) + [blank] + lane_rows(bup_ref[...]) + lane_rows(vector_ref[...])
    rows += [blank] * (PACK_ROWS - len(rows))
    pack_ref[0:PACK_ROWS] = jnp.concatenate(rows, axis=0).astype(bf)
    n_listed, n_slots = blocks_ref.shape
    pack_ref[PACK_ROWS:PACK_SMALL] = jnp.zeros((PACK_SMALL - PACK_ROWS, feat), bf)
    pack_ref[PACK_ROWS : PACK_ROWS + n_listed, 0:n_slots] = blocks_ref[...].astype(f32).astype(bf)
    at = PACK_SMALL
    features = features_ref[...]
    high = features.astype(bf)
    pack_ref[at : at + n_features] = high
    pack_ref[at + n_features : at + 2 * n_features] = (features - high.astype(f32)).astype(bf)
    at += 2 * n_features
    for part in range(2):
        pack_ref[at : at + part_width] = wout_ref[:, part * feat : (part + 1) * feat]
        at += part_width
    for part in range(n_parts):
        pack_ref[at : at + width] = wqkv_ref[part]
        at += width


def pack_weights(wqkv, wout, features, bqkv, bup, vectors, blocks):
    n_parts, width, part_width = wqkv.shape
    n_features, feat = features.shape
    n_rows = PACK_SMALL + 2 * n_features + 2 * part_width + n_parts * width
    return pl.pallas_call(
        pack_kernel,
        out_shape=jax.ShapeDtypeStruct((n_rows, feat), bf),
        in_specs=[WHOLE] * 7,
        out_specs=WHOLE,
        compiler_params=pltpu.CompilerParams(vmem_limit_bytes=16 * MIB),
        cost_estimate=SHORT,
        name="pack_weights",
    )(wqkv, wout, features, bqkv, bup, vectors, blocks)


def attn_forward_kernel(layer_no, n_heads, length_ref, blocks_ref, *refs):
    if layer_no == 0:
        x_ref, refs = refs[0], refs[1:]
    else:
        rows_in, refs = refs[:3], refs[3:]
        small_prev, refs = refs[:4], refs[4:]
    pack_c, refs = refs[:4], refs[4:]
    if layer_no == 1:
        x_ref, refs = refs[0], refs[1:]
    (branch_ref, qkv_out, normed_out, probs_out, qf_out, kf_out, mt_out, mixed_out) = refs[:8]
    (pack, qkv, normed, probs, qfeat, kfeat, mt, mixed, fcat, perf, qstack,
     in_sem, out_sem) = refs[8:21]
    seq, width = normed.shape
    n_chunks = seq // ROWS
    pairs = n_heads // 2
    part_width = qkv.shape[2]
    feat = pack.shape[1]
    small = pack.at[0:PACK_ROWS]
    source = pick_source(layer_no)
    if layer_no == 1:
        small_before, hidden_ref, part_a, part_b, row_sem = refs[21:]
        row_loads = [
            pltpu.make_async_copy(item, target, row_sem.at[number])
            for number, (item, target) in enumerate(zip(rows_in, (hidden_ref, part_a, part_b)))
        ]
        for load in row_loads:
            load.start()
        before = pick_source(0)
        start_pick(before, small_part(small_prev), small_before, in_sem.at[1])
    start_pick(source, pack_c, pack, in_sem.at[0])
    wait_pick(pack_c, pack, in_sem.at[0])
    if layer_no == 1:
        wait_pick(small_part(small_prev), small_before, in_sem.at[1])
        for load in row_loads:
            load.wait()
    length = length_ref[0]
    gain = 1.0 + vector_row(small, 0, width)
    shift = vector_row(small, 1, width)

    @pl.loop(0, n_chunks)
    def _(chunk):
        rows = pl.ds(pl.multiple_of(chunk * ROWS, ROWS), ROWS)
        if layer_no == 0:
            x = x_ref[rows, :].astype(f32)
        else:
            total = part_a[rows, :].astype(f32) + part_b[rows, :].astype(f32)
            x_low = (hidden_ref[rows, :].astype(f32) + total + vector_row(small_before, 5, width)).astype(bf)
            x_ref[rows, :] = x_low
            x = x_low.astype(f32)
        zhat, _ = norm_stats(x)
        low = (zhat * gain + shift).astype(bf)
        normed[rows, :] = low
        for part in range(3):
            cols = n_heads * HEAD
            out = jnp.dot(low, qkv_weight(pack, n_heads, width, part), preferred_element_type=f32)
            qkv[part, rows, :] = (out + small_row(small, part, cols)).astype(bf)

    copies = [
        pltpu.make_async_copy(qkv, qkv_out, out_sem.at[0]),
        pltpu.make_async_copy(normed, normed_out, out_sem.at[1]),
    ]
    for copy in copies:
        copy.start()
    in_first, in_second = lane_masks()
    masks = (in_first, in_second)
    key_row = lax.broadcasted_iota(jnp.int32, (BLOCK, 2 * HEAD), 0)
    for pair in range(pairs):
        cols = slice(pair * 2 * HEAD, (pair + 1) * 2 * HEAD)
        zero = jnp.zeros((HEAD, feat), bf)
        for a in range(2):
            scaled = feature_rows(pack, n_heads, 2 * pair + a) * (F_SCALE * LOG2E)
            high = scaled.astype(bf)
            rest = (scaled - high.astype(f32)).astype(bf)
            for part, piece in enumerate((high, rest)):
                row = part * 2 * HEAD + a * HEAD
                fcat[row : row + HEAD, a * feat : (a + 1) * feat] = piece
                fcat[row : row + HEAD, (1 - a) * feat : (2 - a) * feat] = zero

        def features(vectors):
            proj = jnp.dot(
                jnp.concatenate([vectors, vectors], axis=1), fcat[...], preferred_element_type=f32
            )
            value = vectors.astype(f32)
            square = value * value * (0.5 * F_SCALE * F_SCALE * LOG2E)
            return [
                jnp.exp2(
                    proj[:, a * feat : (a + 1) * feat]
                    - jnp.sum(jnp.where(masks[a], square, 0.0), axis=-1, keepdims=True)
                )
                for a in range(2)
            ]

        @pl.loop(0, n_chunks)
        def _(chunk):
            base = pl.multiple_of(chunk * ROWS, ROWS)
            rows = pl.ds(base, ROWS)
            live = lax.broadcasted_iota(jnp.int32, (ROWS, 1), 0) + base < length
            found = features(qkv[1, rows, cols])
            for a in range(2):
                kfeat[pair, rows, a * feat : (a + 1) * feat] = jnp.where(live, found[a], 0.0).astype(bf)

        values = qkv[2, :, cols].astype(f32)
        for a in range(2):
            extended = jnp.where(masks[a], values, 1.0).astype(bf)
            moment = contract(extended, kfeat[pair, :, a * feat : (a + 1) * feat], 0, 0)
            mt[2 * pair + a] = moment.astype(bf)

        @pl.loop(0, n_chunks)
        def _(chunk):
            rows = pl.ds(pl.multiple_of(chunk * ROWS, ROWS), ROWS)
            query = qkv[0, rows, cols]
            found = features(query)
            out = None
            for a in range(2):
                low = found[a].astype(bf)
                qfeat[pair, rows, a * feat : (a + 1) * feat] = low
                numer = contract(low, mt[2 * pair + a], 1, 1)
                value = numer / swap_halves(numer)
                out = value if a == 0 else jnp.where(in_first, out, value)
            perf[rows, :] = out
            stack_heads(qstack, chunk, query.astype(f32) * (HEAD ** -0.5), masks)

        @pl.loop(0, seq // BLOCK, unroll=SPARSE_UNROLL)
        def _(block):
            rows = pl.ds(pl.multiple_of(block * BLOCK, BLOCK), BLOCK)
            starts = listed_starts(blocks_ref, pair, block, seq // BLOCK)
            keys = pick_rows(qkv, 1, cols, starts, in_first)
            values = pick_rows(qkv, 2, cols, starts, in_first)
            scores = contract(keys, qstack[block], 1, 1)
            pieces = [scores[:BLOCK]]
            for slot, (one, two) in enumerate(starts):
                room = length - jnp.where(in_first, one, two)
                piece = scores[(slot + 1) * BLOCK : (slot + 2) * BLOCK]
                pieces.append(jnp.where(key_row < room, piece, -1e30))
            scores = jnp.concatenate(pieces, axis=0)
            raw = jnp.exp(scores - jnp.max(scores, axis=0, keepdims=True))
            low = (raw * (1.0 / jnp.sum(raw, axis=0, keepdims=True))).astype(bf)
            probs[pair, block] = low
            both = contract(low, values, 0, 0)
            out = jnp.where(in_first, both[:BLOCK], both[BLOCK:])
            mixed[rows, cols] = (out + perf[rows, :]).astype(bf)

        more = [
            pltpu.make_async_copy(probs.at[pair], probs_out.at[pair], out_sem.at[2 + 4 * pair]),
            pltpu.make_async_copy(qfeat.at[pair], qf_out.at[pair], out_sem.at[3 + 4 * pair]),
            pltpu.make_async_copy(kfeat.at[pair], kf_out.at[pair], out_sem.at[4 + 4 * pair]),
            pltpu.make_async_copy(mt.at[2 * pair : 2 * pair + 2], mt_out.at[2 * pair : 2 * pair + 2], out_sem.at[5 + 4 * pair]),
        ]
        for copy in more:
            copy.start()
        copies += more

    @pl.loop(0, n_chunks)
    def _(chunk):
        rows = pl.ds(pl.multiple_of(chunk * ROWS, ROWS), ROWS)
        low = mixed[rows, :]
        mixed_out[rows, :] = low
        for part, weight in enumerate(out_weights(pack, n_heads, part_width)):
            here = slice(part * feat, (part + 1) * feat)
            branch_ref[rows, here] = jnp.dot(low, weight, preferred_element_type=f32).astype(bf)

    for copy in copies:
        copy.wait()


def attn_forward(layer_no, n_heads, length, blocks, x_parts, pack_c, small_before):
    part_width, feat = n_heads * HEAD, pack_c[0].shape[1]
    seq, width = x_parts[0].shape
    pairs = n_heads // 2
    shape = jax.ShapeDtypeStruct
    outs = [
        shape((seq, width), bf),
        shape((3, seq, part_width), bf),
        shape((seq, width), bf),
        shape((pairs, seq // BLOCK, 4 * BLOCK, 2 * HEAD), bf),
        shape((pairs, seq, 2 * feat), bf),
        shape((pairs, seq, 2 * feat), bf),
        shape((n_heads, 2 * HEAD, feat), bf),
        shape((seq, part_width), bf),
    ]
    out_specs = [WHOLE, ANY, ANY, ANY, ANY, ANY, ANY, WHOLE]
    scratch = [
        pltpu.VMEM(pack_c[0].shape, bf),
        pltpu.VMEM((3, seq, part_width), bf),
        pltpu.VMEM((seq, width), bf),
        pltpu.VMEM((pairs, seq // BLOCK, 4 * BLOCK, 2 * HEAD), bf),
        pltpu.VMEM((pairs, seq, 2 * feat), bf),
        pltpu.VMEM((pairs, seq, 2 * feat), bf),
        pltpu.VMEM((n_heads, 2 * HEAD, feat), bf),
        pltpu.VMEM((seq, part_width), bf),
        pltpu.VMEM((4 * HEAD, 2 * feat), bf),
        pltpu.VMEM((seq, 2 * HEAD), f32),
        pltpu.VMEM((seq // BLOCK, 2 * BLOCK, 2 * HEAD), bf),
        pltpu.SemaphoreType.DMA((2,)),
        pltpu.SemaphoreType.DMA((2 + 4 * pairs,)),
    ]
    operands = list(x_parts)
    specs = [WHOLE if layer_no == 0 else ANY] * len(x_parts)
    if layer_no == 1:
        operands += list(small_before)
        specs += [ANY] * 4
        outs = [shape((seq, width), bf)] + outs
        out_specs = [WHOLE] + out_specs
        scratch.append(pltpu.VMEM((PACK_ROWS, feat), bf))
        scratch += [pltpu.VMEM((seq, width), bf)] * 3 + [pltpu.SemaphoreType.DMA((3,))]
    operands += list(pack_c)
    specs += [ANY] * 4
    return pl.pallas_call(
        functools.partial(attn_forward_kernel, layer_no, n_heads),
        out_shape=outs,
        in_specs=[SCALARS, SCALARS] + specs,
        out_specs=out_specs,
        scratch_shapes=scratch,
        compiler_params=pltpu.CompilerParams(vmem_limit_bytes=60 * MIB),
        cost_estimate=SHORT,
        name=f"attn_forward_{layer_no}",
    )(length, blocks, *operands)


def gelu_parts(value):
    inverse = 1.0 / (1.0 + (0.3275911 * 0.5 ** 0.5) * jnp.abs(value))
    bell = jnp.exp2(value * value * (-0.5 * LOG2E))
    poly = inverse * (
        0.127414796
        + inverse
        * (-0.142248368 + inverse * (0.7107068705 + inverse * (-0.7265760135 + inverse * 0.5307027145)))
    )
    tail = poly * bell
    below = jnp.where(value >= 0.0, 1.0 - tail, tail)
    return value * below, below + value * bell * (0.5 / 3.141592653589793) ** 0.5


def down_rows(wide, width, at, step):
    part, row = at // width, at % width
    return wide[width + row : width + row + step, part * width : (part + 1) * width]


def ffn_forward_kernel(layer_no, *refs):
    x_ref, part_a, part_b = refs[:3]
    small_c, wide_c = refs[3:7], refs[7:11]
    out_ref, hidden_ref, normed_ref, active_ref, slope_ref = refs[11:16]
    small, wide, sems = refs[16:]

    @pl.when(pl.program_id(0) == 0)
    def _():
        source = pick_source(layer_no)
        start_pick(source, small_part(small_c), small, sems.at[0])
        start_pick(source, wide_c, wide, sems.at[1])
        wait_pick(small_part(small_c), small, sems.at[0])
        wait_pick(wide_c, wide, sems.at[1])

    width = x_ref.shape[1]
    units = wide.shape[1]
    branch = part_a[...].astype(f32) + part_b[...].astype(f32)
    hidden = x_ref[...].astype(f32) + branch + vector_row(small, 4, width)
    hidden_ref[...] = hidden.astype(bf)
    zhat, _ = norm_stats(hidden)
    low = (zhat * (1.0 + vector_row(small, 2, width)) + vector_row(small, 3, width)).astype(bf)
    normed_ref[...] = low
    total = None
    step = 256
    for at in range(0, units, step):
        upper = jnp.dot(low, wide[:width, at : at + step], preferred_element_type=f32)
        active, slope = gelu_parts(upper + small_row(small, 4 + at // step, step))
        active = active.astype(bf)
        active_ref[:, at : at + step] = active
        slope_ref[:, at : at + step] = slope.astype(bf)
        term = jnp.dot(active, down_rows(wide, width, at, step), preferred_element_type=f32)
        total = term if total is None else total + term
    out_ref[...] = total.astype(bf)


def ffn_forward(layer_no, x, part_a, part_b, weights):
    small_c, wide_c = weights
    seq, width = x.shape
    units = wide_c[0].shape[1]
    shape = jax.ShapeDtypeStruct
    rows = lambda cols: pl.BlockSpec((FFN_ROWS, cols), lambda i: (i, 0))
    return pl.pallas_call(
        functools.partial(ffn_forward_kernel, layer_no),
        grid=(seq // FFN_ROWS,),
        out_shape=[
            shape((seq, width), bf),
            shape((seq, width), bf),
            shape((seq, width), bf),
            shape((seq, units), bf),
            shape((seq, units), bf),
        ],
        in_specs=[rows(width)] * 3 + [ANY] * 8,
        out_specs=[rows(width), rows(width), rows(width), rows(units), rows(units)],
        scratch_shapes=[
            pltpu.VMEM((PACK_ROWS, small_c[0].shape[1]), bf),
            pltpu.VMEM(wide_c[0].shape, bf),
            pltpu.SemaphoreType.DMA((2,)),
        ],
        compiler_params=pltpu.CompilerParams(vmem_limit_bytes=(60, 22)[layer_no] * MIB),
        cost_estimate=SHORT,
        name=f"ffn_forward_{layer_no}",
    )(x, part_a, part_b, *small_c, *wide_c)


def ffn_backward_kernel(layer_no, grad_ref, slope_ref, *refs):
    wide_c = refs[:4]
    out_ref, gupper_ref, bias_ref = refs[4:7]
    wide, sems = refs[7:]

    @pl.when(pl.program_id(0) == 0)
    def _():
        source = pick_source(layer_no)
        start_pick(source, wide_c, wide, sems.at[0])
        bias_ref[...] = jnp.zeros_like(bias_ref)
        wait_pick(wide_c, wide, sems.at[0])

    width = grad_ref.shape[1]
    units = wide.shape[1]
    grad = grad_ref[...]
    total = None
    step = 256
    for at in range(0, units, step):
        gactive = contract(grad, down_rows(wide, width, at, step), 1, 1)
        gupper = (gactive * slope_ref[:, at : at + step].astype(f32)).astype(bf)
        gupper_ref[:, at : at + step] = gupper
        bias_ref[:, at : at + step] += fold_rows(gupper.astype(f32))
        term = contract(gupper, wide[:width, at : at + step], 1, 1)
        total = term if total is None else total + term
    out_ref[...] = total.astype(bf)


def fold_rows(value):
    rows, cols = value.shape
    return jnp.sum(value.reshape(rows // 8, 8, cols), axis=0)


def ffn_backward(layer_no, grad, slope, weights):
    (wide_c,) = weights
    seq, width = grad.shape
    units = wide_c[0].shape[1]
    shape = jax.ShapeDtypeStruct
    rows = lambda cols: pl.BlockSpec((FFN_ROWS, cols), lambda i: (i, 0))
    return pl.pallas_call(
        functools.partial(ffn_backward_kernel, layer_no),
        grid=(seq // FFN_ROWS,),
        out_shape=[shape((seq, width), bf), shape((seq, units), bf), shape((8, units), f32)],
        in_specs=[rows(width), rows(units)] + [ANY] * 4,
        out_specs=[rows(width), rows(units), pl.BlockSpec((8, units), lambda i: (0, 0))],
        scratch_shapes=[
            pltpu.VMEM(wide_c[0].shape, bf),
            pltpu.SemaphoreType.DMA((1,)),
        ],
        compiler_params=pltpu.CompilerParams(vmem_limit_bytes=18 * MIB),
        cost_estimate=SHORT,
        name=f"ffn_backward_{layer_no}",
    )(grad, slope, *wide_c)


def attn_backward_kernel(layer_no, n_heads, blocks_ref, *refs):
    rows_in = refs[:5]
    qkv_in, probs_in, qf_in, kf_in, mt_in = refs[5:10]
    pack_c, refs = refs[10:14], refs[14:]
    out_ref, gbranch_ref, dqkv_ref, first_ref, vec_ref, bias_ref, refs = *refs[:6], refs[6:]
    (pack, qkv, probs, qfeat, kfeat, mt, gmix, gstack, qstack, gext, gt, fback,
     dq, dk, dv, gy_ref, part_a, part_b, hidden_ref, x_ref, sem, row_sem) = refs
    seq, width = gy_ref.shape
    n_chunks = seq // ROWS
    pairs = n_heads // 2
    part_width = qkv.shape[2]
    feat = pack.shape[1]
    small = pack.at[0:PACK_ROWS]
    source = pick_source(layer_no)
    start_pick(source, pack_c, pack, sem.at[0])
    row_loads = [
        pltpu.make_async_copy(item, target, row_sem.at[number])
        for number, (item, target) in enumerate(
            zip(rows_in, (gy_ref, part_a, part_b, hidden_ref, x_ref))
        )
    ]
    for load in row_loads:
        load.start()
    loads = [
        pltpu.make_async_copy(qkv_in, qkv, sem.at[2]),
        pltpu.make_async_copy(mt_in, mt, sem.at[3]),
        pltpu.make_async_copy(qf_in, qfeat, sem.at[4]),
        pltpu.make_async_copy(kf_in, kfeat, sem.at[5]),
        pltpu.make_async_copy(probs_in, probs, sem.at[6]),
    ]
    for load in loads:
        load.start()
    first_ref[...] = jnp.zeros_like(first_ref)
    vec_ref[...] = jnp.zeros_like(vec_ref)
    bias_ref[...] = jnp.zeros_like(bias_ref)
    wait_pick(pack_c, pack, sem.at[0])
    for load in row_loads[:4]:
        load.wait()
    gain = 1.0 + vector_row(small, 2, width)
    in_first, in_second = lane_masks()
    masks = (in_first, in_second)

    @pl.loop(0, n_chunks)
    def _(chunk):
        rows = pl.ds(pl.multiple_of(chunk * ROWS, ROWS), ROWS)
        gnormed = part_a[rows, :].astype(f32) + part_b[rows, :].astype(f32)
        zhat, scale = norm_stats(hidden_ref[rows, :].astype(f32))
        scaled = gnormed * gain
        gy = gy_ref[rows, :].astype(f32)
        mean_one = jnp.mean(scaled, axis=-1, keepdims=True)
        mean_two = jnp.mean(scaled * zhat, axis=-1, keepdims=True)
        ghidden = gy + (scaled - mean_one - zhat * mean_two) * scale
        low = ghidden.astype(bf)
        gbranch_ref[rows, :] = low
        vec_ref[0] += fold_rows(gnormed * zhat)
        vec_ref[1] += fold_rows(gnormed)
        vec_ref[2] += fold_rows(low.astype(f32))
        vec_ref[3] += fold_rows(gy)
        first, second = out_weights(pack, n_heads, part_width)
        gmix[rows, :] = (contract(low[:, :feat], first, 1, 1) + contract(low[:, feat:], second, 1, 1)).astype(bf)

    for load in loads[:4]:
        load.wait()
    for pair in range(pairs):
        cols = slice(pair * 2 * HEAD, (pair + 1) * 2 * HEAD)
        for a in range(2):
            plain = feature_rows(pack, n_heads, 2 * pair + a) * F_SCALE
            high = plain.astype(bf).astype(f32)
            ones = jnp.ones((HEAD, feat), f32)
            none = jnp.zeros((HEAD, feat), f32)
            stack = [high, ones] if a == 0 else [ones, high]
            stack += [plain - high, none] if a == 0 else [none, plain - high]
            fback[a] = jnp.concatenate(stack, axis=0).astype(bf)

        def feature_back(a, gfeat, feats, vectors):
            gexpo = (gfeat * feats.astype(f32)).astype(bf)
            both = contract(gexpo, fback[a], 1, 1)
            both = both[:, : 2 * HEAD] + both[:, 2 * HEAD :]
            return both - (F_SCALE * F_SCALE) * swap_halves(both) * vectors

        @pl.loop(0, n_chunks)
        def _(chunk):
            rows = pl.ds(pl.multiple_of(chunk * ROWS, ROWS), ROWS)
            grad = gmix[rows, cols].astype(f32)
            query = qkv[0, rows, cols].astype(f32)
            out = None
            for a in range(2):
                feats = qfeat[pair, rows, a * feat : (a + 1) * feat]
                moment = mt[2 * pair + a]
                numer = contract(feats, moment, 1, 1)
                inverse = 1.0 / swap_halves(numer)
                gnumer = grad * inverse
                other = swap_halves(gnumer * numer * inverse)
                both = jnp.where(masks[a], gnumer, -other).astype(bf)
                gext[a, rows, :] = both
                gfeat = jnp.dot(both, moment, preferred_element_type=f32)
                value = feature_back(a, gfeat, feats, query)
                out = value if a == 0 else jnp.where(in_first, out, value)
            dq[rows, :] = out
            stack_heads(gstack, chunk, grad, masks)
            stack_heads(qstack, chunk, query * (HEAD ** -0.5), masks)

        for a in range(2):
            gt[a] = contract(gext[a], qfeat[pair, :, a * feat : (a + 1) * feat], 0, 0).astype(bf)

        @pl.loop(0, n_chunks)
        def _(chunk):
            rows = pl.ds(pl.multiple_of(chunk * ROWS, ROWS), ROWS)
            key = qkv[1, rows, cols].astype(f32)
            value_f = qkv[2, rows, cols].astype(f32)
            dk_out, dv_out = None, None
            for a in range(2):
                extended = jnp.where(masks[a], value_f, 1.0).astype(bf)
                feats = kfeat[pair, rows, a * feat : (a + 1) * feat]
                gfeat = jnp.dot(extended, gt[a], preferred_element_type=f32)
                dk_one = feature_back(a, gfeat, feats, key)
                dv_one = contract(feats, gt[a], 1, 1)
                dk_out = dk_one if a == 0 else jnp.where(in_first, dk_out, dk_one)
                dv_out = dv_one if a == 0 else jnp.where(in_first, dv_out, dv_one)
            dk[rows, :] = dk_out
            dv[rows, :] = dv_out

        if pair == 0:
            loads[4].wait()

        @pl.loop(0, seq // BLOCK, unroll=SPARSE_UNROLL)
        def _(block):
            rows = pl.ds(pl.multiple_of(block * BLOCK, BLOCK), BLOCK)
            starts = listed_starts(blocks_ref, pair, block, seq // BLOCK)
            keys = pick_rows(qkv, 1, cols, starts, in_first)
            values = pick_rows(qkv, 2, cols, starts, in_first)
            weights = probs[pair, block]
            weights_f = weights.astype(f32)
            grad = gstack[block]
            gweights = contract(values, grad, 1, 1)
            inner = jnp.sum(weights_f * gweights, axis=0, keepdims=True)
            gscores = (weights_f * (gweights - inner)).astype(bf)
            both = contract(gscores, keys, 0, 0)
            out = jnp.where(in_first, both[:BLOCK], both[BLOCK:]) * (HEAD ** -0.5)
            dkeys = jnp.dot(gscores, qstack[block], preferred_element_type=f32)
            dvalues = jnp.dot(weights, grad, preferred_element_type=f32)
            for total, part in ((dk, dkeys), (dv, dvalues)):
                total[0:BLOCK, :] += part[:BLOCK]
                for slot, (one, two) in enumerate(starts):
                    piece = part[(slot + 1) * BLOCK : (slot + 2) * BLOCK]
                    total[pl.ds(one, BLOCK), :] += jnp.where(in_first, piece, 0.0)
                    total[pl.ds(two, BLOCK), :] += jnp.where(in_first, 0.0, piece)
            dq[rows, :] += out

        @pl.loop(0, n_chunks)
        def _(chunk):
            rows = pl.ds(pl.multiple_of(chunk * ROWS, ROWS), ROWS)
            for part, total in enumerate((dq, dk, dv)):
                low = total[rows, :].astype(bf)
                dqkv_ref[part, rows, cols] = low
                bias_ref[part, :, cols] += fold_rows(low.astype(f32))


    row_loads[4].wait()

    @pl.loop(0, n_chunks)
    def _(chunk):
        rows = pl.ds(pl.multiple_of(chunk * ROWS, ROWS), ROWS)
        total = None
        for part in range(3):
            term = contract(dqkv_ref[part, rows, :], qkv_weight(pack, n_heads, width, part), 1, 1)
            total = term if total is None else total + term
        low = total.astype(bf)
        out_ref[rows, :] = low
        zhat, _ = norm_stats(x_ref[rows, :].astype(f32))
        total = low.astype(f32)
        first_ref[0] += fold_rows(total * zhat)
        first_ref[1] += fold_rows(total)


def attn_backward(layer_no, n_heads, blocks, gy, part_a, part_b, hidden, x, kept, pack_c):
    seq, width = gy.shape
    part_width, feat = n_heads * HEAD, pack_c[0].shape[1]
    pairs = n_heads // 2
    shape = jax.ShapeDtypeStruct
    operands = [gy, part_a, part_b, hidden, x, *kept, *pack_c]
    return pl.pallas_call(
        functools.partial(attn_backward_kernel, layer_no, n_heads),
        out_shape=[
            shape((seq, width), bf),
            shape((seq, width), bf),
            shape((3, seq, part_width), bf),
            shape((2, 8, width), f32),
            shape((4, 8, width), f32),
            shape((3, 8, part_width), f32),
        ],
        in_specs=[SCALARS] + [ANY] * 14,
        out_specs=[WHOLE] * 6,
        scratch_shapes=[
            pltpu.VMEM(pack_c[0].shape, bf),
            pltpu.VMEM((3, seq, part_width), bf),
            pltpu.VMEM((pairs, seq // BLOCK, 4 * BLOCK, 2 * HEAD), bf),
            pltpu.VMEM((pairs, seq, 2 * feat), bf),
            pltpu.VMEM((pairs, seq, 2 * feat), bf),
            pltpu.VMEM((n_heads, 2 * HEAD, feat), bf),
            pltpu.VMEM((seq, part_width), bf),
            pltpu.VMEM((seq // BLOCK, 2 * BLOCK, 2 * HEAD), bf),
            pltpu.VMEM((seq // BLOCK, 2 * BLOCK, 2 * HEAD), bf),
            pltpu.VMEM((2, seq, 2 * HEAD), bf),
            pltpu.VMEM((2, 2 * HEAD, feat), bf),
            pltpu.VMEM((2, 4 * HEAD, feat), bf),
            pltpu.VMEM((seq, 2 * HEAD), f32),
            pltpu.VMEM((seq, 2 * HEAD), f32),
            pltpu.VMEM((seq, 2 * HEAD), f32),
            *[pltpu.VMEM((seq, width), bf)] * 5,
            pltpu.SemaphoreType.DMA((7,)),
            pltpu.SemaphoreType.DMA((5,)),
        ],
        compiler_params=pltpu.CompilerParams(vmem_limit_bytes=(53, 46)[layer_no] * MIB),
        cost_estimate=SHORT,
        name=f"attn_backward_{layer_no}",
    )(blocks, *operands)


def norm_backward_kernel(layer_no, x_ref, part_a, part_b, ghidden_ref, *refs):
    small_c = refs[:4]
    low_ref, small, sems = refs[4:]

    @pl.when(pl.program_id(0) == 0)
    def _():
        start_pick(pick_source(layer_no), small_part(small_c), small, sems.at[0])
        wait_pick(small_part(small_c), small, sems.at[0])

    width = x_ref.shape[1]
    gnormed = part_a[...].astype(f32) + part_b[...].astype(f32)
    zhat, scale = norm_stats(x_ref[...].astype(f32))
    scaled = gnormed * (1.0 + vector_row(small, 0, width))
    mean_one = jnp.mean(scaled, axis=-1, keepdims=True)
    mean_two = jnp.mean(scaled * zhat, axis=-1, keepdims=True)
    total = ghidden_ref[...].astype(f32) + (scaled - mean_one - zhat * mean_two) * scale
    low_ref[...] = total.astype(bf)


def norm_backward(layer_no, x, part_a, part_b, ghidden, small_c):
    seq, width = x.shape
    shape = jax.ShapeDtypeStruct
    rows = pl.BlockSpec((FFN_ROWS, width), lambda i: (i, 0))
    return pl.pallas_call(
        functools.partial(norm_backward_kernel, layer_no),
        grid=(seq // FFN_ROWS,),
        out_shape=shape((seq, width), bf),
        in_specs=[rows] * 4 + [ANY] * 4,
        out_specs=rows,
        scratch_shapes=[pltpu.VMEM((PACK_ROWS, small_c[0].shape[1]), bf), pltpu.SemaphoreType.DMA((1,))],
        compiler_params=pltpu.CompilerParams(vmem_limit_bytes=(60, 12)[layer_no] * MIB),
        cost_estimate=SHORT,
        name=f"norm_backward_{layer_no}",
    )(x, part_a, part_b, ghidden, *small_c)


def tiny_rows(first, moved, vec, bias_qkv, bias_up):
    half = vec.shape[2] // 2
    here = pl.ds(pl.multiple_of(lax.rem(lax.axis_index("dp"), 2) * half, half), half)
    total = lambda value: jnp.sum(value, axis=0, keepdims=True)
    rows = [total(first[i, :, here] + moved[i, :, here]) for i in range(2)]
    rows += [total(vec[i, :, here]) for i in range(4)]
    rows += [total(bias_qkv[i]) for i in range(3)] + [total(bias_up[...])]
    return [row[:, at : at + LANES] for row in rows for at in range(0, row.shape[1], LANES)]


def weight_grad_kernel(n_first, n_extra, left_a, left_b, right_a, right_b, *refs):
    keep_ref, away_ref, turned = refs[-3:]
    extra, sums = refs[:n_extra], refs[n_extra:-3]
    step = pl.program_id(0)
    shard = left_a.shape[1] // lax.axis_size("dp")
    per_half = pl.num_programs(0) // 2
    width = right_a.shape[1]
    n_rows = left_a.shape[1]
    first = step < n_first

    @pl.when(step == 0)
    def _():
        turned[...] = left_a[...].T
        for source, target in zip(extra, (keep_ref, away_ref)):
            target[:, per_half * width :] = source[...]
        if sums:
            rows = tiny_rows(*sums[:5]) + tiny_rows(*sums[5:])
            low = jnp.concatenate(rows, axis=0).astype(bf)
            low = jnp.concatenate([low, jnp.zeros((shard - low.shape[0], LANES), bf)], axis=0)
            for target in (keep_ref, away_ref):
                for at in range(0, n_rows, shard):
                    target[at : at + shard, per_half * width :] = low

    @pl.when(step == n_first)
    def _():
        turned[...] = left_b[...].T

    right = jnp.where(first, right_a[...], right_b[...])
    result = jnp.dot(turned[...], right, preferred_element_type=f32).astype(bf)
    here = pl.ds(pl.multiple_of(lax.rem(step, per_half) * width, width), width)
    keep = step // per_half == lax.axis_index("section")
    for wanted, target in ((keep, keep_ref), (jnp.logical_not(keep), away_ref)):

        @pl.when(wanted)
        def _():
            target[:n_rows, here] = result


def weight_grads(name, step, left_a, right_a, left_b, right_b, extra=(), sums=()):
    seq, width = left_a.shape
    if right_a.ndim == 3:
        n_first = right_a.shape[0]
        spec_a = pl.BlockSpec((None, seq, step), lambda i: (jnp.minimum(i, n_first - 1), 0, 0))
    else:
        n_first = right_a.shape[1] // step
        spec_a = pl.BlockSpec((seq, step), lambda i: (0, jnp.minimum(i, n_first - 1)))
    n_second = right_b.shape[1] // step
    spec_b = pl.BlockSpec((seq, step), lambda i: (0, jnp.maximum(i - n_first, 0)))
    whole = pl.BlockSpec((seq, width), lambda i: (0, 0))
    n_steps = n_first + n_second
    cols = step * (n_steps // 2) + (extra[0].shape[1] if extra else 0)
    shape = (width, cols + (LANES if sums else 0))
    fixed = lambda shape: pl.BlockSpec(shape, lambda i: (0,) * len(shape))
    return pl.pallas_call(
        functools.partial(weight_grad_kernel, n_first, len(extra)),
        grid=(n_steps,),
        out_shape=[jax.ShapeDtypeStruct(shape, bf)] * 2,
        in_specs=[whole, whole, spec_a, spec_b] + [fixed(item.shape) for item in (*extra, *sums)],
        out_specs=[fixed(shape)] * 2,
        scratch_shapes=[pltpu.VMEM((width, seq), bf)],
        compiler_params=pltpu.CompilerParams(vmem_limit_bytes=20 * MIB),
        cost_estimate=SHORT,
        name=name,
    )(left_a, left_b, right_a, right_b, *extra, *sums)


ALL_AXES = ("section", "tensor", "dp")


def send(value, sizes, target):
    n_section, n_tensor, n_dp = sizes
    pairs = []
    for s in range(n_section):
        for t in range(n_tensor):
            for d in range(n_dp):
                goal = target(s, t, d // 2, d % 2)
                if goal is not None:
                    gs, gt, gz, gc = goal
                    number = (s * n_tensor + t) * n_dp + d
                    pairs.append((number, (gs * n_tensor + gt) * n_dp + 2 * gz + gc))
    return lax.ppermute(value, ALL_AXES, pairs)


def other_core(value, sizes):
    return send(value, sizes, lambda s, t, z, c: (s, t, z, 1 - c))


def chip_shards(
    sizes,
    inputs,
    cotangent,
    lengths,
    blocks,
    feature_map,
    w_qkv,
    b_qkv,
    w_out,
    w_up,
    b_up,
    w_down,
    vector_params,
):
    n_dp = sizes[2]
    n_z = n_dp // 2
    section_no = lax.axis_index("section")
    tensor_no = lax.axis_index("tensor")
    dp_no = lax.axis_index("dp")
    z_no, core = dp_no // 2, dp_no % 2
    same = core == tensor_no
    is_first = section_no == 0
    width = inputs.shape[2]
    half = inputs.shape[1]
    n_heads, n_blocks, n_listed = blocks.shape[1:]
    feat = feature_map.shape[3]
    part_width = w_qkv.shape[3]

    def after(value, earlier):
        return lax.optimization_barrier((value, earlier))[0]

    def share_y(array):
        return send(array, sizes, lambda s, t, z, c: (1 - s, t, z, c) if c == t else None)

    def share_x(array):
        return send(array, sizes, lambda s, t, z, c: (s, 1 - t, z, c) if c == t else None)

    wide = jnp.concatenate(
        [w_up[0], jnp.concatenate([w_down[0][:width], w_down[0][width:]], axis=1)], axis=0
    )
    def halves(own, first, second):
        near = jnp.where(same, own, first)
        far = jnp.where(same, first, second)
        swap = tensor_no == 1
        return jnp.concatenate(
            [jnp.where(swap, far, near), jnp.where(swap, near, far)], axis=0
        )

    def cross(own):
        return send(
            own,
            sizes,
            lambda s, t, z, c: (s, t, z, 1 - c) if c == t else (s, 1 - t, z, c),
        )

    def to_sequence(own, first):
        second = send(first, sizes, lambda s, t, z, c: (s, t, z, 1 - c) if c == t else None)
        return halves(own, first, second)

    x_own = inputs[section_no]
    x_arrived = cross(x_own)
    pack = pack_weights(
        w_qkv[0].transpose(1, 0, 2),
        w_out[0],
        feature_map[0].reshape(n_heads * HEAD, feat),
        b_qkv[0],
        b_up,
        vector_params[0],
        blocks[0].reshape(n_heads * n_blocks, n_listed),
    )
    x_first = to_sequence(x_own, x_arrived)
    pack_y = share_y(pack)
    pack_x = share_x(pack)
    pack_both = share_x(after(pack_y, pack_x))
    pack_c = (pack, pack_y, pack_x, pack_both)
    wide_y = share_y(after(wide, pack_y))

    def share_wide(layer_no, earlier):
        def share(array, section):
            return send(
                after(array, earlier),
                sizes,
                lambda s, t, z, c: (s, 1 - t, z, c) if c == t and s == section else None,
            )

        return (wide, wide_y, share(wide, layer_no), share(wide_y, 1 - layer_no))

    lengths_here = jnp.where(same, lengths, other_core(lengths, sizes))
    length = lax.dynamic_slice_in_dim(lengths_here[:, 0], section_no, 1)

    weights = [(pack_c, share_wide(0, (pack_both, x_first, length)))]

    def of_layer(layer_no, candidates):
        mine = section_no == layer_no
        return jnp.where(
            same,
            jnp.where(mine, candidates[0], candidates[1]),
            jnp.where(mine, candidates[2], candidates[3]),
        )

    def exchange(value):
        return value, other_core(value, sizes)

    kept = []
    x_parts = (x_first,)
    outputs = []
    for layer_no in range(2):
        listed = of_layer(
            layer_no,
            [item[PACK_ROWS : PACK_ROWS + n_heads * n_blocks, :n_listed] for item in pack_c],
        )
        listed = listed.astype(jnp.int32)
        made = attn_forward(layer_no, n_heads, length, listed, x_parts, pack_c, pack_c)
        if layer_no == 0:
            x = x_first
        else:
            x, made = made[0], made[1:]
            outputs.append(x)
        branch, qkv, normed, probs, qfeat, kfeat, mt, mixed = made
        if layer_no == 0:
            grad_own = after(cotangent[section_no], (weights[0][1][2:], branch))
            grad_arrived = cross(grad_own)
            weights.append((pack_c, share_wide(1, (weights[0][1][2:], branch))))
        result, hidden, normed_two, active, slope = ffn_forward(
            layer_no, x, *exchange(branch), weights[layer_no]
        )
        x_parts = (hidden, *exchange(result))
        kept.append(
            (x, normed, mixed, hidden, normed_two, active, slope, listed,
             (qkv, probs, qfeat, kfeat, mt))
        )

    grad = to_sequence(grad_own, grad_arrived)

    def my_half(array):
        return lax.dynamic_slice_in_dim(array, core * half, half)

    def deliver(first_rows, second_rows):
        mine = jnp.where(is_first, first_rows, second_rows)
        theirs = jnp.where(is_first, second_rows, first_rows)
        own = send(mine, sizes, lambda s, t, z, c: (s, c, z, t))
        other = send(theirs, sizes, lambda s, t, z, c: (1 - s, c, z, t))
        return own, other

    hidden, part_a, part_b = x_parts
    last_bias = of_layer(1, [lane[18:20].reshape(1, width) for lane in pack_c]).astype(f32)
    last = my_half(hidden).astype(f32) + (my_half(part_a).astype(f32) + my_half(part_b).astype(f32)) + last_bias

    def plane_send(keep, away, hold=None):
        by_x = send(keep, sizes, lambda s, t, z, c: None if c == t else (s, 1 - t, z, c))
        by_y = share_y(away)
        late = away if hold is None else after(away, hold)
        by_both = send(late, sizes, lambda s, t, z, c: None if c == t else (1 - s, 1 - t, z, c))
        return keep, by_x, by_y, by_both

    def plane_sum(terms):
        total = terms[0].astype(f32)
        for term in terms[1:]:
            total = total + term.astype(f32)
        return total.astype(bf)

    def line_send(arrays):
        def shard_for(step):
            at = ((z_no + step) % n_z) * pair
            rows = [lax.dynamic_slice_in_dim(array, at, pair) for array in arrays]
            return jnp.concatenate(rows, axis=1)

        def turn(step):
            return lambda s, t, z, c: (s, t, (z + step) % n_z, c) if c == t else None

        return [shard_for(0)] + [
            send(shard_for(step), sizes, turn(step)) for step in range(1, n_z)
        ]

    def line_sum(found):
        total = found[0].astype(f32)
        for part in found[1:]:
            total = total + part.astype(f32)
        return total

    def ffn_part(layer_no, grad, hold):
        normed_two, active, slope = kept[layer_no][4:7]
        gnormed_two, gupper, bias_up = ffn_backward(
            layer_no, after(grad, hold), slope, (weights[layer_no][1],)
        )
        parts = exchange(gnormed_two)
        return parts, gupper, bias_up

    def ffn_grads(layer_no, grad, gupper, hold, extra=()):
        normed_two, active = kept[layer_no][4:6]
        return weight_grads(
            f"ffn_grads_{layer_no}", 512, after(normed_two, hold), gupper, grad, active, extra
        )

    def attn_part(layer_no, grad, parts, hold):
        hidden, listed, attn_kept = kept[layer_no][3], kept[layer_no][7], kept[layer_no][8]
        gnormed, *rest = attn_backward(
            layer_no, n_heads, listed, grad, after(parts[0], hold), parts[1], hidden,
            kept[layer_no][0], attn_kept, pack_c,
        )
        gbranch, gproj, vec_one, vec_two, bias_qkv = rest
        sums = (vec_one, other_core(vec_one, sizes), vec_two, bias_qkv)
        return exchange(gnormed), gbranch, gproj, sums

    def attn_grads(layer_no, gproj, gbranch, hold, sums=()):
        normed, mixed = kept[layer_no][1:3]
        return weight_grads(
            f"attn_grads_{layer_no}", part_width, after(normed, hold), gproj, gbranch, mixed, (), sums
        )

    def norm_part(layer_no, parts, gbranch, hold):
        return norm_backward(
            layer_no, kept[layer_no][0], after(parts[0], hold), parts[1], gbranch, pack_c
        )

    shard, pair = width // n_dp, width // n_z
    units = wide.shape[1]
    parts, gupper, bias_up = ffn_part(1, grad, x_parts[0])
    keep, away = ffn_grads(1, grad, gupper, parts[0])
    parts, gbranch, gproj, sums = attn_part(1, grad, parts, (keep, x_parts))
    wide_one = plane_send(keep, away, gbranch)
    sums_one = (*sums, bias_up)
    extra = attn_grads(1, gproj, gbranch, parts[0])
    grad = norm_part(1, parts, gbranch, extra[0])
    upper_grad = grad
    parts, gupper, bias_up = ffn_part(0, grad, grad)
    keep, away = ffn_grads(0, grad, gupper, parts[0], extra)
    keep, away, wide_one = after((keep, away, wide_one), keep)
    wide_zero = plane_send(keep, away)
    parts, gbranch, gproj, sums = attn_part(0, grad, parts, (keep, wide_one))
    wide_zero, wide_one = after((wide_zero, wide_one), gbranch)
    keep, away = attn_grads(
        0, gproj, gbranch, parts[0], (*sums_one, *sums, bias_up)
    )
    keep, away, wide_zero, wide_one = after((keep, away, wide_zero, wide_one), keep)
    keep, away, parts = after((keep, away, parts), (wide_zero, parts))
    narrow_zero = plane_send(keep, away)
    out_pair = deliver(*after((my_half(outputs[0]), last.astype(bf)), narrow_zero))
    line_wide = line_send([plane_sum(wide_one), plane_sum(wide_zero)])
    grad = norm_part(0, parts, gbranch, keep)
    line_narrow = line_send([after(plane_sum(narrow_zero), (line_wide, out_pair))])
    grad_pair = deliver(*after((my_half(grad), my_half(upper_grad)), line_narrow[0]))
    line_narrow = line_sum(after(line_narrow, grad_pair))
    line_wide = line_sum(line_wide)
    n_narrow = line_narrow.shape[1] - LANES
    rest = line_narrow[:, n_narrow:]
    first_sum = jnp.concatenate([line_wide[:, units : 2 * units], line_narrow], axis=1)
    second_sum = jnp.concatenate([line_wide[:, :units], line_wide[:, 2 * units :], rest], axis=1)

    def for_core(layer, number):
        return lax.dynamic_slice_in_dim(layer, number * shard, shard)

    mine = jnp.where(is_first, first_sum, second_sum)
    theirs = jnp.where(is_first, second_sum, first_sum)

    def cast(value, target):
        return send(
            value.astype(bf), sizes, lambda s, t, z, c: target(s, t, z) if c == t else None
        ).astype(f32)

    near = cast(for_core(mine, 1 - core), lambda s, t, z: (s, t, z, 1 - t))
    far = cast(for_core(theirs, core), lambda s, t, z: (1 - s, t, z, t))
    cross_far = cast(for_core(theirs, 1 - core), lambda s, t, z: (1 - s, t, z, 1 - t))
    stay = jnp.where(same, for_core(mine, core), near)
    arrived = jnp.where(same, far, cross_far)
    low_half = jnp.where(is_first, stay, arrived)
    high_half = jnp.where(is_first, arrived, stay)
    grad_up, grad_down = low_half[:, :units], high_half[:, :units]
    narrow = jnp.concatenate(
        [low_half[:, units : units + n_narrow], high_half[:, units : units + n_narrow]], axis=1
    )
    rows = stay[:, units + n_narrow :]
    n_rows = 9 * (width // 2 // LANES) + units // LANES
    rows = jnp.where(is_first, rows[n_rows : 2 * n_rows], rows[:n_rows])
    halves_found = rows[: n_rows - units // LANES].reshape(9, width // 2)

    def own_columns(array):
        cols = array.reshape(-1, n_dp, array.shape[1] // n_dp)
        return lax.dynamic_index_in_dim(cols, dp_no, axis=1, keepdims=False)

    grad_vectors = own_columns(halves_found[:6])
    grad_bqkv = own_columns(halves_found[6:])
    grad_bup = own_columns(rows[n_rows - units // LANES :].reshape(1, -1))[0]

    def placed(pair, dtype):
        own, other = pair
        return jnp.stack(
            [jnp.where(is_first, own, other), jnp.where(is_first, other, own)]
        )[None].astype(dtype)

    section_outputs = placed(out_pair, bf)
    input_grads = placed(grad_pair, f32)
    grad_qkv = narrow[:, : 3 * part_width].reshape(shard, 3, part_width)
    grad_out = narrow[:, 3 * part_width :].T
    return (
        section_outputs,
        input_grads,
        grad_qkv[None],
        grad_bqkv[None],
        grad_out[None],
        grad_up[None],
        grad_bup[None],
        grad_down.T[None],
        grad_vectors[None],
    )


HEAD = 64
BLOCK = 64
SEQ_LEN = 1024


norm_eps = 1e-05
bfloat = jnp.bfloat16
single = jnp.float32


def shifted(value, axis, steps):
    count = lax.axis_size(axis)
    first, last = (max(0, -steps), min(count, count - steps))
    return lax.ppermute(value, axis, [(source, source + steps) for source in range(first, last)])


def norm_rows(residual, gain_vec, shift_vec):
    row_mean = jnp.mean(residual, axis=-1, keepdims=True)
    centred = residual - row_mean
    variance = jnp.mean(centred * centred, axis=-1, keepdims=True)
    return centred * lax.rsqrt(variance + norm_eps) * (1.0 + gain_vec) + shift_vec


def gelu_exact(pre_active):
    return jax.nn.gelu(pre_active, approximate=False)


def select_tree(flag_value, when_true, when_false):
    return jax.tree.map(
        lambda left_arr, right_arr: jnp.where(flag_value, left_arr, right_arr),
        when_true,
        when_false,
    )


def split_pieces(operand):
    if operand.dtype == bfloat:
        return (operand,)
    upper_part = operand.astype(bfloat)
    lower_part = (operand - upper_part.astype(single)).astype(bfloat)
    return (upper_part, lower_part)


def split_dot(form, left, right):
    left_pieces = split_pieces(left)
    right_pieces = split_pieces(right)
    total = None
    for left_no, left_piece in enumerate(left_pieces):
        for right_no, right_piece in enumerate(right_pieces):
            if left_no + right_no > 1:
                continue
            term = jnp.einsum(form, left_piece, right_piece, preferred_element_type=single)
            total = term if total is None else total + term
    return total


def sparse_layout(block_list, length):
    head_count, block_count = (block_list.shape[0], block_list.shape[1])
    chosen = jnp.concatenate(
        [jnp.zeros((head_count, block_count, 1), jnp.int32), block_list], axis=2
    )
    key_live = (jnp.arange(SEQ_LEN) < length).astype(single)
    picked_live = key_live.reshape(block_count, BLOCK)[chosen].reshape(head_count, block_count, -1)
    return (chosen, key_live, picked_live)


def pick_blocks(table_in, chosen):
    head_count, block_count = (chosen.shape[0], chosen.shape[1])
    blocks_in = table_in.reshape(head_count, block_count, BLOCK, table_in.shape[-1])
    taken_rows = jax.vmap(lambda one_table, index_rows: one_table[index_rows])(blocks_in, chosen)
    return taken_rows.reshape(head_count, block_count, -1, table_in.shape[-1])


def place_blocks(values_in, chosen):
    head_count, block_count, slot_count = chosen.shape
    parts_in = values_in.reshape(head_count, block_count, slot_count, BLOCK, values_in.shape[-1])
    zero_blocks = jnp.zeros((head_count, block_count, BLOCK, values_in.shape[-1]), single)
    placed = jax.vmap(lambda base_arr, index_rows, one_part: base_arr.at[index_rows].add(one_part))(
        zero_blocks, chosen, parts_in
    )
    return placed.reshape(head_count, SEQ_LEN, values_in.shape[-1])


def feature_of(vectors_low, features):
    feature_scale = HEAD ** (-0.25)
    vectors = vectors_low.astype(single)
    projected = split_dot("hld,hdf->hlf", vectors_low, features) * feature_scale
    return jnp.exp(
        projected
        - jnp.sum(vectors * vectors, axis=-1, keepdims=True) * (0.5 * feature_scale * feature_scale)
    )


def block_scores(query_blocks, picked_keys, picked_live):
    scores = jnp.einsum(
        "hnqd,hnkd->hnqk", query_blocks, picked_keys, preferred_element_type=single
    ) * HEAD ** (-0.5)
    return jnp.where(picked_live[:, :, None, :] > 0.5, scores, -1e30)


def attend_forward(queries, key_vecs, value_vecs, chosen, key_live, picked_live, features):
    head_count, block_count = (chosen.shape[0], chosen.shape[1])
    query_blocks = queries.reshape(head_count, block_count, BLOCK, HEAD)
    picked_keys = pick_blocks(key_vecs, chosen)
    picked_values = pick_blocks(value_vecs, chosen)
    scores = block_scores(query_blocks, picked_keys, picked_live)
    row_max = jnp.max(scores, axis=-1, keepdims=True)
    weights_raw = jnp.exp(scores - row_max) * picked_live[:, :, None, :]
    row_total = jnp.sum(weights_raw, axis=-1, keepdims=True)
    log_total = row_max + jnp.log(row_total)
    weights_low = (weights_raw / row_total).astype(bfloat)
    sparse_out = jnp.einsum(
        "hnqk,hnkd->hnqd", weights_low, picked_values, preferred_element_type=single
    )
    sparse_out = sparse_out.reshape(head_count, SEQ_LEN, HEAD)
    query_feats = feature_of(queries, features)
    key_feats = feature_of(key_vecs, features) * key_live[None, :, None]
    moments = split_dot("hlf,hld->hfd", key_feats, value_vecs)
    totals = jnp.sum(key_feats, axis=1)
    numerator = split_dot("hlf,hfd->hld", query_feats, moments)
    denominator = split_dot("hlf,hf->hl", query_feats, totals)
    perf_out = numerator / denominator[:, :, None]
    return (
        sparse_out + perf_out,
        (log_total, query_feats, key_feats, moments, totals, denominator, perf_out),
    )


def attend_backward(
    grad_heads, queries, key_vecs, value_vecs, chosen, picked_live, features, attn_keep
):
    log_total, query_feats, key_feats, moments, totals, denominator, perf_out = attn_keep
    head_count, block_count = (chosen.shape[0], chosen.shape[1])
    score_scale = HEAD ** (-0.5)
    query_blocks = queries.reshape(head_count, block_count, BLOCK, HEAD)
    grad_blocks = grad_heads.reshape(head_count, block_count, BLOCK, HEAD)
    picked_keys = pick_blocks(key_vecs, chosen)
    picked_values = pick_blocks(value_vecs, chosen)
    scores = block_scores(query_blocks, picked_keys, picked_live)
    weights_f = jnp.exp(scores - log_total) * picked_live[:, :, None, :]
    grad_weights = jnp.einsum(
        "hnqd,hnkd->hnqk", grad_blocks, picked_values, preferred_element_type=single
    )
    row_inner = jnp.sum(weights_f * grad_weights, axis=-1, keepdims=True)
    grad_scores = (weights_f * (grad_weights - row_inner)).astype(bfloat)
    grad_query = jnp.einsum(
        "hnqk,hnkd->hnqd", grad_scores, picked_keys, preferred_element_type=single
    )
    grad_query = grad_query.reshape(head_count, SEQ_LEN, HEAD) * score_scale
    grad_keys = place_blocks(
        jnp.einsum("hnqk,hnqd->hnkd", grad_scores, query_blocks, preferred_element_type=single)
        * score_scale,
        chosen,
    )
    grad_values = place_blocks(
        jnp.einsum(
            "hnqk,hnqd->hnkd", weights_f.astype(bfloat), grad_blocks, preferred_element_type=single
        ),
        chosen,
    )
    grad_float = grad_heads.astype(single)
    grad_numer = grad_float / denominator[:, :, None]
    grad_denom = -jnp.sum(grad_float * perf_out, axis=-1) / denominator
    grad_qfeat = (
        split_dot("hld,hfd->hlf", grad_numer, moments) + grad_denom[:, :, None] * totals[:, None, :]
    )
    grad_moments = split_dot("hlf,hld->hfd", query_feats, grad_numer)
    grad_totals = split_dot("hlf,hl->hf", query_feats, grad_denom)
    grad_kfeat = split_dot("hld,hfd->hlf", value_vecs, grad_moments) + grad_totals[:, None, :]
    grad_values = grad_values + split_dot("hlf,hfd->hld", key_feats, grad_moments)
    feature_scale = HEAD ** (-0.25)

    def feature_back(grad_feat, feats, vectors_low):
        grad_expo = grad_feat * feats
        direct = split_dot("hlf,hdf->hld", grad_expo, features) * feature_scale
        return direct - feature_scale * feature_scale * jnp.sum(
            grad_expo, axis=-1, keepdims=True
        ) * vectors_low.astype(single)

    grad_query = grad_query + feature_back(grad_qfeat, query_feats, queries)
    grad_keys = grad_keys + feature_back(grad_kfeat, key_feats, key_vecs)
    return (grad_query, grad_keys, grad_values)


def layer_forward(section_entry, length, layer_params, block_list, features):
    qkv_mat, qkv_bias, out_mat, up_mat, up_bias, down_mat, vectors = layer_params
    residual = section_entry.astype(single)
    normed = norm_rows(residual, vectors[0], vectors[1]).astype(bfloat)
    normed_all = lax.all_gather(normed, "tensor", axis=0, tiled=True)
    projected = (
        jnp.einsum("ld,dce->lce", normed_all, qkv_mat, preferred_element_type=single)
        + qkv_bias[None]
    )
    projected = projected.astype(bfloat)
    seq_len, part_width = (projected.shape[0], projected.shape[2])
    head_count = part_width // HEAD
    head_parts = projected.reshape(seq_len, 3, head_count, HEAD).transpose(1, 2, 0, 3)
    chosen, key_live, picked_live = sparse_layout(block_list, length)
    mixed_heads, attn_keep = attend_forward(
        head_parts[0], head_parts[1], head_parts[2], chosen, key_live, picked_live, features
    )
    mixed_low = mixed_heads.transpose(1, 0, 2).reshape(seq_len, part_width).astype(bfloat)
    row_block = mixed_low
    branch = lax.psum_scatter(
        jnp.dot(row_block, out_mat, preferred_element_type=single).astype(jnp.bfloat16),
        "tensor",
        scatter_dimension=0,
        tiled=True,
    ).astype(jnp.float32)
    hidden_res = residual + branch + vectors[4]
    normed_two = norm_rows(hidden_res, vectors[2], vectors[3]).astype(bfloat)
    normed_two_all = lax.all_gather(normed_two, "tensor", axis=0, tiled=True)
    pre_active = jnp.dot(normed_two_all, up_mat, preferred_element_type=single) + up_bias
    active = gelu_exact(pre_active).astype(bfloat)
    row_block = active
    result = (
        hidden_res
        + lax.psum_scatter(
            jnp.dot(row_block, down_mat, preferred_element_type=single).astype(jnp.bfloat16),
            "tensor",
            scatter_dimension=0,
            tiled=True,
        ).astype(jnp.float32)
        + vectors[5]
    )
    record = (
        residual,
        hidden_res,
        normed_all,
        head_parts,
        mixed_low,
        normed_two_all,
        pre_active,
        active,
        attn_keep,
        length,
    )
    return (result.astype(bfloat), record)


def layer_backward(grad_low, record, layer_params, block_list, features):
    qkv_mat, qkv_bias, out_mat, up_mat, up_bias, down_mat, vectors = layer_params
    (
        residual,
        hidden_res,
        normed_all,
        head_parts,
        mixed_low,
        normed_two_all,
        pre_active,
        active,
        attn_keep,
        length,
    ) = record
    seq_len, part_width = mixed_low.shape
    head_count = part_width // HEAD
    grad_output = grad_low.astype(single)
    grad_all = lax.all_gather(grad_low, "tensor", axis=0, tiled=True)
    grad_wdown = jnp.einsum("lf,ld->fd", active, grad_all, preferred_element_type=single)
    grad_active = jnp.einsum("ld,fd->lf", grad_all, down_mat, preferred_element_type=single)
    _, gelu_pull = jax.vjp(gelu_exact, pre_active)
    grad_upper = gelu_pull(grad_active)[0].astype(bfloat)
    grad_wup = jnp.einsum("ld,lf->df", normed_two_all, grad_upper, preferred_element_type=single)
    grad_bup = jnp.sum(grad_upper.astype(single), axis=0)
    row_block = grad_upper
    grad_normed_two = lax.psum_scatter(
        jnp.einsum("lf,df->ld", row_block, up_mat, preferred_element_type=single).astype(
            jnp.bfloat16
        ),
        "tensor",
        scatter_dimension=0,
        tiled=True,
    ).astype(jnp.float32)
    _, pull_two = jax.vjp(norm_rows, hidden_res, vectors[2], vectors[3])
    grad_hidden, grad_gain_two, grad_shift_two = pull_two(grad_normed_two)
    grad_hidden = grad_hidden + grad_output
    grad_hidden_low = grad_hidden.astype(bfloat)
    hidden_all = lax.all_gather(grad_hidden_low, "tensor", axis=0, tiled=True)
    grad_wout = jnp.einsum("le,ld->ed", mixed_low, hidden_all, preferred_element_type=single)
    grad_mixed = jnp.einsum("ld,ed->le", hidden_all, out_mat, preferred_element_type=single).astype(
        bfloat
    )
    grad_heads = grad_mixed.reshape(seq_len, head_count, HEAD).transpose(1, 0, 2)
    chosen, key_live, picked_live = sparse_layout(block_list, length)
    grad_query, grad_keys, grad_values = attend_backward(
        grad_heads,
        head_parts[0],
        head_parts[1],
        head_parts[2],
        chosen,
        picked_live,
        features,
        attn_keep,
    )
    grad_proj = (
        jnp.stack([grad_query, grad_keys, grad_values])
        .transpose(2, 0, 1, 3)
        .reshape(seq_len, 3, part_width)
        .astype(bfloat)
    )
    grad_wqkv = jnp.einsum("ld,lce->dce", normed_all, grad_proj, preferred_element_type=single)
    grad_bqkv = jnp.sum(grad_proj.astype(single), axis=0)
    row_block = grad_proj
    grad_normed = lax.psum_scatter(
        jnp.einsum("lce,dce->ld", row_block, qkv_mat, preferred_element_type=single).astype(
            jnp.bfloat16
        ),
        "tensor",
        scatter_dimension=0,
        tiled=True,
    ).astype(jnp.float32)
    _, pull_one = jax.vjp(norm_rows, residual, vectors[0], vectors[1])
    grad_resid, grad_gain_one, grad_shift_one = pull_one(grad_normed)
    grad_resid = grad_resid + grad_hidden
    weight_grads = (grad_wqkv, grad_bqkv, grad_wout, grad_wup, grad_bup, grad_wdown)
    vector_grads = jnp.stack(
        [
            grad_gain_one,
            grad_shift_one,
            grad_gain_two,
            grad_shift_two,
            jnp.sum(grad_hidden_low.astype(single), axis=0),
            jnp.sum(grad_output, axis=0),
        ]
    )
    return (grad_resid, weight_grads, vector_grads)


def shards(
    inputs,
    cotangent,
    lengths,
    blocks,
    feature_map,
    w_qkv,
    b_qkv,
    w_out,
    w_up,
    b_up,
    w_down,
    vector_params,
):
    section_no = lax.axis_index("section")
    is_first = section_no == 0
    is_last = section_no == lax.axis_size("section") - 1
    layer_params = (
        w_qkv[0],
        b_qkv[0].astype(single),
        w_out[0],
        w_up[0],
        b_up[0].astype(single),
        w_down[0],
        vector_params[0].astype(single),
    )
    block_list = blocks[0]
    features = feature_map[0]
    batch_count = inputs.shape[0]
    carried = jnp.zeros_like(inputs[0])
    records = []
    results = []
    for tick_no in range(batch_count + 1):
        batch_no = jnp.clip(tick_no - section_no, 0, batch_count - 1)
        section_entry = jnp.where(is_first, inputs[min(tick_no, batch_count - 1)], carried)
        result, record = layer_forward(
            section_entry, lengths[batch_no, 0], layer_params, block_list, features
        )
        records.append(record)
        results.append(result)
        if tick_no < batch_count:
            carried = shifted(result, "section", 1)
    section_outputs = jnp.stack(
        [
            jnp.where(is_first, results[batch_idx], results[batch_idx + 1])
            for batch_idx in range(batch_count)
        ]
    )[None]
    received = jnp.zeros_like(cotangent[0])
    grad_list = []
    local_sum = None
    vector_total = jnp.zeros((6, inputs.shape[2]), single)
    for tick_no in range(batch_count + 1):
        record = select_tree(
            is_last, records[min(tick_no + 1, batch_count)], records[max(tick_no - 1, 0)]
        )
        valid_flag = jnp.where(is_last, float(tick_no < batch_count), float(tick_no >= 1)).astype(
            single
        )
        grad_entry = jnp.where(is_last, cotangent[min(tick_no, batch_count - 1)], received)
        grad_resid, weight_grads, vector_grads = layer_backward(
            grad_entry, record, layer_params, block_list, features
        )
        weight_grads = tuple((valid_flag * addend for addend in weight_grads))
        vector_total = vector_total + valid_flag * vector_grads
        local_sum = (
            weight_grads
            if local_sum is None
            else tuple((summed + addend for summed, addend in zip(local_sum, weight_grads)))
        )
        grad_list.append(grad_resid)
        if tick_no < batch_count:
            received = shifted(grad_resid.astype(bfloat), "section", -1)
    final_grads = (
        lax.psum_scatter(
            local_sum[0].astype(jnp.bfloat16), "dp", scatter_dimension=0, tiled=True
        ).astype(jnp.float32),
        lax.psum_scatter(
            local_sum[1].astype(jnp.bfloat16), "dp", scatter_dimension=1, tiled=True
        ).astype(jnp.float32),
        lax.psum_scatter(
            local_sum[2].astype(jnp.bfloat16), "dp", scatter_dimension=1, tiled=True
        ).astype(jnp.float32),
        lax.psum_scatter(
            local_sum[3].astype(jnp.bfloat16), "dp", scatter_dimension=0, tiled=True
        ).astype(jnp.float32),
        lax.psum_scatter(
            local_sum[4].astype(jnp.bfloat16), "dp", scatter_dimension=0, tiled=True
        ).astype(jnp.float32),
        lax.psum_scatter(
            local_sum[5].astype(jnp.bfloat16), "dp", scatter_dimension=1, tiled=True
        ).astype(jnp.float32),
    )
    input_grads = jnp.stack(
        [
            jnp.where(is_first, grad_list[batch_idx + 1], grad_list[batch_idx])
            for batch_idx in range(batch_count)
        ]
    )[None]
    grad_vectors = lax.psum_scatter(
        vector_total, ("tensor", "dp"), scatter_dimension=1, tiled=True
    )[None]
    grad_wqkv, grad_bqkv, grad_wout, grad_wup, grad_bup, grad_wdown = final_grads
    return (
        section_outputs,
        input_grads,
        grad_wqkv[None],
        grad_bqkv[None],
        grad_wout[None],
        grad_wup[None],
        grad_bup[None],
        grad_wdown[None],
        grad_vectors,
    )


def solution(mesh):
    placed = (
        P(None, ("dp", "tensor"), None),
        P(None, ("dp", "tensor"), None),
        P(None, "dp"),
        P("section", "tensor", None, None),
        P("section", "tensor", None, None),
        P("section", None, None, "tensor"),
        P("section", None, "tensor"),
        P("section", "tensor", None),
        P("section", None, "tensor"),
        P("section", "tensor"),
        P("section", "tensor", None),
        P("section", None, None),
    )
    sizes = tuple(mesh.shape[axis] for axis in ALL_AXES)
    if sizes[0] == 2 and sizes[1] == 2 and sizes[2] % 2 == 0:
        body = functools.partial(chip_shards, sizes)
    else:
        body = shards
    return jax.shard_map(
        body,
        mesh=mesh,
        in_specs=placed,
        out_specs=(
            P("section", None, ("dp", "tensor"), None),
            P("section", None, ("dp", "tensor"), None),
            P("section", "dp", None, "tensor"),
            P("section", None, ("tensor", "dp")),
            P("section", "tensor", "dp"),
            P("section", "dp", "tensor"),
            P("section", ("tensor", "dp")),
            P("section", "tensor", "dp"),
            P("section", None, ("tensor", "dp")),
        ),
        check_vma=False,
    )
```
